32 devices in a mesh: dp: 8 (over z, y), seq: 4 (over x, core).
Axes of the slice: x: 2, y: 2, z: 4, core: 2. Of those that a mesh axis runs over, the one named last changes fastest.
Arguments:
- frames: bfloat16 [8, 1536, 1024], P('dp', 'seq'), may hold values from -6 to 6
- output_gradient: bfloat16 [8, 1536, 1024], P('dp', 'seq'), may hold values from -6 to 6
- segment_lengths: int32 [8, 4], P('dp'), may hold values from 1 to 1533, as said below
- time_index: int32 [8, 4], P('dp'), may hold values from 0 to 999
- query_weight: bfloat16 [1024, 1024], P(('dp', 'seq')), may hold values from -0.1875 to 0.1875
- query_bias: bfloat16 [1024], P(('dp', 'seq')), may hold values from -3 to 3
- key_weight: bfloat16 [1024, 1024], P(('dp', 'seq')), may hold values from -0.1875 to 0.1875
- key_bias: bfloat16 [1024], P(('dp', 'seq')), may hold values from -3 to 3
- value_weight: bfloat16 [1024, 1024], P(('dp', 'seq')), may hold values from -0.1875 to 0.1875
- value_bias: bfloat16 [1024], P(('dp', 'seq')), may hold values from -3 to 3
- output_projection: bfloat16 [1024, 1024], P(('dp', 'seq')), may hold values from -2.5 to 2.5
- output_bias: bfloat16 [1024], P(('dp', 'seq')), may hold values from -3 to 3
- up_weight: bfloat16 [1024, 2048], P(('dp', 'seq')), may hold values from -0.1875 to 0.1875
- up_bias: bfloat16 [2048], P(('dp', 'seq')), may hold values from -3 to 3
- down_weight: bfloat16 [2048, 1024], P(('dp', 'seq')), may hold values from -0.125 to 0.125
- down_bias: bfloat16 [1024], P(('dp', 'seq')), may hold values from -3 to 3
- modulation_weight: bfloat16 [1024, 6144], P(('dp', 'seq')), may hold values from -0.1875 to 0.1875
- modulation_bias: bfloat16 [6144], P(('dp', 'seq')), may hold values from -3 to 3
Outputs:
- layer_output: bfloat16 [8, 1536, 1024], P('dp', 'seq')
- frames_grad: bfloat16 [8, 1536, 1024], P('dp', 'seq')
- query_weight_grad: float32 [1024, 1024], P(('dp', 'seq'))
- query_bias_grad: float32 [1024], P(('dp', 'seq'))
- key_weight_grad: float32 [1024, 1024], P(('dp', 'seq'))
- key_bias_grad: float32 [1024], P(('dp', 'seq'))
- value_weight_grad: float32 [1024, 1024], P(('dp', 'seq'))
- value_bias_grad: float32 [1024], P(('dp', 'seq'))
- output_weight_grad: float32 [1024, 1024], P(('dp', 'seq'))
- output_bias_grad: float32 [1024], P(('dp', 'seq'))
- up_weight_grad: float32 [1024, 2048], P(('dp', 'seq'))
- up_bias_grad: float32 [2048], P(('dp', 'seq'))
- down_weight_grad: float32 [2048, 1024], P(('dp', 'seq'))
- down_bias_grad: float32 [1024], P(('dp', 'seq'))
- modulation_weight_grad: float32 [1024, 6144], P(('dp', 'seq'))
- modulation_bias_grad: float32 [6144], P(('dp', 'seq'))
The draws below stay inside these ranges and needn't reach their ends.
Inputs may be any that keep to these rules, and one draw needn't show every extreme that they name: `segment_lengths`: in each packed row the 4 lengths sum to 1536; one utterance is longer than 1152, the others shorter than 96; in one row of every draw the others have a single frame each.
All inputs are finite; a program needn't handle non-finite values.
Results may differ from the reference program's by a relative error of at most 0.035.
Values may be sent and summed in bfloat16 or wider, within the bound.
A program may use at most 192 MiB of HBM per device.

```python
import math
import jax
import jax.numpy as jnp
from jax import lax

HEADS = 16
HEAD_DIM = 64
MODEL_WIDTH = 1024
FF = 2048
SEGS = 4
SPAN = 384
ROWS_DEV = 1
ROW_FRAMES = 1536
PACKED_ROWS = 8
N_DP = 8


def draw_segment_lengths(key, part):
    key = jax.random.fold_in(key, 7)
    short_key, long_key, chosen_key = jax.random.split(key, 3)
    shorts = jax.random.randint(short_key, (PACKED_ROWS, SEGS), 1, SPAN // SEGS)
    longest_utterance = jax.random.randint(long_key, (PACKED_ROWS, 1), 0, SEGS)
    chosen = jax.random.randint(chosen_key, (), 0, PACKED_ROWS)
    row_numbers = jnp.arange(PACKED_ROWS)[:, None]
    shorts = jnp.where(row_numbers == chosen, 1, shorts)
    frame_places = jnp.arange(SEGS)[None, :]
    other_rows = jnp.where(frame_places == longest_utterance, 0, shorts)
    remaining_frames = jnp.sum(other_rows, axis=1, keepdims=True)
    return jnp.where(frame_places == longest_utterance, ROW_FRAMES - remaining_frames, other_rows).astype(jnp.int32)


def with_ends(values, stream_key, least, top_value):
    place = [jax.random.randint(jax.random.fold_in(stream_key, axis), (), 0, length) for axis, length in enumerate(values.shape)]
    widest = values.shape.index(max(values.shape))
    beside = place[:widest] + [(place[widest] + 1) % values.shape[widest]] + place[widest + 1:]
    return values.at[tuple(place)].set(least).at[tuple(beside)].set(top_value)


def block_scale(stream_key, extent, shards, least, largest):
    loudness, own = 1.0, jax.random.fold_in(stream_key, 6)
    for position, parts in shards:
        heights = jnp.exp(jax.random.uniform(jax.random.fold_in(own, position), (parts,), jnp.float32, least / len(shards), largest / len(shards)))
        loudness = loudness * jnp.repeat(heights, extent[position] // parts).reshape([-1 if axis == position else 1 for axis in range(len(extent))])
    return loudness


def normal_values(stream_key, shape, deviation, bound, cuts=(), kind=jnp.bfloat16):
    array = deviation * jax.random.normal(stream_key, shape, jnp.float32)
    if cuts:
        array = array * block_scale(stream_key, shape, cuts, -0.22, 0.18)
    return jnp.clip(array, -bound, bound).astype(kind)


def setup_inputs(seed: int = 0) -> dict:
    streams_of = jax.random.split(jax.random.key(seed), 19)
    frames = normal_values(streams_of[0], (PACKED_ROWS, ROW_FRAMES, MODEL_WIDTH), 1.0, 6.0, ((0, 8), (1, 4)))
    output_gradient = normal_values(streams_of[1], (PACKED_ROWS, ROW_FRAMES, MODEL_WIDTH), 1.0, 6.0, ((0, 8), (1, 4)))
    segment_lengths = draw_segment_lengths(jax.random.fold_in(streams_of[18], 71), 0)
    time_index = with_ends(jax.random.randint(streams_of[3], (PACKED_ROWS, SEGS), 0, 1000), jax.random.fold_in(streams_of[3], 1), 0, 999).astype(jnp.int32)
    query_weight = normal_values(streams_of[4], (MODEL_WIDTH, MODEL_WIDTH), MODEL_WIDTH ** -0.5, 0.1875, ((0, 32),))
    query_bias = normal_values(streams_of[5], (MODEL_WIDTH,), 0.5, 3.0, ((0, 32),))
    key_weight = normal_values(streams_of[6], (MODEL_WIDTH, MODEL_WIDTH), MODEL_WIDTH ** -0.5, 0.1875, ((0, 32),))
    key_bias = normal_values(streams_of[7], (MODEL_WIDTH,), 0.5, 3.0, ((0, 32),))
    value_weight = normal_values(streams_of[8], (MODEL_WIDTH, MODEL_WIDTH), MODEL_WIDTH ** -0.5, 0.1875, ((0, 32),))
    value_bias = normal_values(streams_of[9], (MODEL_WIDTH,), 0.5, 3.0, ((0, 32),))
    output_projection = normal_values(streams_of[10], (MODEL_WIDTH, MODEL_WIDTH), (max(1, 8 * MODEL_WIDTH // ROW_FRAMES)) ** -0.5, 2.5, ((0, 32),))
    output_bias = normal_values(streams_of[11], (MODEL_WIDTH,), 0.5, 3.0, ((0, 32),))
    up_weight = normal_values(streams_of[12], (MODEL_WIDTH, FF), MODEL_WIDTH ** -0.5, 0.1875, ((0, 32),))
    up_bias = normal_values(streams_of[13], (FF,), 0.5, 3.0, ((0, 32),))
    down_weight = normal_values(streams_of[14], (FF, MODEL_WIDTH), FF ** -0.5, 0.125, ((0, 32),))
    down_bias = normal_values(streams_of[15], (MODEL_WIDTH,), 0.5, 3.0, ((0, 32),))
    modulation_weight = normal_values(streams_of[16], (MODEL_WIDTH, 6 * MODEL_WIDTH), MODEL_WIDTH ** -0.5, 0.1875, ((0, 32),))
    modulation_bias = normal_values(streams_of[17], (6 * MODEL_WIDTH,), 0.5, 3.0, ((0, 32),))
    return {"frames": frames, "output_gradient": output_gradient, "segment_lengths": segment_lengths, "time_index": time_index, "query_weight": query_weight, "query_bias": query_bias, "key_weight": key_weight, "key_bias": key_bias, "value_weight": value_weight, "value_bias": value_bias, "output_projection": output_projection, "output_bias": output_bias, "up_weight": up_weight, "up_bias": up_bias, "down_weight": down_weight, "down_bias": down_bias, "modulation_weight": modulation_weight, "modulation_bias": modulation_bias}


EPSILON = 1e-06
NEGATIVE = -1e+30
HIGHEST = lax.Precision.HIGHEST

@jax.custom_vjp
def low(v):
    return lax.optimization_barrier(v.astype(jnp.bfloat16)).astype(jnp.float32)

@jax.custom_vjp
def low_back(v):
    return v

def low_keep(v):
    return (low(v), None)

def low_pass(kept, grad):
    return (grad,)

def back_keep(v):
    return (v, None)

def back_low(kept, grad):
    return (low(grad),)
low.defvjp(low_keep, low_pass)
low_back.defvjp(back_keep, back_low)

def modulated_norm(values, shift_part, scale_part):
    center = lax.optimization_barrier(jnp.mean(values, axis=-1, keepdims=True))
    centered = values - center
    variance = lax.optimization_barrier(jnp.mean(centered * centered, axis=-1, keepdims=True))
    return centered * lax.rsqrt(variance + EPSILON) * (1.0 + scale_part) + shift_part

def rotate(values, cosines, sines_table):
    shaped = values.reshape(values.shape[:-1] + (values.shape[-1] // HEAD_DIM, HEAD_DIM))
    first_half = shaped[..., :HEAD_DIM // 2]
    second_half = shaped[..., HEAD_DIM // 2:]
    cosine = cosines[..., None, :]
    sine_part = sines_table[..., None, :]
    turned = jnp.concatenate([first_half * cosine - second_half * sine_part, second_half * cosine + first_half * sine_part], axis=-1)
    return turned.reshape(values.shape)

def gelu_tanh(values):
    return jax.nn.gelu(values, approximate=True)

def time_features(time_index):
    halfway = MODEL_WIDTH // 2
    frequency = jnp.exp(jnp.arange(halfway, dtype=jnp.float32) * (-math.log(10000.0) / halfway))
    angles = time_index.astype(jnp.float32)[..., None] * frequency
    return jnp.concatenate([jnp.sin(angles), jnp.cos(angles)], axis=-1)

def segment_starts(segment_lengths):
    return (jnp.cumsum(segment_lengths, axis=1) - segment_lengths).astype(jnp.int32)

def segment_numbers(segment_lengths, frame_positions):
    starts = segment_starts(segment_lengths)
    inside = (frame_positions[None, :, None] >= starts[:, None, :]).astype(jnp.int32)
    return (lax.optimization_barrier(jnp.sum(inside, axis=2)) - 1).astype(jnp.int32)

def segment_layout(segment_lengths, frame_positions):
    starts = segment_starts(segment_lengths)
    segment = segment_numbers(segment_lengths, frame_positions)
    onehot = (segment[..., None] == jnp.arange(SEGS, dtype=jnp.int32)).astype(jnp.float32)
    offset = lax.optimization_barrier(jnp.sum(onehot * starts[:, None, :].astype(jnp.float32), axis=2))
    relative = frame_positions[None, :].astype(jnp.float32) - offset
    return (onehot, relative)

def rope_tables(relative):
    halfway = HEAD_DIM // 2
    frequency = jnp.exp(jnp.arange(halfway, dtype=jnp.float32) * (-math.log(10000.0) / halfway))
    angles = relative[..., None] * frequency
    return (jnp.cos(angles), jnp.sin(angles))

def project(values, matrix, offset):
    return jnp.einsum('rld,de->rle', values, matrix, precision=HIGHEST) + offset

def attend(queries, keys, values, segment):
    row_length = queries.shape[1]
    block_rows = min(512, row_length)
    block_count = row_length // block_rows
    scaling = HEAD_DIM ** (-0.5)

    def one_row(row_inputs):
        query_row, key_row, value_row, segment_row = row_inputs

        def one_block(block_inputs):
            query_block, segment_block = block_inputs
            scores = low_back(jnp.einsum('bhd,khd->hbk', query_block, key_row, precision=HIGHEST) * scaling)
            scores = jnp.where((segment_block[:, None] == segment_row[None, :])[None], scores, NEGATIVE)
            highest = lax.optimization_barrier(jnp.max(scores, axis=2, keepdims=True))
            weights = jnp.exp(scores - highest)
            probabilities = low(weights / lax.optimization_barrier(jnp.sum(weights, axis=2, keepdims=True)))
            return jnp.einsum('hbk,khd->bhd', probabilities, value_row, precision=HIGHEST)
        query_blocks = query_row.reshape((block_count, block_rows) + query_row.shape[1:])
        segment_blocks = segment_row.reshape(block_count, block_rows)
        mixed_heads = lax.map(jax.checkpoint(one_block), (query_blocks, segment_blocks))
        return mixed_heads.reshape(query_row.shape)
    return lax.map(jax.checkpoint(one_row), (queries, keys, values, segment))

def layer(inputs, params, time_low, onehot, segment, cosines, sines_table):
    query_weight, query_bias, key_weight, key_bias, value_weight, value_bias, output_projection, output_bias, up_weight, up_bias, down_weight, down_bias, modulation_weight, modulation_bias = params
    modulation = jnp.einsum('rsd,dc->rsc', time_low, modulation_weight, precision=HIGHEST) + modulation_bias
    per_frame = jnp.einsum('rls,rsc->rlc', onehot, modulation, precision=HIGHEST)
    shift_one, scale_one, gate_one, shift_two, scale_two, gate_two = jnp.split(per_frame, 6, axis=-1)
    normed = low(modulated_norm(inputs, shift_one, scale_one))
    query_pre = low_back(project(normed, query_weight, query_bias))
    key_pre = low_back(project(normed, key_weight, key_bias))
    value_rows = low(low_back(project(normed, value_weight, value_bias)))
    query_rows = low(low_back(rotate(query_pre, cosines, sines_table)))
    key_rows = low(low_back(rotate(key_pre, cosines, sines_table)))
    head_shape = inputs.shape[:2] + (HEADS, HEAD_DIM)
    mixed_heads = attend(query_rows.reshape(head_shape), key_rows.reshape(head_shape), value_rows.reshape(head_shape), segment)
    attention = low(low_back(mixed_heads.reshape(inputs.shape)))
    branch = low_back(project(attention, output_projection, output_bias))
    middle = inputs + gate_one * branch
    normed_two = low(modulated_norm(middle, shift_two, scale_two))
    hidden = low_back(project(normed_two, up_weight, up_bias))
    activated = low(gelu_tanh(hidden))
    branch_two = low_back(project(activated, down_weight, down_bias))
    return middle + gate_two * branch_two

def reference(frames, output_gradient, segment_lengths, time_index, query_weight, query_bias, key_weight, key_bias, value_weight, value_bias, output_projection, output_bias, up_weight, up_bias, down_weight, down_bias, modulation_weight, modulation_bias):
    params = tuple((member.astype(jnp.float32) for member in (query_weight, query_bias, key_weight, key_bias, value_weight, value_bias, output_projection, output_bias, up_weight, up_bias, down_weight, down_bias, modulation_weight, modulation_bias)))
    frame_positions = jnp.arange(ROW_FRAMES, dtype=jnp.int32)
    group_frames = frames.reshape((N_DP, ROWS_DEV) + frames.shape[1:])
    group_cotangent = output_gradient.reshape((N_DP, ROWS_DEV) + frames.shape[1:])
    group_lengths = segment_lengths.reshape(N_DP, ROWS_DEV, SEGS)
    group_time = time_index.reshape(N_DP, ROWS_DEV, SEGS)

    def one_group(running, group_inputs):
        part_frames, part_cotangent, part_lengths, part_time = group_inputs
        segment = segment_numbers(part_lengths, frame_positions)
        onehot, relative = segment_layout(part_lengths, frame_positions)
        cosines, sines_table = rope_tables(relative)
        time_low = low(jax.nn.silu(time_features(part_time)))

        def forward(inputs, weights_tuple):
            return layer(inputs, weights_tuple, time_low, onehot, segment, cosines, sines_table)
        result, pullback = jax.vjp(forward, part_frames.astype(jnp.float32), params)
        grad_inputs, grad_params = pullback(part_cotangent.astype(jnp.float32))
        running = tuple((running_sum + member for running_sum, member in zip(running, grad_params)))
        return (running, (result.astype(jnp.bfloat16), grad_inputs.astype(jnp.bfloat16)))
    initial = tuple((jnp.zeros(member.shape, jnp.float32) for member in params))
    totals, (outputs, gradients) = lax.scan(one_group, initial, (group_frames, group_cotangent, group_lengths, group_time))
    return (outputs.reshape(frames.shape), gradients.reshape(frames.shape), totals[0], totals[1], totals[2], totals[3], totals[4], totals[5], totals[6], totals[7], totals[8], totals[9], totals[10], totals[11], totals[12], totals[13])
```

```python
from functools import partial
import math

import jax
import jax.numpy as jnp
from jax import lax
from jax.experimental import pallas as pl
from jax.experimental.pallas import tpu as pltpu
from jax.sharding import PartitionSpec as P

HEAD_DIM = 64
MODEL_WIDTH = 1024
SEGS = 4
EPSILON = 1e-06
NEGATIVE = -1e30
HIGHEST = lax.Precision.HIGHEST
F32 = jnp.float32
BF16 = jnp.bfloat16
LANES = 128


class Mover:
    def __init__(self, send_sems, recv_sems, local_sems):
        self.send_sems, self.recv_sems, self.local_sems = send_sems, recv_sems, local_sems
        self.count = self.local_count = 0
        self.sent = []

    def send(self, source, target, device):
        slot = self.count
        self.count += 1
        copy = pltpu.make_async_remote_copy(
            src_ref=source,
            dst_ref=target,
            send_sem=self.send_sems.at[slot],
            recv_sem=self.recv_sems.at[slot],
            device_id=device,
            device_id_type=pl.DeviceIdType.MESH,
        )
        copy.start()
        self.sent.append(copy)
        return copy

    def local(self, source, target):
        slot = self.local_count
        self.local_count += 1
        copy = pltpu.make_async_copy(source, target, self.local_sems.at[slot])
        copy.start()
        return copy

    def finish(self):
        for copy in self.sent:
            copy.wait_send()


class Place:
    def __init__(self, depth):
        dp, seq = lax.axis_index("dp"), lax.axis_index("seq")
        self.depth = depth
        self.z, self.y = dp // 2, dp % 2
        self.x, self.c = seq // 2, seq % 2
        self.seq = seq
        self.index = dp * 4 + seq

    def at(self, z, y, x, c):
        return {"dp": z * 2 + y, "seq": x * 2 + c}

    def core(self):
        return self.at(self.z, self.y, self.x, 1 - self.c)

    def across_x(self):
        return self.at(self.z, self.y, 1 - self.x, self.c)

    def across_y(self):
        return self.at(self.z, 1 - self.y, self.x, self.c)

    def ahead(self, step):
        return (self.z + step) % self.depth

    def along_z(self, step):
        return self.at(self.ahead(step), self.y, self.x, self.c)

    def row_peer(self, step):
        return {"dp": self.z * 2 + self.y, "seq": (self.seq + step) % 4}

    def enter(self):
        barrier = pltpu.get_barrier_semaphore()
        peers = [self.row_peer(step) for step in (1, 2, 3)] + [self.across_y()]
        peers += [self.along_z(step) for step in range(1, self.depth)]
        for peer in peers:
            pl.semaphore_signal(barrier, 1, device_id=peer, device_id_type=pl.DeviceIdType.MESH)
        pl.semaphore_wait(barrier, len(peers))


def lanes_of(shape, axis=1):
    return lax.broadcasted_iota(jnp.int32, shape, axis)


def frame_segments(lens, first_row, rows, width):
    position = lanes_of((rows, width), 0) + first_row
    first, second, third = lens[0, 0], lens[0, 0] + lens[0, 1], lens[0, 0] + lens[0, 1] + lens[0, 2]
    segment = (
        (position >= first).astype(jnp.int32)
        + (position >= second).astype(jnp.int32)
        + (position >= third).astype(jnp.int32)
    )
    start = jnp.where(
        segment == 0, 0, jnp.where(segment == 1, first, jnp.where(segment == 2, second, third))
    )
    return segment, position - start


def three_parts(values):
    high = values.astype(BF16).astype(F32)
    rest = values - high
    middle = rest.astype(BF16).astype(F32)
    return high, middle, (rest - middle).astype(BF16).astype(F32)


def swap_halves(values, lane):
    return jnp.where(
        lane % HEAD_DIM < HEAD_DIM // 2, pltpu.roll(values, 96, 1), pltpu.roll(values, 32, 1)
    )


def head_only(values, lane, head):
    return jnp.where((lane >= HEAD_DIM) == bool(head), values.astype(F32), 0.0).astype(BF16)


def across(left, right):
    return lax.dot_general(left, right, (((1,), (1,)), ((), ())), preferred_element_type=F32)


def product(left, right):
    return jnp.dot(left, right, preferred_element_type=F32)


def forward_kernel(
    depth,
    lens, times, frames, biases, wq, wk, wv, wo, up, down, mw,
    att, oh, qs, ks, vs, lse, normed, wg, mods, cosr, sinr, bb, low, wo_all, up_all, down_all,
    xall, mwst, tb, part, recva, suma, recvb, sumb, recvc, sumc, recvd, modh, bmat, mod3, qbias,
    ka, va, qaug, send_sems, recv_sems, local_sems,
):
    here = Place(depth)
    z, y, x, c, g = here.z, here.y, here.x, here.c, here.seq
    span = frames.shape[0]
    rows_all = span * 4
    move = Mover(send_sems, recv_sems, local_sems)
    steps_z = range(1, depth)

    row = lanes_of((16, LANES), 0) % 4
    own_times = jnp.where(
        row == 0, times[0, 0], jnp.where(row == 1, times[0, 1], jnp.where(row == 2, times[0, 2], times[0, 3]))
    )
    tb[z, y] = own_times.astype(F32)
    bb[z, y, x, c] = biases[...]
    weights = (wq, wk, wv)
    own_width = wg.shape[-1]
    locals_first = [
        move.local(weights[j].at[:, pl.ds(pl.multiple_of(g * own_width, LANES), own_width)], wg.at[j, z, y, g])
        for j in range(3)
    ]
    strip = mw.shape[1] // 4
    local_mw = [
        move.local(mw.at[:, pl.ds(j * strip, strip)], mwst.at[pl.ds(j * 32, 32)]) for j in range(4)
    ]
    local_frames = move.local(frames, xall.at[g])
    here.enter()

    times_z = [move.send(tb.at[z, y], tb.at[z, y], here.along_z(k)) for k in steps_z]
    bias_z = [move.send(bb.at[z, y, x, c], bb.at[z, y, x, c], here.along_z(k)) for k in steps_z]
    qkv_row = []
    for j in range(3):
        for k in (1, 2, 3):
            peer = (g + k) % 4
            qkv_row.append(
                move.send(
                    weights[j].at[:, pl.ds(pl.multiple_of(peer * own_width, LANES), own_width)],
                    wg.at[j, z, y, g],
                    here.row_peer(k),
                )
            )
    frames_x = move.send(frames, xall.at[g], here.across_x())
    frames_core = move.send(frames, xall.at[g], here.core())
    for copy in times_z:
        copy.wait_recv()
    times_y = move.send(tb.at[:, y], tb.at[:, y], here.across_y())
    for copy in locals_first:
        copy.wait()
    for copy in qkv_row:
        copy.wait_recv()
    qkv_z = [
        [move.send(wg.at[j, z, y], wg.at[j, z, y], here.along_z(k)) for k in steps_z] for j in range(3)
    ]
    for copy in bias_z:
        copy.wait_recv()
    bias_y = move.send(bb.at[:, y, x, c], bb.at[:, y, x, c], here.across_y())

    times_y.wait_recv()
    lane = lanes_of((16 * 2 * depth, LANES))
    row = lanes_of((16 * 2 * depth, LANES), 0)
    feature = here.index * 32 + lane % 32
    halfway = MODEL_WIDTH // 2
    frequency = jnp.exp((feature % halfway).astype(F32) * (-math.log(10000.0) / halfway))
    angle = tb[...].reshape(16 * 2 * depth, LANES) * frequency
    wave = jnp.where(feature < halfway, jnp.sin(angle), jnp.cos(angle))
    gated = wave / (1.0 + jnp.exp(-wave))
    low[...] = jnp.where(lane // 32 == (row % 16) // 4, gated, 0.0).astype(BF16)
    for copy in local_mw:
        copy.wait()
    half = strip // 2
    for side in range(2):
        share = product(low[...], mwst[:, side * half : (side + 1) * half])
        part[side] = share.astype(BF16).reshape(depth, 2, 16, half)
    mod_core = move.send(part.at[1 - c], recva, here.core())
    bias_y.wait_recv()
    bias_x = move.send(bb.at[:, :, x, c], bb.at[:, :, x, c], here.across_x())

    block = 128

    def tables(step, carry):
        rows = pl.ds(pl.multiple_of(step * block, block), block)
        segment, relative = frame_segments(lens, step * block, block, LANES)
        lane = lanes_of((block, LANES))
        quarter = HEAD_DIM // 2
        frequency = jnp.exp((lane % quarter).astype(F32) * (-math.log(10000.0) / quarter))
        angle = relative.astype(F32) * frequency
        cosr[rows, :] = jnp.cos(angle)
        sine = jnp.sin(angle)
        sinr[rows, :] = jnp.where(lane % HEAD_DIM < quarter, -sine, sine)
        same = segment == lane
        qaug[rows, :] = jnp.where((lane < SEGS) & jnp.logical_not(same), NEGATIVE, 0.0).astype(BF16)
        keyside = jnp.where((lane < SEGS) & same, 1.0, jnp.where((lane >= 4) & (lane < 7), 1.0, 0.0))
        for pair in range(2):
            ka[pair, rows, LANES:] = keyside.astype(BF16)
            va[pair, rows, LANES:] = jnp.where(lane < 3, 1.0, 0.0).astype(BF16)
        return carry

    lax.fori_loop(0, rows_all // (2 * block), tables, 0)
    mod_core.wait_recv()
    suma[...] = (part[c].astype(F32) + recva[...].astype(F32)).astype(BF16)
    mod_y = move.send(suma.at[:, 1 - y], recvb, here.across_y())
    bias_x.wait_recv()
    bias_core = move.send(bb.at[:, :, :, c], bb.at[:, :, :, c], here.core())
    lax.fori_loop(rows_all // (2 * block), rows_all // block, tables, 0)
    mod_y.wait_recv()
    sumb[...] = (suma[:, y].astype(F32) + recvb[...].astype(F32)).astype(BF16)
    mod_z = [move.send(sumb.at[here.ahead(k)], recvc.at[k - 1], here.along_z(k)) for k in steps_z]
    qkv_y = []
    for j in range(3):
        for copy in qkv_z[j]:
            copy.wait_recv()
        qkv_y.append(move.send(wg.at[j, :, y], wg.at[j, :, y], here.across_y()))
    total = sumb[z].astype(F32)
    for k in steps_z:
        mod_z[k - 1].wait_recv()
        total = total + recvc[k - 1].astype(F32)
    sumc[...] = total
    mod_x = move.send(sumc, recvd, here.across_x())

    def first_leg(source, target):
        own = move.local(source, target.at[z, y, x, c])
        sends = [move.send(source, target.at[z, y, x, c], here.along_z(k)) for k in steps_z]
        return own, sends

    legs = {}
    wo_top, wo_low = wo.at[pl.ds(0, 16)], wo.at[pl.ds(16, 16)]
    wo_all_top, wo_all_low = wo_all.at[:, :, :, :, pl.ds(0, 16)], wo_all.at[:, :, :, :, pl.ds(16, 16)]
    flows = [(wo_top, wo_all_top, 0), (wo_low, wo_all_low, 1), (up, up_all, 0), (down, down_all, 1)]
    for number, (source, target, _) in enumerate(flows):
        legs[number] = first_leg(source, target)

    def second_leg(number):
        _, target, order = flows[number]
        own, sends = legs[number]
        own.wait()
        for copy in sends:
            copy.wait_recv()
        peer = here.across_x() if order else here.across_y()
        legs[number] = move.send(target.at[:, y, x, c], target.at[:, y, x, c], peer)

    def third_leg(number):
        _, target, order = flows[number]
        legs[number].wait_recv()
        if order:
            legs[number] = move.send(target.at[:, y, :, c], target.at[:, y, :, c], here.across_y())
        else:
            legs[number] = move.send(target.at[:, :, x, c], target.at[:, :, x, c], here.across_x())

    def fourth_leg(number):
        _, target, _ = flows[number]
        legs[number].wait_recv()
        legs[number] = move.send(target.at[:, :, :, c], target.at[:, :, :, c], here.core())

    bias_core.wait_recv()
    bmat[...] = bb[...].reshape(16 * 2 * depth * 2, LANES).astype(BF16)

    place = lanes_of((LANES, own_width), 0)
    column = lanes_of((LANES, own_width))
    spread = jnp.where(column % 32 == place, 1.0, 0.0).astype(BF16)
    held = product(bmat[pl.ds(pl.multiple_of(g * 64, 64), 64), :], spread)
    brow, bcol = lanes_of((64, own_width), 0), lanes_of((64, own_width))
    for j in range(3):
        mine = (brow % 8 == j) & (brow // 8 == bcol // 32)
        qbias[j : j + 1, :] = jnp.sum(jnp.where(mine, held, 0.0), axis=0, keepdims=True)

    frames_x.wait_recv()
    frames_on = move.send(xall.at[(g + 2) % 4], xall.at[(g + 2) % 4], here.core())
    mod_x.wait_recv()
    modh[c] = sumc[...] + recvd[...]
    mod_last = move.send(modh.at[c], modh.at[c], here.core())

    place = lanes_of((LANES, half), 0)
    column = lanes_of((LANES, half))
    spread_a = jnp.where(column % 192 == place, 1.0, 0.0).astype(BF16)
    spread_b = jnp.where(column % 192 == place + LANES, 1.0, 0.0).astype(BF16)
    brow, bcol = lanes_of((32, half), 0), lanes_of((32, half))
    mod_last.wait_recv()
    for q in range(8):
        rows = bmat[q * 32 : (q + 1) * 32, :]
        inside = brow // 8 == bcol // 192
        terms = jnp.where(inside & (brow % 8 == 6), product(rows, spread_a), 0.0)
        terms = terms + jnp.where(inside & (brow % 8 == 7), product(rows, spread_b), 0.0)
        offset = jnp.sum(terms, axis=0, keepdims=True)
        j, side = q // 2, q % 2
        mods[0:4, q * half : (q + 1) * half] = modh[side, 4 * j : 4 * j + 4, :] + offset
    mods[4:8, :] = jnp.zeros((4, mods.shape[1]), F32)
    high, middle, rest = three_parts(mods[0:4, 0 : 2 * MODEL_WIDTH])
    mod3[0:4, :] = high
    mod3[4:8, :] = middle
    mod3[8:12, :] = rest
    mod3[12:16, :] = jnp.zeros((4, 2 * MODEL_WIDTH), F32)

    def project_rows(step, carry):
        rows = pl.ds(pl.multiple_of(step * block, block), block)
        per = span // block
        source = step // per
        values = xall[source, pl.ds(pl.multiple_of((step % per) * block, block), block), :].astype(F32)
        center = jnp.mean(values, axis=1, keepdims=True)
        centered = values - center
        variance = jnp.mean(centered * centered, axis=1, keepdims=True)
        segment, _ = frame_segments(lens, step * block, block, 16)
        slot = lanes_of((block, 16))
        chosen = jnp.where((slot < 12) & (slot % 4 == segment), 1.0, 0.0).astype(BF16)
        parts = mod3[...].astype(BF16)
        shift = product(chosen, parts[:, :MODEL_WIDTH])
        scale = product(chosen, parts[:, MODEL_WIDTH:])
        result = (centered * lax.rsqrt(variance + EPSILON) * (1.0 + scale) + shift).astype(BF16)
        normed[rows, :] = result
        cosine, sine = cosr[rows, :], sinr[rows, :]
        lane = lanes_of((block, LANES))
        for j in range(3):
            weight = wg[j].reshape(MODEL_WIDTH, own_width)
            full = product(result, weight) + qbias[j : j + 1, :]
            for pair in range(2):
                piece = full[:, pair * LANES : (pair + 1) * LANES]
                if j < 2:
                    piece = piece * cosine + swap_halves(piece, lane) * sine
                if j == 0:
                    qs[pair, rows, :] = (piece.astype(BF16).astype(F32) * HEAD_DIM**-0.5).astype(BF16)
                elif j == 1:
                    ks[pair, rows, :] = piece.astype(BF16)
                    ka[pair, rows, :LANES] = piece.astype(BF16)
                else:
                    vs[pair, rows, :] = piece.astype(BF16)
                    va[pair, rows, :LANES] = piece.astype(BF16)
        return carry

    for copy in qkv_y:
        copy.wait_recv()
    local_frames.wait()
    frames_core.wait_recv()
    second_leg(0)
    second_leg(1)
    frames_on.wait_recv()
    lax.fori_loop(0, rows_all // block, project_rows, 0)

    tall = 256

    def attend(pair, step):
        rows = pl.ds(pl.multiple_of(step * tall, tall), tall)
        query = qs[pair, rows, :]
        lane = lanes_of((tall, LANES))
        outs, sums = [], []
        for head in range(2):
            left = jnp.concatenate([head_only(query, lane, head), qaug[rows, :]], axis=1)
            scores = across(left, ka[pair])
            highest = jnp.max(scores, axis=1, keepdims=True)
            mixed = product(jnp.exp(scores - highest).astype(BF16), va[pair])
            total = mixed[:, LANES : LANES + 1]
            outs.append(mixed[:, :LANES] / total)
            sums.append(highest + jnp.log(total))
        oh[pair, rows, :] = jnp.where(lane < HEAD_DIM, outs[0], outs[1]).astype(BF16)
        before = jnp.zeros((tall, LANES), F32) if pair == 0 else lse[rows, :]
        lse[rows, :] = jnp.where(
            lane == 2 * pair, sums[0], jnp.where(lane == 2 * pair + 1, sums[1], before)
        )

    def attend_some(pair, first, last):
        lax.fori_loop(first, last, lambda step, carry: (attend(pair, step), carry)[1], 0)

    steps = rows_all // tall
    arrivals = []
    pair_locals = []

    def deliver(pair):
        columns = pl.ds(pl.multiple_of(g * own_width + pair * LANES, LANES), LANES)
        pair_locals.append(
            move.local(oh.at[pair, pl.ds(pl.multiple_of(g * span, span), span)], att.at[:, columns])
        )
        for k in (1, 2, 3):
            peer = (g + k) % 4
            arrivals.append(
                move.send(
                    oh.at[pair, pl.ds(pl.multiple_of(peer * span, span), span)],
                    att.at[:, columns],
                    here.row_peer(k),
                )
            )

    attend_some(0, 0, steps // 2)
    second_leg(2)
    second_leg(3)
    third_leg(0)
    third_leg(1)
    attend_some(0, steps // 2, steps)
    deliver(0)
    fourth_leg(0)
    fourth_leg(1)
    attend_some(1, 0, steps // 2)
    third_leg(2)
    third_leg(3)
    attend_some(1, steps // 2, steps)
    deliver(1)
    fourth_leg(2)
    fourth_leg(3)
    for number in range(4):
        legs[number].wait_recv()
    for copy in arrivals:
        copy.wait_recv()
    for copy in pair_locals:
        copy.wait()
    move.finish()


def forward_call(depth, span, own_rows, down_rows, hidden, args):
    rows_all, own_width = 4 * span, MODEL_WIDTH // 4
    half = 6 * MODEL_WIDTH // 8
    vmem, anywhere, scalar = (
        pl.BlockSpec(memory_space=pltpu.VMEM),
        pl.BlockSpec(memory_space=pl.ANY),
        pl.BlockSpec(memory_space=pltpu.SMEM),
    )

    def out(shape, dtype):
        return jax.ShapeDtypeStruct(shape, dtype)

    outs = [
        (out((span, MODEL_WIDTH), BF16), anywhere),
        (out((2, rows_all, LANES), BF16), vmem),
        (out((2, rows_all, LANES), BF16), vmem),
        (out((2, rows_all, LANES), BF16), vmem),
        (out((2, rows_all, LANES), BF16), vmem),
        (out((rows_all, LANES), F32), vmem),
        (out((rows_all, MODEL_WIDTH), BF16), vmem),
        (out((3, depth, 2, 4, own_rows, own_width), BF16), vmem),
        (out((8, 6 * MODEL_WIDTH), F32), vmem),
        (out((rows_all, LANES), F32), vmem),
        (out((rows_all, LANES), F32), vmem),
        (out((depth, 2, 2, 2, 8, LANES), F32), vmem),
        (out((32 * depth, LANES), BF16), vmem),
        (out((depth, 2, 2, 2, own_rows, MODEL_WIDTH), BF16), anywhere),
        (out((depth, 2, 2, 2, own_rows, hidden), BF16), anywhere),
        (out((depth, 2, 2, 2, down_rows, MODEL_WIDTH), BF16), anywhere),
    ]
    scratch = [
        pltpu.VMEM((4, span, MODEL_WIDTH), BF16),
        pltpu.VMEM((LANES, 2 * half), BF16),
        pltpu.VMEM((depth, 2, 16, LANES), F32),
        pltpu.VMEM((2, depth, 2, 16, half), BF16),
        pltpu.VMEM((depth, 2, 16, half), BF16),
        pltpu.VMEM((depth, 2, 16, half), BF16),
        pltpu.VMEM((depth, 16, half), BF16),
        pltpu.VMEM((depth, 16, half), BF16),
        pltpu.VMEM((depth - 1, 16, half), BF16),
        pltpu.VMEM((16, half), F32),
        pltpu.VMEM((16, half), F32),
        pltpu.VMEM((2, 16, half), F32),
        pltpu.VMEM((64 * depth, LANES), BF16),
        pltpu.VMEM((16, 2 * MODEL_WIDTH), F32),
        pltpu.VMEM((8, own_width), F32),
        pltpu.VMEM((2, rows_all, 2 * LANES), BF16),
        pltpu.VMEM((2, rows_all, 2 * LANES), BF16),
        pltpu.VMEM((rows_all, LANES), BF16),
        pltpu.SemaphoreType.DMA((96,)),
        pltpu.SemaphoreType.DMA((96,)),
        pltpu.SemaphoreType.DMA((24,)),
    ]
    return pl.pallas_call(
        partial(forward_kernel, depth),
        out_shape=[shape for shape, _ in outs],
        in_specs=[scalar, scalar, anywhere, vmem] + [anywhere] * 7,
        out_specs=[spec for _, spec in outs],
        scratch_shapes=scratch,
        compiler_params=pltpu.CompilerParams(
            collective_id=0, has_side_effects=True, vmem_limit_bytes=56 * 1024 * 1024
        ),
        cost_estimate=pl.CostEstimate(flops=8 * 10**9, bytes_accessed=40 * 10**6, transcendentals=10**7),
    )(*args)


def bias_block(query_bias, key_bias, value_bias, output_bias, up_bias, down_bias, modulation_bias):
    rows = [query_bias, key_bias, value_bias, output_bias, up_bias, down_bias]
    rows += [modulation_bias[:LANES], modulation_bias[LANES:]]
    return jnp.stack([jnp.pad(row, (0, LANES - row.shape[0])) for row in rows]).astype(F32)


def modulated_norm(values, shift_part, scale_part):
    center = jnp.mean(values, axis=-1, keepdims=True)
    centered = values - center
    variance = jnp.mean(centered * centered, axis=-1, keepdims=True)
    return centered * lax.rsqrt(variance + EPSILON) * (1.0 + scale_part) + shift_part


def rotate(values, cosines, sines_table):
    shaped = values.reshape(values.shape[:-1] + (values.shape[-1] // HEAD_DIM, HEAD_DIM))
    first_half = shaped[..., : HEAD_DIM // 2]
    second_half = shaped[..., HEAD_DIM // 2 :]
    cosine = cosines[..., None, :]
    sine_part = sines_table[..., None, :]
    turned = jnp.concatenate(
        [
            first_half * cosine - second_half * sine_part,
            second_half * cosine + first_half * sine_part,
        ],
        axis=-1,
    )
    return turned.reshape(values.shape)


def gelu_tanh(values):
    return jax.nn.gelu(values, approximate=True)


def time_features(time_index):
    halfway = MODEL_WIDTH // 2
    frequency = jnp.exp(jnp.arange(halfway, dtype=jnp.float32) * (-math.log(10000.0) / halfway))
    angles = time_index.astype(jnp.float32)[..., None] * frequency
    return jnp.concatenate([jnp.sin(angles), jnp.cos(angles)], axis=-1)


def segment_starts(segment_lengths):
    return jnp.cumsum(segment_lengths, axis=1) - segment_lengths


def segment_numbers(segment_lengths, frame_positions):
    starts = segment_starts(segment_lengths)
    inside = (frame_positions[None, :, None] >= starts[:, None, :]).astype(jnp.int32)
    return jnp.sum(inside, axis=2) - 1


def segment_layout(segment_lengths, frame_positions):
    starts = segment_starts(segment_lengths)
    segment = segment_numbers(segment_lengths, frame_positions)
    onehot = (segment[..., None] == jnp.arange(SEGS, dtype=jnp.int32)).astype(jnp.float32)
    offset = jnp.sum(onehot * starts[:, None, :].astype(jnp.float32), axis=2)
    relative = frame_positions[None, :].astype(jnp.float32) - offset
    return (onehot, relative)


def rope_tables(relative):
    halfway = HEAD_DIM // 2
    frequency = jnp.exp(jnp.arange(halfway, dtype=jnp.float32) * (-math.log(10000.0) / halfway))
    angles = relative[..., None] * frequency
    return (jnp.cos(angles), jnp.sin(angles))


def project(values, matrix, offset):
    return jnp.einsum(
        "rld,de->rle", values, matrix, preferred_element_type=jnp.float32
    ) + offset.astype(jnp.float32)


def project_back(gradient, matrix):
    return jnp.einsum("rle,de->rld", gradient, matrix, preferred_element_type=jnp.float32)


def weight_gradient(values, gradient):
    return jnp.einsum("rld,rle->de", values, gradient, preferred_element_type=jnp.float32)


def bias_gradient(gradient):
    return jnp.sum(gradient.astype(jnp.float32), axis=(0, 1))


def lift_up(member):
    return member.reshape((1, 1) + member.shape)


def settle(member):
    return member.reshape((-1,) + member.shape[3:])


def spread(member, wide_count, narrow_count):
    return member.reshape((wide_count, narrow_count, -1) + member.shape[1:])


def unpack(member):
    return member.reshape(member.shape[2:])


def on_device(
    frames,
    output_gradient,
    segment_lengths,
    time_index,
    query_weight,
    query_bias,
    key_weight,
    key_bias,
    value_weight,
    value_bias,
    output_projection,
    output_bias,
    up_weight,
    up_bias,
    down_weight,
    down_bias,
    modulation_weight,
    modulation_bias,
):
    narrow_count = lax.axis_size("seq")
    wide_count = lax.axis_size("dp")
    seq_index = lax.axis_index("seq")
    row_count, span_frames, width_total = frames.shape
    row_length = span_frames * narrow_count
    block_rows = min(512, row_length)
    block_count = row_length // block_rows
    local_weights = (
        query_weight,
        query_bias,
        key_weight,
        key_bias,
        value_weight,
        value_bias,
        output_projection,
        output_bias,
        up_weight,
        up_bias,
        down_weight,
        down_bias,
        modulation_bias,
    )
    lifted = [lift_up(member) for member in local_weights]
    halfway_set = (
        lax.all_gather(lifted[0], "dp", axis=0, tiled=True),
        lax.all_gather(lifted[1], "dp", axis=0, tiled=True),
        lax.all_gather(lifted[2], "dp", axis=0, tiled=True),
        lax.all_gather(lifted[3], "dp", axis=0, tiled=True),
        lax.all_gather(lifted[4], "dp", axis=0, tiled=True),
        lax.all_gather(lifted[5], "dp", axis=0, tiled=True),
        lax.all_gather(lifted[6], "dp", axis=0, tiled=True),
        lax.all_gather(lifted[7], "dp", axis=0, tiled=True),
        lax.all_gather(lifted[8], "dp", axis=0, tiled=True),
        lax.all_gather(lifted[9], "dp", axis=0, tiled=True),
        lax.all_gather(lifted[10], "dp", axis=0, tiled=True),
        lax.all_gather(lifted[11], "dp", axis=0, tiled=True),
        lax.all_gather(lifted[12], "dp", axis=0, tiled=True),
    )
    complete_set = (
        lax.all_gather(halfway_set[0], "seq", axis=1, tiled=True),
        lax.all_gather(halfway_set[1], "seq", axis=1, tiled=True),
        lax.all_gather(halfway_set[2], "seq", axis=1, tiled=True),
        lax.all_gather(halfway_set[3], "seq", axis=1, tiled=True),
        lax.all_gather(halfway_set[4], "seq", axis=1, tiled=True),
        lax.all_gather(halfway_set[5], "seq", axis=1, tiled=True),
        lax.all_gather(halfway_set[6], "seq", axis=1, tiled=True),
        lax.all_gather(halfway_set[7], "seq", axis=1, tiled=True),
        lax.all_gather(halfway_set[8], "seq", axis=1, tiled=True),
        lax.all_gather(halfway_set[9], "seq", axis=1, tiled=True),
        lax.all_gather(halfway_set[10], "seq", axis=1, tiled=True),
        lax.all_gather(halfway_set[11], "seq", axis=1, tiled=True),
        lax.all_gather(halfway_set[12], "seq", axis=1, tiled=True),
    )
    gathered = [settle(member) for member in complete_set]
    (
        full_query,
        full_query_bias,
        full_key,
        full_key_bias,
        full_value,
        full_value_bias,
        full_output,
        full_output_bias,
        full_up,
        full_up_bias,
        full_down,
        full_down_bias,
        full_modulation_bias,
    ) = gathered
    local_positions = seq_index * span_frames + jnp.arange(span_frames, dtype=jnp.int32)
    local_onehot, local_relative = segment_layout(segment_lengths, local_positions)
    row_segment = segment_numbers(segment_lengths, jnp.arange(row_length, dtype=jnp.int32))
    cosines, sines_table = rope_tables(local_relative)
    turning = partial(rotate, cosines=cosines, sines_table=sines_table)
    owned_rows = modulation_weight.shape[0]
    owned_start = (lax.axis_index("dp") * narrow_count + seq_index) * owned_rows
    every_time = lax.all_gather(time_index, "dp", axis=0, tiled=True)
    every_low = jax.nn.silu(time_features(every_time)).astype(jnp.bfloat16)
    owned_low = lax.dynamic_slice_in_dim(every_low, owned_start, owned_rows, 2)
    partial_modulation = jnp.einsum(
        "rsd,dc->rsc", owned_low, modulation_weight, preferred_element_type=jnp.float32
    )
    row_share = lax.psum_scatter(partial_modulation, "dp", scatter_dimension=0, tiled=True)
    modulation = lax.psum(row_share.astype(jnp.bfloat16), "seq").astype(
        jnp.float32
    ) + full_modulation_bias.astype(jnp.float32)
    per_frame = jnp.einsum("rls,rsc->rlc", local_onehot, modulation, precision=HIGHEST)
    shift_one, scale_one, gate_one, shift_two, scale_two, gate_two = jnp.split(
        per_frame, 6, axis=-1
    )
    inputs = frames.astype(jnp.float32)
    normed, norm_back = jax.vjp(modulated_norm, inputs, shift_one, scale_one)
    normed_low = normed.astype(jnp.bfloat16)
    query_pre = project(normed_low, full_query, full_query_bias)
    key_pre = project(normed_low, full_key, full_key_bias)
    value_low = project(normed_low, full_value, full_value_bias).astype(jnp.bfloat16)
    query_turned, query_back = jax.vjp(turning, query_pre)
    key_turned, key_back = jax.vjp(turning, key_pre)
    query_heads, key_heads, value_heads = (
        lax.all_to_all(
            query_turned.astype(jnp.bfloat16), "seq", split_axis=2, concat_axis=1, tiled=True
        ),
        lax.all_to_all(
            key_turned.astype(jnp.bfloat16), "seq", split_axis=2, concat_axis=1, tiled=True
        ),
        lax.all_to_all(value_low, "seq", split_axis=2, concat_axis=1, tiled=True),
    )
    local_heads = query_heads.shape[2] // HEAD_DIM
    head_shape = (row_count, row_length, local_heads, HEAD_DIM)
    queries = query_heads.reshape(head_shape)
    keys_all = key_heads.reshape(head_shape)
    values_all = value_heads.reshape(head_shape)
    scaling = HEAD_DIM ** (-0.5)
    positions_all = jnp.arange(row_count * block_count, dtype=jnp.int32)

    def fetch_block(position):
        row_index = position // block_count
        start_row = position % block_count * block_rows
        key_row = lax.dynamic_index_in_dim(keys_all, row_index, 0, keepdims=False)
        value_row = lax.dynamic_index_in_dim(values_all, row_index, 0, keepdims=False)
        segment_row = lax.dynamic_index_in_dim(row_segment, row_index, 0, keepdims=False)
        query_block = lax.dynamic_slice_in_dim(
            lax.dynamic_index_in_dim(queries, row_index, 0, keepdims=False),
            start_row,
            block_rows,
            0,
        )
        segment_block = lax.dynamic_slice_in_dim(segment_row, start_row, block_rows, 0)
        scores = (
            jnp.einsum("bhd,khd->hbk", query_block, key_row, preferred_element_type=jnp.float32)
            * scaling
        )
        scores = jnp.where((segment_block[:, None] == segment_row[None, :])[None], scores, NEGATIVE)
        return (row_index, start_row, query_block, key_row, value_row, scores)

    def forward_block(position):
        row_index, start_row, query_block, key_row, value_row, scores = fetch_block(position)
        highest = jnp.max(scores, axis=2, keepdims=True)
        weights = jnp.exp(scores - highest)
        totals = jnp.sum(weights, axis=2, keepdims=True)
        probabilities = (weights / totals).astype(jnp.bfloat16)
        mixed_block = jnp.einsum(
            "hbk,khd->bhd", probabilities, value_row, preferred_element_type=jnp.float32
        )
        return (
            mixed_block.astype(jnp.bfloat16).reshape(block_rows, -1),
            (highest + jnp.log(totals))[..., 0],
        )

    mixed_blocks, logsums = lax.map(forward_block, positions_all)
    attention_heads = mixed_blocks.reshape(row_count, row_length, -1)
    attention_frames = lax.all_to_all(
        attention_heads, "seq", split_axis=1, concat_axis=2, tiled=True
    )
    branch = project(attention_frames, full_output, full_output_bias)
    middle = inputs + gate_one * branch
    normed_two, norm_two_back = jax.vjp(modulated_norm, middle, shift_two, scale_two)
    normed_two_low = normed_two.astype(jnp.bfloat16)
    hidden = project(normed_two_low, full_up, full_up_bias)
    activated, gelu_back = jax.vjp(gelu_tanh, hidden)
    activated_low = activated.astype(jnp.bfloat16)
    branch_two = project(activated_low, full_down, full_down_bias)
    layer_output = (middle + gate_two * branch_two).astype(jnp.bfloat16)
    cotangent = output_gradient.astype(jnp.float32)
    grad_branch_two = (gate_two * cotangent).astype(jnp.bfloat16)
    grad_gate_two = cotangent * branch_two
    grad_activated = project_back(grad_branch_two, full_down)
    grad_hidden = gelu_back(grad_activated)[0].astype(jnp.bfloat16)
    grad_normed_two = project_back(grad_hidden, full_up)
    grad_middle_part, grad_shift_two, grad_scale_two = norm_two_back(grad_normed_two)
    grad_middle = cotangent + grad_middle_part
    grad_gate_one = grad_middle * branch
    grad_branch = (gate_one * grad_middle).astype(jnp.bfloat16)
    grad_attention = project_back(grad_branch, full_output).astype(jnp.bfloat16)
    grad_heads = lax.all_to_all(grad_attention, "seq", split_axis=2, concat_axis=1, tiled=True)
    grad_outputs = grad_heads.reshape(head_shape)

    def backward_block(running, pair_inputs):
        grad_keys, grad_values = running
        position, logsum = pair_inputs
        row_index, start_row, query_block, key_row, value_row, scores = fetch_block(position)
        grad_block = lax.dynamic_slice_in_dim(
            lax.dynamic_index_in_dim(grad_outputs, row_index, 0, keepdims=False),
            start_row,
            block_rows,
            0,
        )
        probabilities = jnp.exp(scores - logsum[..., None])
        grad_probabilities = jnp.einsum(
            "bhd,khd->hbk", grad_block, value_row, preferred_element_type=jnp.float32
        )
        delta_sum = jnp.sum(probabilities * grad_probabilities, axis=2, keepdims=True)
        grad_scores = (probabilities * (grad_probabilities - delta_sum)).astype(jnp.bfloat16)
        grad_query_block = (
            jnp.einsum("hbk,khd->bhd", grad_scores, key_row, preferred_element_type=jnp.float32)
            * scaling
        )
        key_part = (
            jnp.einsum("hbk,bhd->khd", grad_scores, query_block, preferred_element_type=jnp.float32)
            * scaling
        )
        value_part = jnp.einsum(
            "hbk,bhd->khd",
            probabilities.astype(jnp.bfloat16),
            grad_block,
            preferred_element_type=jnp.float32,
        )
        grad_keys = lax.dynamic_update_index_in_dim(
            grad_keys,
            lax.dynamic_index_in_dim(grad_keys, row_index, 0, keepdims=False) + key_part,
            row_index,
            0,
        )
        grad_values = lax.dynamic_update_index_in_dim(
            grad_values,
            lax.dynamic_index_in_dim(grad_values, row_index, 0, keepdims=False) + value_part,
            row_index,
            0,
        )
        return (
            (grad_keys, grad_values),
            grad_query_block.astype(jnp.bfloat16).reshape(block_rows, -1),
        )

    zero_heads = jnp.zeros(head_shape, jnp.float32)
    (grad_keys_all, grad_values_all), grad_query_blocks = lax.scan(
        backward_block, (zero_heads, zero_heads), (positions_all, logsums)
    )
    flat_shape = (row_count, row_length, -1)
    grad_query_frames, grad_key_frames, grad_value_frames = (
        lax.all_to_all(
            grad_query_blocks.reshape(flat_shape), "seq", split_axis=1, concat_axis=2, tiled=True
        ),
        lax.all_to_all(
            grad_keys_all.reshape(flat_shape).astype(jnp.bfloat16),
            "seq",
            split_axis=1,
            concat_axis=2,
            tiled=True,
        ),
        lax.all_to_all(
            grad_values_all.reshape(flat_shape).astype(jnp.bfloat16),
            "seq",
            split_axis=1,
            concat_axis=2,
            tiled=True,
        ),
    )
    grad_query_pre = query_back(grad_query_frames.astype(jnp.float32))[0].astype(jnp.bfloat16)
    grad_key_pre = key_back(grad_key_frames.astype(jnp.float32))[0].astype(jnp.bfloat16)
    grad_normed = (
        project_back(grad_query_pre, full_query)
        + project_back(grad_key_pre, full_key)
        + project_back(grad_value_frames, full_value)
    )
    grad_inputs_part, grad_shift_one, grad_scale_one = norm_back(grad_normed)
    frames_grad = (grad_middle + grad_inputs_part).astype(jnp.bfloat16)
    grad_per_frame = jnp.concatenate(
        [
            grad_shift_one,
            grad_scale_one,
            grad_gate_one,
            grad_shift_two,
            grad_scale_two,
            grad_gate_two,
        ],
        axis=-1,
    )
    grad_modulation = jnp.einsum("rls,rlc->rsc", local_onehot, grad_per_frame, precision=HIGHEST)
    gradients = (
        weight_gradient(normed_low, grad_query_pre),
        bias_gradient(grad_query_pre),
        weight_gradient(normed_low, grad_key_pre),
        bias_gradient(grad_key_pre),
        weight_gradient(normed_low, grad_value_frames),
        bias_gradient(grad_value_frames),
        weight_gradient(attention_frames, grad_branch),
        bias_gradient(grad_branch),
        weight_gradient(normed_two_low, grad_hidden),
        bias_gradient(grad_hidden),
        weight_gradient(activated_low, grad_branch_two),
        bias_gradient(grad_branch_two),
        jnp.sum(grad_modulation, axis=(0, 1)),
    )
    row_total = lax.psum(grad_modulation.astype(jnp.bfloat16), "seq").astype(jnp.float32)
    every_grad = lax.all_gather(row_total.astype(jnp.bfloat16), "dp", axis=0, tiled=True).astype(
        row_total.dtype
    )
    modulation_weight_grad = jnp.einsum(
        "rsd,rsc->dc", owned_low.astype(jnp.float32), every_grad, precision=HIGHEST
    )
    spreaded = [spread(member, wide_count, narrow_count) for member in gradients]
    first_pass = (
        lax.psum_scatter(
            spreaded[0].astype(jnp.bfloat16), "seq", scatter_dimension=1, tiled=True
        ).astype(jnp.float32),
        lax.psum_scatter(
            spreaded[1].astype(jnp.bfloat16), "seq", scatter_dimension=1, tiled=True
        ).astype(jnp.float32),
        lax.psum_scatter(
            spreaded[2].astype(jnp.bfloat16), "seq", scatter_dimension=1, tiled=True
        ).astype(jnp.float32),
        lax.psum_scatter(
            spreaded[3].astype(jnp.bfloat16), "seq", scatter_dimension=1, tiled=True
        ).astype(jnp.float32),
        lax.psum_scatter(
            spreaded[4].astype(jnp.bfloat16), "seq", scatter_dimension=1, tiled=True
        ).astype(jnp.float32),
        lax.psum_scatter(
            spreaded[5].astype(jnp.bfloat16), "seq", scatter_dimension=1, tiled=True
        ).astype(jnp.float32),
        lax.psum_scatter(
            spreaded[6].astype(jnp.bfloat16), "seq", scatter_dimension=1, tiled=True
        ).astype(jnp.float32),
        lax.psum_scatter(
            spreaded[7].astype(jnp.bfloat16), "seq", scatter_dimension=1, tiled=True
        ).astype(jnp.float32),
        lax.psum_scatter(
            spreaded[8].astype(jnp.bfloat16), "seq", scatter_dimension=1, tiled=True
        ).astype(jnp.float32),
        lax.psum_scatter(
            spreaded[9].astype(jnp.bfloat16), "seq", scatter_dimension=1, tiled=True
        ).astype(jnp.float32),
        lax.psum_scatter(
            spreaded[10].astype(jnp.bfloat16), "seq", scatter_dimension=1, tiled=True
        ).astype(jnp.float32),
        lax.psum_scatter(
            spreaded[11].astype(jnp.bfloat16), "seq", scatter_dimension=1, tiled=True
        ).astype(jnp.float32),
        lax.psum_scatter(
            spreaded[12].astype(jnp.bfloat16), "seq", scatter_dimension=1, tiled=True
        ).astype(jnp.float32),
    )
    second_pass = (
        lax.psum_scatter(first_pass[0], "dp", scatter_dimension=0, tiled=True),
        lax.psum_scatter(first_pass[1], "dp", scatter_dimension=0, tiled=True),
        lax.psum_scatter(first_pass[2], "dp", scatter_dimension=0, tiled=True),
        lax.psum_scatter(first_pass[3], "dp", scatter_dimension=0, tiled=True),
        lax.psum_scatter(first_pass[4], "dp", scatter_dimension=0, tiled=True),
        lax.psum_scatter(first_pass[5], "dp", scatter_dimension=0, tiled=True),
        lax.psum_scatter(first_pass[6], "dp", scatter_dimension=0, tiled=True),
        lax.psum_scatter(first_pass[7], "dp", scatter_dimension=0, tiled=True),
        lax.psum_scatter(first_pass[8], "dp", scatter_dimension=0, tiled=True),
        lax.psum_scatter(first_pass[9], "dp", scatter_dimension=0, tiled=True),
        lax.psum_scatter(first_pass[10], "dp", scatter_dimension=0, tiled=True),
        lax.psum_scatter(first_pass[11], "dp", scatter_dimension=0, tiled=True),
        lax.psum_scatter(first_pass[12], "dp", scatter_dimension=0, tiled=True),
    )
    reduced = [unpack(member) for member in second_pass]
    return (
        layer_output,
        frames_grad,
        reduced[0],
        reduced[1],
        reduced[2],
        reduced[3],
        reduced[4],
        reduced[5],
        reduced[6],
        reduced[7],
        reduced[8],
        reduced[9],
        reduced[10],
        reduced[11],
        modulation_weight_grad,
        reduced[12],
    )


def on_device_fast(frames, output_gradient, segment_lengths, time_index, query_weight, query_bias, key_weight,
                   key_bias, value_weight, value_bias, output_projection, output_bias, up_weight, up_bias,
                   down_weight, down_bias, modulation_weight, modulation_bias):
    narrow_count = lax.axis_size("seq")
    wide_count = lax.axis_size("dp")
    seq_index = lax.axis_index("seq")
    row_count, span_frames, width_total = frames.shape
    row_length = span_frames * narrow_count
    block_rows = min(512, row_length)
    block_count = row_length // block_rows
    blocks = bias_block(query_bias, key_bias, value_bias, output_bias, up_bias, down_bias, modulation_bias)
    (att, oh, qs, ks, vs, lse, normed_all, wg, mods, cosr, sinr, bb, low, wo_all, up_all, down_all) = forward_call(
        wide_count // 2, span_frames, query_weight.shape[0], down_weight.shape[0], up_weight.shape[1],
        (segment_lengths, time_index, frames[0], blocks, query_weight, key_weight, value_weight,
         output_projection, up_weight, down_weight, modulation_weight))
    gathered_bias = bb.reshape(-1, 8, LANES)
    full_output_bias = gathered_bias[:, 3, : output_bias.shape[0]].reshape(-1)
    full_up_bias = gathered_bias[:, 4, : up_bias.shape[0]].reshape(-1)
    full_down_bias = gathered_bias[:, 5, : down_bias.shape[0]].reshape(-1)
    full_output = wo_all.reshape(width_total, width_total)
    full_up = up_all.reshape(width_total, -1)
    full_down = down_all.reshape(-1, width_total)
    lifted = [lift_up(m) for m in (query_weight, key_weight, value_weight)]
    lifted = [lax.all_gather(m, "dp", axis=0, tiled=True) for m in lifted]
    full_query, full_key, full_value = [settle(lax.all_gather(m, "seq", axis=1, tiled=True)) for m in lifted]
    local_positions = seq_index * span_frames + jnp.arange(span_frames, dtype=jnp.int32)
    local_onehot, local_relative = segment_layout(segment_lengths, local_positions)
    row_segment = segment_numbers(segment_lengths, jnp.arange(row_length, dtype=jnp.int32))
    cosines, sines_table = rope_tables(local_relative)
    turning = partial(rotate, cosines=cosines, sines_table=sines_table)
    owned_rows = modulation_weight.shape[0]
    owned_start = (lax.axis_index("dp") * narrow_count + seq_index) * owned_rows
    every_time = lax.all_gather(time_index, "dp", axis=0, tiled=True)
    every_low = jax.nn.silu(time_features(every_time)).astype(jnp.bfloat16)
    owned_low = lax.dynamic_slice_in_dim(every_low, owned_start, owned_rows, 2)
    modulation = mods[None, :SEGS]
    per_frame = jnp.einsum("rls,rsc->rlc", local_onehot, modulation, precision=HIGHEST)
    shift_one, scale_one, gate_one, shift_two, scale_two, gate_two = jnp.split(per_frame, 6, axis=-1)
    inputs = frames.astype(jnp.float32)
    normed, norm_back = jax.vjp(modulated_norm, inputs, shift_one, scale_one)
    normed_low = normed.astype(jnp.bfloat16)
    zero = jnp.zeros(inputs.shape, jnp.float32)
    _, query_back = jax.vjp(turning, zero)
    _, key_back = jax.vjp(turning, zero)
    local_heads = full_query.shape[1] // narrow_count // HEAD_DIM
    head_shape = (row_count, row_length, local_heads, HEAD_DIM)
    side = lambda t: t.transpose(1, 0, 2).reshape(head_shape)
    queries, keys_all, values_all = side(qs * 8), side(ks), side(vs)
    scaling = HEAD_DIM ** (-0.5)
    positions_all = jnp.arange(row_count * block_count, dtype=jnp.int32)

    def fetch_block(position):
        row_index = position // block_count
        start_row = position % block_count * block_rows
        key_row = lax.dynamic_index_in_dim(keys_all, row_index, 0, keepdims=False)
        value_row = lax.dynamic_index_in_dim(values_all, row_index, 0, keepdims=False)
        segment_row = lax.dynamic_index_in_dim(row_segment, row_index, 0, keepdims=False)
        query_block = lax.dynamic_slice_in_dim(
            lax.dynamic_index_in_dim(queries, row_index, 0, keepdims=False),
            start_row,
            block_rows,
            0,
        )
        segment_block = lax.dynamic_slice_in_dim(segment_row, start_row, block_rows, 0)
        scores = (
            jnp.einsum("bhd,khd->hbk", query_block, key_row, preferred_element_type=jnp.float32)
            * scaling
        )
        scores = jnp.where((segment_block[:, None] == segment_row[None, :])[None], scores, NEGATIVE)
        return (row_index, start_row, query_block, key_row, value_row, scores)

    logsums = lse[:, :local_heads].T.reshape(local_heads, block_count, block_rows).transpose(1, 0, 2)
    attention_frames = att[None]
    branch = project(attention_frames, full_output, full_output_bias)
    middle = inputs + gate_one * branch
    normed_two, norm_two_back = jax.vjp(modulated_norm, middle, shift_two, scale_two)
    normed_two_low = normed_two.astype(jnp.bfloat16)
    hidden = project(normed_two_low, full_up, full_up_bias)
    activated, gelu_back = jax.vjp(gelu_tanh, hidden)
    activated_low = activated.astype(jnp.bfloat16)
    branch_two = project(activated_low, full_down, full_down_bias)
    layer_output = (middle + gate_two * branch_two).astype(jnp.bfloat16)
    cotangent = output_gradient.astype(jnp.float32)
    grad_branch_two = (gate_two * cotangent).astype(jnp.bfloat16)
    grad_gate_two = cotangent * branch_two
    grad_activated = project_back(grad_branch_two, full_down)
    grad_hidden = gelu_back(grad_activated)[0].astype(jnp.bfloat16)
    grad_normed_two = project_back(grad_hidden, full_up)
    grad_middle_part, grad_shift_two, grad_scale_two = norm_two_back(grad_normed_two)
    grad_middle = cotangent + grad_middle_part
    grad_gate_one = grad_middle * branch
    grad_branch = (gate_one * grad_middle).astype(jnp.bfloat16)
    grad_attention = project_back(grad_branch, full_output).astype(jnp.bfloat16)
    grad_heads = lax.all_to_all(grad_attention, "seq", split_axis=2, concat_axis=1, tiled=True)
    grad_outputs = grad_heads.reshape(head_shape)

    def backward_block(running, pair_inputs):
        grad_keys, grad_values = running
        position, logsum = pair_inputs
        row_index, start_row, query_block, key_row, value_row, scores = fetch_block(position)
        grad_block = lax.dynamic_slice_in_dim(
            lax.dynamic_index_in_dim(grad_outputs, row_index, 0, keepdims=False),
            start_row,
            block_rows,
            0,
        )
        probabilities = jnp.exp(scores - logsum[..., None])
        grad_probabilities = jnp.einsum(
            "bhd,khd->hbk", grad_block, value_row, preferred_element_type=jnp.float32
        )
        delta_sum = jnp.sum(probabilities * grad_probabilities, axis=2, keepdims=True)
        grad_scores = (probabilities * (grad_probabilities - delta_sum)).astype(jnp.bfloat16)
        grad_query_block = (
            jnp.einsum("hbk,khd->bhd", grad_scores, key_row, preferred_element_type=jnp.float32)
            * scaling
        )
        key_part = (
            jnp.einsum("hbk,bhd->khd", grad_scores, query_block, preferred_element_type=jnp.float32)
            * scaling
        )
        value_part = jnp.einsum(
            "hbk,bhd->khd",
            probabilities.astype(jnp.bfloat16),
            grad_block,
            preferred_element_type=jnp.float32,
        )
        grad_keys = lax.dynamic_update_index_in_dim(
            grad_keys,
            lax.dynamic_index_in_dim(grad_keys, row_index, 0, keepdims=False) + key_part,
            row_index,
            0,
        )
        grad_values = lax.dynamic_update_index_in_dim(
            grad_values,
            lax.dynamic_index_in_dim(grad_values, row_index, 0, keepdims=False) + value_part,
            row_index,
            0,
        )
        return (
            (grad_keys, grad_values),
            grad_query_block.astype(jnp.bfloat16).reshape(block_rows, -1),
        )

    zero_heads = jnp.zeros(head_shape, jnp.float32)
    (grad_keys_all, grad_values_all), grad_query_blocks = lax.scan(
        backward_block, (zero_heads, zero_heads), (positions_all, logsums)
    )
    flat_shape = (row_count, row_length, -1)
    grad_query_frames, grad_key_frames, grad_value_frames = (
        lax.all_to_all(
            grad_query_blocks.reshape(flat_shape), "seq", split_axis=1, concat_axis=2, tiled=True
        ),
        lax.all_to_all(
            grad_keys_all.reshape(flat_shape).astype(jnp.bfloat16),
            "seq",
            split_axis=1,
            concat_axis=2,
            tiled=True,
        ),
        lax.all_to_all(
            grad_values_all.reshape(flat_shape).astype(jnp.bfloat16),
            "seq",
            split_axis=1,
            concat_axis=2,
            tiled=True,
        ),
    )
    grad_query_pre = query_back(grad_query_frames.astype(jnp.float32))[0].astype(jnp.bfloat16)
    grad_key_pre = key_back(grad_key_frames.astype(jnp.float32))[0].astype(jnp.bfloat16)
    grad_normed = (
        project_back(grad_query_pre, full_query)
        + project_back(grad_key_pre, full_key)
        + project_back(grad_value_frames, full_value)
    )
    grad_inputs_part, grad_shift_one, grad_scale_one = norm_back(grad_normed)
    frames_grad = (grad_middle + grad_inputs_part).astype(jnp.bfloat16)
    grad_per_frame = jnp.concatenate(
        [
            grad_shift_one,
            grad_scale_one,
            grad_gate_one,
            grad_shift_two,
            grad_scale_two,
            grad_gate_two,
        ],
        axis=-1,
    )
    grad_modulation = jnp.einsum("rls,rlc->rsc", local_onehot, grad_per_frame, precision=HIGHEST)
    gradients = (
        weight_gradient(normed_low, grad_query_pre),
        bias_gradient(grad_query_pre),
        weight_gradient(normed_low, grad_key_pre),
        bias_gradient(grad_key_pre),
        weight_gradient(normed_low, grad_value_frames),
        bias_gradient(grad_value_frames),
        weight_gradient(attention_frames, grad_branch),
        bias_gradient(grad_branch),
        weight_gradient(normed_two_low, grad_hidden),
        bias_gradient(grad_hidden),
        weight_gradient(activated_low, grad_branch_two),
        bias_gradient(grad_branch_two),
        jnp.sum(grad_modulation, axis=(0, 1)),
    )
    row_total = lax.psum(grad_modulation.astype(jnp.bfloat16), "seq").astype(jnp.float32)
    every_grad = lax.all_gather(row_total.astype(jnp.bfloat16), "dp", axis=0, tiled=True).astype(
        row_total.dtype
    )
    modulation_weight_grad = jnp.einsum(
        "rsd,rsc->dc", owned_low.astype(jnp.float32), every_grad, precision=HIGHEST
    )
    spreaded = [spread(member, wide_count, narrow_count) for member in gradients]
    first_pass = (
        lax.psum_scatter(
            spreaded[0].astype(jnp.bfloat16), "seq", scatter_dimension=1, tiled=True
        ).astype(jnp.float32),
        lax.psum_scatter(
            spreaded[1].astype(jnp.bfloat16), "seq", scatter_dimension=1, tiled=True
        ).astype(jnp.float32),
        lax.psum_scatter(
            spreaded[2].astype(jnp.bfloat16), "seq", scatter_dimension=1, tiled=True
        ).astype(jnp.float32),
        lax.psum_scatter(
            spreaded[3].astype(jnp.bfloat16), "seq", scatter_dimension=1, tiled=True
        ).astype(jnp.float32),
        lax.psum_scatter(
            spreaded[4].astype(jnp.bfloat16), "seq", scatter_dimension=1, tiled=True
        ).astype(jnp.float32),
        lax.psum_scatter(
            spreaded[5].astype(jnp.bfloat16), "seq", scatter_dimension=1, tiled=True
        ).astype(jnp.float32),
        lax.psum_scatter(
            spreaded[6].astype(jnp.bfloat16), "seq", scatter_dimension=1, tiled=True
        ).astype(jnp.float32),
        lax.psum_scatter(
            spreaded[7].astype(jnp.bfloat16), "seq", scatter_dimension=1, tiled=True
        ).astype(jnp.float32),
        lax.psum_scatter(
            spreaded[8].astype(jnp.bfloat16), "seq", scatter_dimension=1, tiled=True
        ).astype(jnp.float32),
        lax.psum_scatter(
            spreaded[9].astype(jnp.bfloat16), "seq", scatter_dimension=1, tiled=True
        ).astype(jnp.float32),
        lax.psum_scatter(
            spreaded[10].astype(jnp.bfloat16), "seq", scatter_dimension=1, tiled=True
        ).astype(jnp.float32),
        lax.psum_scatter(
            spreaded[11].astype(jnp.bfloat16), "seq", scatter_dimension=1, tiled=True
        ).astype(jnp.float32),
        lax.psum_scatter(
            spreaded[12].astype(jnp.bfloat16), "seq", scatter_dimension=1, tiled=True
        ).astype(jnp.float32),
    )
    second_pass = (
        lax.psum_scatter(first_pass[0], "dp", scatter_dimension=0, tiled=True),
        lax.psum_scatter(first_pass[1], "dp", scatter_dimension=0, tiled=True),
        lax.psum_scatter(first_pass[2], "dp", scatter_dimension=0, tiled=True),
        lax.psum_scatter(first_pass[3], "dp", scatter_dimension=0, tiled=True),
        lax.psum_scatter(first_pass[4], "dp", scatter_dimension=0, tiled=True),
        lax.psum_scatter(first_pass[5], "dp", scatter_dimension=0, tiled=True),
        lax.psum_scatter(first_pass[6], "dp", scatter_dimension=0, tiled=True),
        lax.psum_scatter(first_pass[7], "dp", scatter_dimension=0, tiled=True),
        lax.psum_scatter(first_pass[8], "dp", scatter_dimension=0, tiled=True),
        lax.psum_scatter(first_pass[9], "dp", scatter_dimension=0, tiled=True),
        lax.psum_scatter(first_pass[10], "dp", scatter_dimension=0, tiled=True),
        lax.psum_scatter(first_pass[11], "dp", scatter_dimension=0, tiled=True),
        lax.psum_scatter(first_pass[12], "dp", scatter_dimension=0, tiled=True),
    )
    reduced = [unpack(member) for member in second_pass]
    return (
        layer_output,
        frames_grad,
        reduced[0],
        reduced[1],
        reduced[2],
        reduced[3],
        reduced[4],
        reduced[5],
        reduced[6],
        reduced[7],
        reduced[8],
        reduced[9],
        reduced[10],
        reduced[11],
        modulation_weight_grad,
        reduced[12],
    )


def fits(mesh, frames, *parameters):
    dp, seq = mesh.shape["dp"], mesh.shape["seq"]
    rows = parameters[3].shape[0] // (dp * seq)
    return seq == 4 and dp % 2 == 0 and rows == 32 and frames.shape[0] == dp


def solution(mesh):
    def run(*arrays):
        return mapped(mesh, on_device_fast if fits(mesh, *arrays) else on_device)(*arrays)

    return run


def mapped(mesh, body):
    return jax.shard_map(
        body,
        mesh=mesh,
        in_specs=(
            P("dp", "seq", None),
            P("dp", "seq", None),
            P("dp", None),
            P("dp", None),
            P(("dp", "seq"), None),
            P(("dp", "seq")),
            P(("dp", "seq"), None),
            P(("dp", "seq")),
            P(("dp", "seq"), None),
            P(("dp", "seq")),
            P(("dp", "seq"), None),
            P(("dp", "seq")),
            P(("dp", "seq"), None),
            P(("dp", "seq")),
            P(("dp", "seq"), None),
            P(("dp", "seq")),
            P(("dp", "seq"), None),
            P(("dp", "seq")),
        ),
        out_specs=(
            P("dp", "seq", None),
            P("dp", "seq", None),
            P(("dp", "seq"), None),
            P(("dp", "seq")),
            P(("dp", "seq"), None),
            P(("dp", "seq")),
            P(("dp", "seq"), None),
            P(("dp", "seq")),
            P(("dp", "seq"), None),
            P(("dp", "seq")),
            P(("dp", "seq"), None),
            P(("dp", "seq")),
            P(("dp", "seq"), None),
            P(("dp", "seq")),
            P(("dp", "seq"), None),
            P(("dp", "seq")),
        ),
        check_vma=False,
    )
```

```python
from functools import partial
import math

import jax
import jax.numpy as jnp
from jax import lax
from jax.experimental import pallas as pl
from jax.experimental.pallas import tpu as pltpu
from jax.sharding import PartitionSpec as P

HEAD_DIM = 64
MODEL_WIDTH = 1024
SEGS = 4
EPSILON = 1e-06
NEGATIVE = -1e30
HIGHEST = lax.Precision.HIGHEST
F32 = jnp.float32
BF16 = jnp.bfloat16
LANES = 128


class Mover:
    def __init__(self, send_sems, recv_sems, local_sems):
        self.send_sems, self.recv_sems, self.local_sems = send_sems, recv_sems, local_sems
        self.count = self.local_count = 0
        self.sent = []

    def send(self, source, target, device):
        slot = self.count
        self.count += 1
        copy = pltpu.make_async_remote_copy(
            src_ref=source,
            dst_ref=target,
            send_sem=self.send_sems.at[slot],
            recv_sem=self.recv_sems.at[slot],
            device_id=device,
            device_id_type=pl.DeviceIdType.MESH,
        )
        copy.start()
        self.sent.append(copy)
        return copy

    def local(self, source, target):
        slot = self.local_count
        self.local_count += 1
        copy = pltpu.make_async_copy(source, target, self.local_sems.at[slot])
        copy.start()
        return copy

    def finish(self, but=()):
        for copy in self.sent:
            if not any(copy is other for other in but):
                copy.wait_send()


class Place:
    def __init__(self, depth):
        dp, seq = lax.axis_index("dp"), lax.axis_index("seq")
        self.depth = depth
        self.z, self.y = dp // 2, dp % 2
        self.x, self.c = seq // 2, seq % 2
        self.seq = seq
        self.index = dp * 4 + seq

    def at(self, z, y, x, c):
        return {"dp": z * 2 + y, "seq": x * 2 + c}

    def core(self):
        return self.at(self.z, self.y, self.x, 1 - self.c)

    def across_x(self):
        return self.at(self.z, self.y, 1 - self.x, self.c)

    def across_y(self):
        return self.at(self.z, 1 - self.y, self.x, self.c)

    def ahead(self, step):
        return (self.z + step) % self.depth

    def along_z(self, step):
        return self.at(self.ahead(step), self.y, self.x, self.c)

    def row_peer(self, step):
        return {"dp": self.z * 2 + self.y, "seq": (self.seq + step) % 4}

    def enter(self):
        barrier = pltpu.get_barrier_semaphore()
        peers = [self.row_peer(step) for step in (1, 2, 3)] + [self.across_y()]
        peers += [self.along_z(step) for step in range(1, self.depth)]
        for peer in peers:
            pl.semaphore_signal(barrier, 1, device_id=peer, device_id_type=pl.DeviceIdType.MESH)
        pl.semaphore_wait(barrier, len(peers))


def lanes_of(shape, axis=1):
    return lax.broadcasted_iota(jnp.int32, shape, axis)


def frame_segments(lens, first_row, rows, width):
    position = lanes_of((rows, width), 0) + first_row
    first, second, third = lens[0, 0], lens[0, 0] + lens[0, 1], lens[0, 0] + lens[0, 1] + lens[0, 2]
    segment = (
        (position >= first).astype(jnp.int32)
        + (position >= second).astype(jnp.int32)
        + (position >= third).astype(jnp.int32)
    )
    start = jnp.where(
        segment == 0, 0, jnp.where(segment == 1, first, jnp.where(segment == 2, second, third))
    )
    return segment, position - start


def three_parts(values):
    high = values.astype(BF16).astype(F32)
    rest = values - high
    middle = rest.astype(BF16).astype(F32)
    return high, middle, (rest - middle).astype(BF16).astype(F32)


def swap_halves(values, lane):
    return jnp.where(
        lane % HEAD_DIM < HEAD_DIM // 2, pltpu.roll(values, 96, 1), pltpu.roll(values, 32, 1)
    )


def head_only(values, lane, head):
    return jnp.where((lane >= HEAD_DIM) == bool(head), values.astype(F32), 0.0).astype(BF16)


def across(left, right):
    return lax.dot_general(left, right, (((1,), (1,)), ((), ())), preferred_element_type=F32)


def product(left, right):
    return jnp.dot(left, right, preferred_element_type=F32)


def forward_kernel(
    depth,
    lens, times, frames, biases, wq, wk, wv, wo, up, down, mw,
    att, oh, qs, ks, vs, lse, normed, wg, mods, cosr, sinr, bb, low, wo_all, up_all, down_all,
    xall, mwst, tb, part, recva, suma, recvb, sumb, recvc, sumc, recvd, modh, bmat, mod3, qbias,
    ka, va, qaug, send_sems, recv_sems, local_sems,
):
    here = Place(depth)
    z, y, x, c, g = here.z, here.y, here.x, here.c, here.seq
    span = frames.shape[0]
    rows_all = span * 4
    move = Mover(send_sems, recv_sems, local_sems)
    steps_z = range(1, depth)

    row = lanes_of((16, LANES), 0) % 4
    own_times = jnp.where(
        row == 0, times[0, 0], jnp.where(row == 1, times[0, 1], jnp.where(row == 2, times[0, 2], times[0, 3]))
    )
    tb[z, y] = own_times.astype(F32)
    bb[z, y, x, c] = biases[...]
    weights = (wq, wk, wv)
    own_width = wg.shape[-1]
    locals_first = [
        move.local(weights[j].at[:, pl.ds(pl.multiple_of(g * own_width, LANES), own_width)], wg.at[j, z, y, g])
        for j in range(3)
    ]
    strip = mw.shape[1] // 4
    local_mw = [
        move.local(mw.at[:, pl.ds(j * strip, strip)], mwst.at[pl.ds(j * 32, 32)]) for j in range(4)
    ]
    local_frames = move.local(frames, xall.at[g])
    here.enter()

    times_z = [move.send(tb.at[z, y], tb.at[z, y], here.along_z(k)) for k in steps_z]
    bias_z = [move.send(bb.at[z, y, x, c], bb.at[z, y, x, c], here.along_z(k)) for k in steps_z]
    qkv_row = []
    for j in range(3):
        for k in (1, 2, 3):
            peer = (g + k) % 4
            qkv_row.append(
                move.send(
                    weights[j].at[:, pl.ds(pl.multiple_of(peer * own_width, LANES), own_width)],
                    wg.at[j, z, y, g],
                    here.row_peer(k),
                )
            )
    frames_x = move.send(frames, xall.at[g], here.across_x())
    frames_core = move.send(frames, xall.at[g], here.core())
    for copy in times_z:
        copy.wait_recv()
    times_y = move.send(tb.at[:, y], tb.at[:, y], here.across_y())
    for copy in locals_first:
        copy.wait()
    for copy in qkv_row:
        copy.wait_recv()
    qkv_z = [
        [move.send(wg.at[j, z, y], wg.at[j, z, y], here.along_z(k)) for k in steps_z] for j in range(3)
    ]
    for copy in bias_z:
        copy.wait_recv()
    bias_y = move.send(bb.at[:, y, x, c], bb.at[:, y, x, c], here.across_y())

    times_y.wait_recv()
    lane = lanes_of((16 * 2 * depth, LANES))
    row = lanes_of((16 * 2 * depth, LANES), 0)
    feature = here.index * 32 + lane % 32
    halfway = MODEL_WIDTH // 2
    frequency = jnp.exp((feature % halfway).astype(F32) * (-math.log(10000.0) / halfway))
    angle = tb[...].reshape(16 * 2 * depth, LANES) * frequency
    wave = jnp.where(feature < halfway, jnp.sin(angle), jnp.cos(angle))
    gated = wave / (1.0 + jnp.exp(-wave))
    low[...] = jnp.where(lane // 32 == (row % 16) // 4, gated, 0.0).astype(BF16)
    for copy in local_mw:
        copy.wait()
    half = strip // 2
    for side in range(2):
        share = product(low[...], mwst[:, side * half : (side + 1) * half])
        part[side] = share.astype(BF16).reshape(depth, 2, 16, half)
    mod_core = move.send(part.at[1 - c], recva, here.core())
    bias_y.wait_recv()
    bias_x = move.send(bb.at[:, :, x, c], bb.at[:, :, x, c], here.across_x())

    block = 128

    def tables(step, carry):
        rows = pl.ds(pl.multiple_of(step * block, block), block)
        segment, relative = frame_segments(lens, step * block, block, LANES)
        lane = lanes_of((block, LANES))
        quarter = HEAD_DIM // 2
        frequency = jnp.exp((lane % quarter).astype(F32) * (-math.log(10000.0) / quarter))
        angle = relative.astype(F32) * frequency
        cosr[rows, :] = jnp.cos(angle)
        sine = jnp.sin(angle)
        sinr[rows, :] = jnp.where(lane % HEAD_DIM < quarter, -sine, sine)
        same = segment == lane
        qaug[rows, :] = jnp.where((lane < SEGS) & jnp.logical_not(same), NEGATIVE, 0.0).astype(BF16)
        keyside = jnp.where((lane < SEGS) & same, 1.0, jnp.where((lane >= 4) & (lane < 7), 1.0, 0.0))
        for pair in range(2):
            ka[pair, rows, LANES:] = keyside.astype(BF16)
            va[pair, rows, LANES:] = jnp.where(lane < 3, 1.0, 0.0).astype(BF16)
        return carry

    lax.fori_loop(0, rows_all // (2 * block), tables, 0)
    mod_core.wait_recv()
    suma[...] = (part[c].astype(F32) + recva[...].astype(F32)).astype(BF16)
    mod_y = move.send(suma.at[:, 1 - y], recvb, here.across_y())
    bias_x.wait_recv()
    bias_core = move.send(bb.at[:, :, :, c], bb.at[:, :, :, c], here.core())
    lax.fori_loop(rows_all // (2 * block), rows_all // block, tables, 0)
    mod_y.wait_recv()
    sumb[...] = (suma[:, y].astype(F32) + recvb[...].astype(F32)).astype(BF16)
    mod_z = [move.send(sumb.at[here.ahead(k)], recvc.at[k - 1], here.along_z(k)) for k in steps_z]
    qkv_y = []
    for j in range(3):
        for copy in qkv_z[j]:
            copy.wait_recv()
        qkv_y.append(move.send(wg.at[j, :, y], wg.at[j, :, y], here.across_y()))
    total = sumb[z].astype(F32)
    for k in steps_z:
        mod_z[k - 1].wait_recv()
        total = total + recvc[k - 1].astype(F32)
    sumc[...] = total
    mod_x = move.send(sumc, recvd, here.across_x())

    def first_leg(source, target):
        own = move.local(source, target.at[z, y, x, c])
        sends = [move.send(source, target.at[z, y, x, c], here.along_z(k)) for k in steps_z]
        return own, sends

    legs = {}
    wo_top, wo_low = wo.at[pl.ds(0, 16)], wo.at[pl.ds(16, 16)]
    wo_all_top, wo_all_low = wo_all.at[:, :, :, :, pl.ds(0, 16)], wo_all.at[:, :, :, :, pl.ds(16, 16)]
    flows = [(wo_top, wo_all_top, 0), (wo_low, wo_all_low, 1), (up, up_all, 0), (down, down_all, 1)]
    for number, (source, target, _) in enumerate(flows):
        legs[number] = first_leg(source, target)

    def second_leg(number):
        _, target, order = flows[number]
        own, sends = legs[number]
        own.wait()
        for copy in sends:
            copy.wait_recv()
        peer = here.across_x() if order else here.across_y()
        legs[number] = move.send(target.at[:, y, x, c], target.at[:, y, x, c], peer)

    def third_leg(number):
        _, target, order = flows[number]
        legs[number].wait_recv()
        if order:
            legs[number] = move.send(target.at[:, y, :, c], target.at[:, y, :, c], here.across_y())
        else:
            legs[number] = move.send(target.at[:, :, x, c], target.at[:, :, x, c], here.across_x())

    def fourth_leg(number):
        _, target, _ = flows[number]
        legs[number].wait_recv()
        legs[number] = move.send(target.at[:, :, :, c], target.at[:, :, :, c], here.core())

    bias_core.wait_recv()
    bmat[...] = bb[...].reshape(16 * 2 * depth * 2, LANES).astype(BF16)

    place = lanes_of((LANES, own_width), 0)
    column = lanes_of((LANES, own_width))
    spread = jnp.where(column % 32 == place, 1.0, 0.0).astype(BF16)
    held = product(bmat[pl.ds(pl.multiple_of(g * 64, 64), 64), :], spread)
    brow, bcol = lanes_of((64, own_width), 0), lanes_of((64, own_width))
    for j in range(3):
        mine = (brow % 8 == j) & (brow // 8 == bcol // 32)
        qbias[j : j + 1, :] = jnp.sum(jnp.where(mine, held, 0.0), axis=0, keepdims=True)

    frames_x.wait_recv()
    frames_on = move.send(xall.at[(g + 2) % 4], xall.at[(g + 2) % 4], here.core())
    mod_x.wait_recv()
    modh[c] = sumc[...] + recvd[...]
    mod_last = move.send(modh.at[c], modh.at[c], here.core())

    place = lanes_of((LANES, half), 0)
    column = lanes_of((LANES, half))
    spread_a = jnp.where(column % 192 == place, 1.0, 0.0).astype(BF16)
    spread_b = jnp.where(column % 192 == place + LANES, 1.0, 0.0).astype(BF16)
    brow, bcol = lanes_of((32, half), 0), lanes_of((32, half))
    mod_last.wait_recv()
    for q in range(8):
        rows = bmat[q * 32 : (q + 1) * 32, :]
        inside = brow // 8 == bcol // 192
        terms = jnp.where(inside & (brow % 8 == 6), product(rows, spread_a), 0.0)
        terms = terms + jnp.where(inside & (brow % 8 == 7), product(rows, spread_b), 0.0)
        offset = jnp.sum(terms, axis=0, keepdims=True)
        j, side = q // 2, q % 2
        mods[0:4, q * half : (q + 1) * half] = modh[side, 4 * j : 4 * j + 4, :] + offset
    mods[4:8, :] = jnp.zeros((4, mods.shape[1]), F32)
    high, middle, rest = three_parts(mods[0:4, 0 : 2 * MODEL_WIDTH])
    mod3[0:4, :] = high
    mod3[4:8, :] = middle
    mod3[8:12, :] = rest
    mod3[12:16, :] = jnp.zeros((4, 2 * MODEL_WIDTH), F32)

    def project_rows(step, carry):
        rows = pl.ds(pl.multiple_of(step * block, block), block)
        per = span // block
        source = step // per
        values = xall[source, pl.ds(pl.multiple_of((step % per) * block, block), block), :].astype(F32)
        center = jnp.mean(values, axis=1, keepdims=True)
        centered = values - center
        variance = jnp.mean(centered * centered, axis=1, keepdims=True)
        segment, _ = frame_segments(lens, step * block, block, 16)
        slot = lanes_of((block, 16))
        chosen = jnp.where((slot < 12) & (slot % 4 == segment), 1.0, 0.0).astype(BF16)
        parts = mod3[...].astype(BF16)
        shift = product(chosen, parts[:, :MODEL_WIDTH])
        scale = product(chosen, parts[:, MODEL_WIDTH:])
        result = (centered * lax.rsqrt(variance + EPSILON) * (1.0 + scale) + shift).astype(BF16)
        normed[rows, :] = result
        cosine, sine = cosr[rows, :], sinr[rows, :]
        lane = lanes_of((block, LANES))
        for j in range(3):
            weight = wg[j].reshape(MODEL_WIDTH, own_width)
            full = product(result, weight) + qbias[j : j + 1, :]
            for pair in range(2):
                piece = full[:, pair * LANES : (pair + 1) * LANES]
                if j < 2:
                    piece = piece * cosine + swap_halves(piece, lane) * sine
                if j == 0:
                    qs[pair, rows, :] = (piece.astype(BF16).astype(F32) * HEAD_DIM**-0.5).astype(BF16)
                elif j == 1:
                    ks[pair, rows, :] = piece.astype(BF16)
                    ka[pair, rows, :LANES] = piece.astype(BF16)
                else:
                    vs[pair, rows, :] = piece.astype(BF16)
                    va[pair, rows, :LANES] = piece.astype(BF16)
        return carry

    for copy in qkv_y:
        copy.wait_recv()
    local_frames.wait()
    frames_core.wait_recv()
    second_leg(0)
    second_leg(1)
    frames_on.wait_recv()
    lax.fori_loop(0, rows_all // block, project_rows, 0)

    tall = 256

    def attend(pair, step):
        rows = pl.ds(pl.multiple_of(step * tall, tall), tall)
        query = qs[pair, rows, :]
        lane = lanes_of((tall, LANES))
        outs, sums = [], []
        for head in range(2):
            left = jnp.concatenate([head_only(query, lane, head), qaug[rows, :]], axis=1)
            scores = across(left, ka[pair])
            highest = jnp.max(scores, axis=1, keepdims=True)
            mixed = product(jnp.exp(scores - highest).astype(BF16), va[pair])
            total = mixed[:, LANES : LANES + 1]
            outs.append(mixed[:, :LANES] / total)
            sums.append(highest + jnp.log(total))
        oh[pair, rows, :] = jnp.where(lane < HEAD_DIM, outs[0], outs[1]).astype(BF16)
        before = jnp.zeros((tall, LANES), F32) if pair == 0 else lse[rows, :]
        lse[rows, :] = jnp.where(
            lane == 2 * pair, sums[0], jnp.where(lane == 2 * pair + 1, sums[1], before)
        )

    def attend_some(pair, first, last):
        lax.fori_loop(first, last, lambda step, carry: (attend(pair, step), carry)[1], 0)

    steps = rows_all // tall
    arrivals = []
    pair_locals = []

    def deliver(pair):
        columns = pl.ds(pl.multiple_of(g * own_width + pair * LANES, LANES), LANES)
        pair_locals.append(
            move.local(oh.at[pair, pl.ds(pl.multiple_of(g * span, span), span)], att.at[:, columns])
        )
        for k in (1, 2, 3):
            peer = (g + k) % 4
            arrivals.append(
                move.send(
                    oh.at[pair, pl.ds(pl.multiple_of(peer * span, span), span)],
                    att.at[:, columns],
                    here.row_peer(k),
                )
            )

    attend_some(0, 0, steps // 2)
    second_leg(2)
    second_leg(3)
    third_leg(0)
    third_leg(1)
    attend_some(0, steps // 2, steps)
    deliver(0)
    fourth_leg(0)
    fourth_leg(1)
    attend_some(1, 0, steps // 2)
    third_leg(2)
    third_leg(3)
    attend_some(1, steps // 2, steps)
    deliver(1)
    fourth_leg(2)
    fourth_leg(3)
    for number in range(4):
        legs[number].wait_recv()
    for copy in arrivals:
        copy.wait_recv()
    for copy in pair_locals:
        copy.wait()
    move.finish()


def forward_call(depth, span, own_rows, down_rows, hidden, args):
    rows_all, own_width = 4 * span, MODEL_WIDTH // 4
    half = 6 * MODEL_WIDTH // 8
    vmem, anywhere, scalar = (
        pl.BlockSpec(memory_space=pltpu.VMEM),
        pl.BlockSpec(memory_space=pl.ANY),
        pl.BlockSpec(memory_space=pltpu.SMEM),
    )

    def out(shape, dtype):
        return jax.ShapeDtypeStruct(shape, dtype)

    outs = [
        (out((span, MODEL_WIDTH), BF16), anywhere),
        (out((2, rows_all, LANES), BF16), vmem),
        (out((2, rows_all, LANES), BF16), vmem),
        (out((2, rows_all, LANES), BF16), vmem),
        (out((2, rows_all, LANES), BF16), vmem),
        (out((rows_all, LANES), F32), vmem),
        (out((rows_all, MODEL_WIDTH), BF16), vmem),
        (out((3, depth, 2, 4, own_rows, own_width), BF16), vmem),
        (out((8, 6 * MODEL_WIDTH), F32), vmem),
        (out((rows_all, LANES), F32), vmem),
        (out((rows_all, LANES), F32), vmem),
        (out((depth, 2, 2, 2, 8, LANES), F32), vmem),
        (out((32 * depth, LANES), BF16), vmem),
        (out((depth, 2, 2, 2, own_rows, MODEL_WIDTH), BF16), anywhere),
        (out((depth, 2, 2, 2, own_rows, hidden), BF16), anywhere),
        (out((depth, 2, 2, 2, down_rows, MODEL_WIDTH), BF16), anywhere),
    ]
    scratch = [
        pltpu.VMEM((4, span, MODEL_WIDTH), BF16),
        pltpu.VMEM((LANES, 2 * half), BF16),
        pltpu.VMEM((depth, 2, 16, LANES), F32),
        pltpu.VMEM((2, depth, 2, 16, half), BF16),
        pltpu.VMEM((depth, 2, 16, half), BF16),
        pltpu.VMEM((depth, 2, 16, half), BF16),
        pltpu.VMEM((depth, 16, half), BF16),
        pltpu.VMEM((depth, 16, half), BF16),
        pltpu.VMEM((depth - 1, 16, half), BF16),
        pltpu.VMEM((16, half), F32),
        pltpu.VMEM((16, half), F32),
        pltpu.VMEM((2, 16, half), F32),
        pltpu.VMEM((64 * depth, LANES), BF16),
        pltpu.VMEM((16, 2 * MODEL_WIDTH), F32),
        pltpu.VMEM((8, own_width), F32),
        pltpu.VMEM((2, rows_all, 2 * LANES), BF16),
        pltpu.VMEM((2, rows_all, 2 * LANES), BF16),
        pltpu.VMEM((rows_all, LANES), BF16),
        pltpu.SemaphoreType.DMA((96,)),
        pltpu.SemaphoreType.DMA((96,)),
        pltpu.SemaphoreType.DMA((24,)),
    ]
    return pl.pallas_call(
        partial(forward_kernel, depth),
        out_shape=[shape for shape, _ in outs],
        in_specs=[scalar, scalar, anywhere, vmem] + [anywhere] * 7,
        out_specs=[spec for _, spec in outs],
        scratch_shapes=scratch,
        compiler_params=pltpu.CompilerParams(
            collective_id=0, has_side_effects=True, vmem_limit_bytes=56 * 1024 * 1024
        ),
        cost_estimate=pl.CostEstimate(flops=8 * 10**9, bytes_accessed=40 * 10**6, transcendentals=10**7),
    )(*args)


def bias_block(query_bias, key_bias, value_bias, output_bias, up_bias, down_bias, modulation_bias):
    rows = [query_bias, key_bias, value_bias, output_bias, up_bias, down_bias]
    rows += [modulation_bias[:LANES], modulation_bias[LANES:]]
    return jnp.stack([jnp.pad(row, (0, LANES - row.shape[0])) for row in rows]).astype(F32)


def turn_back(values, cosine, sine, lane):
    return values * cosine - swap_halves(values, lane) * sine


def from_rows(left, right):
    return lax.dot_general(left, right, (((0,), (0,)), ((), ())), preferred_element_type=F32)


def backward_kernel(
    depth,
    lens, ga, qs_in, ks_in, vs_in, oh_in, lse_in, normed_in, wg_in, cos_in, sin_in, low, mods, frames, gmid,
    mg_in, bias_in, gwo, gup, gdown,
    fgrad, dwq, dwk, dwv, dwo, dup, ddown, dmw, mbias, btile,
    qs, do, oh, lse, normed, wg, cosr, sinr, ka, va, qaug, dk_sum, dv_sum, gr, gw, gwy, gwz, gsum,
    gnp, gnr, gnx, mod3, acc_shift, acc_scale, mg, mgr, mgs, mgx, ev, brecv, bz,
    *rest,
):
    send_sems, recv_sems, local_sems = rest[-3:]
    buffers = rest[:-3]
    here = Place(depth)
    z, y, x, c, g = here.z, here.y, here.x, here.c, here.seq
    span = frames.shape[0]
    rows_all = span * 4
    own_width = wg.shape[-1]
    move = Mover(send_sems, recv_sems, local_sems)
    steps_z = range(1, depth)

    shard = gwo.shape[4]
    width = MODEL_WIDTH
    pieces = []
    for side in range(2):
        pieces.append(
            (gwo.at[:, :, :, :, pl.ds(side * shard // 2, shard // 2)], dwo.at[pl.ds(side * shard // 2, shard // 2)], side)
        )
    for side in range(2):
        pieces.append((gup.at[:, :, :, :, :, pl.ds(side * width, width)], dup.at[:, pl.ds(side * width, width)], 0))
        pieces.append((gdown.at[:, :, :, :, pl.ds(side * shard, shard)], ddown.at[pl.ds(side * shard, shard)], 1))
    own = [buffers[5 * f] for f in range(6)]
    first = [buffers[5 * f + 1] for f in range(6)]
    second = [buffers[5 * f + 2] for f in range(6)]
    third = [buffers[5 * f + 3] for f in range(6)]
    fourth = [buffers[5 * f + 4] for f in range(6)]
    legs = {}

    loads = [
        move.local(ks_in, ka.at[:, :, pl.ds(0, LANES)]),
        move.local(vs_in, va.at[:, :, pl.ds(0, LANES)]),
        move.local(qs_in, qs),
        move.local(oh_in, oh),
        move.local(lse_in, lse),
        move.local(cos_in, cosr),
        move.local(sin_in, sinr),
    ]
    here.enter()
    arrivals = []
    for pair in range(2):
        columns = pl.ds(pl.multiple_of(g * own_width + pair * LANES, LANES), LANES)
        mine = pl.ds(pl.multiple_of(g * span, span), span)
        loads.append(move.local(ga.at[:, columns], do.at[pair, mine]))
        for k in (1, 2, 3):
            peer = (g + k) % 4
            theirs = pl.ds(pl.multiple_of(peer * own_width + pair * LANES, LANES), LANES)
            arrivals.append(move.send(ga.at[:, theirs], do.at[pair, mine], here.row_peer(k)))
    held = []
    for f in range(6):
        source = pieces[f][0]
        legs[f] = move.send(source.at[:, :, :, 1 - c], first[f], here.core())
        held.append(move.local(source.at[:, :, :, c], own[f]))
    late_loads = [move.local(normed_in, normed), move.local(wg_in, wg)]

    def sum_first(f):
        legs[f].wait_recv()
        held[f].wait()

        def add(step, carry):
            own[f][step] = own[f][step] + first[f][step]
            return carry

        lax.fori_loop(0, depth, add, 0)
        if pieces[f][2]:
            legs[f] = move.send(own[f].at[:, :, 1 - x], second[f], here.across_x())
        else:
            legs[f] = move.send(own[f].at[:, 1 - y], second[f], here.across_y())

    def sum_second(f):
        legs[f].wait_recv()

        def add(step, carry):
            for other in range(2):
                if pieces[f][2]:
                    own[f][step, other, x] = own[f][step, other, x] + second[f][step, other]
                else:
                    own[f][step, y, other] = own[f][step, y, other] + second[f][step, other]
            return carry

        lax.fori_loop(0, depth, add, 0)
        if pieces[f][2]:
            legs[f] = move.send(own[f].at[:, 1 - y, x], third[f], here.across_y())
        else:
            legs[f] = move.send(own[f].at[:, y, 1 - x], third[f], here.across_x())

    def sum_third(f):
        legs[f].wait_recv()

        def add(step, carry):
            own[f][step, y, x] = own[f][step, y, x] + third[f][step]
            return carry

        lax.fori_loop(0, depth, add, 0)
        legs[f] = [
            move.send(own[f].at[here.ahead(k), y, x], fourth[f].at[k - 1], here.along_z(k)) for k in steps_z
        ]

    def sum_last(f):
        total = own[f][z, y, x].astype(F32)
        for k in steps_z:
            legs[f][k - 1].wait_recv()
            total = total + fourth[f][k - 1].astype(F32)
        pieces[f][1][...] = total

    def bias_round(peer, slot):
        return move.send(btile, brecv.at[slot], peer)

    block = 128
    for copy in loads:
        copy.wait()

    def columns_of_segments(step, carry):
        rows = pl.ds(pl.multiple_of(step * block, block), block)
        segment, _ = frame_segments(lens, step * block, block, LANES)
        lane = lanes_of((block, LANES))
        same = segment == lane
        qaug[rows, :] = jnp.where((lane < SEGS) & jnp.logical_not(same), NEGATIVE, 0.0).astype(BF16)
        keyside = jnp.where((lane < SEGS) & same, 1.0, jnp.where((lane >= 4) & (lane < 7), 1.0, 0.0))
        for pair in range(2):
            ka[pair, rows, LANES:] = keyside.astype(BF16)
            va[pair, rows, LANES:] = jnp.where(lane < 3, 1.0, 0.0).astype(BF16)
        return carry

    lax.fori_loop(0, rows_all // block, columns_of_segments, 0)

    tall = 256
    steps = rows_all // tall

    def back_block(pair, step):
        rows = pl.ds(pl.multiple_of(step * tall, tall), tall)
        lane = lanes_of((tall, LANES))
        query, given = qs[pair, rows, :], do[pair, rows, :]
        overlap = given.astype(F32) * oh[pair, rows, :].astype(F32)
        mask_columns = qaug[rows, :].astype(F32)
        sums = lse[rows, :]
        grads_q, add_k, add_v = [], 0.0, 0.0
        for head in range(2):
            delta = jnp.sum(jnp.where((lane >= HEAD_DIM) == bool(head), overlap, 0.0), axis=1, keepdims=True)
            logsum = jnp.sum(jnp.where(lane == 2 * pair + head, sums, 0.0), axis=1, keepdims=True)
            a, b, d = three_parts(logsum)
            side = jnp.where(lane == 4, -a, jnp.where(lane == 5, -b, jnp.where(lane == 6, -d, mask_columns)))
            query_head = head_only(query, lane, head)
            left = jnp.concatenate([query_head, side.astype(BF16)], axis=1)
            a, b, d = three_parts(delta)
            side = jnp.where(lane == 0, -a, jnp.where(lane == 1, -b, jnp.where(lane == 2, -d, 0.0)))
            given_head = head_only(given, lane, head)
            right = jnp.concatenate([given_head, side.astype(BF16)], axis=1)
            weights = jnp.exp(across(ka[pair], left))
            grads = (weights * across(va[pair], right)).astype(BF16)
            add_v = add_v + product(weights.astype(BF16), given_head)
            add_k = add_k + product(grads, query_head)
            grads_q.append(from_rows(grads, ka[pair, :, :LANES]))
        dv_sum[...] += add_v
        dk_sum[...] += add_k
        grad_query = jnp.where(lane < HEAD_DIM, grads_q[0], grads_q[1]) * HEAD_DIM**-0.5
        gr[0, rows, pair * LANES : (pair + 1) * LANES] = turn_back(
            grad_query, cosr[rows, :], sinr[rows, :], lane
        ).astype(BF16)

    def back_some(pair, start, stop):
        lax.fori_loop(start, stop, lambda step, carry: (back_block(pair, step), carry)[1], 0)

    def settle_pair(pair):
        def body(step, carry):
            rows = pl.ds(pl.multiple_of(step * block, block), block)
            lane = lanes_of((block, LANES))
            part = slice(pair * LANES, (pair + 1) * LANES)
            gr[1, rows, part] = turn_back(dk_sum[rows, :], cosr[rows, :], sinr[rows, :], lane).astype(BF16)
            gr[2, rows, part] = dv_sum[rows, :].astype(BF16)
            return carry

        lax.fori_loop(0, rows_all // block, body, 0)

    def clear():
        dk_sum[...] = jnp.zeros_like(dk_sum)
        dv_sum[...] = jnp.zeros_like(dv_sum)

    clear()
    sum_first(0)
    sum_first(1)
    sum_first(2)
    sum_first(3)
    for copy in arrivals:
        copy.wait_recv()
    back_some(0, 0, 1)
    sum_first(4)
    sum_first(5)
    back_some(0, 1, 2)
    sum_second(0)
    sum_second(1)
    back_some(0, 2, 4)
    sum_second(2)
    sum_second(3)
    sum_third(0)
    sum_third(1)
    back_some(0, 4, 6)
    settle_pair(0)
    clear()
    sum_second(4)
    sum_second(5)
    sum_third(2)
    sum_third(3)
    back_some(1, 0, 3)
    sum_last(0)
    sum_last(1)
    sum_third(4)
    sum_third(5)
    back_some(1, 3, 6)
    settle_pair(1)
    sum_last(2)
    sum_last(3)
    for copy in late_loads:
        copy.wait()

    def back_rows(target):
        def body(step, carry):
            rows = pl.ds(pl.multiple_of(target * span + step * block, block), block)
            total = 0.0
            for j in range(3):
                total = total + across(gr[j, rows, :], wg[j].reshape(MODEL_WIDTH, own_width))
            gnp[target, pl.ds(pl.multiple_of(step * block, block), block), :] = total.astype(BF16)
            return carry

        lax.fori_loop(0, span // block, body, 0)

    away_other, away_same = (1 - x) * 2 + (1 - c), (1 - x) * 2 + c
    home_other = x * 2 + (1 - c)
    back_rows(away_other)
    gn_core = [move.send(gnp.at[away_other], gnr.at[0], here.core())]
    back_rows(away_same)
    gn_core[0].wait_recv()

    def add_rows(step, carry):
        rows = pl.ds(pl.multiple_of(step * block, block), block)
        gnp[away_same, rows, :] = gnp[away_same, rows, :] + gnr[0, rows, :]
        return carry

    lax.fori_loop(0, span // block, add_rows, 0)
    gn_x = move.send(gnp.at[away_same], gnx, here.across_x())

    tile = 256

    def weight_rows(j):
        def body(step, carry):
            columns = pl.ds(pl.multiple_of(step * tile, tile), tile)
            result = from_rows(normed[:, columns], gr[j]).astype(BF16)
            per = 2 * 4 * shard // tile
            lead = result.reshape(tile // (4 * shard), 4, shard, own_width)
            for n in range(tile // (4 * shard)):
                gw[j, step // per, (step % per) * (tile // (4 * shard)) + n] = lead[n]
            return carry

        lax.fori_loop(0, MODEL_WIDTH // tile, body, 0)

    gw_y, gw_z = [], []
    for j in range(3):
        weight_rows(j)
        gw_y.append(move.send(gw.at[j, :, 1 - y], gwy.at[j], here.across_y()))
    ones = jnp.ones((16, rows_all), BF16)
    btile[...] = bias_in[...]
    for j in range(3):
        sums = product(ones, gr[j])
        for half in range(2):
            btile[pl.ds(8 * j + g * 2 + half, 1), :] = sums[0:1, half * LANES : (half + 1) * LANES]
    bias_core = move.send(btile, brecv.at[0], here.core())
    back_rows(home_other)
    gn_core.append(move.send(gnp.at[home_other], gnr.at[1], here.core()))
    back_rows(g)
    sum_last(4)
    sum_last(5)
    bias_core.wait()
    btile[...] = btile[...] + brecv[0]
    bias_x = move.send(btile, brecv.at[1], here.across_x())

    def sum_gw(j):
        gw_y[j].wait_recv()

        def add(step, carry):
            gw[j, step, y] = gw[j, step, y] + gwy[j, step]
            return carry

        lax.fori_loop(0, depth, add, 0)
        gw_z.append(
            [move.send(gw.at[j, here.ahead(k), y], gwz.at[j, k - 1], here.along_z(k)) for k in steps_z]
        )

    for j in range(3):
        sum_gw(j)
    bias_x.wait()
    btile[...] = btile[...] + brecv[1]
    bias_y = move.send(btile, brecv.at[2], here.across_y())

    high, middle, rest_part = three_parts(mods[0:4, MODEL_WIDTH : 2 * MODEL_WIDTH])
    mod3[0:4, :] = high
    mod3[4:8, :] = middle
    mod3[8:12, :] = rest_part
    mod3[12:16, :] = jnp.zeros((4, MODEL_WIDTH), F32)
    acc_shift[...] = jnp.zeros_like(acc_shift)
    acc_scale[...] = jnp.zeros_like(acc_scale)
    gn_core[1].wait_recv()
    gn_x.wait_recv()

    def two_parts(values):
        top = values.astype(BF16)
        return top, (values - top.astype(F32)).astype(BF16)

    def norm_rows(step, carry):
        rows = pl.ds(pl.multiple_of(step * block, block), block)
        grad = gnp[g, rows, :].astype(F32) + gnr[1, rows, :].astype(F32) + gnx[rows, :].astype(F32)
        values = frames[rows, :].astype(F32)
        center = jnp.mean(values, axis=1, keepdims=True)
        centered = values - center
        scaled = lax.rsqrt(jnp.mean(centered * centered, axis=1, keepdims=True) + EPSILON)
        hat = centered * scaled
        base = g * span + step * block
        segment, _ = frame_segments(lens, base, block, 16)
        slot = lanes_of((block, 16))
        chosen = jnp.where((slot < 12) & (slot % 4 == segment), 1.0, 0.0).astype(BF16)
        inner = grad * (1.0 + product(chosen, mod3[...].astype(BF16)))
        mean_one = jnp.mean(inner, axis=1, keepdims=True)
        mean_two = jnp.mean(inner * hat, axis=1, keepdims=True)
        fgrad[rows, :] = (gmid[rows, :] + scaled * (inner - mean_one - hat * mean_two)).astype(BF16)
        position = base + lanes_of((16, block))
        begin = [lens[0, 0], lens[0, 0] + lens[0, 1], lens[0, 0] + lens[0, 1] + lens[0, 2]]
        inside = sum((position >= edge).astype(jnp.int32) for edge in begin)
        members = jnp.where(inside == lanes_of((16, block), 0), 1.0, 0.0).astype(BF16)
        for values, target in ((grad, acc_shift), (grad * hat, acc_scale)):
            top, bottom = two_parts(values)
            target[...] += product(members, top) + product(members, bottom)
        return carry

    lax.fori_loop(0, span // block, norm_rows, 0)

    half = 6 * MODEL_WIDTH // 8
    for side in range(2):
        mg[side] = mg_in[:, side * half : (side + 1) * half]
    for q in range(8):
        if q * half >= 2 * MODEL_WIDTH:
            break
        j, side = q // 2, q % 2
        for target, start in ((acc_shift, 0), (acc_scale, MODEL_WIDTH)):
            low_end, high_end = max(q * half, start), min((q + 1) * half, start + MODEL_WIDTH)
            if low_end < high_end:
                mg[side, 4 * j : 4 * j + 4, low_end - q * half : high_end - q * half] = target[
                    0:4, low_end - start : high_end - start
                ]
    mod_core = move.send(mg.at[1 - c], mgr, here.core())
    mod_core.wait_recv()
    mgs[...] = mg[c] + mgr[...]
    mod_x = move.send(mgs, mgx, here.across_x())
    bias_y.wait()
    btile[...] = btile[...] + brecv[2]
    bias_z = [move.send(btile, bz.at[k - 1], here.along_z(k)) for k in steps_z]
    outs = (dwq, dwk, dwv)
    final = []
    final_locals = []

    def last_gw(j):
        total = gw[j, z, y].astype(F32)
        for k in steps_z:
            gw_z[j][k - 1].wait_recv()
            total = total + gwz[j, k - 1].astype(F32)
        gsum[j] = total
        columns = pl.ds(pl.multiple_of(g * own_width, LANES), own_width)
        final_locals.append(move.local(gsum.at[j, g], outs[j].at[:, columns]))
        for k in (1, 2, 3):
            final.append(move.send(gsum.at[j, (g + k) % 4], outs[j].at[:, columns], here.row_peer(k)))

    last_gw(0)
    mod_x.wait_recv()
    ev[z, y, c] = (mgs[...] + mgx[...]).astype(BF16)
    mod_z = [move.send(ev.at[z, y, c], ev.at[z, y, c], here.along_z(k)) for k in steps_z]
    last_gw(1)
    for copy in mod_z:
        copy.wait_recv()
    mod_y = move.send(ev.at[:, y, c], ev.at[:, y, c], here.across_y())
    last_gw(2)
    for copy in bias_z:
        copy.wait()
    total = btile[...]
    for k in steps_z:
        total = total + bz[k - 1]
    btile[...] = total
    mod_y.wait_recv()
    mod_last = move.send(ev.at[:, :, c], ev.at[:, :, c], here.core())
    picks = jnp.where(
        lanes_of((16, 32 * depth), 0) == (lanes_of((16, 32 * depth)) % 16) // 4, 1.0, 0.0
    ).astype(BF16)

    def finish_side(side):
        every = ev[:, :, side].reshape(32 * depth, half)
        result = from_rows(low[...], every)
        summed = product(picks, every)
        for j in range(4):
            dmw[:, j * 2 * half + side * half : j * 2 * half + (side + 1) * half] = result[32 * j : 32 * (j + 1), :]
        mbias[:, side * half : (side + 1) * half] = summed[0:8, :]

    mod_last.wait_recv()
    finish_side(0)
    finish_side(1)
    for copy in final_locals:
        copy.wait()
    for copy in final:
        copy.wait_recv()
    move.finish(but=[bias_core, bias_x, bias_y] + bias_z)


def backward_call(depth, span, own_rows, down_rows, hidden, args):
    rows_all, own_width = 4 * span, MODEL_WIDTH // 4
    half = 6 * MODEL_WIDTH // 8
    vmem, anywhere, scalar = (
        pl.BlockSpec(memory_space=pltpu.VMEM),
        pl.BlockSpec(memory_space=pl.ANY),
        pl.BlockSpec(memory_space=pltpu.SMEM),
    )

    def out(shape, dtype):
        return jax.ShapeDtypeStruct(shape, dtype)

    outs = [
        (out((span, MODEL_WIDTH), BF16), vmem),
        (out((own_rows, MODEL_WIDTH), F32), anywhere),
        (out((own_rows, MODEL_WIDTH), F32), anywhere),
        (out((own_rows, MODEL_WIDTH), F32), anywhere),
        (out((own_rows, MODEL_WIDTH), F32), vmem),
        (out((own_rows, hidden), F32), vmem),
        (out((down_rows, MODEL_WIDTH), F32), vmem),
        (out((own_rows, 6 * MODEL_WIDTH), F32), vmem),
        (out((8, 2 * half), F32), vmem),
        (out((56, LANES), F32), vmem),
    ]
    pair_rows = pltpu.VMEM((2, rows_all, LANES), BF16)
    wide_rows = pltpu.VMEM((2, rows_all, 2 * LANES), BF16)
    table = pltpu.VMEM((rows_all, LANES), F32)
    scratch = [
        pair_rows, pair_rows, pair_rows, table,
        pltpu.VMEM((rows_all, MODEL_WIDTH), BF16),
        pltpu.VMEM((3, depth, 2, 4, own_rows, own_width), BF16),
        table, table, wide_rows, wide_rows,
        pltpu.VMEM((rows_all, LANES), BF16),
        table, table,
        pltpu.VMEM((3, rows_all, own_width), BF16),
        pltpu.VMEM((3, depth, 2, 4, own_rows, own_width), BF16),
        pltpu.VMEM((3, depth, 4, own_rows, own_width), BF16),
        pltpu.VMEM((3, depth - 1, 4, own_rows, own_width), BF16),
        pltpu.VMEM((3, 4, own_rows, own_width), F32),
        pltpu.VMEM((4, span, MODEL_WIDTH), BF16),
        pltpu.VMEM((2, span, MODEL_WIDTH), BF16),
        pltpu.VMEM((span, MODEL_WIDTH), BF16),
        pltpu.VMEM((16, MODEL_WIDTH), F32),
        pltpu.VMEM((16, MODEL_WIDTH), F32),
        pltpu.VMEM((16, MODEL_WIDTH), F32),
        pltpu.VMEM((2, 16, half), F32),
        pltpu.VMEM((16, half), F32),
        pltpu.VMEM((16, half), F32),
        pltpu.VMEM((16, half), F32),
        pltpu.VMEM((depth, 2, 2, 16, half), BF16),
        pltpu.VMEM((3, 56, LANES), F32),
        pltpu.VMEM((depth - 1, 56, LANES), F32),
    ]
    for f in range(6):
        rows = own_rows // 2 if f < 2 else own_rows
        piece = (rows, MODEL_WIDTH)
        scratch += [
            pltpu.VMEM((depth, 2, 2) + piece, BF16),
            pltpu.VMEM((depth, 2, 2) + piece, BF16),
            pltpu.VMEM((depth, 2) + piece, BF16),
            pltpu.VMEM((depth,) + piece, BF16),
            pltpu.VMEM((depth - 1,) + piece, BF16),
        ]
    scratch += [pltpu.SemaphoreType.DMA((96,)), pltpu.SemaphoreType.DMA((96,)), pltpu.SemaphoreType.DMA((32,))]
    return pl.pallas_call(
        partial(backward_kernel, depth),
        out_shape=[shape for shape, _ in outs],
        in_specs=[scalar] + [anywhere] * 10 + [vmem] * 6 + [anywhere] * 3,
        out_specs=[spec for _, spec in outs],
        scratch_shapes=scratch,
        compiler_params=pltpu.CompilerParams(
            collective_id=1, has_side_effects=True, vmem_limit_bytes=62 * 1024 * 1024
        ),
        cost_estimate=pl.CostEstimate(flops=2 * 10**10, bytes_accessed=40 * 10**6, transcendentals=10**7),
    )(*args)


def modulated_norm(values, shift_part, scale_part):
    center = jnp.mean(values, axis=-1, keepdims=True)
    centered = values - center
    variance = jnp.mean(centered * centered, axis=-1, keepdims=True)
    return centered * lax.rsqrt(variance + EPSILON) * (1.0 + scale_part) + shift_part


def rotate(values, cosines, sines_table):
    shaped = values.reshape(values.shape[:-1] + (values.shape[-1] // HEAD_DIM, HEAD_DIM))
    first_half = shaped[..., : HEAD_DIM // 2]
    second_half = shaped[..., HEAD_DIM // 2 :]
    cosine = cosines[..., None, :]
    sine_part = sines_table[..., None, :]
    turned = jnp.concatenate(
        [
            first_half * cosine - second_half * sine_part,
            second_half * cosine + first_half * sine_part,
        ],
        axis=-1,
    )
    return turned.reshape(values.shape)


def gelu_tanh(values):
    return jax.nn.gelu(values, approximate=True)


def time_features(time_index):
    halfway = MODEL_WIDTH // 2
    frequency = jnp.exp(jnp.arange(halfway, dtype=jnp.float32) * (-math.log(10000.0) / halfway))
    angles = time_index.astype(jnp.float32)[..., None] * frequency
    return jnp.concatenate([jnp.sin(angles), jnp.cos(angles)], axis=-1)


def segment_starts(segment_lengths):
    return jnp.cumsum(segment_lengths, axis=1) - segment_lengths


def segment_numbers(segment_lengths, frame_positions):
    starts = segment_starts(segment_lengths)
    inside = (frame_positions[None, :, None] >= starts[:, None, :]).astype(jnp.int32)
    return jnp.sum(inside, axis=2) - 1


def segment_layout(segment_lengths, frame_positions):
    starts = segment_starts(segment_lengths)
    segment = segment_numbers(segment_lengths, frame_positions)
    onehot = (segment[..., None] == jnp.arange(SEGS, dtype=jnp.int32)).astype(jnp.float32)
    offset = jnp.sum(onehot * starts[:, None, :].astype(jnp.float32), axis=2)
    relative = frame_positions[None, :].astype(jnp.float32) - offset
    return (onehot, relative)


def rope_tables(relative):
    halfway = HEAD_DIM // 2
    frequency = jnp.exp(jnp.arange(halfway, dtype=jnp.float32) * (-math.log(10000.0) / halfway))
    angles = relative[..., None] * frequency
    return (jnp.cos(angles), jnp.sin(angles))


def project(values, matrix, offset):
    return jnp.einsum(
        "rld,de->rle", values, matrix, preferred_element_type=jnp.float32
    ) + offset.astype(jnp.float32)


def project_back(gradient, matrix):
    return jnp.einsum("rle,de->rld", gradient, matrix, preferred_element_type=jnp.float32)


def weight_gradient(values, gradient):
    return jnp.einsum("rld,rle->de", values, gradient, preferred_element_type=jnp.float32)


def bias_gradient(gradient):
    return jnp.sum(gradient.astype(jnp.float32), axis=(0, 1))


def lift_up(member):
    return member.reshape((1, 1) + member.shape)


def settle(member):
    return member.reshape((-1,) + member.shape[3:])


def spread(member, wide_count, narrow_count):
    return member.reshape((wide_count, narrow_count, -1) + member.shape[1:])


def unpack(member):
    return member.reshape(member.shape[2:])


def on_device(
    frames,
    output_gradient,
    segment_lengths,
    time_index,
    query_weight,
    query_bias,
    key_weight,
    key_bias,
    value_weight,
    value_bias,
    output_projection,
    output_bias,
    up_weight,
    up_bias,
    down_weight,
    down_bias,
    modulation_weight,
    modulation_bias,
):
    narrow_count = lax.axis_size("seq")
    wide_count = lax.axis_size("dp")
    seq_index = lax.axis_index("seq")
    row_count, span_frames, width_total = frames.shape
    row_length = span_frames * narrow_count
    block_rows = min(512, row_length)
    block_count = row_length // block_rows
    local_weights = (
        query_weight,
        query_bias,
        key_weight,
        key_bias,
        value_weight,
        value_bias,
        output_projection,
        output_bias,
        up_weight,
        up_bias,
        down_weight,
        down_bias,
        modulation_bias,
    )
    lifted = [lift_up(member) for member in local_weights]
    halfway_set = (
        lax.all_gather(lifted[0], "dp", axis=0, tiled=True),
        lax.all_gather(lifted[1], "dp", axis=0, tiled=True),
        lax.all_gather(lifted[2], "dp", axis=0, tiled=True),
        lax.all_gather(lifted[3], "dp", axis=0, tiled=True),
        lax.all_gather(lifted[4], "dp", axis=0, tiled=True),
        lax.all_gather(lifted[5], "dp", axis=0, tiled=True),
        lax.all_gather(lifted[6], "dp", axis=0, tiled=True),
        lax.all_gather(lifted[7], "dp", axis=0, tiled=True),
        lax.all_gather(lifted[8], "dp", axis=0, tiled=True),
        lax.all_gather(lifted[9], "dp", axis=0, tiled=True),
        lax.all_gather(lifted[10], "dp", axis=0, tiled=True),
        lax.all_gather(lifted[11], "dp", axis=0, tiled=True),
        lax.all_gather(lifted[12], "dp", axis=0, tiled=True),
    )
    complete_set = (
        lax.all_gather(halfway_set[0], "seq", axis=1, tiled=True),
        lax.all_gather(halfway_set[1], "seq", axis=1, tiled=True),
        lax.all_gather(halfway_set[2], "seq", axis=1, tiled=True),
        lax.all_gather(halfway_set[3], "seq", axis=1, tiled=True),
        lax.all_gather(halfway_set[4], "seq", axis=1, tiled=True),
        lax.all_gather(halfway_set[5], "seq", axis=1, tiled=True),
        lax.all_gather(halfway_set[6], "seq", axis=1, tiled=True),
        lax.all_gather(halfway_set[7], "seq", axis=1, tiled=True),
        lax.all_gather(halfway_set[8], "seq", axis=1, tiled=True),
        lax.all_gather(halfway_set[9], "seq", axis=1, tiled=True),
        lax.all_gather(halfway_set[10], "seq", axis=1, tiled=True),
        lax.all_gather(halfway_set[11], "seq", axis=1, tiled=True),
        lax.all_gather(halfway_set[12], "seq", axis=1, tiled=True),
    )
    gathered = [settle(member) for member in complete_set]
    (
        full_query,
        full_query_bias,
        full_key,
        full_key_bias,
        full_value,
        full_value_bias,
        full_output,
        full_output_bias,
        full_up,
        full_up_bias,
        full_down,
        full_down_bias,
        full_modulation_bias,
    ) = gathered
    local_positions = seq_index * span_frames + jnp.arange(span_frames, dtype=jnp.int32)
    local_onehot, local_relative = segment_layout(segment_lengths, local_positions)
    row_segment = segment_numbers(segment_lengths, jnp.arange(row_length, dtype=jnp.int32))
    cosines, sines_table = rope_tables(local_relative)
    turning = partial(rotate, cosines=cosines, sines_table=sines_table)
    owned_rows = modulation_weight.shape[0]
    owned_start = (lax.axis_index("dp") * narrow_count + seq_index) * owned_rows
    every_time = lax.all_gather(time_index, "dp", axis=0, tiled=True)
    every_low = jax.nn.silu(time_features(every_time)).astype(jnp.bfloat16)
    owned_low = lax.dynamic_slice_in_dim(every_low, owned_start, owned_rows, 2)
    partial_modulation = jnp.einsum(
        "rsd,dc->rsc", owned_low, modulation_weight, preferred_element_type=jnp.float32
    )
    row_share = lax.psum_scatter(partial_modulation, "dp", scatter_dimension=0, tiled=True)
    modulation = lax.psum(row_share.astype(jnp.bfloat16), "seq").astype(
        jnp.float32
    ) + full_modulation_bias.astype(jnp.float32)
    per_frame = jnp.einsum("rls,rsc->rlc", local_onehot, modulation, precision=HIGHEST)
    shift_one, scale_one, gate_one, shift_two, scale_two, gate_two = jnp.split(
        per_frame, 6, axis=-1
    )
    inputs = frames.astype(jnp.float32)
    normed, norm_back = jax.vjp(modulated_norm, inputs, shift_one, scale_one)
    normed_low = normed.astype(jnp.bfloat16)
    query_pre = project(normed_low, full_query, full_query_bias)
    key_pre = project(normed_low, full_key, full_key_bias)
    value_low = project(normed_low, full_value, full_value_bias).astype(jnp.bfloat16)
    query_turned, query_back = jax.vjp(turning, query_pre)
    key_turned, key_back = jax.vjp(turning, key_pre)
    query_heads, key_heads, value_heads = (
        lax.all_to_all(
            query_turned.astype(jnp.bfloat16), "seq", split_axis=2, concat_axis=1, tiled=True
        ),
        lax.all_to_all(
            key_turned.astype(jnp.bfloat16), "seq", split_axis=2, concat_axis=1, tiled=True
        ),
        lax.all_to_all(value_low, "seq", split_axis=2, concat_axis=1, tiled=True),
    )
    local_heads = query_heads.shape[2] // HEAD_DIM
    head_shape = (row_count, row_length, local_heads, HEAD_DIM)
    queries = query_heads.reshape(head_shape)
    keys_all = key_heads.reshape(head_shape)
    values_all = value_heads.reshape(head_shape)
    scaling = HEAD_DIM ** (-0.5)
    positions_all = jnp.arange(row_count * block_count, dtype=jnp.int32)

    def fetch_block(position):
        row_index = position // block_count
        start_row = position % block_count * block_rows
        key_row = lax.dynamic_index_in_dim(keys_all, row_index, 0, keepdims=False)
        value_row = lax.dynamic_index_in_dim(values_all, row_index, 0, keepdims=False)
        segment_row = lax.dynamic_index_in_dim(row_segment, row_index, 0, keepdims=False)
        query_block = lax.dynamic_slice_in_dim(
            lax.dynamic_index_in_dim(queries, row_index, 0, keepdims=False),
            start_row,
            block_rows,
            0,
        )
        segment_block = lax.dynamic_slice_in_dim(segment_row, start_row, block_rows, 0)
        scores = (
            jnp.einsum("bhd,khd->hbk", query_block, key_row, preferred_element_type=jnp.float32)
            * scaling
        )
        scores = jnp.where((segment_block[:, None] == segment_row[None, :])[None], scores, NEGATIVE)
        return (row_index, start_row, query_block, key_row, value_row, scores)

    def forward_block(position):
        row_index, start_row, query_block, key_row, value_row, scores = fetch_block(position)
        highest = jnp.max(scores, axis=2, keepdims=True)
        weights = jnp.exp(scores - highest)
        totals = jnp.sum(weights, axis=2, keepdims=True)
        probabilities = (weights / totals).astype(jnp.bfloat16)
        mixed_block = jnp.einsum(
            "hbk,khd->bhd", probabilities, value_row, preferred_element_type=jnp.float32
        )
        return (
            mixed_block.astype(jnp.bfloat16).reshape(block_rows, -1),
            (highest + jnp.log(totals))[..., 0],
        )

    mixed_blocks, logsums = lax.map(forward_block, positions_all)
    attention_heads = mixed_blocks.reshape(row_count, row_length, -1)
    attention_frames = lax.all_to_all(
        attention_heads, "seq", split_axis=1, concat_axis=2, tiled=True
    )
    branch = project(attention_frames, full_output, full_output_bias)
    middle = inputs + gate_one * branch
    normed_two, norm_two_back = jax.vjp(modulated_norm, middle, shift_two, scale_two)
    normed_two_low = normed_two.astype(jnp.bfloat16)
    hidden = project(normed_two_low, full_up, full_up_bias)
    activated, gelu_back = jax.vjp(gelu_tanh, hidden)
    activated_low = activated.astype(jnp.bfloat16)
    branch_two = project(activated_low, full_down, full_down_bias)
    layer_output = (middle + gate_two * branch_two).astype(jnp.bfloat16)
    cotangent = output_gradient.astype(jnp.float32)
    grad_branch_two = (gate_two * cotangent).astype(jnp.bfloat16)
    grad_gate_two = cotangent * branch_two
    grad_activated = project_back(grad_branch_two, full_down)
    grad_hidden = gelu_back(grad_activated)[0].astype(jnp.bfloat16)
    grad_normed_two = project_back(grad_hidden, full_up)
    grad_middle_part, grad_shift_two, grad_scale_two = norm_two_back(grad_normed_two)
    grad_middle = cotangent + grad_middle_part
    grad_gate_one = grad_middle * branch
    grad_branch = (gate_one * grad_middle).astype(jnp.bfloat16)
    grad_attention = project_back(grad_branch, full_output).astype(jnp.bfloat16)
    grad_heads = lax.all_to_all(grad_attention, "seq", split_axis=2, concat_axis=1, tiled=True)
    grad_outputs = grad_heads.reshape(head_shape)

    def backward_block(running, pair_inputs):
        grad_keys, grad_values = running
        position, logsum = pair_inputs
        row_index, start_row, query_block, key_row, value_row, scores = fetch_block(position)
        grad_block = lax.dynamic_slice_in_dim(
            lax.dynamic_index_in_dim(grad_outputs, row_index, 0, keepdims=False),
            start_row,
            block_rows,
            0,
        )
        probabilities = jnp.exp(scores - logsum[..., None])
        grad_probabilities = jnp.einsum(
            "bhd,khd->hbk", grad_block, value_row, preferred_element_type=jnp.float32
        )
        delta_sum = jnp.sum(probabilities * grad_probabilities, axis=2, keepdims=True)
        grad_scores = (probabilities * (grad_probabilities - delta_sum)).astype(jnp.bfloat16)
        grad_query_block = (
            jnp.einsum("hbk,khd->bhd", grad_scores, key_row, preferred_element_type=jnp.float32)
            * scaling
        )
        key_part = (
            jnp.einsum("hbk,bhd->khd", grad_scores, query_block, preferred_element_type=jnp.float32)
            * scaling
        )
        value_part = jnp.einsum(
            "hbk,bhd->khd",
            probabilities.astype(jnp.bfloat16),
            grad_block,
            preferred_element_type=jnp.float32,
        )
        grad_keys = lax.dynamic_update_index_in_dim(
            grad_keys,
            lax.dynamic_index_in_dim(grad_keys, row_index, 0, keepdims=False) + key_part,
            row_index,
            0,
        )
        grad_values = lax.dynamic_update_index_in_dim(
            grad_values,
            lax.dynamic_index_in_dim(grad_values, row_index, 0, keepdims=False) + value_part,
            row_index,
            0,
        )
        return (
            (grad_keys, grad_values),
            grad_query_block.astype(jnp.bfloat16).reshape(block_rows, -1),
        )

    zero_heads = jnp.zeros(head_shape, jnp.float32)
    (grad_keys_all, grad_values_all), grad_query_blocks = lax.scan(
        backward_block, (zero_heads, zero_heads), (positions_all, logsums)
    )
    flat_shape = (row_count, row_length, -1)
    grad_query_frames, grad_key_frames, grad_value_frames = (
        lax.all_to_all(
            grad_query_blocks.reshape(flat_shape), "seq", split_axis=1, concat_axis=2, tiled=True
        ),
        lax.all_to_all(
            grad_keys_all.reshape(flat_shape).astype(jnp.bfloat16),
            "seq",
            split_axis=1,
            concat_axis=2,
            tiled=True,
        ),
        lax.all_to_all(
            grad_values_all.reshape(flat_shape).astype(jnp.bfloat16),
            "seq",
            split_axis=1,
            concat_axis=2,
            tiled=True,
        ),
    )
    grad_query_pre = query_back(grad_query_frames.astype(jnp.float32))[0].astype(jnp.bfloat16)
    grad_key_pre = key_back(grad_key_frames.astype(jnp.float32))[0].astype(jnp.bfloat16)
    grad_normed = (
        project_back(grad_query_pre, full_query)
        + project_back(grad_key_pre, full_key)
        + project_back(grad_value_frames, full_value)
    )
    grad_inputs_part, grad_shift_one, grad_scale_one = norm_back(grad_normed)
    frames_grad = (grad_middle + grad_inputs_part).astype(jnp.bfloat16)
    grad_per_frame = jnp.concatenate(
        [
            grad_shift_one,
            grad_scale_one,
            grad_gate_one,
            grad_shift_two,
            grad_scale_two,
            grad_gate_two,
        ],
        axis=-1,
    )
    grad_modulation = jnp.einsum("rls,rlc->rsc", local_onehot, grad_per_frame, precision=HIGHEST)
    gradients = (
        weight_gradient(normed_low, grad_query_pre),
        bias_gradient(grad_query_pre),
        weight_gradient(normed_low, grad_key_pre),
        bias_gradient(grad_key_pre),
        weight_gradient(normed_low, grad_value_frames),
        bias_gradient(grad_value_frames),
        weight_gradient(attention_frames, grad_branch),
        bias_gradient(grad_branch),
        weight_gradient(normed_two_low, grad_hidden),
        bias_gradient(grad_hidden),
        weight_gradient(activated_low, grad_branch_two),
        bias_gradient(grad_branch_two),
        jnp.sum(grad_modulation, axis=(0, 1)),
    )
    row_total = lax.psum(grad_modulation.astype(jnp.bfloat16), "seq").astype(jnp.float32)
    every_grad = lax.all_gather(row_total.astype(jnp.bfloat16), "dp", axis=0, tiled=True).astype(
        row_total.dtype
    )
    modulation_weight_grad = jnp.einsum(
        "rsd,rsc->dc", owned_low.astype(jnp.float32), every_grad, precision=HIGHEST
    )
    spreaded = [spread(member, wide_count, narrow_count) for member in gradients]
    first_pass = (
        lax.psum_scatter(
            spreaded[0].astype(jnp.bfloat16), "seq", scatter_dimension=1, tiled=True
        ).astype(jnp.float32),
        lax.psum_scatter(
            spreaded[1].astype(jnp.bfloat16), "seq", scatter_dimension=1, tiled=True
        ).astype(jnp.float32),
        lax.psum_scatter(
            spreaded[2].astype(jnp.bfloat16), "seq", scatter_dimension=1, tiled=True
        ).astype(jnp.float32),
        lax.psum_scatter(
            spreaded[3].astype(jnp.bfloat16), "seq", scatter_dimension=1, tiled=True
        ).astype(jnp.float32),
        lax.psum_scatter(
            spreaded[4].astype(jnp.bfloat16), "seq", scatter_dimension=1, tiled=True
        ).astype(jnp.float32),
        lax.psum_scatter(
            spreaded[5].astype(jnp.bfloat16), "seq", scatter_dimension=1, tiled=True
        ).astype(jnp.float32),
        lax.psum_scatter(
            spreaded[6].astype(jnp.bfloat16), "seq", scatter_dimension=1, tiled=True
        ).astype(jnp.float32),
        lax.psum_scatter(
            spreaded[7].astype(jnp.bfloat16), "seq", scatter_dimension=1, tiled=True
        ).astype(jnp.float32),
        lax.psum_scatter(
            spreaded[8].astype(jnp.bfloat16), "seq", scatter_dimension=1, tiled=True
        ).astype(jnp.float32),
        lax.psum_scatter(
            spreaded[9].astype(jnp.bfloat16), "seq", scatter_dimension=1, tiled=True
        ).astype(jnp.float32),
        lax.psum_scatter(
            spreaded[10].astype(jnp.bfloat16), "seq", scatter_dimension=1, tiled=True
        ).astype(jnp.float32),
        lax.psum_scatter(
            spreaded[11].astype(jnp.bfloat16), "seq", scatter_dimension=1, tiled=True
        ).astype(jnp.float32),
        lax.psum_scatter(
            spreaded[12].astype(jnp.bfloat16), "seq", scatter_dimension=1, tiled=True
        ).astype(jnp.float32),
    )
    second_pass = (
        lax.psum_scatter(first_pass[0], "dp", scatter_dimension=0, tiled=True),
        lax.psum_scatter(first_pass[1], "dp", scatter_dimension=0, tiled=True),
        lax.psum_scatter(first_pass[2], "dp", scatter_dimension=0, tiled=True),
        lax.psum_scatter(first_pass[3], "dp", scatter_dimension=0, tiled=True),
        lax.psum_scatter(first_pass[4], "dp", scatter_dimension=0, tiled=True),
        lax.psum_scatter(first_pass[5], "dp", scatter_dimension=0, tiled=True),
        lax.psum_scatter(first_pass[6], "dp", scatter_dimension=0, tiled=True),
        lax.psum_scatter(first_pass[7], "dp", scatter_dimension=0, tiled=True),
        lax.psum_scatter(first_pass[8], "dp", scatter_dimension=0, tiled=True),
        lax.psum_scatter(first_pass[9], "dp", scatter_dimension=0, tiled=True),
        lax.psum_scatter(first_pass[10], "dp", scatter_dimension=0, tiled=True),
        lax.psum_scatter(first_pass[11], "dp", scatter_dimension=0, tiled=True),
        lax.psum_scatter(first_pass[12], "dp", scatter_dimension=0, tiled=True),
    )
    reduced = [unpack(member) for member in second_pass]
    return (
        layer_output,
        frames_grad,
        reduced[0],
        reduced[1],
        reduced[2],
        reduced[3],
        reduced[4],
        reduced[5],
        reduced[6],
        reduced[7],
        reduced[8],
        reduced[9],
        reduced[10],
        reduced[11],
        modulation_weight_grad,
        reduced[12],
    )


def on_device_fast(
    frames, output_gradient, segment_lengths, time_index, query_weight, query_bias, key_weight, key_bias,
    value_weight, value_bias, output_projection, output_bias, up_weight, up_bias, down_weight, down_bias,
    modulation_weight, modulation_bias,
):
    seq_index, dp_index = lax.axis_index("seq"), lax.axis_index("dp")
    depth = lax.axis_size("dp") // 2
    own_index = dp_index * 4 + seq_index
    _, span, width = frames.shape
    own_rows, hidden = up_weight.shape
    down_rows = down_weight.shape[0]
    blocks = bias_block(query_bias, key_bias, value_bias, output_bias, up_bias, down_bias, modulation_bias)
    (att, oh, qs, ks, vs, lse, normed, wg, mods, cosr, sinr, bb, low, wo_all, up_all, down_all) = forward_call(
        depth, span, own_rows, down_rows, hidden,
        (segment_lengths, time_index, frames[0], blocks, query_weight, key_weight, value_weight,
         output_projection, up_weight, down_weight, modulation_weight),
    )
    gathered_bias = bb.reshape(-1, 8, LANES)
    full_output_bias = gathered_bias[:, 3, : output_bias.shape[0]].reshape(-1)
    full_up_bias = gathered_bias[:, 4, : up_bias.shape[0]].reshape(-1)
    full_down_bias = gathered_bias[:, 5, : down_bias.shape[0]].reshape(-1)
    full_output = wo_all.reshape(width, width)
    full_up = up_all.reshape(width, hidden)
    full_down = down_all.reshape(hidden, width)
    local_positions = seq_index * span + jnp.arange(span, dtype=jnp.int32)
    onehot, _ = segment_layout(segment_lengths, local_positions)
    onehot = onehot[0]
    per_frame = jnp.einsum("ls,sc->lc", onehot, mods[:SEGS, 2 * width :], precision=HIGHEST)
    gate_one, shift_two, scale_two, gate_two = jnp.split(per_frame, 4, axis=-1)
    inputs = frames[0].astype(F32)
    branch = product(att, full_output) + full_output_bias
    middle = inputs + gate_one * branch
    normed_two, norm_two_back = jax.vjp(modulated_norm, middle, shift_two, scale_two)
    normed_two_low = normed_two.astype(BF16)
    hidden_rows = product(normed_two_low, full_up) + full_up_bias
    activated, gelu_back = jax.vjp(gelu_tanh, hidden_rows)
    activated_low = activated.astype(BF16)
    branch_two = product(activated_low, full_down) + full_down_bias
    layer_output = (middle + gate_two * branch_two).astype(BF16)
    cotangent = output_gradient[0].astype(F32)
    grad_branch_two = (gate_two * cotangent).astype(BF16)
    grad_gate_two = cotangent * branch_two
    grad_activated = across(grad_branch_two, full_down)
    grad_hidden = gelu_back(grad_activated)[0].astype(BF16)
    grad_normed_two = across(grad_hidden, full_up)
    grad_middle_part, grad_shift_two, grad_scale_two = norm_two_back(grad_normed_two)
    grad_middle = cotangent + grad_middle_part
    grad_gate_one = grad_middle * branch
    grad_branch = (gate_one * grad_middle).astype(BF16)
    grad_attention = across(grad_branch, full_output).astype(BF16)
    grad_per_frame = jnp.concatenate([grad_gate_one, grad_shift_two, grad_scale_two, grad_gate_two], axis=-1)
    grad_mods = jnp.einsum("ls,lc->sc", onehot, grad_per_frame, precision=HIGHEST)
    mg_in = jnp.pad(grad_mods, ((0, 0), (2 * width, 0)))
    mg_in = mg_in.reshape(SEGS, 4, -1).transpose(1, 0, 2).reshape(16, -1)

    def pieces(grad, rows):
        return grad.astype(BF16).reshape(depth, 2, 2, 2, rows, -1)

    def column_sums(grad):
        return jnp.sum(grad.astype(F32), axis=0).reshape(-1, LANES)

    bias_in = jnp.concatenate(
        [jnp.zeros((24, LANES), F32), column_sums(grad_branch), column_sums(grad_hidden), column_sums(grad_branch_two)]
    )
    (fgrad, dwq, dwk, dwv, dwo, dup, ddown, dmw, mbias, btile) = backward_call(
        depth, span, own_rows, down_rows, hidden,
        (segment_lengths, grad_attention, qs, ks, vs, oh, lse, normed, wg, cosr, sinr, low, mods, frames[0],
         grad_middle, mg_in, bias_in,
         pieces(from_rows(att, grad_branch), own_rows),
         pieces(from_rows(normed_two_low, grad_hidden), own_rows),
         pieces(from_rows(activated_low, grad_branch_two), down_rows)),
    )
    sums = btile.reshape(-1)

    def own_part(vector, start, size):
        return lax.dynamic_slice_in_dim(vector, start + own_index * size, size)

    lengths = [member.shape[0] for member in (query_bias, key_bias, value_bias, output_bias, up_bias, down_bias)]
    starts = [sum(lengths[:n]) * depth * 8 for n in range(6)]
    bq, bk, bv, bo, bu, bd = [own_part(sums, start, size) for start, size in zip(starts, lengths)]
    bm = own_part(mbias[:4].reshape(-1), 0, modulation_bias.shape[0])
    return (
        layer_output[None], fgrad[None], dwq, bq, dwk, bk, dwv, bv, dwo, bo, dup, bu, ddown, bd, dmw, bm,
    )


def fits(mesh, frames, *parameters):
    dp, seq = mesh.shape["dp"], mesh.shape["seq"]
    rows = parameters[3].shape[0] // (dp * seq)
    return seq == 4 and dp % 2 == 0 and rows == 32 and frames.shape[0] == dp


def solution(mesh):
    def run(*arrays):
        return mapped(mesh, on_device_fast if fits(mesh, *arrays) else on_device)(*arrays)

    return run


def mapped(mesh, body):
    return jax.shard_map(
        body,
        mesh=mesh,
        in_specs=(
            P("dp", "seq", None),
            P("dp", "seq", None),
            P("dp", None),
            P("dp", None),
            P(("dp", "seq"), None),
            P(("dp", "seq")),
            P(("dp", "seq"), None),
            P(("dp", "seq")),
            P(("dp", "seq"), None),
            P(("dp", "seq")),
            P(("dp", "seq"), None),
            P(("dp", "seq")),
            P(("dp", "seq"), None),
            P(("dp", "seq")),
            P(("dp", "seq"), None),
            P(("dp", "seq")),
            P(("dp", "seq"), None),
            P(("dp", "seq")),
        ),
        out_specs=(
            P("dp", "seq", None),
            P("dp", "seq", None),
            P(("dp", "seq"), None),
            P(("dp", "seq")),
            P(("dp", "seq"), None),
            P(("dp", "seq")),
            P(("dp", "seq"), None),
            P(("dp", "seq")),
            P(("dp", "seq"), None),
            P(("dp", "seq")),
            P(("dp", "seq"), None),
            P(("dp", "seq")),
            P(("dp", "seq"), None),
            P(("dp", "seq")),
            P(("dp", "seq"), None),
            P(("dp", "seq")),
        ),
        check_vma=False,
    )
```

```python
from functools import partial
import math

import jax
import jax.numpy as jnp
from jax import lax
from jax.experimental import pallas as pl
from jax.experimental.pallas import tpu as pltpu
from jax.sharding import PartitionSpec as P

HEAD_DIM = 64
MODEL_WIDTH = 1024
SEGS = 4
EPSILON = 1e-06
NEGATIVE = -1e30
HIGHEST = lax.Precision.HIGHEST
F32 = jnp.float32
BF16 = jnp.bfloat16
LANES = 128


class Mover:
    def __init__(self, send_sems, recv_sems, local_sems):
        self.send_sems, self.recv_sems, self.local_sems = send_sems, recv_sems, local_sems
        self.count = self.local_count = 0
        self.sent = []

    def send(self, source, target, device):
        slot = self.count
        self.count += 1
        copy = pltpu.make_async_remote_copy(
            src_ref=source,
            dst_ref=target,
            send_sem=self.send_sems.at[slot],
            recv_sem=self.recv_sems.at[slot],
            device_id=device,
            device_id_type=pl.DeviceIdType.MESH,
        )
        copy.start()
        self.sent.append(copy)
        return copy

    def local(self, source, target):
        slot = self.local_count
        self.local_count += 1
        copy = pltpu.make_async_copy(source, target, self.local_sems.at[slot])
        copy.start()
        return copy

    def finish(self, but=()):
        for copy in self.sent:
            if not any(copy is other for other in but):
                copy.wait_send()


class Place:
    def __init__(self, depth):
        dp, seq = lax.axis_index("dp"), lax.axis_index("seq")
        self.depth = depth
        self.z, self.y = dp // 2, dp % 2
        self.x, self.c = seq // 2, seq % 2
        self.seq = seq
        self.index = dp * 4 + seq

    def at(self, z, y, x, c):
        return {"dp": z * 2 + y, "seq": x * 2 + c}

    def core(self):
        return self.at(self.z, self.y, self.x, 1 - self.c)

    def across_x(self):
        return self.at(self.z, self.y, 1 - self.x, self.c)

    def across_y(self):
        return self.at(self.z, 1 - self.y, self.x, self.c)

    def ahead(self, step):
        return (self.z + step) % self.depth

    def along_z(self, step):
        return self.at(self.ahead(step), self.y, self.x, self.c)

    def row_peer(self, step):
        return {"dp": self.z * 2 + self.y, "seq": (self.seq + step) % 4}

    def enter(self):
        barrier = pltpu.get_barrier_semaphore()
        peers = [self.row_peer(step) for step in (1, 2, 3)] + [self.across_y()]
        peers += [self.along_z(step) for step in range(1, self.depth)]
        for peer in peers:
            pl.semaphore_signal(barrier, 1, device_id=peer, device_id_type=pl.DeviceIdType.MESH)
        pl.semaphore_wait(barrier, len(peers))


def lanes_of(shape, axis=1):
    return lax.broadcasted_iota(jnp.int32, shape, axis)


def frame_segments(lens, first_row, rows, width):
    position = lanes_of((rows, width), 0) + first_row
    first, second, third = lens[0, 0], lens[0, 0] + lens[0, 1], lens[0, 0] + lens[0, 1] + lens[0, 2]
    segment = (
        (position >= first).astype(jnp.int32)
        + (position >= second).astype(jnp.int32)
        + (position >= third).astype(jnp.int32)
    )
    start = jnp.where(
        segment == 0, 0, jnp.where(segment == 1, first, jnp.where(segment == 2, second, third))
    )
    return segment, position - start


def three_parts(values):
    high = values.astype(BF16).astype(F32)
    rest = values - high
    middle = rest.astype(BF16).astype(F32)
    return high, middle, (rest - middle).astype(BF16).astype(F32)


def swap_halves(values, lane):
    return jnp.where(
        lane % HEAD_DIM < HEAD_DIM // 2, pltpu.roll(values, 96, 1), pltpu.roll(values, 32, 1)
    )


def head_only(values, lane, head):
    return jnp.where((lane >= HEAD_DIM) == bool(head), values.astype(F32), 0.0).astype(BF16)


def across(left, right):
    return lax.dot_general(left, right, (((1,), (1,)), ((), ())), preferred_element_type=F32)


def product(left, right):
    return jnp.dot(left, right, preferred_element_type=F32)


def forward_kernel(
    depth,
    lens, times, frames, bq, bk, bv, bo, bu, bd, bm, wq, wk, wv, wo, up, down, mw,
    att, oh, qs, ks, vs, lse, normed, wg, mods, cosr, sinr, rowbias, low, wo_all, up_all, down_all,
    bb, xall, mwst, tb, part, recva, suma, recvb, sumb, recvc, sumc, recvd, modh, bmat, mod3, qbias,
    ka, va, qaug, send_sems, recv_sems, local_sems,
):
    here = Place(depth)
    z, y, x, c, g = here.z, here.y, here.x, here.c, here.seq
    span = frames.shape[0]
    rows_all = span * 4
    move = Mover(send_sems, recv_sems, local_sems)
    steps_z = range(1, depth)

    row = lanes_of((16, LANES), 0) % 4
    own_times = jnp.where(
        row == 0, times[0, 0], jnp.where(row == 1, times[0, 1], jnp.where(row == 2, times[0, 2], times[0, 3]))
    )
    tb[z, y] = own_times.astype(F32)
    bb[z, y, x, c] = jnp.zeros((8, LANES), F32)
    for n, vector in enumerate((bq, bk, bv, bo, bu, bd)):
        bb[z, y, x, c, n : n + 1, : vector.shape[1]] = vector[...].astype(F32)
    bb[z, y, x, c, 6:7, :] = bm[:, :LANES].astype(F32)
    bb[z, y, x, c, 7:8, : bm.shape[1] - LANES] = bm[:, LANES:].astype(F32)
    weights = (wq, wk, wv)
    own_width = wg.shape[-1]
    locals_first = [
        move.local(weights[j].at[:, pl.ds(pl.multiple_of(g * own_width, LANES), own_width)], wg.at[j, z, y, g])
        for j in range(3)
    ]
    strip = mw.shape[1] // 4
    local_mw = [
        move.local(mw.at[:, pl.ds(j * strip, strip)], mwst.at[pl.ds(j * 32, 32)]) for j in range(4)
    ]
    local_frames = move.local(frames, xall.at[g])
    here.enter()

    legs = {}
    shard, wide = wo.shape[0], MODEL_WIDTH
    thin = shard // 2
    flows = []

    def add_flow(source, target, first_row, columns=None):
        rows = pl.ds(first_row, thin)
        if columns is None:
            flows.append((source.at[rows], target.at[:, :, :, :, rows], len(flows) % 2))
        else:
            columns = pl.ds(columns, wide)
            flows.append((source.at[rows, columns], target.at[:, :, :, :, rows, columns], len(flows) % 2))

    for side in range(2):
        add_flow(wo, wo_all, side * thin)
    for side in range(2):
        add_flow(up, up_all, side * thin, 0)
        add_flow(up, up_all, side * thin, wide)
    for side in range(4):
        add_flow(down, down_all, side * thin)
    count = len(flows)

    def first_leg(number):
        source, target, _ = flows[number]
        own = move.local(source, target.at[z, y, x, c])
        sends = [move.send(source, target.at[z, y, x, c], here.along_z(k)) for k in steps_z]
        legs[number] = own, sends

    def second_leg(number):
        _, target, order = flows[number]
        own, sends = legs[number]
        own.wait()
        for copy in sends:
            copy.wait_recv()
        peer = here.across_x() if order else here.across_y()
        legs[number] = move.send(target.at[:, y, x, c], target.at[:, y, x, c], peer)

    def third_leg(number):
        _, target, order = flows[number]
        legs[number].wait_recv()
        if order:
            legs[number] = move.send(target.at[:, y, :, c], target.at[:, y, :, c], here.across_y())
        else:
            legs[number] = move.send(target.at[:, :, x, c], target.at[:, :, x, c], here.across_x())

    def fourth_leg(number):
        _, target, _ = flows[number]
        legs[number].wait_recv()
        legs[number] = move.send(target.at[:, :, :, c], target.at[:, :, :, c], here.core())

    early = 4

    def advance(*moves):
        for number, leg in moves:
            (second_leg, third_leg, fourth_leg)[leg - 2](number)

    times_z = [move.send(tb.at[z, y], tb.at[z, y], here.along_z(k)) for k in steps_z]
    qkv_row = [
        [
            move.send(
                weights[j].at[:, pl.ds(pl.multiple_of((g + k) % 4 * own_width, LANES), own_width)],
                wg.at[j, z, y, g],
                here.row_peer(k),
            )
            for k in (1, 2, 3)
        ]
        for j in range(3)
    ]
    bias_z = [move.send(bb.at[z, y, x, c], bb.at[z, y, x, c], here.along_z(k)) for k in steps_z]
    part_rows = span // 2
    frame_parts = [pl.ds(n * part_rows, part_rows) for n in range(2)]
    frames_x = []
    for number in range(early):
        first_leg(number)
    for copy in times_z:
        copy.wait_recv()
    times_y = move.send(tb.at[:, y], tb.at[:, y], here.across_y())
    for copy in locals_first:
        copy.wait()
    qkv_z, qkv_y = {}, {}

    def columns_z(j):
        for copy in qkv_row[j]:
            copy.wait_recv()
        qkv_z[j] = [move.send(wg.at[j, z, y], wg.at[j, z, y], here.along_z(k)) for k in steps_z]

    def columns_y(j):
        for copy in qkv_z[j]:
            copy.wait_recv()
        qkv_y[j] = move.send(wg.at[j, :, y], wg.at[j, :, y], here.across_y())

    times_y.wait_recv()
    lane = lanes_of((16 * 2 * depth, LANES))
    row = lanes_of((16 * 2 * depth, LANES), 0)
    feature = here.index * 32 + lane % 32
    halfway = MODEL_WIDTH // 2
    frequency = jnp.exp((feature % halfway).astype(F32) * (-math.log(10000.0) / halfway))
    angle = tb[...].reshape(16 * 2 * depth, LANES) * frequency
    wave = jnp.where(feature < halfway, jnp.sin(angle), jnp.cos(angle))
    gated = wave / (1.0 + jnp.exp(-wave))
    low[...] = jnp.where(lane // 32 == (row % 16) // 4, gated, 0.0).astype(BF16)
    for copy in local_mw:
        copy.wait()
    half = strip // 2
    for side in range(2):
        share = product(low[...], mwst[:, side * half : (side + 1) * half])
        part[side] = share.astype(BF16).reshape(depth, 2, 16, half)
    mod_core = move.send(part.at[1 - c], recva, here.core())
    frames_core = move.send(frames, xall.at[g], here.core())
    for copy in bias_z:
        copy.wait_recv()
    bias_y = move.send(bb.at[:, y, x, c], bb.at[:, y, x, c], here.across_y())

    advance((0, 2), (1, 2))
    block = 128

    def tables(step, carry):
        rows = pl.ds(pl.multiple_of(step * block, block), block)
        segment, relative = frame_segments(lens, step * block, block, LANES)
        lane = lanes_of((block, LANES))
        quarter = HEAD_DIM // 2
        frequency = jnp.exp((lane % quarter).astype(F32) * (-math.log(10000.0) / quarter))
        angle = relative.astype(F32) * frequency
        cosr[rows, :] = jnp.cos(angle)
        sine = jnp.sin(angle)
        sinr[rows, :] = jnp.where(lane % HEAD_DIM < quarter, -sine, sine)
        same = segment == lane
        qaug[rows, :] = jnp.where((lane < SEGS) & jnp.logical_not(same), NEGATIVE, 0.0).astype(BF16)
        keyside = jnp.where((lane < SEGS) & same, 1.0, jnp.where((lane >= 4) & (lane < 7), 1.0, 0.0))
        for pair in range(2):
            ka[pair, rows, LANES:] = keyside.astype(BF16)
            va[pair, rows, LANES:] = jnp.where(lane < 3, 1.0, 0.0).astype(BF16)
        return carry

    mod_core.wait_recv()
    suma[...] = (part[c].astype(F32) + recva[...].astype(F32)).astype(BF16)
    mod_y = move.send(suma.at[:, 1 - y], recvb, here.across_y())
    bias_y.wait_recv()
    bias_x = move.send(bb.at[:, :, x, c], bb.at[:, :, x, c], here.across_x())
    advance((2, 2), (0, 3))
    lax.fori_loop(0, rows_all // (2 * block), tables, 0)
    mod_y.wait_recv()
    sumb[...] = (suma[:, y].astype(F32) + recvb[...].astype(F32)).astype(BF16)
    mod_z = [move.send(sumb.at[here.ahead(k)], recvc.at[k - 1], here.along_z(k)) for k in steps_z]
    for j in range(3):
        columns_z(j)

    for number in range(early, count):
        first_leg(number)
    advance((3, 2), (1, 3))
    lax.fori_loop(rows_all // (2 * block), rows_all // block, tables, 0)
    bias_x.wait_recv()
    bias_core = move.send(bb.at[:, :, :, c], bb.at[:, :, :, c], here.core())
    total = sumb[z].astype(F32)
    for k in steps_z:
        mod_z[k - 1].wait_recv()
        total = total + recvc[k - 1].astype(F32)
    sumc[...] = total
    mod_x = move.send(sumc, recvd, here.across_x())
    for rows in frame_parts:
        frames_x.append(move.send(frames.at[rows], xall.at[g, rows], here.across_x()))
    columns_y(0)
    advance((2, 3))

    bias_core.wait_recv()
    bmat[...] = bb[...].reshape(16 * 2 * depth * 2, LANES).astype(BF16)

    place = lanes_of((LANES, own_width), 0)
    column = lanes_of((LANES, own_width))
    brow, bcol = lanes_of((64, own_width), 0), lanes_of((64, own_width))
    spread = jnp.where(column % 32 == place, 1.0, 0.0).astype(BF16)
    for j in range(3):
        mine = (brow % 8 == j) & (brow // 8 == bcol // 32)
        held = product(bmat[pl.ds(pl.multiple_of(g * 64, 64), 64), :], spread)
        qbias[j : j + 1, :] = jnp.sum(jnp.where(mine, held, 0.0), axis=0, keepdims=True)

    tile = 256
    trow, tcol = lanes_of((16 * 2 * depth * 2, tile), 0), lanes_of((16 * 2 * depth * 2, tile))
    place, column = lanes_of((LANES, tile), 0), lanes_of((LANES, tile))

    def row_vector(step, size, source):
        spread = jnp.where(column % size == place, 1.0, 0.0).astype(BF16)
        chosen = (trow % 8 == source) & (trow // 8 == (tcol + step * tile) // size)
        return jnp.sum(jnp.where(chosen, product(bmat[...], spread), 0.0), axis=0, keepdims=True)

    def narrow_vectors(step, carry):
        columns = pl.ds(pl.multiple_of(step * tile, tile), tile)
        rowbias[0:1, columns] = row_vector(step, 32, 3)
        rowbias[2:3, columns] = row_vector(step, 32, 5)
        return carry

    def wide_vector(step, carry):
        rowbias[1:2, pl.ds(pl.multiple_of(step * tile, tile), tile)] = row_vector(step, 64, 4)
        return carry

    lax.fori_loop(0, MODEL_WIDTH // tile, narrow_vectors, 0)
    lax.fori_loop(0, up.shape[1] // tile, wide_vector, 0)

    place = lanes_of((LANES, half), 0)
    column = lanes_of((LANES, half))
    spread_a = jnp.where(column % 192 == place, 1.0, 0.0).astype(BF16)
    spread_b = jnp.where(column % 192 == place + LANES, 1.0, 0.0).astype(BF16)
    brow, bcol = lanes_of((32, half), 0), lanes_of((32, half))
    inside = brow // 8 == bcol // 192
    for q in range(8):
        rows = bmat[q * 32 : (q + 1) * 32, :]
        terms = jnp.where(inside & (brow % 8 == 6), product(rows, spread_a), 0.0)
        terms = terms + jnp.where(inside & (brow % 8 == 7), product(rows, spread_b), 0.0)
        mods[4:5, q * half : (q + 1) * half] = jnp.sum(terms, axis=0, keepdims=True)
    mod_x.wait_recv()
    modh[c] = sumc[...] + recvd[...]
    mod_last = move.send(modh.at[c], modh.at[c], here.core())
    columns_y(1)
    advance((3, 3), (0, 4), (1, 4))
    frames_on = []

    def pass_frames(n):
        frames_x[n].wait_recv()
        theirs = xall.at[(g + 2) % 4, frame_parts[n]]
        frames_on.append(move.send(theirs, theirs, here.core()))

    mod_last.wait_recv()
    for q in range(8):
        j, side = q // 2, q % 2
        columns = slice(q * half, (q + 1) * half)
        mods[0:4, columns] = modh[side, 4 * j : 4 * j + 4, :] + mods[4:5, columns]
    high, middle, rest = three_parts(mods[0:4, 0 : 2 * MODEL_WIDTH])
    mod3[0:4, :] = high
    mod3[4:8, :] = middle
    mod3[8:12, :] = rest
    mod3[12:16, :] = jnp.zeros((4, 2 * MODEL_WIDTH), F32)
    columns_y(2)
    pass_frames(0)
    advance((2, 4), (4, 2), (3, 4), (5, 2))
    pass_frames(1)

    def project_rows(step, carry):
        rows = pl.ds(pl.multiple_of(step * block, block), block)
        per = span // block
        source = step // per
        values = xall[source, pl.ds(pl.multiple_of((step % per) * block, block), block), :].astype(F32)
        center = jnp.mean(values, axis=1, keepdims=True)
        centered = values - center
        variance = jnp.mean(centered * centered, axis=1, keepdims=True)
        segment, _ = frame_segments(lens, step * block, block, 16)
        slot = lanes_of((block, 16))
        chosen = jnp.where((slot < 12) & (slot % 4 == segment), 1.0, 0.0).astype(BF16)
        parts = mod3[...].astype(BF16)
        shift = product(chosen, parts[:, :MODEL_WIDTH])
        scale = product(chosen, parts[:, MODEL_WIDTH:])
        result = (centered * lax.rsqrt(variance + EPSILON) * (1.0 + scale) + shift).astype(BF16)
        normed[rows, :] = result
        cosine, sine = cosr[rows, :], sinr[rows, :]
        lane = lanes_of((block, LANES))
        for j in range(3):
            weight = wg[j].reshape(MODEL_WIDTH, own_width)
            full = product(result, weight) + qbias[j : j + 1, :]
            for pair in range(2):
                piece = full[:, pair * LANES : (pair + 1) * LANES]
                if j < 2:
                    piece = piece * cosine + swap_halves(piece, lane) * sine
                if j == 0:
                    qs[pair, rows, :] = (piece.astype(BF16).astype(F32) * HEAD_DIM**-0.5).astype(BF16)
                elif j == 1:
                    ks[pair, rows, :] = piece.astype(BF16)
                    ka[pair, rows, :LANES] = piece.astype(BF16)
                else:
                    vs[pair, rows, :] = piece.astype(BF16)
                    va[pair, rows, :LANES] = piece.astype(BF16)
        return carry

    local_frames.wait()
    frames_core.wait_recv()
    for j in range(3):
        qkv_y[j].wait_recv()
    span_steps = span // block

    def project_span(number):
        lax.fori_loop(number * span_steps, (number + 1) * span_steps, project_rows, 0)

    project_span(x * 2)
    advance((6, 2), (4, 3))
    project_span(x * 2 + 1)
    advance((7, 2), (5, 3))
    for copy in frames_on:
        copy.wait_recv()
    project_span(2 - x * 2)
    advance((8, 2), (6, 3))
    project_span(3 - x * 2)
    advance((9, 2), (4, 4))

    tall = 256

    def attend(pair, step):
        rows = pl.ds(pl.multiple_of(step * tall, tall), tall)
        query = qs[pair, rows, :]
        lane = lanes_of((tall, LANES))
        outs, sums = [], []
        for head in range(2):
            left = jnp.concatenate([head_only(query, lane, head), qaug[rows, :]], axis=1)
            scores = across(left, ka[pair])
            highest = jnp.max(scores, axis=1, keepdims=True)
            mixed = product(jnp.exp(scores - highest).astype(BF16), va[pair])
            total = mixed[:, LANES : LANES + 1]
            outs.append(mixed[:, :LANES] / total)
            sums.append(highest + jnp.log(total))
        oh[pair, rows, :] = jnp.where(lane < HEAD_DIM, outs[0], outs[1]).astype(BF16)
        before = jnp.zeros((tall, LANES), F32) if pair == 0 else lse[rows, :]
        lse[rows, :] = jnp.where(
            lane == 2 * pair, sums[0], jnp.where(lane == 2 * pair + 1, sums[1], before)
        )

    def attend_some(pair, first, last):
        lax.fori_loop(first, last, lambda step, carry: (attend(pair, step), carry)[1], 0)

    steps = rows_all // tall
    arrivals = []
    pair_locals = []

    def deliver(pair):
        columns = pl.ds(pl.multiple_of(g * own_width + pair * LANES, LANES), LANES)
        pair_locals.append(
            move.local(oh.at[pair, pl.ds(pl.multiple_of(g * span, span), span)], att.at[:, columns])
        )
        for k in (1, 2, 3):
            peer = (g + k) % 4
            arrivals.append(
                move.send(
                    oh.at[pair, pl.ds(pl.multiple_of(peer * span, span), span)],
                    att.at[:, columns],
                    here.row_peer(k),
                )
            )

    attend_some(0, 0, 3)
    advance((7, 3), (5, 4))
    attend_some(0, 3, steps)
    deliver(0)
    advance((8, 3), (6, 4))
    attend_some(1, 0, 3)
    advance((9, 3), (7, 4))
    attend_some(1, 3, steps)
    deliver(1)
    advance((8, 4), (9, 4))
    for number in range(count):
        legs[number].wait_recv()
    for copy in arrivals:
        copy.wait_recv()
    for copy in pair_locals:
        copy.wait()
    move.finish()


def forward_call(depth, span, own_rows, down_rows, hidden, args):
    rows_all, own_width = 4 * span, MODEL_WIDTH // 4
    half = 6 * MODEL_WIDTH // 8
    vmem, anywhere, scalar = (
        pl.BlockSpec(memory_space=pltpu.VMEM),
        pl.BlockSpec(memory_space=pl.ANY),
        pl.BlockSpec(memory_space=pltpu.SMEM),
    )

    def out(shape, dtype):
        return jax.ShapeDtypeStruct(shape, dtype)

    outs = [
        (out((span, MODEL_WIDTH), BF16), anywhere),
        (out((2, rows_all, LANES), BF16), vmem),
        (out((2, rows_all, LANES), BF16), vmem),
        (out((2, rows_all, LANES), BF16), vmem),
        (out((2, rows_all, LANES), BF16), vmem),
        (out((rows_all, LANES), F32), vmem),
        (out((rows_all, MODEL_WIDTH), BF16), vmem),
        (out((3, depth, 2, 4, own_rows, own_width), BF16), vmem),
        (out((8, 6 * MODEL_WIDTH), F32), vmem),
        (out((rows_all, LANES), F32), vmem),
        (out((rows_all, LANES), F32), vmem),
        (out((8, hidden), F32), vmem),
        (out((32 * depth, LANES), BF16), vmem),
        (out((depth, 2, 2, 2, own_rows, MODEL_WIDTH), BF16), anywhere),
        (out((depth, 2, 2, 2, own_rows, hidden), BF16), anywhere),
        (out((depth, 2, 2, 2, down_rows, MODEL_WIDTH), BF16), anywhere),
    ]
    scratch = [
        pltpu.VMEM((depth, 2, 2, 2, 8, LANES), F32),
        pltpu.VMEM((4, span, MODEL_WIDTH), BF16),
        pltpu.VMEM((LANES, 2 * half), BF16),
        pltpu.VMEM((depth, 2, 16, LANES), F32),
        pltpu.VMEM((2, depth, 2, 16, half), BF16),
        pltpu.VMEM((depth, 2, 16, half), BF16),
        pltpu.VMEM((depth, 2, 16, half), BF16),
        pltpu.VMEM((depth, 16, half), BF16),
        pltpu.VMEM((depth, 16, half), BF16),
        pltpu.VMEM((depth - 1, 16, half), BF16),
        pltpu.VMEM((16, half), F32),
        pltpu.VMEM((16, half), F32),
        pltpu.VMEM((2, 16, half), F32),
        pltpu.VMEM((64 * depth, LANES), BF16),
        pltpu.VMEM((16, 2 * MODEL_WIDTH), F32),
        pltpu.VMEM((8, own_width), F32),
        pltpu.VMEM((2, rows_all, 2 * LANES), BF16),
        pltpu.VMEM((2, rows_all, 2 * LANES), BF16),
        pltpu.VMEM((rows_all, LANES), BF16),
        pltpu.SemaphoreType.DMA((128,)),
        pltpu.SemaphoreType.DMA((128,)),
        pltpu.SemaphoreType.DMA((32,)),
    ]
    return pl.pallas_call(
        partial(forward_kernel, depth),
        out_shape=[shape for shape, _ in outs],
        in_specs=[scalar, scalar, anywhere] + [vmem] * 7 + [anywhere] * 7,
        out_specs=[spec for _, spec in outs],
        scratch_shapes=scratch,
        compiler_params=pltpu.CompilerParams(
            collective_id=0, has_side_effects=True, vmem_limit_bytes=56 * 1024 * 1024
        ),
        cost_estimate=pl.CostEstimate(flops=8 * 10**9, bytes_accessed=40 * 10**6, transcendentals=10**7),
    )(*args)


def turn_back(values, cosine, sine, lane):
    return values * cosine - swap_halves(values, lane) * sine


def from_rows(left, right):
    return lax.dot_general(left, right, (((0,), (0,)), ((), ())), preferred_element_type=F32)


def backward_kernel(
    depth,
    lens, ga, qs_in, ks_in, vs_in, oh_in, lse_in, normed_in, wg_in, cos_in, sin_in, low, mods, frames, gmid,
    mg_in, bias_in, gwo, gup, gdown,
    fgrad, dwq, dwk, dwv, dwo, dup, ddown, dmw, mbias, btile,
    qs, do, oh, lse, normed, wg, cosr, sinr, ka, va, qaug, dk_sum, dv_sum, gr, gw, gwy, gwz, gsum,
    gnp, gnr, gnx, mod3, acc_shift, acc_scale, mg, mgr, mgs, mgx, ev, brecv, bz,
    *rest,
):
    send_sems, recv_sems, local_sems = rest[-3:]
    buffers = rest[:-3]
    here = Place(depth)
    z, y, x, c, g = here.z, here.y, here.x, here.c, here.seq
    span = frames.shape[0]
    rows_all = span * 4
    own_width = wg.shape[-1]
    move = Mover(send_sems, recv_sems, local_sems)
    steps_z = range(1, depth)

    shard = gwo.shape[4]
    width = MODEL_WIDTH
    pieces = []
    for side in range(2):
        pieces.append(
            (gwo.at[:, :, :, :, pl.ds(side * shard // 2, shard // 2)], dwo.at[pl.ds(side * shard // 2, shard // 2)], side)
        )
    for side in range(2):
        pieces.append((gup.at[:, :, :, :, :, pl.ds(side * width, width)], dup.at[:, pl.ds(side * width, width)], 0))
        pieces.append((gdown.at[:, :, :, :, pl.ds(side * shard, shard)], ddown.at[pl.ds(side * shard, shard)], 1))
    own = [buffers[5 * f] for f in range(6)]
    first = [buffers[5 * f + 1] for f in range(6)]
    second = [buffers[5 * f + 2] for f in range(6)]
    third = [buffers[5 * f + 3] for f in range(6)]
    fourth = [buffers[5 * f + 4] for f in range(6)]
    legs = {}

    loads = [
        move.local(ks_in, ka.at[:, :, pl.ds(0, LANES)]),
        move.local(vs_in, va.at[:, :, pl.ds(0, LANES)]),
        move.local(qs_in, qs),
        move.local(oh_in, oh),
        move.local(lse_in, lse),
        move.local(cos_in, cosr),
        move.local(sin_in, sinr),
    ]
    here.enter()
    arrivals = []
    for pair in range(2):
        columns = pl.ds(pl.multiple_of(g * own_width + pair * LANES, LANES), LANES)
        mine = pl.ds(pl.multiple_of(g * span, span), span)
        loads.append(move.local(ga.at[:, columns], do.at[pair, mine]))
        for k in (1, 2, 3):
            peer = (g + k) % 4
            theirs = pl.ds(pl.multiple_of(peer * own_width + pair * LANES, LANES), LANES)
            arrivals.append(move.send(ga.at[:, theirs], do.at[pair, mine], here.row_peer(k)))
    held = []
    for f in range(6):
        source = pieces[f][0]
        legs[f] = move.send(source.at[:, :, :, 1 - c], first[f], here.core())
        held.append(move.local(source.at[:, :, :, c], own[f]))
    late_loads = [move.local(normed_in, normed), move.local(wg_in, wg)]

    def sum_first(f):
        legs[f].wait_recv()
        held[f].wait()

        def add(step, carry):
            own[f][step] = own[f][step] + first[f][step]
            return carry

        lax.fori_loop(0, depth, add, 0)
        if pieces[f][2]:
            legs[f] = move.send(own[f].at[:, :, 1 - x], second[f], here.across_x())
        else:
            legs[f] = move.send(own[f].at[:, 1 - y], second[f], here.across_y())

    def sum_second(f):
        legs[f].wait_recv()

        def add(step, carry):
            for other in range(2):
                if pieces[f][2]:
                    own[f][step, other, x] = own[f][step, other, x] + second[f][step, other]
                else:
                    own[f][step, y, other] = own[f][step, y, other] + second[f][step, other]
            return carry

        lax.fori_loop(0, depth, add, 0)
        if pieces[f][2]:
            legs[f] = move.send(own[f].at[:, 1 - y, x], third[f], here.across_y())
        else:
            legs[f] = move.send(own[f].at[:, y, 1 - x], third[f], here.across_x())

    def sum_third(f):
        legs[f].wait_recv()

        def add(step, carry):
            own[f][step, y, x] = own[f][step, y, x] + third[f][step]
            return carry

        lax.fori_loop(0, depth, add, 0)
        legs[f] = [
            move.send(own[f].at[here.ahead(k), y, x], fourth[f].at[k - 1], here.along_z(k)) for k in steps_z
        ]

    def sum_last(f):
        total = own[f][z, y, x].astype(F32)
        for k in steps_z:
            legs[f][k - 1].wait_recv()
            total = total + fourth[f][k - 1].astype(F32)
        pieces[f][1][...] = total

    def bias_round(peer, slot):
        return move.send(btile, brecv.at[slot], peer)

    block = 128
    for copy in loads:
        copy.wait()

    def columns_of_segments(step, carry):
        rows = pl.ds(pl.multiple_of(step * block, block), block)
        segment, _ = frame_segments(lens, step * block, block, LANES)
        lane = lanes_of((block, LANES))
        same = segment == lane
        qaug[rows, :] = jnp.where((lane < SEGS) & jnp.logical_not(same), NEGATIVE, 0.0).astype(BF16)
        keyside = jnp.where((lane < SEGS) & same, 1.0, jnp.where((lane >= 4) & (lane < 7), 1.0, 0.0))
        for pair in range(2):
            ka[pair, rows, LANES:] = keyside.astype(BF16)
            va[pair, rows, LANES:] = jnp.where(lane < 3, 1.0, 0.0).astype(BF16)
        return carry

    lax.fori_loop(0, rows_all // block, columns_of_segments, 0)

    tall = 256
    steps = rows_all // tall

    def back_block(pair, step):
        rows = pl.ds(pl.multiple_of(step * tall, tall), tall)
        lane = lanes_of((tall, LANES))
        query, given = qs[pair, rows, :], do[pair, rows, :]
        overlap = given.astype(F32) * oh[pair, rows, :].astype(F32)
        mask_columns = qaug[rows, :].astype(F32)
        sums = lse[rows, :]
        grads_q, add_k, add_v = [], 0.0, 0.0
        for head in range(2):
            delta = jnp.sum(jnp.where((lane >= HEAD_DIM) == bool(head), overlap, 0.0), axis=1, keepdims=True)
            logsum = jnp.sum(jnp.where(lane == 2 * pair + head, sums, 0.0), axis=1, keepdims=True)
            a, b, d = three_parts(logsum)
            side = jnp.where(lane == 4, -a, jnp.where(lane == 5, -b, jnp.where(lane == 6, -d, mask_columns)))
            query_head = head_only(query, lane, head)
            left = jnp.concatenate([query_head, side.astype(BF16)], axis=1)
            a, b, d = three_parts(delta)
            side = jnp.where(lane == 0, -a, jnp.where(lane == 1, -b, jnp.where(lane == 2, -d, 0.0)))
            given_head = head_only(given, lane, head)
            right = jnp.concatenate([given_head, side.astype(BF16)], axis=1)
            weights = jnp.exp(across(ka[pair], left))
            grads = (weights * across(va[pair], right)).astype(BF16)
            add_v = add_v + product(weights.astype(BF16), given_head)
            add_k = add_k + product(grads, query_head)
            grads_q.append(from_rows(grads, ka[pair, :, :LANES]))
        dv_sum[...] += add_v
        dk_sum[...] += add_k
        grad_query = jnp.where(lane < HEAD_DIM, grads_q[0], grads_q[1]) * HEAD_DIM**-0.5
        gr[0, rows, pair * LANES : (pair + 1) * LANES] = turn_back(
            grad_query, cosr[rows, :], sinr[rows, :], lane
        ).astype(BF16)

    def back_some(pair, start, stop):
        lax.fori_loop(start, stop, lambda step, carry: (back_block(pair, step), carry)[1], 0)

    def settle_pair(pair):
        def body(step, carry):
            rows = pl.ds(pl.multiple_of(step * block, block), block)
            lane = lanes_of((block, LANES))
            part = slice(pair * LANES, (pair + 1) * LANES)
            gr[1, rows, part] = turn_back(dk_sum[rows, :], cosr[rows, :], sinr[rows, :], lane).astype(BF16)
            gr[2, rows, part] = dv_sum[rows, :].astype(BF16)
            return carry

        lax.fori_loop(0, rows_all // block, body, 0)

    def clear():
        dk_sum[...] = jnp.zeros_like(dk_sum)
        dv_sum[...] = jnp.zeros_like(dv_sum)

    clear()
    sum_first(0)
    sum_first(1)
    sum_first(2)
    sum_first(3)
    for copy in arrivals:
        copy.wait_recv()
    back_some(0, 0, 1)
    sum_first(4)
    sum_first(5)
    back_some(0, 1, 2)
    sum_second(0)
    sum_second(1)
    back_some(0, 2, 4)
    sum_second(2)
    sum_second(3)
    sum_third(0)
    sum_third(1)
    back_some(0, 4, 6)
    settle_pair(0)
    clear()
    sum_second(4)
    sum_second(5)
    sum_third(2)
    sum_third(3)
    back_some(1, 0, 3)
    sum_last(0)
    sum_last(1)
    sum_third(4)
    sum_third(5)
    back_some(1, 3, 6)
    settle_pair(1)
    sum_last(2)
    sum_last(3)
    for copy in late_loads:
        copy.wait()

    def back_rows(target):
        def body(step, carry):
            rows = pl.ds(pl.multiple_of(target * span + step * block, block), block)
            total = 0.0
            for j in range(3):
                total = total + across(gr[j, rows, :], wg[j].reshape(MODEL_WIDTH, own_width))
            gnp[target, pl.ds(pl.multiple_of(step * block, block), block), :] = total.astype(BF16)
            return carry

        lax.fori_loop(0, span // block, body, 0)

    away_other, away_same = (1 - x) * 2 + (1 - c), (1 - x) * 2 + c
    home_other = x * 2 + (1 - c)
    back_rows(away_other)
    gn_core = [move.send(gnp.at[away_other], gnr.at[0], here.core())]
    back_rows(away_same)
    gn_core[0].wait_recv()

    def add_rows(step, carry):
        rows = pl.ds(pl.multiple_of(step * block, block), block)
        gnp[away_same, rows, :] = gnp[away_same, rows, :] + gnr[0, rows, :]
        return carry

    lax.fori_loop(0, span // block, add_rows, 0)
    gn_x = move.send(gnp.at[away_same], gnx, here.across_x())

    tile = 256

    def weight_rows(j):
        def body(step, carry):
            columns = pl.ds(pl.multiple_of(step * tile, tile), tile)
            result = from_rows(normed[:, columns], gr[j]).astype(BF16)
            per = 2 * 4 * shard // tile
            lead = result.reshape(tile // (4 * shard), 4, shard, own_width)
            for n in range(tile // (4 * shard)):
                gw[j, step // per, (step % per) * (tile // (4 * shard)) + n] = lead[n]
            return carry

        lax.fori_loop(0, MODEL_WIDTH // tile, body, 0)

    gw_y, gw_z = [], []
    for j in range(3):
        weight_rows(j)
        gw_y.append(move.send(gw.at[j, :, 1 - y], gwy.at[j], here.across_y()))
    ones = jnp.ones((16, rows_all), BF16)
    btile[...] = bias_in[...]
    for j in range(3):
        sums = product(ones, gr[j])
        for half in range(2):
            btile[pl.ds(8 * j + g * 2 + half, 1), :] = sums[0:1, half * LANES : (half + 1) * LANES]
    bias_core = move.send(btile, brecv.at[0], here.core())
    back_rows(home_other)
    gn_core.append(move.send(gnp.at[home_other], gnr.at[1], here.core()))
    back_rows(g)
    sum_last(4)
    sum_last(5)
    bias_core.wait()
    btile[...] = btile[...] + brecv[0]
    bias_x = move.send(btile, brecv.at[1], here.across_x())

    def sum_gw(j):
        gw_y[j].wait_recv()

        def add(step, carry):
            gw[j, step, y] = gw[j, step, y] + gwy[j, step]
            return carry

        lax.fori_loop(0, depth, add, 0)
        gw_z.append(
            [move.send(gw.at[j, here.ahead(k), y], gwz.at[j, k - 1], here.along_z(k)) for k in steps_z]
        )

    for j in range(3):
        sum_gw(j)
    bias_x.wait()
    btile[...] = btile[...] + brecv[1]
    bias_y = move.send(btile, brecv.at[2], here.across_y())

    high, middle, rest_part = three_parts(mods[0:4, MODEL_WIDTH : 2 * MODEL_WIDTH])
    mod3[0:4, :] = high
    mod3[4:8, :] = middle
    mod3[8:12, :] = rest_part
    mod3[12:16, :] = jnp.zeros((4, MODEL_WIDTH), F32)
    acc_shift[...] = jnp.zeros_like(acc_shift)
    acc_scale[...] = jnp.zeros_like(acc_scale)
    gn_core[1].wait_recv()
    gn_x.wait_recv()

    def two_parts(values):
        top = values.astype(BF16)
        return top, (values - top.astype(F32)).astype(BF16)

    def norm_rows(step, carry):
        rows = pl.ds(pl.multiple_of(step * block, block), block)
        grad = gnp[g, rows, :].astype(F32) + gnr[1, rows, :].astype(F32) + gnx[rows, :].astype(F32)
        values = frames[rows, :].astype(F32)
        center = jnp.mean(values, axis=1, keepdims=True)
        centered = values - center
        scaled = lax.rsqrt(jnp.mean(centered * centered, axis=1, keepdims=True) + EPSILON)
        hat = centered * scaled
        base = g * span + step * block
        segment, _ = frame_segments(lens, base, block, 16)
        slot = lanes_of((block, 16))
        chosen = jnp.where((slot < 12) & (slot % 4 == segment), 1.0, 0.0).astype(BF16)
        inner = grad * (1.0 + product(chosen, mod3[...].astype(BF16)))
        mean_one = jnp.mean(inner, axis=1, keepdims=True)
        mean_two = jnp.mean(inner * hat, axis=1, keepdims=True)
        fgrad[rows, :] = (gmid[rows, :] + scaled * (inner - mean_one - hat * mean_two)).astype(BF16)
        position = base + lanes_of((16, block))
        begin = [lens[0, 0], lens[0, 0] + lens[0, 1], lens[0, 0] + lens[0, 1] + lens[0, 2]]
        inside = sum((position >= edge).astype(jnp.int32) for edge in begin)
        members = jnp.where(inside == lanes_of((16, block), 0), 1.0, 0.0).astype(BF16)
        for values, target in ((grad, acc_shift), (grad * hat, acc_scale)):
            top, bottom = two_parts(values)
            target[...] += product(members, top) + product(members, bottom)
        return carry

    lax.fori_loop(0, span // block, norm_rows, 0)

    half = 6 * MODEL_WIDTH // 8
    for side in range(2):
        mg[side] = mg_in[:, side * half : (side + 1) * half]
    for q in range(8):
        if q * half >= 2 * MODEL_WIDTH:
            break
        j, side = q // 2, q % 2
        for target, start in ((acc_shift, 0), (acc_scale, MODEL_WIDTH)):
            low_end, high_end = max(q * half, start), min((q + 1) * half, start + MODEL_WIDTH)
            if low_end < high_end:
                mg[side, 4 * j : 4 * j + 4, low_end - q * half : high_end - q * half] = target[
                    0:4, low_end - start : high_end - start
                ]
    mod_core = move.send(mg.at[1 - c], mgr, here.core())
    mod_core.wait_recv()
    mgs[...] = mg[c] + mgr[...]
    mod_x = move.send(mgs, mgx, here.across_x())
    bias_y.wait()
    btile[...] = btile[...] + brecv[2]
    bias_z = [move.send(btile, bz.at[k - 1], here.along_z(k)) for k in steps_z]
    outs = (dwq, dwk, dwv)
    final = []
    final_locals = []

    def last_gw(j):
        total = gw[j, z, y].astype(F32)
        for k in steps_z:
            gw_z[j][k - 1].wait_recv()
            total = total + gwz[j, k - 1].astype(F32)
        gsum[j] = total
        columns = pl.ds(pl.multiple_of(g * own_width, LANES), own_width)
        final_locals.append(move.local(gsum.at[j, g], outs[j].at[:, columns]))
        for k in (1, 2, 3):
            final.append(move.send(gsum.at[j, (g + k) % 4], outs[j].at[:, columns], here.row_peer(k)))

    last_gw(0)
    mod_x.wait_recv()
    ev[z, y, c] = (mgs[...] + mgx[...]).astype(BF16)
    mod_z = [move.send(ev.at[z, y, c], ev.at[z, y, c], here.along_z(k)) for k in steps_z]
    last_gw(1)
    for copy in mod_z:
        copy.wait_recv()
    mod_y = move.send(ev.at[:, y, c], ev.at[:, y, c], here.across_y())
    last_gw(2)
    for copy in bias_z:
        copy.wait()
    total = btile[...]
    for k in steps_z:
        total = total + bz[k - 1]
    btile[...] = total
    mod_y.wait_recv()
    mod_last = move.send(ev.at[:, :, c], ev.at[:, :, c], here.core())
    picks = jnp.where(
        lanes_of((16, 32 * depth), 0) == (lanes_of((16, 32 * depth)) % 16) // 4, 1.0, 0.0
    ).astype(BF16)

    def finish_side(side):
        every = ev[:, :, side].reshape(32 * depth, half)
        result = from_rows(low[...], every)
        summed = product(picks, every)
        for j in range(4):
            dmw[:, j * 2 * half + side * half : j * 2 * half + (side + 1) * half] = result[32 * j : 32 * (j + 1), :]
        mbias[:, side * half : (side + 1) * half] = summed[0:8, :]

    mod_last.wait_recv()
    finish_side(0)
    finish_side(1)
    for copy in final_locals:
        copy.wait()
    for copy in final:
        copy.wait_recv()
    move.finish(but=[bias_core, bias_x, bias_y] + bias_z)


def backward_call(depth, span, own_rows, down_rows, hidden, args):
    rows_all, own_width = 4 * span, MODEL_WIDTH // 4
    half = 6 * MODEL_WIDTH // 8
    vmem, anywhere, scalar = (
        pl.BlockSpec(memory_space=pltpu.VMEM),
        pl.BlockSpec(memory_space=pl.ANY),
        pl.BlockSpec(memory_space=pltpu.SMEM),
    )

    def out(shape, dtype):
        return jax.ShapeDtypeStruct(shape, dtype)

    outs = [
        (out((span, MODEL_WIDTH), BF16), vmem),
        (out((own_rows, MODEL_WIDTH), F32), anywhere),
        (out((own_rows, MODEL_WIDTH), F32), anywhere),
        (out((own_rows, MODEL_WIDTH), F32), anywhere),
        (out((own_rows, MODEL_WIDTH), F32), vmem),
        (out((own_rows, hidden), F32), vmem),
        (out((down_rows, MODEL_WIDTH), F32), vmem),
        (out((own_rows, 6 * MODEL_WIDTH), F32), vmem),
        (out((8, 2 * half), F32), vmem),
        (out((56, LANES), F32), vmem),
    ]
    pair_rows = pltpu.VMEM((2, rows_all, LANES), BF16)
    wide_rows = pltpu.VMEM((2, rows_all, 2 * LANES), BF16)
    table = pltpu.VMEM((rows_all, LANES), F32)
    scratch = [
        pair_rows, pair_rows, pair_rows, table,
        pltpu.VMEM((rows_all, MODEL_WIDTH), BF16),
        pltpu.VMEM((3, depth, 2, 4, own_rows, own_width), BF16),
        table, table, wide_rows, wide_rows,
        pltpu.VMEM((rows_all, LANES), BF16),
        table, table,
        pltpu.VMEM((3, rows_all, own_width), BF16),
        pltpu.VMEM((3, depth, 2, 4, own_rows, own_width), BF16),
        pltpu.VMEM((3, depth, 4, own_rows, own_width), BF16),
        pltpu.VMEM((3, depth - 1, 4, own_rows, own_width), BF16),
        pltpu.VMEM((3, 4, own_rows, own_width), F32),
        pltpu.VMEM((4, span, MODEL_WIDTH), BF16),
        pltpu.VMEM((2, span, MODEL_WIDTH), BF16),
        pltpu.VMEM((span, MODEL_WIDTH), BF16),
        pltpu.VMEM((16, MODEL_WIDTH), F32),
        pltpu.VMEM((16, MODEL_WIDTH), F32),
        pltpu.VMEM((16, MODEL_WIDTH), F32),
        pltpu.VMEM((2, 16, half), F32),
        pltpu.VMEM((16, half), F32),
        pltpu.VMEM((16, half), F32),
        pltpu.VMEM((16, half), F32),
        pltpu.VMEM((depth, 2, 2, 16, half), BF16),
        pltpu.VMEM((3, 56, LANES), F32),
        pltpu.VMEM((depth - 1, 56, LANES), F32),
    ]
    for f in range(6):
        rows = own_rows // 2 if f < 2 else own_rows
        piece = (rows, MODEL_WIDTH)
        scratch += [
            pltpu.VMEM((depth, 2, 2) + piece, BF16),
            pltpu.VMEM((depth, 2, 2) + piece, BF16),
            pltpu.VMEM((depth, 2) + piece, BF16),
            pltpu.VMEM((depth,) + piece, BF16),
            pltpu.VMEM((depth - 1,) + piece, BF16),
        ]
    scratch += [pltpu.SemaphoreType.DMA((96,)), pltpu.SemaphoreType.DMA((96,)), pltpu.SemaphoreType.DMA((32,))]
    return pl.pallas_call(
        partial(backward_kernel, depth),
        out_shape=[shape for shape, _ in outs],
        in_specs=[scalar] + [anywhere] * 10 + [vmem] * 6 + [anywhere] * 3,
        out_specs=[spec for _, spec in outs],
        scratch_shapes=scratch,
        compiler_params=pltpu.CompilerParams(
            collective_id=1, has_side_effects=True, vmem_limit_bytes=62 * 1024 * 1024
        ),
        cost_estimate=pl.CostEstimate(flops=2 * 10**10, bytes_accessed=40 * 10**6, transcendentals=10**7),
    )(*args)


def middle_kernel(
    lens, att_in, wo_in, up_in, down_in, mods, rowbias, frames, given,
    output, ga, gmid, mg, btile, gwo, gup, gdown,
    att, wo, up, down, mod3, branch, middle, normed, active, slope, gbt, gh, gn, gb, sums, swo, sup, sdown,
    local_sems,
):
    g = lax.axis_index("seq")
    span, width = frames.shape
    hidden = up.shape[1]
    move = Mover(None, None, local_sems)
    loads = [move.local(a, b) for a, b in ((att_in, att), (wo_in, wo), (up_in, up), (down_in, down))]
    base = g * span
    tile, block = 256, 128
    high, mid, rest = three_parts(mods[0:4, 2 * width :])
    mod3[0:4, :] = high
    mod3[4:8, :] = mid
    mod3[8:12, :] = rest
    mod3[12:16, :] = jnp.zeros((4, 4 * width), F32)

    def tile_at(step):
        return pl.ds(pl.multiple_of(step * tile, tile), tile)

    def per_frame(part, first, rows, columns):
        segment, _ = frame_segments(lens, base + first, rows, 16)
        slot = lanes_of((rows, 16))
        chosen = jnp.where((slot < 12) & (slot % 4 == segment), 1.0, 0.0).astype(BF16)
        return product(chosen, mod3[:, columns].astype(BF16))

    def members(first, rows):
        position = base + first + lanes_of((16, rows))
        edges = [lens[0, 0], lens[0, 0] + lens[0, 1], lens[0, 0] + lens[0, 1] + lens[0, 2]]
        inside = sum((position >= edge).astype(jnp.int32) for edge in edges)
        return jnp.where(inside == lanes_of((16, rows), 0), 1.0, 0.0).astype(BF16)

    def by_segment(inside, values):
        top = values.astype(BF16)
        return product(inside, top) + product(inside, (values - top.astype(F32)).astype(BF16))

    def shifted(part, step):
        return pl.ds(pl.multiple_of(part * width + step * tile, tile), tile)

    loads[0].wait()
    loads[1].wait()

    def project_out(step, carry):
        columns = tile_at(step)
        branch[:, columns] = product(att[...], wo[:, columns]) + rowbias[0:1, columns]
        return carry

    lax.fori_loop(0, width // tile, project_out, 0)

    def norm_forward(step, carry):
        rows = pl.ds(pl.multiple_of(step * block, block), block)
        gate = per_frame(0, step * block, block, slice(0, width))
        values = frames[rows, :].astype(F32) + gate * branch[rows, :]
        middle[rows, :] = values
        centered = values - jnp.mean(values, axis=1, keepdims=True)
        hat = centered * lax.rsqrt(jnp.mean(centered * centered, axis=1, keepdims=True) + EPSILON)
        shift = per_frame(1, step * block, block, slice(width, 2 * width))
        scale = per_frame(2, step * block, block, slice(2 * width, 3 * width))
        normed[rows, :] = (hat * (1.0 + scale) + shift).astype(BF16)
        return carry

    lax.fori_loop(0, span // block, norm_forward, 0)

    loads[2].wait()
    root = math.sqrt(2.0 / math.pi)

    def go_up(step, carry):
        columns = tile_at(step)
        value = product(normed[...], up[:, columns]) + rowbias[1:2, columns]
        square = value * value
        turn = jnp.tanh(root * value * (1.0 + 0.044715 * square))
        half = 0.5 * (1.0 + turn)
        active[:, columns] = (value * half).astype(BF16)
        slope[:, columns] = half + 0.5 * value * (1.0 - turn * turn) * root * (1.0 + 3 * 0.044715 * square)
        return carry

    lax.fori_loop(0, hidden // tile, go_up, 0)
    loads[3].wait()

    def go_down(step, carry):
        columns = tile_at(step)
        value = product(active[...], down[:, columns]) + rowbias[2:3, columns]
        gate = per_frame(3, 0, span, shifted(3, step))
        back = given[:, columns].astype(F32)
        output[:, columns] = (middle[:, columns] + gate * value).astype(BF16)
        gbt[:, columns] = (gate * back).astype(BF16)
        sums[:, shifted(3, step)] = by_segment(members(0, span), back * value)
        return carry

    lax.fori_loop(0, width // tile, go_down, 0)

    def back_down(step, carry):
        rows = tile_at(step)
        sdown[rows, :] = from_rows(active[:, rows], gbt[...]).astype(BF16)
        gh[:, rows] = (across(gbt[...], down[rows, :]) * slope[:, rows]).astype(BF16)
        return carry

    lax.fori_loop(0, hidden // tile, back_down, 0)
    stores = [move.local(sdown, gdown)]

    def back_up(step, carry):
        rows = tile_at(step)
        sup[rows, :] = from_rows(normed[:, rows], gh[...]).astype(BF16)
        gn[:, rows] = across(gh[...], up[rows, :])
        return carry

    lax.fori_loop(0, width // tile, back_up, 0)
    stores.append(move.local(sup, gup))
    sums[:, : 3 * width] = jnp.zeros((16, 3 * width), F32)

    def norm_back(step, carry):
        rows = pl.ds(pl.multiple_of(step * block, block), block)
        grad, values = gn[rows, :], middle[rows, :]
        centered = values - jnp.mean(values, axis=1, keepdims=True)
        scaled = lax.rsqrt(jnp.mean(centered * centered, axis=1, keepdims=True) + EPSILON)
        hat = centered * scaled
        inner = grad * (1.0 + per_frame(2, step * block, block, slice(2 * width, 3 * width)))
        mean_one = jnp.mean(inner, axis=1, keepdims=True)
        mean_two = jnp.mean(inner * hat, axis=1, keepdims=True)
        total = given[rows, :].astype(F32) + scaled * (inner - mean_one - hat * mean_two)
        gmid[rows, :] = total
        gb[rows, :] = (per_frame(0, step * block, block, slice(0, width)) * total).astype(BF16)
        inside = members(step * block, block)
        sums[:, :width] += by_segment(inside, total * branch[rows, :])
        sums[:, width : 2 * width] += by_segment(inside, grad)
        sums[:, 2 * width : 3 * width] += by_segment(inside, grad * hat)
        return carry

    lax.fori_loop(0, span // block, norm_back, 0)

    def back_out(step, carry):
        rows = tile_at(step)
        ga[:, rows] = across(gb[...], wo[rows, :]).astype(BF16)
        swo[rows, :] = from_rows(att[:, rows], gb[...]).astype(BF16)
        return carry

    lax.fori_loop(0, width // tile, back_out, 0)
    stores.append(move.local(swo, gwo))

    ones = jnp.ones((16, span), BF16)
    btile[0:24, :] = jnp.zeros((24, LANES), F32)
    start = 24
    for grads, size in ((gb, width), (gh, hidden), (gbt, width)):
        total = product(ones, grads[...])
        for n in range(size // LANES):
            btile[start + n : start + n + 1, :] = total[0:1, n * LANES : (n + 1) * LANES]
        start += size // LANES
    mg[...] = jnp.zeros_like(mg)
    strip = 6 * width // 4
    for n in range(4 * width // tile):
        column = 2 * width + n * tile
        j, offset = column // strip, column % strip
        mg[4 * j : 4 * j + 4, offset : offset + tile] = sums[0:4, n * tile : (n + 1) * tile]
    for copy in stores:
        copy.wait()


def middle_call(span, hidden, args):
    width = MODEL_WIDTH
    vmem, anywhere, scalar = (
        pl.BlockSpec(memory_space=pltpu.VMEM),
        pl.BlockSpec(memory_space=pl.ANY),
        pl.BlockSpec(memory_space=pltpu.SMEM),
    )

    def out(shape, dtype):
        return jax.ShapeDtypeStruct(shape, dtype)

    outs = [
        (out((span, width), BF16), vmem),
        (out((span, width), BF16), vmem),
        (out((span, width), F32), vmem),
        (out((16, 6 * width // 4), F32), vmem),
        (out((56, LANES), F32), vmem),
        (out((width, width), BF16), anywhere),
        (out((width, hidden), BF16), anywhere),
        (out((hidden, width), BF16), anywhere),
    ]
    low, wide = pltpu.VMEM((span, width), BF16), pltpu.VMEM((span, width), F32)
    scratch = [
        low,
        pltpu.VMEM((width, width), BF16),
        pltpu.VMEM((width, hidden), BF16),
        pltpu.VMEM((hidden, width), BF16),
        pltpu.VMEM((16, 4 * width), F32),
        wide,
        wide,
        low,
        pltpu.VMEM((span, hidden), BF16),
        pltpu.VMEM((span, hidden), F32),
        low,
        pltpu.VMEM((span, hidden), BF16),
        wide,
        low,
        pltpu.VMEM((16, 4 * width), F32),
        pltpu.VMEM((width, width), BF16),
        pltpu.VMEM((width, hidden), BF16),
        pltpu.VMEM((hidden, width), BF16),
        pltpu.SemaphoreType.DMA((8,)),
    ]
    return pl.pallas_call(
        middle_kernel,
        out_shape=[shape for shape, _ in outs],
        in_specs=[scalar] + [anywhere] * 4 + [vmem] * 4,
        out_specs=[spec for _, spec in outs],
        scratch_shapes=scratch,
        compiler_params=pltpu.CompilerParams(vmem_limit_bytes=58 * 1024 * 1024),
        cost_estimate=pl.CostEstimate(flops=12 * 10**9, bytes_accessed=30 * 10**6, transcendentals=10**6),
    )(*args)


def modulated_norm(values, shift_part, scale_part):
    center = jnp.mean(values, axis=-1, keepdims=True)
    centered = values - center
    variance = jnp.mean(centered * centered, axis=-1, keepdims=True)
    return centered * lax.rsqrt(variance + EPSILON) * (1.0 + scale_part) + shift_part


def rotate(values, cosines, sines_table):
    shaped = values.reshape(values.shape[:-1] + (values.shape[-1] // HEAD_DIM, HEAD_DIM))
    first_half = shaped[..., : HEAD_DIM // 2]
    second_half = shaped[..., HEAD_DIM // 2 :]
    cosine = cosines[..., None, :]
    sine_part = sines_table[..., None, :]
    turned = jnp.concatenate(
        [
            first_half * cosine - second_half * sine_part,
            second_half * cosine + first_half * sine_part,
        ],
        axis=-1,
    )
    return turned.reshape(values.shape)


def gelu_tanh(values):
    return jax.nn.gelu(values, approximate=True)


def time_features(time_index):
    halfway = MODEL_WIDTH // 2
    frequency = jnp.exp(jnp.arange(halfway, dtype=jnp.float32) * (-math.log(10000.0) / halfway))
    angles = time_index.astype(jnp.float32)[..., None] * frequency
    return jnp.concatenate([jnp.sin(angles), jnp.cos(angles)], axis=-1)


def segment_starts(segment_lengths):
    return jnp.cumsum(segment_lengths, axis=1) - segment_lengths


def segment_numbers(segment_lengths, frame_positions):
    starts = segment_starts(segment_lengths)
    inside = (frame_positions[None, :, None] >= starts[:, None, :]).astype(jnp.int32)
    return jnp.sum(inside, axis=2) - 1


def segment_layout(segment_lengths, frame_positions):
    starts = segment_starts(segment_lengths)
    segment = segment_numbers(segment_lengths, frame_positions)
    onehot = (segment[..., None] == jnp.arange(SEGS, dtype=jnp.int32)).astype(jnp.float32)
    offset = jnp.sum(onehot * starts[:, None, :].astype(jnp.float32), axis=2)
    relative = frame_positions[None, :].astype(jnp.float32) - offset
    return (onehot, relative)


def rope_tables(relative):
    halfway = HEAD_DIM // 2
    frequency = jnp.exp(jnp.arange(halfway, dtype=jnp.float32) * (-math.log(10000.0) / halfway))
    angles = relative[..., None] * frequency
    return (jnp.cos(angles), jnp.sin(angles))


def project(values, matrix, offset):
    return jnp.einsum(
        "rld,de->rle", values, matrix, preferred_element_type=jnp.float32
    ) + offset.astype(jnp.float32)


def project_back(gradient, matrix):
    return jnp.einsum("rle,de->rld", gradient, matrix, preferred_element_type=jnp.float32)


def weight_gradient(values, gradient):
    return jnp.einsum("rld,rle->de", values, gradient, preferred_element_type=jnp.float32)


def bias_gradient(gradient):
    return jnp.sum(gradient.astype(jnp.float32), axis=(0, 1))


def lift_up(member):
    return member.reshape((1, 1) + member.shape)


def settle(member):
    return member.reshape((-1,) + member.shape[3:])


def spread(member, wide_count, narrow_count):
    return member.reshape((wide_count, narrow_count, -1) + member.shape[1:])


def unpack(member):
    return member.reshape(member.shape[2:])


def on_device(
    frames,
    output_gradient,
    segment_lengths,
    time_index,
    query_weight,
    query_bias,
    key_weight,
    key_bias,
    value_weight,
    value_bias,
    output_projection,
    output_bias,
    up_weight,
    up_bias,
    down_weight,
    down_bias,
    modulation_weight,
    modulation_bias,
):
    narrow_count = lax.axis_size("seq")
    wide_count = lax.axis_size("dp")
    seq_index = lax.axis_index("seq")
    row_count, span_frames, width_total = frames.shape
    row_length = span_frames * narrow_count
    block_rows = min(512, row_length)
    block_count = row_length // block_rows
    local_weights = (
        query_weight,
        query_bias,
        key_weight,
        key_bias,
        value_weight,
        value_bias,
        output_projection,
        output_bias,
        up_weight,
        up_bias,
        down_weight,
        down_bias,
        modulation_bias,
    )
    lifted = [lift_up(member) for member in local_weights]
    halfway_set = (
        lax.all_gather(lifted[0], "dp", axis=0, tiled=True),
        lax.all_gather(lifted[1], "dp", axis=0, tiled=True),
        lax.all_gather(lifted[2], "dp", axis=0, tiled=True),
        lax.all_gather(lifted[3], "dp", axis=0, tiled=True),
        lax.all_gather(lifted[4], "dp", axis=0, tiled=True),
        lax.all_gather(lifted[5], "dp", axis=0, tiled=True),
        lax.all_gather(lifted[6], "dp", axis=0, tiled=True),
        lax.all_gather(lifted[7], "dp", axis=0, tiled=True),
        lax.all_gather(lifted[8], "dp", axis=0, tiled=True),
        lax.all_gather(lifted[9], "dp", axis=0, tiled=True),
        lax.all_gather(lifted[10], "dp", axis=0, tiled=True),
        lax.all_gather(lifted[11], "dp", axis=0, tiled=True),
        lax.all_gather(lifted[12], "dp", axis=0, tiled=True),
    )
    complete_set = (
        lax.all_gather(halfway_set[0], "seq", axis=1, tiled=True),
        lax.all_gather(halfway_set[1], "seq", axis=1, tiled=True),
        lax.all_gather(halfway_set[2], "seq", axis=1, tiled=True),
        lax.all_gather(halfway_set[3], "seq", axis=1, tiled=True),
        lax.all_gather(halfway_set[4], "seq", axis=1, tiled=True),
        lax.all_gather(halfway_set[5], "seq", axis=1, tiled=True),
        lax.all_gather(halfway_set[6], "seq", axis=1, tiled=True),
        lax.all_gather(halfway_set[7], "seq", axis=1, tiled=True),
        lax.all_gather(halfway_set[8], "seq", axis=1, tiled=True),
        lax.all_gather(halfway_set[9], "seq", axis=1, tiled=True),
        lax.all_gather(halfway_set[10], "seq", axis=1, tiled=True),
        lax.all_gather(halfway_set[11], "seq", axis=1, tiled=True),
        lax.all_gather(halfway_set[12], "seq", axis=1, tiled=True),
    )
    gathered = [settle(member) for member in complete_set]
    (
        full_query,
        full_query_bias,
        full_key,
        full_key_bias,
        full_value,
        full_value_bias,
        full_output,
        full_output_bias,
        full_up,
        full_up_bias,
        full_down,
        full_down_bias,
        full_modulation_bias,
    ) = gathered
    local_positions = seq_index * span_frames + jnp.arange(span_frames, dtype=jnp.int32)
    local_onehot, local_relative = segment_layout(segment_lengths, local_positions)
    row_segment = segment_numbers(segment_lengths, jnp.arange(row_length, dtype=jnp.int32))
    cosines, sines_table = rope_tables(local_relative)
    turning = partial(rotate, cosines=cosines, sines_table=sines_table)
    owned_rows = modulation_weight.shape[0]
    owned_start = (lax.axis_index("dp") * narrow_count + seq_index) * owned_rows
    every_time = lax.all_gather(time_index, "dp", axis=0, tiled=True)
    every_low = jax.nn.silu(time_features(every_time)).astype(jnp.bfloat16)
    owned_low = lax.dynamic_slice_in_dim(every_low, owned_start, owned_rows, 2)
    partial_modulation = jnp.einsum(
        "rsd,dc->rsc", owned_low, modulation_weight, preferred_element_type=jnp.float32
    )
    row_share = lax.psum_scatter(partial_modulation, "dp", scatter_dimension=0, tiled=True)
    modulation = lax.psum(row_share.astype(jnp.bfloat16), "seq").astype(
        jnp.float32
    ) + full_modulation_bias.astype(jnp.float32)
    per_frame = jnp.einsum("rls,rsc->rlc", local_onehot, modulation, precision=HIGHEST)
    shift_one, scale_one, gate_one, shift_two, scale_two, gate_two = jnp.split(
        per_frame, 6, axis=-1
    )
    inputs = frames.astype(jnp.float32)
    normed, norm_back = jax.vjp(modulated_norm, inputs, shift_one, scale_one)
    normed_low = normed.astype(jnp.bfloat16)
    query_pre = project(normed_low, full_query, full_query_bias)
    key_pre = project(normed_low, full_key, full_key_bias)
    value_low = project(normed_low, full_value, full_value_bias).astype(jnp.bfloat16)
    query_turned, query_back = jax.vjp(turning, query_pre)
    key_turned, key_back = jax.vjp(turning, key_pre)
    query_heads, key_heads, value_heads = (
        lax.all_to_all(
            query_turned.astype(jnp.bfloat16), "seq", split_axis=2, concat_axis=1, tiled=True
        ),
        lax.all_to_all(
            key_turned.astype(jnp.bfloat16), "seq", split_axis=2, concat_axis=1, tiled=True
        ),
        lax.all_to_all(value_low, "seq", split_axis=2, concat_axis=1, tiled=True),
    )
    local_heads = query_heads.shape[2] // HEAD_DIM
    head_shape = (row_count, row_length, local_heads, HEAD_DIM)
    queries = query_heads.reshape(head_shape)
    keys_all = key_heads.reshape(head_shape)
    values_all = value_heads.reshape(head_shape)
    scaling = HEAD_DIM ** (-0.5)
    positions_all = jnp.arange(row_count * block_count, dtype=jnp.int32)

    def fetch_block(position):
        row_index = position // block_count
        start_row = position % block_count * block_rows
        key_row = lax.dynamic_index_in_dim(keys_all, row_index, 0, keepdims=False)
        value_row = lax.dynamic_index_in_dim(values_all, row_index, 0, keepdims=False)
        segment_row = lax.dynamic_index_in_dim(row_segment, row_index, 0, keepdims=False)
        query_block = lax.dynamic_slice_in_dim(
            lax.dynamic_index_in_dim(queries, row_index, 0, keepdims=False),
            start_row,
            block_rows,
            0,
        )
        segment_block = lax.dynamic_slice_in_dim(segment_row, start_row, block_rows, 0)
        scores = (
            jnp.einsum("bhd,khd->hbk", query_block, key_row, preferred_element_type=jnp.float32)
            * scaling
        )
        scores = jnp.where((segment_block[:, None] == segment_row[None, :])[None], scores, NEGATIVE)
        return (row_index, start_row, query_block, key_row, value_row, scores)

    def forward_block(position):
        row_index, start_row, query_block, key_row, value_row, scores = fetch_block(position)
        highest = jnp.max(scores, axis=2, keepdims=True)
        weights = jnp.exp(scores - highest)
        totals = jnp.sum(weights, axis=2, keepdims=True)
        probabilities = (weights / totals).astype(jnp.bfloat16)
        mixed_block = jnp.einsum(
            "hbk,khd->bhd", probabilities, value_row, preferred_element_type=jnp.float32
        )
        return (
            mixed_block.astype(jnp.bfloat16).reshape(block_rows, -1),
            (highest + jnp.log(totals))[..., 0],
        )

    mixed_blocks, logsums = lax.map(forward_block, positions_all)
    attention_heads = mixed_blocks.reshape(row_count, row_length, -1)
    attention_frames = lax.all_to_all(
        attention_heads, "seq", split_axis=1, concat_axis=2, tiled=True
    )
    branch = project(attention_frames, full_output, full_output_bias)
    middle = inputs + gate_one * branch
    normed_two, norm_two_back = jax.vjp(modulated_norm, middle, shift_two, scale_two)
    normed_two_low = normed_two.astype(jnp.bfloat16)
    hidden = project(normed_two_low, full_up, full_up_bias)
    activated, gelu_back = jax.vjp(gelu_tanh, hidden)
    activated_low = activated.astype(jnp.bfloat16)
    branch_two = project(activated_low, full_down, full_down_bias)
    layer_output = (middle + gate_two * branch_two).astype(jnp.bfloat16)
    cotangent = output_gradient.astype(jnp.float32)
    grad_branch_two = (gate_two * cotangent).astype(jnp.bfloat16)
    grad_gate_two = cotangent * branch_two
    grad_activated = project_back(grad_branch_two, full_down)
    grad_hidden = gelu_back(grad_activated)[0].astype(jnp.bfloat16)
    grad_normed_two = project_back(grad_hidden, full_up)
    grad_middle_part, grad_shift_two, grad_scale_two = norm_two_back(grad_normed_two)
    grad_middle = cotangent + grad_middle_part
    grad_gate_one = grad_middle * branch
    grad_branch = (gate_one * grad_middle).astype(jnp.bfloat16)
    grad_attention = project_back(grad_branch, full_output).astype(jnp.bfloat16)
    grad_heads = lax.all_to_all(grad_attention, "seq", split_axis=2, concat_axis=1, tiled=True)
    grad_outputs = grad_heads.reshape(head_shape)

    def backward_block(running, pair_inputs):
        grad_keys, grad_values = running
        position, logsum = pair_inputs
        row_index, start_row, query_block, key_row, value_row, scores = fetch_block(position)
        grad_block = lax.dynamic_slice_in_dim(
            lax.dynamic_index_in_dim(grad_outputs, row_index, 0, keepdims=False),
            start_row,
            block_rows,
            0,
        )
        probabilities = jnp.exp(scores - logsum[..., None])
        grad_probabilities = jnp.einsum(
            "bhd,khd->hbk", grad_block, value_row, preferred_element_type=jnp.float32
        )
        delta_sum = jnp.sum(probabilities * grad_probabilities, axis=2, keepdims=True)
        grad_scores = (probabilities * (grad_probabilities - delta_sum)).astype(jnp.bfloat16)
        grad_query_block = (
            jnp.einsum("hbk,khd->bhd", grad_scores, key_row, preferred_element_type=jnp.float32)
            * scaling
        )
        key_part = (
            jnp.einsum("hbk,bhd->khd", grad_scores, query_block, preferred_element_type=jnp.float32)
            * scaling
        )
        value_part = jnp.einsum(
            "hbk,bhd->khd",
            probabilities.astype(jnp.bfloat16),
            grad_block,
            preferred_element_type=jnp.float32,
        )
        grad_keys = lax.dynamic_update_index_in_dim(
            grad_keys,
            lax.dynamic_index_in_dim(grad_keys, row_index, 0, keepdims=False) + key_part,
            row_index,
            0,
        )
        grad_values = lax.dynamic_update_index_in_dim(
            grad_values,
            lax.dynamic_index_in_dim(grad_values, row_index, 0, keepdims=False) + value_part,
            row_index,
            0,
        )
        return (
            (grad_keys, grad_values),
            grad_query_block.astype(jnp.bfloat16).reshape(block_rows, -1),
        )

    zero_heads = jnp.zeros(head_shape, jnp.float32)
    (grad_keys_all, grad_values_all), grad_query_blocks = lax.scan(
        backward_block, (zero_heads, zero_heads), (positions_all, logsums)
    )
    flat_shape = (row_count, row_length, -1)
    grad_query_frames, grad_key_frames, grad_value_frames = (
        lax.all_to_all(
            grad_query_blocks.reshape(flat_shape), "seq", split_axis=1, concat_axis=2, tiled=True
        ),
        lax.all_to_all(
            grad_keys_all.reshape(flat_shape).astype(jnp.bfloat16),
            "seq",
            split_axis=1,
            concat_axis=2,
            tiled=True,
        ),
        lax.all_to_all(
            grad_values_all.reshape(flat_shape).astype(jnp.bfloat16),
            "seq",
            split_axis=1,
            concat_axis=2,
            tiled=True,
        ),
    )
    grad_query_pre = query_back(grad_query_frames.astype(jnp.float32))[0].astype(jnp.bfloat16)
    grad_key_pre = key_back(grad_key_frames.astype(jnp.float32))[0].astype(jnp.bfloat16)
    grad_normed = (
        project_back(grad_query_pre, full_query)
        + project_back(grad_key_pre, full_key)
        + project_back(grad_value_frames, full_value)
    )
    grad_inputs_part, grad_shift_one, grad_scale_one = norm_back(grad_normed)
    frames_grad = (grad_middle + grad_inputs_part).astype(jnp.bfloat16)
    grad_per_frame = jnp.concatenate(
        [
            grad_shift_one,
            grad_scale_one,
            grad_gate_one,
            grad_shift_two,
            grad_scale_two,
            grad_gate_two,
        ],
        axis=-1,
    )
    grad_modulation = jnp.einsum("rls,rlc->rsc", local_onehot, grad_per_frame, precision=HIGHEST)
    gradients = (
        weight_gradient(normed_low, grad_query_pre),
        bias_gradient(grad_query_pre),
        weight_gradient(normed_low, grad_key_pre),
        bias_gradient(grad_key_pre),
        weight_gradient(normed_low, grad_value_frames),
        bias_gradient(grad_value_frames),
        weight_gradient(attention_frames, grad_branch),
        bias_gradient(grad_branch),
        weight_gradient(normed_two_low, grad_hidden),
        bias_gradient(grad_hidden),
        weight_gradient(activated_low, grad_branch_two),
        bias_gradient(grad_branch_two),
        jnp.sum(grad_modulation, axis=(0, 1)),
    )
    row_total = lax.psum(grad_modulation.astype(jnp.bfloat16), "seq").astype(jnp.float32)
    every_grad = lax.all_gather(row_total.astype(jnp.bfloat16), "dp", axis=0, tiled=True).astype(
        row_total.dtype
    )
    modulation_weight_grad = jnp.einsum(
        "rsd,rsc->dc", owned_low.astype(jnp.float32), every_grad, precision=HIGHEST
    )
    spreaded = [spread(member, wide_count, narrow_count) for member in gradients]
    first_pass = (
        lax.psum_scatter(
            spreaded[0].astype(jnp.bfloat16), "seq", scatter_dimension=1, tiled=True
        ).astype(jnp.float32),
        lax.psum_scatter(
            spreaded[1].astype(jnp.bfloat16), "seq", scatter_dimension=1, tiled=True
        ).astype(jnp.float32),
        lax.psum_scatter(
            spreaded[2].astype(jnp.bfloat16), "seq", scatter_dimension=1, tiled=True
        ).astype(jnp.float32),
        lax.psum_scatter(
            spreaded[3].astype(jnp.bfloat16), "seq", scatter_dimension=1, tiled=True
        ).astype(jnp.float32),
        lax.psum_scatter(
            spreaded[4].astype(jnp.bfloat16), "seq", scatter_dimension=1, tiled=True
        ).astype(jnp.float32),
        lax.psum_scatter(
            spreaded[5].astype(jnp.bfloat16), "seq", scatter_dimension=1, tiled=True
        ).astype(jnp.float32),
        lax.psum_scatter(
            spreaded[6].astype(jnp.bfloat16), "seq", scatter_dimension=1, tiled=True
        ).astype(jnp.float32),
        lax.psum_scatter(
            spreaded[7].astype(jnp.bfloat16), "seq", scatter_dimension=1, tiled=True
        ).astype(jnp.float32),
        lax.psum_scatter(
            spreaded[8].astype(jnp.bfloat16), "seq", scatter_dimension=1, tiled=True
        ).astype(jnp.float32),
        lax.psum_scatter(
            spreaded[9].astype(jnp.bfloat16), "seq", scatter_dimension=1, tiled=True
        ).astype(jnp.float32),
        lax.psum_scatter(
            spreaded[10].astype(jnp.bfloat16), "seq", scatter_dimension=1, tiled=True
        ).astype(jnp.float32),
        lax.psum_scatter(
            spreaded[11].astype(jnp.bfloat16), "seq", scatter_dimension=1, tiled=True
        ).astype(jnp.float32),
        lax.psum_scatter(
            spreaded[12].astype(jnp.bfloat16), "seq", scatter_dimension=1, tiled=True
        ).astype(jnp.float32),
    )
    second_pass = (
        lax.psum_scatter(first_pass[0], "dp", scatter_dimension=0, tiled=True),
        lax.psum_scatter(first_pass[1], "dp", scatter_dimension=0, tiled=True),
        lax.psum_scatter(first_pass[2], "dp", scatter_dimension=0, tiled=True),
        lax.psum_scatter(first_pass[3], "dp", scatter_dimension=0, tiled=True),
        lax.psum_scatter(first_pass[4], "dp", scatter_dimension=0, tiled=True),
        lax.psum_scatter(first_pass[5], "dp", scatter_dimension=0, tiled=True),
        lax.psum_scatter(first_pass[6], "dp", scatter_dimension=0, tiled=True),
        lax.psum_scatter(first_pass[7], "dp", scatter_dimension=0, tiled=True),
        lax.psum_scatter(first_pass[8], "dp", scatter_dimension=0, tiled=True),
        lax.psum_scatter(first_pass[9], "dp", scatter_dimension=0, tiled=True),
        lax.psum_scatter(first_pass[10], "dp", scatter_dimension=0, tiled=True),
        lax.psum_scatter(first_pass[11], "dp", scatter_dimension=0, tiled=True),
        lax.psum_scatter(first_pass[12], "dp", scatter_dimension=0, tiled=True),
    )
    reduced = [unpack(member) for member in second_pass]
    return (
        layer_output,
        frames_grad,
        reduced[0],
        reduced[1],
        reduced[2],
        reduced[3],
        reduced[4],
        reduced[5],
        reduced[6],
        reduced[7],
        reduced[8],
        reduced[9],
        reduced[10],
        reduced[11],
        modulation_weight_grad,
        reduced[12],
    )


def on_device_fast(
    frames, output_gradient, segment_lengths, time_index, query_weight, query_bias, key_weight, key_bias,
    value_weight, value_bias, output_projection, output_bias, up_weight, up_bias, down_weight, down_bias,
    modulation_weight, modulation_bias,
):
    seq_index, dp_index = lax.axis_index("seq"), lax.axis_index("dp")
    depth = lax.axis_size("dp") // 2
    own_index = dp_index * 4 + seq_index
    _, span, width = frames.shape
    own_rows, hidden = up_weight.shape
    down_rows = down_weight.shape[0]
    vectors = (query_bias, key_bias, value_bias, output_bias, up_bias, down_bias, modulation_bias)
    biases = [vector.reshape(1, -1) for vector in vectors]
    (att, oh, qs, ks, vs, lse, normed, wg, mods, cosr, sinr, rowbias, low, wo_all, up_all, down_all) = forward_call(
        depth, span, own_rows, down_rows, hidden,
        (segment_lengths, time_index, frames[0], *biases, query_weight, key_weight, value_weight,
         output_projection, up_weight, down_weight, modulation_weight),
    )
    (output, grad_attention, grad_middle, mg_in, bias_in, gwo, gup, gdown) = middle_call(
        span, hidden,
        (segment_lengths, att, wo_all.reshape(width, width), up_all.reshape(width, hidden),
         down_all.reshape(hidden, width), mods, rowbias, frames[0], output_gradient[0]),
    )

    def pieces(grad, rows):
        return grad.reshape(depth, 2, 2, 2, rows, -1)

    (fgrad, dwq, dwk, dwv, dwo, dup, ddown, dmw, mbias, btile) = backward_call(
        depth, span, own_rows, down_rows, hidden,
        (segment_lengths, grad_attention, qs, ks, vs, oh, lse, normed, wg, cosr, sinr, low, mods, frames[0],
         grad_middle, mg_in, bias_in,
         pieces(gwo, own_rows), pieces(gup, own_rows), pieces(gdown, down_rows)),
    )
    sums = btile.reshape(-1)

    def own_part(vector, start, size):
        return lax.dynamic_slice_in_dim(vector, start + own_index * size, size)

    lengths = [member.shape[0] for member in (query_bias, key_bias, value_bias, output_bias, up_bias, down_bias)]
    starts = [sum(lengths[:n]) * depth * 8 for n in range(6)]
    bq, bk, bv, bo, bu, bd = [own_part(sums, start, size) for start, size in zip(starts, lengths)]
    bm = own_part(mbias[:4].reshape(-1), 0, modulation_bias.shape[0])
    return (
        output[None], fgrad[None], dwq, bq, dwk, bk, dwv, bv, dwo, bo, dup, bu, ddown, bd, dmw, bm,
    )


def fits(mesh, frames, *parameters):
    dp, seq = mesh.shape["dp"], mesh.shape["seq"]
    rows = parameters[3].shape[0] // (dp * seq)
    return seq == 4 and dp % 2 == 0 and rows == 32 and frames.shape[0] == dp


def solution(mesh):
    def run(*arrays):
        return mapped(mesh, on_device_fast if fits(mesh, *arrays) else on_device)(*arrays)

    return run


def mapped(mesh, body):
    return jax.shard_map(
        body,
        mesh=mesh,
        in_specs=(
            P("dp", "seq", None),
            P("dp", "seq", None),
            P("dp", None),
            P("dp", None),
            P(("dp", "seq"), None),
            P(("dp", "seq")),
            P(("dp", "seq"), None),
            P(("dp", "seq")),
            P(("dp", "seq"), None),
            P(("dp", "seq")),
            P(("dp", "seq"), None),
            P(("dp", "seq")),
            P(("dp", "seq"), None),
            P(("dp", "seq")),
            P(("dp", "seq"), None),
            P(("dp", "seq")),
            P(("dp", "seq"), None),
            P(("dp", "seq")),
        ),
        out_specs=(
            P("dp", "seq", None),
            P("dp", "seq", None),
            P(("dp", "seq"), None),
            P(("dp", "seq")),
            P(("dp", "seq"), None),
            P(("dp", "seq")),
            P(("dp", "seq"), None),
            P(("dp", "seq")),
            P(("dp", "seq"), None),
            P(("dp", "seq")),
            P(("dp", "seq"), None),
            P(("dp", "seq")),
            P(("dp", "seq"), None),
            P(("dp", "seq")),
            P(("dp", "seq"), None),
            P(("dp", "seq")),
        ),
        check_vma=False,
    )
```

```python
from functools import partial
import math

import jax
import jax.numpy as jnp
from jax import lax
from jax.experimental import pallas as pl
from jax.experimental.pallas import tpu as pltpu
from jax.sharding import PartitionSpec as P

HEAD_DIM = 64
MODEL_WIDTH = 1024
SEGS = 4
EPSILON = 1e-06
NEGATIVE = -1e30
HIGHEST = lax.Precision.HIGHEST
F32 = jnp.float32
BF16 = jnp.bfloat16
LANES = 128


class Mover:
    def __init__(self, send_sems, recv_sems, local_sems):
        self.send_sems, self.recv_sems, self.local_sems = send_sems, recv_sems, local_sems
        self.count = self.local_count = 0
        self.sent = []

    def send(self, source, target, device):
        slot = self.count
        self.count += 1
        copy = pltpu.make_async_remote_copy(
            src_ref=source,
            dst_ref=target,
            send_sem=self.send_sems.at[slot],
            recv_sem=self.recv_sems.at[slot],
            device_id=device,
            device_id_type=pl.DeviceIdType.MESH,
        )
        copy.start()
        self.sent.append(copy)
        return copy

    def local(self, source, target):
        slot = self.local_count
        self.local_count += 1
        copy = pltpu.make_async_copy(source, target, self.local_sems.at[slot])
        copy.start()
        return copy

    def finish(self, but=()):
        for copy in self.sent:
            if not any(copy is other for other in but):
                copy.wait_send()


class Place:
    def __init__(self, depth):
        dp, seq = lax.axis_index("dp"), lax.axis_index("seq")
        self.depth = depth
        self.z, self.y = dp // 2, dp % 2
        self.x, self.c = seq // 2, seq % 2
        self.seq = seq
        self.index = dp * 4 + seq

    def at(self, z, y, x, c):
        return {"dp": z * 2 + y, "seq": x * 2 + c}

    def core(self):
        return self.at(self.z, self.y, self.x, 1 - self.c)

    def across_x(self):
        return self.at(self.z, self.y, 1 - self.x, self.c)

    def across_y(self):
        return self.at(self.z, 1 - self.y, self.x, self.c)

    def ahead(self, step):
        return (self.z + step) % self.depth

    def along_z(self, step):
        return self.at(self.ahead(step), self.y, self.x, self.c)

    def row_peer(self, step):
        return {"dp": self.z * 2 + self.y, "seq": (self.seq + step) % 4}

    def enter(self, diagonal=False):
        barrier = pltpu.get_barrier_semaphore()
        peers = [self.row_peer(step) for step in (1, 2, 3)] + [self.across_y()]
        peers += [self.along_z(step) for step in range(1, self.depth)]
        if diagonal:
            peers += [self.at(self.ahead(k), 1 - self.y, self.x, self.c) for k in range(1, self.depth)]
        for peer in peers:
            pl.semaphore_signal(barrier, 1, device_id=peer, device_id_type=pl.DeviceIdType.MESH)
        pl.semaphore_wait(barrier, len(peers))


def lanes_of(shape, axis=1):
    return lax.broadcasted_iota(jnp.int32, shape, axis)


def frame_segments(lens, first_row, rows, width):
    position = lanes_of((rows, width), 0) + first_row
    first, second, third = lens[0, 0], lens[0, 0] + lens[0, 1], lens[0, 0] + lens[0, 1] + lens[0, 2]
    segment = (
        (position >= first).astype(jnp.int32)
        + (position >= second).astype(jnp.int32)
        + (position >= third).astype(jnp.int32)
    )
    start = jnp.where(
        segment == 0, 0, jnp.where(segment == 1, first, jnp.where(segment == 2, second, third))
    )
    return segment, position - start


def three_parts(values):
    high = values.astype(BF16).astype(F32)
    rest = values - high
    middle = rest.astype(BF16).astype(F32)
    return high, middle, (rest - middle).astype(BF16).astype(F32)


def swap_halves(values, lane):
    return jnp.where(
        lane % HEAD_DIM < HEAD_DIM // 2, pltpu.roll(values, 96, 1), pltpu.roll(values, 32, 1)
    )


def head_only(values, lane, head):
    return jnp.where((lane >= HEAD_DIM) == bool(head), values.astype(F32), 0.0).astype(BF16)


def across(left, right):
    return lax.dot_general(left, right, (((1,), (1,)), ((), ())), preferred_element_type=F32)


def product(left, right):
    return jnp.dot(left, right, preferred_element_type=F32)


AXES = (
    (1, 2, 0), (0, 2, 1), (2, 0, 1), (0, 2, 1), (0, 1, 2), (0, 1, 2), (0, 2, 1), (0, 2, 1), (2, 1, 0), (0, 1, 2),
)
(
    GATHER_Z, GATHER_TWO, GATHER_THREE, GATHER_CORE, COLUMNS_Z, COLUMNS_Y, PROJECT, ATTEND, GO_UP, FRAMES_X,
    FRAMES_ON, TABLES, TIMES_Y, SHARE, MOD_Y, MOD_Z, MOD_X, MOD_LAST, FRAMES_CORE, BIAS_Y, BIAS_X, BIAS_CORE,
    BIASES, MODS, OUT, GO_DOWN, BACK, GRADS, WAITS,
) = range(29)
FORWARD_ORDER = (
    (FRAMES_X, 0), (GATHER_Z, 9), (GATHER_Z, 1), (TIMES_Y, 0), (BIAS_Y, 0), (FRAMES_CORE, 0), (GATHER_TWO, 9),
    (COLUMNS_Z, 0), (COLUMNS_Z, 1), (SHARE, 0), (GATHER_Z, 4), (GATHER_Z, 8), (BIAS_X, 0), (MOD_Y, 0),
    (COLUMNS_Y, 0), (GATHER_THREE, 9), (COLUMNS_Y, 1), (COLUMNS_Z, 2), (FRAMES_X, 1), (GATHER_Z, 3), (MOD_Z, 0),
    (GATHER_Z, 0), (GATHER_Z, 2), (GATHER_Z, 7), (GATHER_TWO, 8), (GATHER_Z, 6), (TABLES, 1), (BIAS_CORE, 0),
    (GATHER_TWO, 4), (BIASES, 0), (COLUMNS_Y, 2), (TABLES, 0), (GATHER_TWO, 0), (GATHER_TWO, 1), (FRAMES_ON, 1),
    (MOD_X, 0), (GATHER_Z, 5), (GATHER_TWO, 3), (GATHER_THREE, 1), (GATHER_TWO, 2), (MOD_LAST, 0),
    (GATHER_THREE, 4), (MODS, 0), (PROJECT, 0), (GATHER_CORE, 9), (GATHER_THREE, 3), (GATHER_TWO, 7),
    (FRAMES_ON, 0), (PROJECT, 1), (PROJECT, 2), (GATHER_THREE, 0), (GATHER_TWO, 6), (PROJECT, 3),
    (GATHER_CORE, 1), (GATHER_TWO, 5), (GATHER_THREE, 8), (ATTEND, 1), (GATHER_THREE, 2), (ATTEND, 1),
    (GATHER_CORE, 4), (GATHER_CORE, 3), (GATHER_THREE, 5), (GATHER_THREE, 6), (ATTEND, 2), (GATHER_THREE, 7),
    (ATTEND, 3), (GATHER_CORE, 0), (ATTEND, 1), (GATHER_CORE, 6), (GATHER_CORE, 2), (GATHER_CORE, 5), (OUT, 0),
    (GO_UP, 0), (GATHER_CORE, 7), (GATHER_CORE, 8), (GO_UP, 1), (GO_DOWN, 0), (BACK, 0), (GRADS, 0),
)


def forward_kernel(
    depth,
    lens, times, frames, given_in, bq, bk, bv, bo, bu, bd, bm, wq, wk, wv, wo, up, down, mw,
    output, gmid, mg, btile, mods, low, gwo, gup, gdown, do_all, qs_out, ks_out, vs_out, oh_out, lse_out,
    normed_out, wg_out, cos_out, sin_out,
    att, oh, qs, lse, normed, wg, cosr, sinr, rowbias, wo_all, up_all, down_all,
    bb, xall, mwst, tb, part, recva, suma, recvb, sumb, recvc, sumc, recvd, modh, bmat, mod3, qbias,
    ka, va, qaug, given, mod6, branch, middle, normed_two, active, slope, gbt, gh, gn, gb, ga, sums,
    send_sems, recv_sems, local_sems,
):
    here = Place(depth)
    z, y, x, c, g = here.z, here.y, here.x, here.c, here.seq
    span, width = frames.shape
    hidden = up.shape[1]
    rows_all = span * 4
    block, tall, tile = 128, span, 256
    move = Mover(send_sems, recv_sems, local_sems)
    steps_z = range(1, depth)

    row = lanes_of((16, LANES), 0) % 4
    own_times = jnp.where(
        row == 0, times[0, 0], jnp.where(row == 1, times[0, 1], jnp.where(row == 2, times[0, 2], times[0, 3]))
    )
    tb[z, y] = own_times.astype(F32)
    bb[z, y, x, c] = jnp.zeros((8, LANES), F32)
    for n, vector in enumerate((bq, bk, bv, bo, bu, bd)):
        bb[z, y, x, c, n : n + 1, : vector.shape[1]] = vector[...].astype(F32)
    bb[z, y, x, c, 6:7, :] = bm[:, :LANES].astype(F32)
    bb[z, y, x, c, 7:8, : bm.shape[1] - LANES] = bm[:, LANES:].astype(F32)
    weights = (wq, wk, wv)
    own_width = wg.shape[-1]
    locals_first = [
        move.local(weights[j].at[:, pl.ds(pl.multiple_of(g * own_width, LANES), own_width)], wg.at[j, z, y, g])
        for j in range(3)
    ]
    strip = mw.shape[1] // 4
    local_mw = [
        move.local(mw.at[:, pl.ds(j * strip, strip)], mwst.at[pl.ds(j * 32, 32)]) for j in range(4)
    ]
    local_frames = move.local(frames, xall.at[g])
    local_given = move.local(given_in, given)
    here.enter()

    legs = {}
    shard, wide = wo.shape[0], MODEL_WIDTH
    thin = shard // 2
    flows = []

    def add_flow(source, target, first_row, columns=None):
        rows = pl.ds(first_row, thin)
        if columns is None:
            flows.append((source.at[rows], target.at[:, :, :, :, rows]))
        else:
            columns = pl.ds(columns, wide)
            flows.append((source.at[rows, columns], target.at[:, :, :, :, rows, columns]))

    for side in range(2):
        add_flow(wo, wo_all, side * thin)
    for side in range(2):
        add_flow(up, up_all, side * thin, 0)
        add_flow(up, up_all, side * thin, wide)
    for side in range(4):
        add_flow(down, down_all, side * thin)
    count = len(flows)

    legs, outgoing, owned = {}, [], {}
    here_at = (z, y, x)

    def to_axis(axis):
        if axis == 0:
            return [here.along_z(k) for k in steps_z]
        return [here.across_y() if axis == 1 else here.across_x()]

    def held(number, known):
        place = tuple(slice(None) if axis in known else here_at[axis] for axis in range(3))
        return flows[number][1].at[place + (c,)]

    def first_leg(number):
        source = flows[number][0]
        target = held(number, ())
        owned[number] = move.local(source, target)
        legs[number] = [move.send(source, target, peer) for peer in to_axis(AXES[number][0])]

    def next_leg(number, done):
        if done == 1:
            owned[number].wait()
        for copy in legs[number]:
            copy.wait_recv()
        part = held(number, AXES[number][:done])
        peers = [here.core()] if done == 3 else to_axis(AXES[number][done])
        legs[number] = [move.send(part, part, peer) for peer in peers]
        outgoing.extend(legs[number])

    def second_leg(number):
        next_leg(number, 1)

    def third_leg(number):
        next_leg(number, 2)

    def fourth_leg(number):
        next_leg(number, 3)

    def arrived(*numbers):
        for number in numbers:
            for copy in legs[number]:
                copy.wait_recv()

    times_z = [move.send(tb.at[z, y], tb.at[z, y], here.along_z(k)) for k in steps_z]
    qkv_row = [
        [
            move.send(
                weights[j].at[:, pl.ds(pl.multiple_of((g + k) % 4 * own_width, LANES), own_width)],
                wg.at[j, z, y, g],
                here.row_peer(k),
            )
            for k in (1, 2, 3)
        ]
        for j in range(3)
    ]
    bias_z = [move.send(bb.at[z, y, x, c], bb.at[z, y, x, c], here.along_z(k)) for k in steps_z]
    part_rows = span // 2
    frame_parts = [pl.ds(n * part_rows, part_rows) for n in range(2)]
    half = strip // 2
    sent = {}
    stores = []

    def columns_z(j):
        locals_first[j].wait()
        for copy in qkv_row[j]:
            copy.wait_recv()
        sent["q", j] = [move.send(wg.at[j, z, y], wg.at[j, z, y], here.along_z(k)) for k in steps_z]

    def columns_y(j):
        for copy in sent["q", j]:
            copy.wait_recv()
        sent["p", j] = move.send(wg.at[j, :, y], wg.at[j, :, y], here.across_y())

    def times_across():
        for copy in times_z:
            copy.wait_recv()
        sent["ty"] = move.send(tb.at[:, y], tb.at[:, y], here.across_y())

    def mod_share():
        sent["ty"].wait_recv()
        lane = lanes_of((16 * 2 * depth, LANES))
        row = lanes_of((16 * 2 * depth, LANES), 0)
        feature = here.index * 32 + lane % 32
        halfway = MODEL_WIDTH // 2
        frequency = jnp.exp((feature % halfway).astype(F32) * (-math.log(10000.0) / halfway))
        angle = tb[...].reshape(16 * 2 * depth, LANES) * frequency
        wave = jnp.where(feature < halfway, jnp.sin(angle), jnp.cos(angle))
        gated = wave / (1.0 + jnp.exp(-wave))
        low[...] = jnp.where(lane // 32 == (row % 16) // 4, gated, 0.0).astype(BF16)
        for copy in local_mw:
            copy.wait()
        for side in range(2):
            share = product(low[...], mwst[:, side * half : (side + 1) * half])
            part[side] = share.astype(BF16).reshape(depth, 2, 16, half)
        sent["mc"] = move.send(part.at[1 - c], recva, here.core())

    def mod_y():
        sent["mc"].wait_recv()
        suma[...] = (part[c].astype(F32) + recva[...].astype(F32)).astype(BF16)
        sent["my"] = move.send(suma.at[:, 1 - y], recvb, here.across_y())

    def mod_z():
        sent["my"].wait_recv()
        sumb[...] = (suma[:, y].astype(F32) + recvb[...].astype(F32)).astype(BF16)
        sent["mz"] = [move.send(sumb.at[here.ahead(k)], recvc.at[k - 1], here.along_z(k)) for k in steps_z]

    def mod_x():
        total = sumb[z].astype(F32)
        for k in steps_z:
            sent["mz"][k - 1].wait_recv()
            total = total + recvc[k - 1].astype(F32)
        sumc[...] = total
        sent["mx"] = move.send(sumc, recvd, here.across_x())

    def mod_last():
        sent["mx"].wait_recv()
        modh[c] = sumc[...] + recvd[...]
        sent["ml"] = move.send(modh.at[c], modh.at[c], here.core())

    def frames_core():
        sent["fc"] = move.send(frames, xall.at[g], here.core())

    def frames_x(n):
        sent["fx", n] = move.send(frames.at[frame_parts[n]], xall.at[g, frame_parts[n]], here.across_x())

    frames_here = []

    def frames_in(n):
        if n not in frames_here:
            sent["fx", n].wait_recv()
            frames_here.append(n)

    def frames_on(n):
        frames_in(n)
        theirs = xall.at[(g + 2) % 4, frame_parts[n]]
        sent["on", n] = move.send(theirs, theirs, here.core())

    def bias_y():
        for copy in bias_z:
            copy.wait_recv()
        sent["by"] = move.send(bb.at[:, y, x, c], bb.at[:, y, x, c], here.across_y())

    def bias_x():
        sent["by"].wait_recv()
        sent["bx"] = move.send(bb.at[:, :, x, c], bb.at[:, :, x, c], here.across_x())

    def bias_core():
        sent["bx"].wait_recv()
        sent["bc"] = move.send(bb.at[:, :, :, c], bb.at[:, :, :, c], here.core())

    def tables(step, carry):
        rows = pl.ds(pl.multiple_of(step * block, block), block)
        segment, relative = frame_segments(lens, step * block, block, LANES)
        lane = lanes_of((block, LANES))
        quarter = HEAD_DIM // 2
        frequency = jnp.exp((lane % quarter).astype(F32) * (-math.log(10000.0) / quarter))
        angle = relative.astype(F32) * frequency
        cosr[rows, :] = jnp.cos(angle)
        sine = jnp.sin(angle)
        sinr[rows, :] = jnp.where(lane % HEAD_DIM < quarter, -sine, sine)
        same = segment == lane
        qaug[rows, :] = jnp.where((lane < SEGS) & jnp.logical_not(same), NEGATIVE, 0.0).astype(BF16)
        keyside = jnp.where((lane < SEGS) & same, 1.0, jnp.where((lane >= 4) & (lane < 7), 1.0, 0.0))
        for pair in range(2):
            ka[pair, rows, LANES:] = keyside.astype(BF16)
            va[pair, rows, LANES:] = jnp.where(lane < 3, 1.0, 0.0).astype(BF16)
        return carry

    def tables_half(n):
        lax.fori_loop(n * rows_all // (2 * block), (n + 1) * rows_all // (2 * block), tables, 0)

    def bias_vectors():
        sent["bc"].wait_recv()
        bmat[...] = bb[...].reshape(16 * 2 * depth * 2, LANES).astype(BF16)

        place = lanes_of((LANES, own_width), 0)
        column = lanes_of((LANES, own_width))
        brow, bcol = lanes_of((64, own_width), 0), lanes_of((64, own_width))
        spread = jnp.where(column % 32 == place, 1.0, 0.0).astype(BF16)
        for j in range(3):
            mine = (brow % 8 == j) & (brow // 8 == bcol // 32)
            held = product(bmat[pl.ds(pl.multiple_of(g * 64, 64), 64), :], spread)
            qbias[j : j + 1, :] = jnp.sum(jnp.where(mine, held, 0.0), axis=0, keepdims=True)

        trow, tcol = lanes_of((16 * 2 * depth * 2, tile), 0), lanes_of((16 * 2 * depth * 2, tile))
        place, column = lanes_of((LANES, tile), 0), lanes_of((LANES, tile))

        def row_vector(step, size, source):
            spread = jnp.where(column % size == place, 1.0, 0.0).astype(BF16)
            chosen = (trow % 8 == source) & (trow // 8 == (tcol + step * tile) // size)
            return jnp.sum(jnp.where(chosen, product(bmat[...], spread), 0.0), axis=0, keepdims=True)

        def narrow_vectors(step, carry):
            columns = pl.ds(pl.multiple_of(step * tile, tile), tile)
            rowbias[0:1, columns] = row_vector(step, 32, 3)
            rowbias[2:3, columns] = row_vector(step, 32, 5)
            return carry

        def wide_vector(step, carry):
            rowbias[1:2, pl.ds(pl.multiple_of(step * tile, tile), tile)] = row_vector(step, 64, 4)
            return carry

        lax.fori_loop(0, MODEL_WIDTH // tile, narrow_vectors, 0)
        lax.fori_loop(0, up.shape[1] // tile, wide_vector, 0)

        place = lanes_of((LANES, half), 0)
        column = lanes_of((LANES, half))
        spread_a = jnp.where(column % 192 == place, 1.0, 0.0).astype(BF16)
        spread_b = jnp.where(column % 192 == place + LANES, 1.0, 0.0).astype(BF16)
        brow, bcol = lanes_of((32, half), 0), lanes_of((32, half))
        inside = brow // 8 == bcol // 192
        for q in range(8):
            rows = bmat[q * 32 : (q + 1) * 32, :]
            terms = jnp.where(inside & (brow % 8 == 6), product(rows, spread_a), 0.0)
            terms = terms + jnp.where(inside & (brow % 8 == 7), product(rows, spread_b), 0.0)
            mods[4:5, q * half : (q + 1) * half] = jnp.sum(terms, axis=0, keepdims=True)

    def mod_done():
        sent["ml"].wait_recv()
        for q in range(8):
            j, side = q // 2, q % 2
            columns = slice(q * half, (q + 1) * half)
            mods[0:4, columns] = modh[side, 4 * j : 4 * j + 4, :] + mods[4:5, columns]
        for kept, first, last in ((mod3, 0, 2 * width), (mod6, 2 * width, 6 * width)):
            high, mid, rest = three_parts(mods[0:4, first:last])
            kept[0:4, :] = high
            kept[4:8, :] = mid
            kept[8:12, :] = rest
            kept[12:16, :] = jnp.zeros((4, last - first), F32)

    def project_rows(source):
        block, step = span, source
        rows = pl.ds(pl.multiple_of(step * block, block), block)
        values = xall[source].astype(F32)
        center = jnp.mean(values, axis=1, keepdims=True)
        centered = values - center
        variance = jnp.mean(centered * centered, axis=1, keepdims=True)
        segment, _ = frame_segments(lens, step * block, block, 16)
        slot = lanes_of((block, 16))
        chosen = jnp.where((slot < 12) & (slot % 4 == segment), 1.0, 0.0).astype(BF16)
        parts = mod3[...].astype(BF16)
        shift = product(chosen, parts[:, :MODEL_WIDTH])
        scale = product(chosen, parts[:, MODEL_WIDTH:])
        result = (centered * lax.rsqrt(variance + EPSILON) * (1.0 + scale) + shift).astype(BF16)
        normed[rows, :] = result
        cosine, sine = cosr[rows, :], sinr[rows, :]
        lane = lanes_of((block, LANES))
        for j in range(3):
            weight = wg[j].reshape(MODEL_WIDTH, own_width)
            full = product(result, weight) + qbias[j : j + 1, :]
            for pair in range(2):
                piece = full[:, pair * LANES : (pair + 1) * LANES]
                if j < 2:
                    piece = piece * cosine + swap_halves(piece, lane) * sine
                if j == 0:
                    qs[pair, rows, :] = (piece.astype(BF16).astype(F32) * HEAD_DIM**-0.5).astype(BF16)
                elif j == 1:
                    ka[pair, rows, :LANES] = piece.astype(BF16)
                else:
                    va[pair, rows, :LANES] = piece.astype(BF16)

    def project_span(n):
        if n == 0:
            local_frames.wait()
            for j in range(3):
                sent["p", j].wait_recv()
        elif n == 1:
            sent["fc"].wait_recv()
        elif n == 2:
            for m in range(2):
                frames_in(m)
        else:
            for m in range(2):
                sent["on", m].wait_recv()
        number = (g, x * 2 + 1 - c, (1 - x) * 2 + c, (1 - x) * 2 + 1 - c)[n]
        project_rows(number)
        if n == 3:
            for source, target in (
                (qs, qs_out), (ka.at[:, :, pl.ds(0, LANES)], ks_out), (va.at[:, :, pl.ds(0, LANES)], vs_out),
                (normed, normed_out), (wg, wg_out), (cosr, cos_out), (sinr, sin_out),
            ):
                stores.append(move.local(source, target))

    def attend(pair, step):
        rows = pl.ds(pl.multiple_of(step * tall, tall), tall)
        query = qs[pair, rows, :]
        lane = lanes_of((tall, LANES))
        outs, sums = [], []
        for head in range(2):
            left = jnp.concatenate([head_only(query, lane, head), qaug[rows, :]], axis=1)
            scores = across(left, ka[pair])
            highest = jnp.max(scores, axis=1, keepdims=True)
            mixed = product(jnp.exp(scores - highest).astype(BF16), va[pair])
            total = mixed[:, LANES : LANES + 1]
            outs.append(mixed[:, :LANES] / total)
            sums.append(highest + jnp.log(total))
        oh[pair, rows, :] = jnp.where(lane < HEAD_DIM, outs[0], outs[1]).astype(BF16)
        before = jnp.zeros((tall, LANES), F32) if pair == 0 else lse[rows, :]
        lse[rows, :] = jnp.where(
            lane == 2 * pair, sums[0], jnp.where(lane == 2 * pair + 1, sums[1], before)
        )

    delivered = []

    def attend_next():
        pair, at = len(delivered) // 4, len(delivered) % 4
        k = (2, 1, 3, 0)[at]
        target = (g + k) % 4
        attend(pair, target)
        columns = pl.ds(pl.multiple_of(g * own_width + pair * LANES, LANES), LANES)
        source = oh.at[pair, pl.ds(pl.multiple_of(target * span, span), span)]
        if k:
            delivered.append(move.send(source, att.at[:, columns], here.row_peer(k)))
        else:
            delivered.append(move.local(source, att.at[:, columns]))
        if len(delivered) == 8:
            stores.append(move.local(oh, oh_out))
            stores.append(move.local(lse, lse_out))

    base = g * span

    def tile_at(step):
        return pl.ds(pl.multiple_of(step * tile, tile), tile)

    def per_frame(part, first, rows, columns):
        segment, _ = frame_segments(lens, base + first, rows, 16)
        slot = lanes_of((rows, 16))
        chosen = jnp.where((slot < 12) & (slot % 4 == segment), 1.0, 0.0).astype(BF16)
        return product(chosen, mod6[:, columns].astype(BF16))

    def members(first, rows):
        position = base + first + lanes_of((16, rows))
        edges = [lens[0, 0], lens[0, 0] + lens[0, 1], lens[0, 0] + lens[0, 1] + lens[0, 2]]
        inside = sum((position >= edge).astype(jnp.int32) for edge in edges)
        return jnp.where(inside == lanes_of((16, rows), 0), 1.0, 0.0).astype(BF16)

    def by_segment(inside, values):
        top = values.astype(BF16)
        return product(inside, top) + product(inside, (values - top.astype(F32)).astype(BF16))

    def shifted(part, step):
        return pl.ds(pl.multiple_of(part * width + step * tile, tile), tile)

    def wo_columns(columns):
        return wo_all[:, :, :, :, :, columns].reshape(width, tile)

    def up_columns(columns):
        return up_all[:, :, :, :, :, columns].reshape(width, tile)

    def down_columns(columns):
        return down_all[:, :, :, :, :, columns].reshape(hidden, tile)

    def project_out():
        for at, copy in enumerate(delivered):
            copy.wait() if at % 4 == 3 else copy.wait_recv()
        arrived(0, 1)

        def body(step, carry):
            columns = tile_at(step)
            branch[:, columns] = product(att[...], wo_columns(columns)) + rowbias[0:1, columns]
            return carry

        lax.fori_loop(0, width // tile, body, 0)

        def norm_forward(step, carry):
            rows = pl.ds(pl.multiple_of(step * block, block), block)
            gate = per_frame(0, step * block, block, slice(0, width))
            values = xall[g, rows, :].astype(F32) + gate * branch[rows, :]
            middle[rows, :] = values
            centered = values - jnp.mean(values, axis=1, keepdims=True)
            hat = centered * lax.rsqrt(jnp.mean(centered * centered, axis=1, keepdims=True) + EPSILON)
            shift = per_frame(1, step * block, block, slice(width, 2 * width))
            scale = per_frame(2, step * block, block, slice(2 * width, 3 * width))
            normed_two[rows, :] = (hat * (1.0 + scale) + shift).astype(BF16)
            return carry

        lax.fori_loop(0, span // block, norm_forward, 0)

    root = math.sqrt(2.0 / math.pi)

    def go_up(side):
        arrived(2 + side, 4 + side)

        def body(step, carry):
            columns = tile_at(step)
            value = product(normed_two[...], up_columns(columns)) + rowbias[1:2, columns]
            square = value * value
            turn = jnp.tanh(root * value * (1.0 + 0.044715 * square))
            part_one = 0.5 * (1.0 + turn)
            active[:, columns] = (value * part_one).astype(BF16)
            slope[:, columns] = part_one + 0.5 * value * (1.0 - turn * turn) * root * (
                1.0 + 3 * 0.044715 * square
            )
            return carry

        lax.fori_loop(side * width // tile, (side + 1) * width // tile, body, 0)

    def go_down():
        arrived(6, 7, 8, 9)
        local_given.wait()

        def body(step, carry):
            columns = tile_at(step)
            value = product(active[...], down_columns(columns)) + rowbias[2:3, columns]
            gate = per_frame(3, 0, span, shifted(3, step))
            back = given[:, columns].astype(F32)
            output[:, columns] = (middle[:, columns] + gate * value).astype(BF16)
            gbt[:, columns] = (gate * back).astype(BF16)
            sums[:, shifted(3, step)] = by_segment(members(0, span), back * value)
            return carry

        lax.fori_loop(0, width // tile, body, 0)

    def back_values():
        def hidden_tile(step, carry):
            rows = tile_at(step)
            weight = down_all[step // 2, step % 2].reshape(tile, width)
            gh[:, rows] = (across(gbt[...], weight) * slope[:, rows]).astype(BF16)
            return carry

        lax.fori_loop(0, hidden // tile, hidden_tile, 0)

        def normed_tile(step, carry):
            gn[:, tile_at(step)] = across(gh[...], up_all[step].reshape(tile, hidden))
            return carry

        lax.fori_loop(0, width // tile, normed_tile, 0)
        sums[:, : 3 * width] = jnp.zeros((16, 3 * width), F32)

        def norm_back(step, carry):
            rows = pl.ds(pl.multiple_of(step * block, block), block)
            grad, values = gn[rows, :], middle[rows, :]
            centered = values - jnp.mean(values, axis=1, keepdims=True)
            scaled = lax.rsqrt(jnp.mean(centered * centered, axis=1, keepdims=True) + EPSILON)
            hat = centered * scaled
            inner = grad * (1.0 + per_frame(2, step * block, block, slice(2 * width, 3 * width)))
            mean_one = jnp.mean(inner, axis=1, keepdims=True)
            mean_two = jnp.mean(inner * hat, axis=1, keepdims=True)
            total = given[rows, :].astype(F32) + scaled * (inner - mean_one - hat * mean_two)
            gmid[rows, :] = total
            gb[rows, :] = (per_frame(0, step * block, block, slice(0, width)) * total).astype(BF16)
            inside = members(step * block, block)
            sums[:, :width] += by_segment(inside, total * branch[rows, :])
            sums[:, width : 2 * width] += by_segment(inside, grad)
            sums[:, 2 * width : 3 * width] += by_segment(inside, grad * hat)
            return carry

        lax.fori_loop(0, span // block, norm_back, 0)
        sent["o"] = []
        mine = pl.ds(pl.multiple_of(g * span, span), span)
        for k in (1, 2, 3, 0):
            target = (g + k) % 4
            columns = tile_at(target)
            ga[:, columns] = across(gb[...], wo_all[target].reshape(tile, width)).astype(BF16)
            for pair in range(2):
                source = ga.at[:, pl.ds(pl.multiple_of(target * own_width + pair * LANES, LANES), LANES)]
                place = do_all.at[pair, mine]
                if k:
                    sent["o"].append(move.send(source, place, here.row_peer(k)))
                else:
                    stores.append(move.local(source, place))

    def back_weights():
        for copy in outgoing:
            copy.wait_send()

        def down_tile(step, carry):
            grad = from_rows(active[:, tile_at(step)], gbt[...]).astype(BF16)
            down_all[step // 2, step % 2] = grad.reshape(down_all.shape[2:])
            return carry

        lax.fori_loop(0, hidden // tile, down_tile, 0)
        stores.append(move.local(down_all, gdown))

        def up_tile(step, carry):
            grad = from_rows(normed_two[:, tile_at(step)], gh[...]).astype(BF16)
            up_all[step] = grad.reshape(up_all.shape[1:])
            return carry

        lax.fori_loop(0, width // tile, up_tile, 0)
        stores.append(move.local(up_all, gup))

        def out_tile(step, carry):
            grad = from_rows(att[:, tile_at(step)], gb[...]).astype(BF16)
            wo_all[step] = grad.reshape(wo_all.shape[1:])
            return carry

        lax.fori_loop(0, width // tile, out_tile, 0)
        stores.append(move.local(wo_all, gwo))
        ones = jnp.ones((16, span), BF16)
        btile[0:24, :] = jnp.zeros((24, LANES), F32)
        start = 24
        for grads, size in ((gb, width), (gh, hidden), (gbt, width)):
            total = product(ones, grads[...])
            for n in range(size // LANES):
                btile[start + n : start + n + 1, :] = total[0:1, n * LANES : (n + 1) * LANES]
            start += size // LANES
        for n in range(4):
            mg[4 * n : 4 * n + 4, :] = sums[0:4, n * width : (n + 1) * width]

    numbered = {
        GATHER_Z: first_leg, GATHER_TWO: second_leg, GATHER_THREE: third_leg, GATHER_CORE: fourth_leg, COLUMNS_Z: columns_z, COLUMNS_Y: columns_y,
        PROJECT: project_span, GO_UP: go_up, FRAMES_X: frames_x, FRAMES_ON: frames_on, TABLES: tables_half,
    }
    named = {
        TIMES_Y: times_across, SHARE: mod_share, MOD_Y: mod_y, MOD_Z: mod_z, MOD_X: mod_x, MOD_LAST: mod_last,
        FRAMES_CORE: frames_core, BIAS_Y: bias_y, BIAS_X: bias_x, BIAS_CORE: bias_core, BIASES: bias_vectors, MODS: mod_done,
        OUT: project_out, GO_DOWN: go_down, BACK: back_values, GRADS: back_weights,
    }
    for code, number in FORWARD_ORDER:
        if code in named:
            named[code]()
        elif code == ATTEND:
            for _ in range(number):
                attend_next()
        else:
            numbered[code](number)
    for copy in stores:
        copy.wait()
    for copy in sent["o"]:
        copy.wait_recv()
    move.finish(but=outgoing)

def forward_call(depth, span, own_rows, down_rows, hidden, args):
    rows_all, own_width, width = 4 * span, MODEL_WIDTH // 4, MODEL_WIDTH
    half = 6 * MODEL_WIDTH // 8
    vmem, anywhere, scalar = (
        pl.BlockSpec(memory_space=pltpu.VMEM),
        pl.BlockSpec(memory_space=pl.ANY),
        pl.BlockSpec(memory_space=pltpu.SMEM),
    )

    def out(shape, dtype):
        return jax.ShapeDtypeStruct(shape, dtype)

    heads, table = (2, rows_all, LANES), (rows_all, LANES)
    columns = (3, depth, 2, 4, own_rows, own_width)
    wo_shape = (depth, 2, 2, 2, own_rows, width)
    up_shape = (depth, 2, 2, 2, own_rows, hidden)
    down_shape = (depth, 2, 2, 2, down_rows, width)
    outs = [
        (out((span, width), BF16), vmem),
        (out((span, width), F32), vmem),
        (out((16, width), F32), vmem),
        (out((56, LANES), F32), vmem),
        (out((8, 6 * width), F32), vmem),
        (out((32 * depth, LANES), BF16), vmem),
        (out(wo_shape, BF16), anywhere),
        (out(up_shape, BF16), anywhere),
        (out(down_shape, BF16), anywhere),
        (out(heads, BF16), anywhere),
        (out(heads, BF16), anywhere),
        (out(heads, BF16), anywhere),
        (out(heads, BF16), anywhere),
        (out(heads, BF16), anywhere),
        (out(table, F32), anywhere),
        (out((rows_all, width), BF16), anywhere),
        (out(columns, BF16), anywhere),
        (out(table, F32), anywhere),
        (out(table, F32), anywhere),
    ]
    low, wide = pltpu.VMEM((span, width), BF16), pltpu.VMEM((span, width), F32)
    scratch = [
        low,
        pltpu.VMEM(heads, BF16),
        pltpu.VMEM(heads, BF16),
        pltpu.VMEM(table, F32),
        pltpu.VMEM((rows_all, width), BF16),
        pltpu.VMEM(columns, BF16),
        pltpu.VMEM(table, F32),
        pltpu.VMEM(table, F32),
        pltpu.VMEM((8, hidden), F32),
        pltpu.VMEM(wo_shape, BF16),
        pltpu.VMEM(up_shape, BF16),
        pltpu.VMEM(down_shape, BF16),
        pltpu.VMEM((depth, 2, 2, 2, 8, LANES), F32),
        pltpu.VMEM((4, span, width), BF16),
        pltpu.VMEM((LANES, 2 * half), BF16),
        pltpu.VMEM((depth, 2, 16, LANES), F32),
        pltpu.VMEM((2, depth, 2, 16, half), BF16),
        pltpu.VMEM((depth, 2, 16, half), BF16),
        pltpu.VMEM((depth, 2, 16, half), BF16),
        pltpu.VMEM((depth, 16, half), BF16),
        pltpu.VMEM((depth, 16, half), BF16),
        pltpu.VMEM((depth - 1, 16, half), BF16),
        pltpu.VMEM((16, half), F32),
        pltpu.VMEM((16, half), F32),
        pltpu.VMEM((2, 16, half), F32),
        pltpu.VMEM((64 * depth, LANES), BF16),
        pltpu.VMEM((16, 2 * width), F32),
        pltpu.VMEM((8, own_width), F32),
        pltpu.VMEM((2, rows_all, 2 * LANES), BF16),
        pltpu.VMEM((2, rows_all, 2 * LANES), BF16),
        pltpu.VMEM(table, BF16),
        low,
        pltpu.VMEM((16, 4 * width), F32),
        wide,
        wide,
        low,
        pltpu.VMEM((span, hidden), BF16),
        pltpu.VMEM((span, hidden), F32),
        low,
        pltpu.VMEM((span, hidden), BF16),
        wide,
        low,
        low,
        pltpu.VMEM((16, 4 * width), F32),
        pltpu.SemaphoreType.DMA((144,)),
        pltpu.SemaphoreType.DMA((144,)),
        pltpu.SemaphoreType.DMA((48,)),
    ]
    return pl.pallas_call(
        partial(forward_kernel, depth),
        out_shape=[shape for shape, _ in outs],
        in_specs=[scalar, scalar, anywhere, anywhere] + [vmem] * 7 + [anywhere] * 7,
        out_specs=[spec for _, spec in outs],
        scratch_shapes=scratch,
        compiler_params=pltpu.CompilerParams(
            collective_id=0, has_side_effects=True, vmem_limit_bytes=62 * 1024 * 1024
        ),
        cost_estimate=pl.CostEstimate(flops=2 * 10**10, bytes_accessed=60 * 10**6, transcendentals=10**7),
    )(*args)


def turn_back(values, cosine, sine, lane):
    return values * cosine - swap_halves(values, lane) * sine


def from_rows(left, right):
    return lax.dot_general(left, right, (((0,), (0,)), ((), ())), preferred_element_type=F32)


X_FIRST = (0, 1, 0, 0, 1, 0, 0, 1, 0, 1)
(
    SUM_ONE, SUM_TWO, SUM_THREE, SUM_LAST, WEIGHTS_Y, WEIGHTS_Z, WEIGHTS_LAST, ATTEND_BACK, ROWS_AWAY,
    ROWS_ACROSS, ROWS_HOME, NORM, EARLY_CORE, EARLY_X, EARLY_Z, EARLY_Y, EARLY_SHARE, EARLY_DONE, LATE_ROWS,
    LATE_DONE, BIAS_START, BIAS_NEXT, BIAS_DONE,
) = range(23)
BACKWARD_ORDER = (
    (SUM_ONE, 0), (SUM_ONE, 4), (SUM_ONE, 3), (SUM_ONE, 2), (SUM_ONE, 5), (EARLY_CORE, 0), (SUM_ONE, 1),
    (SUM_ONE, 6), (SUM_TWO, 0), (ATTEND_BACK, 3), (SUM_TWO, 3), (ATTEND_BACK, 1), (EARLY_X, 0), (SUM_ONE, 9),
    (ATTEND_BACK, 1), (SUM_TWO, 1), (ATTEND_BACK, 1), (SUM_TWO, 4), (SUM_THREE, 3), (SUM_THREE, 0),
    (ATTEND_BACK, 1), (EARLY_Z, 0), (SUM_TWO, 2), (SUM_TWO, 5), (SUM_ONE, 8), (SUM_TWO, 6), (ATTEND_BACK, 1),
    (SUM_ONE, 7), (SUM_THREE, 1), (ATTEND_BACK, 1), (SUM_TWO, 9), (EARLY_Y, 0), (SUM_THREE, 4), (SUM_THREE, 5),
    (ATTEND_BACK, 2), (SUM_THREE, 2), (SUM_THREE, 6), (ATTEND_BACK, 1), (SUM_THREE, 9), (SUM_TWO, 8),
    (SUM_TWO, 7), (ROWS_AWAY, 0), (WEIGHTS_Y, 0), (ROWS_ACROSS, 0), (SUM_THREE, 8), (SUM_THREE, 7),
    (WEIGHTS_Y, 2), (WEIGHTS_Z, 0), (BIAS_START, 0), (SUM_LAST, 3), (WEIGHTS_Y, 1), (ROWS_HOME, 0),
    (SUM_LAST, 5), (BIAS_NEXT, 0), (WEIGHTS_Z, 2), (WEIGHTS_Z, 1), (WEIGHTS_LAST, 0), (SUM_LAST, 8), (NORM, 0),
    (SUM_LAST, 2), (SUM_LAST, 1), (LATE_ROWS, 0), (SUM_LAST, 4), (BIAS_NEXT, 0), (WEIGHTS_LAST, 1),
    (BIAS_NEXT, 0), (EARLY_SHARE, 0), (WEIGHTS_LAST, 2), (LATE_DONE, 0), (SUM_LAST, 6), (SUM_LAST, 0),
    (EARLY_DONE, 0), (SUM_LAST, 7), (SUM_LAST, 9), (BIAS_DONE, 0),
)


def backward_kernel(
    depth,
    lens, do_in, qs_in, ks_in, vs_in, oh_in, lse_in, normed_in, wg_in, cos_in, sin_in, low, mods, frames, gmid,
    mg_in, bias_in, gwo, gup, gdown,
    fgrad, dwq, dwk, dwv, dwo, dup, ddown, dmw, mbias, btile,
    qs, do, oh, lse, normed, wg, cosr, sinr, ka, va, qaug, dk_sum, dv_sum, gr, gw, gwy, gwz, gsum,
    gnp, gnr, gnx, mod3, acc_shift, acc_scale, mg, mgr, mgs, mgx, ev, late, joined, ez, brecv, bz,
    *rest,
):
    send_sems, recv_sems, local_sems = rest[-3:]
    buffers = rest[:-3]
    here = Place(depth)
    z, y, x, c, g = here.z, here.y, here.x, here.c, here.seq
    span = frames.shape[0]
    rows_all = span * 4
    own_width = wg.shape[-1]
    move = Mover(send_sems, recv_sems, local_sems)
    steps_z = range(1, depth)

    shard, width = gwo.shape[4], MODEL_WIDTH
    thin = shard // 2
    pieces = []

    def add_piece(source, target, first_row, columns=None):
        rows = pl.ds(first_row, thin)
        if columns is None:
            pieces.append((source.at[:, :, :, :, rows], target.at[rows]))
        else:
            columns = pl.ds(columns, width)
            pieces.append((source.at[:, :, :, :, rows, columns], target.at[rows, columns]))

    for n in range(4):
        add_piece(gdown, ddown, n * thin)
    for n in range(2):
        add_piece(gup, dup, n * thin, 0)
        add_piece(gup, dup, n * thin, width)
    for n in range(2):
        add_piece(gwo, dwo, n * thin)
    count = len(pieces)
    own, first, second, third, fourth = (
        [buffers[count * n + f] for f in range(count)] for n in range(5)
    )
    legs = {}

    loads = [
        move.local(ks_in, ka.at[:, :, pl.ds(0, LANES)]),
        move.local(vs_in, va.at[:, :, pl.ds(0, LANES)]),
        move.local(qs_in, qs),
        move.local(do_in, do),
        move.local(oh_in, oh),
        move.local(lse_in, lse),
        move.local(cos_in, cosr),
        move.local(sin_in, sinr),
    ]
    here.enter(diagonal=True)
    held = []
    for f in range(count):
        source = pieces[f][0]
        legs[f] = move.send(source.at[:, :, :, 1 - c], first[f], here.core())
        held.append(move.local(source.at[:, :, :, c], own[f]))
    late_loads = [move.local(normed_in, normed), move.local(wg_in, wg)]

    def sum_first(f):
        legs[f].wait_recv()
        held[f].wait()

        def add(step, carry):
            own[f][step] = own[f][step] + first[f][step]
            return carry

        lax.fori_loop(0, depth, add, 0)
        if X_FIRST[f]:
            legs[f] = move.send(own[f].at[:, :, 1 - x], second[f], here.across_x())
        else:
            legs[f] = move.send(own[f].at[:, 1 - y], second[f], here.across_y())

    def sum_second(f):
        legs[f].wait_recv()

        def add(step, carry):
            for other in range(2):
                if X_FIRST[f]:
                    own[f][step, other, x] = own[f][step, other, x] + second[f][step, other]
                else:
                    own[f][step, y, other] = own[f][step, y, other] + second[f][step, other]
            return carry

        lax.fori_loop(0, depth, add, 0)
        if X_FIRST[f]:
            legs[f] = move.send(own[f].at[:, 1 - y, x], third[f], here.across_y())
        else:
            legs[f] = move.send(own[f].at[:, y, 1 - x], third[f], here.across_x())

    def sum_third(f):
        legs[f].wait_recv()

        def add(step, carry):
            own[f][step, y, x] = own[f][step, y, x] + third[f][step]
            return carry

        lax.fori_loop(0, depth, add, 0)
        legs[f] = [
            move.send(own[f].at[here.ahead(k), y, x], fourth[f].at[k - 1], here.along_z(k)) for k in steps_z
        ]

    def sum_last(f):
        total = own[f][z, y, x].astype(F32)
        for k in steps_z:
            legs[f][k - 1].wait_recv()
            total = total + fourth[f][k - 1].astype(F32)
        pieces[f][1][...] = total

    def bias_round(peer, slot):
        return move.send(btile, brecv.at[slot], peer)

    block = 128
    for copy in loads:
        copy.wait()

    def columns_of_segments(step, carry):
        rows = pl.ds(pl.multiple_of(step * block, block), block)
        segment, _ = frame_segments(lens, step * block, block, LANES)
        lane = lanes_of((block, LANES))
        same = segment == lane
        qaug[rows, :] = jnp.where((lane < SEGS) & jnp.logical_not(same), NEGATIVE, 0.0).astype(BF16)
        keyside = jnp.where((lane < SEGS) & same, 1.0, jnp.where((lane >= 4) & (lane < 7), 1.0, 0.0))
        for pair in range(2):
            ka[pair, rows, LANES:] = keyside.astype(BF16)
            va[pair, rows, LANES:] = jnp.where(lane < 3, 1.0, 0.0).astype(BF16)
        return carry

    lax.fori_loop(0, rows_all // block, columns_of_segments, 0)

    tall = 256
    steps = rows_all // tall

    def back_block(pair, step):
        rows = pl.ds(pl.multiple_of(step * tall, tall), tall)
        lane = lanes_of((tall, LANES))
        query, given = qs[pair, rows, :], do[pair, rows, :]
        overlap = given.astype(F32) * oh[pair, rows, :].astype(F32)
        mask_columns = qaug[rows, :].astype(F32)
        sums = lse[rows, :]
        grads_q, add_k, add_v = [], 0.0, 0.0
        for head in range(2):
            delta = jnp.sum(jnp.where((lane >= HEAD_DIM) == bool(head), overlap, 0.0), axis=1, keepdims=True)
            logsum = jnp.sum(jnp.where(lane == 2 * pair + head, sums, 0.0), axis=1, keepdims=True)
            a, b, d = three_parts(logsum)
            side = jnp.where(lane == 4, -a, jnp.where(lane == 5, -b, jnp.where(lane == 6, -d, mask_columns)))
            query_head = head_only(query, lane, head)
            left = jnp.concatenate([query_head, side.astype(BF16)], axis=1)
            a, b, d = three_parts(delta)
            side = jnp.where(lane == 0, -a, jnp.where(lane == 1, -b, jnp.where(lane == 2, -d, 0.0)))
            given_head = head_only(given, lane, head)
            right = jnp.concatenate([given_head, side.astype(BF16)], axis=1)
            weights = jnp.exp(across(ka[pair], left))
            grads = (weights * across(va[pair], right)).astype(BF16)
            add_v = add_v + product(weights.astype(BF16), given_head)
            add_k = add_k + product(grads, query_head)
            grads_q.append(from_rows(grads, ka[pair, :, :LANES]))
        dv_sum[...] += add_v
        dk_sum[...] += add_k
        grad_query = jnp.where(lane < HEAD_DIM, grads_q[0], grads_q[1]) * HEAD_DIM**-0.5
        gr[0, rows, pair * LANES : (pair + 1) * LANES] = turn_back(
            grad_query, cosr[rows, :], sinr[rows, :], lane
        ).astype(BF16)

    def back_some(pair, start, stop):
        lax.fori_loop(start, stop, lambda step, carry: (back_block(pair, step), carry)[1], 0)

    def settle_pair(pair):
        def body(step, carry):
            rows = pl.ds(pl.multiple_of(step * block, block), block)
            lane = lanes_of((block, LANES))
            part = slice(pair * LANES, (pair + 1) * LANES)
            gr[1, rows, part] = turn_back(dk_sum[rows, :], cosr[rows, :], sinr[rows, :], lane).astype(BF16)
            gr[2, rows, part] = dv_sum[rows, :].astype(BF16)
            return carry

        lax.fori_loop(0, rows_all // block, body, 0)

    def clear():
        dk_sum[...] = jnp.zeros_like(dk_sum)
        dv_sum[...] = jnp.zeros_like(dv_sum)

    def back_rows(target):
        def body(step, carry):
            rows = pl.ds(pl.multiple_of(target * span + step * block, block), block)
            total = 0.0
            for j in range(3):
                total = total + across(gr[j, rows, :], wg[j].reshape(MODEL_WIDTH, own_width))
            gnp[target, pl.ds(pl.multiple_of(step * block, block), block), :] = total.astype(BF16)
            return carry

        lax.fori_loop(0, span // block, body, 0)

    away_other, away_same = (1 - x) * 2 + (1 - c), (1 - x) * 2 + c
    home_other = x * 2 + (1 - c)
    gn = {}

    def rows_away():
        for copy in late_loads:
            copy.wait()
        back_rows(away_other)
        gn["core"] = move.send(gnp.at[away_other], gnr.at[0], here.core())

    def rows_across():
        back_rows(away_same)
        gn["core"].wait_recv()

        def add_rows(step, carry):
            rows = pl.ds(pl.multiple_of(step * block, block), block)
            gnp[away_same, rows, :] = gnp[away_same, rows, :] + gnr[0, rows, :]
            return carry

        lax.fori_loop(0, span // block, add_rows, 0)
        gn["x"] = move.send(gnp.at[away_same], gnx, here.across_x())

    def rows_home():
        back_rows(home_other)
        gn["home"] = move.send(gnp.at[home_other], gnr.at[1], here.core())
        back_rows(g)

    tile = 256

    def weight_rows(j):
        def body(step, carry):
            columns = pl.ds(pl.multiple_of(step * tile, tile), tile)
            result = from_rows(normed[:, columns], gr[j]).astype(BF16)
            per = 2 * 4 * shard // tile
            lead = result.reshape(tile // (4 * shard), 4, shard, own_width)
            for n in range(tile // (4 * shard)):
                gw[j, step // per, (step % per) * (tile // (4 * shard)) + n] = lead[n]
            return carry

        lax.fori_loop(0, MODEL_WIDTH // tile, body, 0)

    gw_y, gw_z = {}, {}

    def weights_y(j):
        weight_rows(j)
        gw_y[j] = move.send(gw.at[j, :, 1 - y], gwy.at[j], here.across_y())

    def weights_z(j):
        gw_y[j].wait_recv()

        def add(step, carry):
            gw[j, step, y] = gw[j, step, y] + gwy[j, step]
            return carry

        lax.fori_loop(0, depth, add, 0)
        gw_z[j] = [move.send(gw.at[j, here.ahead(k), y], gwz.at[j, k - 1], here.along_z(k)) for k in steps_z]

    outs = (dwq, dwk, dwv)
    final = []
    final_locals = []

    def weights_last(j):
        total = gw[j, z, y].astype(F32)
        for k in steps_z:
            gw_z[j][k - 1].wait_recv()
            total = total + gwz[j, k - 1].astype(F32)
        gsum[j] = total
        columns = pl.ds(pl.multiple_of(g * own_width, LANES), own_width)
        final_locals.append(move.local(gsum.at[j, g], outs[j].at[:, columns]))
        for k in (1, 2, 3):
            final.append(move.send(gsum.at[j, (g + k) % 4], outs[j].at[:, columns], here.row_peer(k)))

    bias_legs = []

    def bias_start():
        ones = jnp.ones((16, rows_all), BF16)
        btile[...] = bias_in[...]
        for j in range(3):
            sums = product(ones, gr[j])
            for half in range(2):
                btile[pl.ds(8 * j + g * 2 + half, 1), :] = sums[0:1, half * LANES : (half + 1) * LANES]
        bias_legs.append(move.send(btile, brecv.at[0], here.core()))

    def bias_next():
        done = len(bias_legs)
        bias_legs[-1].wait()
        btile[...] = btile[...] + brecv[done - 1]
        if done < 3:
            peer = (here.across_x, here.across_y)[done - 1]()
            bias_legs.append(move.send(btile, brecv.at[done], peer))
        else:
            bias_legs.extend([move.send(btile, bz.at[k - 1], here.along_z(k)) for k in steps_z])

    def bias_last():
        for copy in bias_legs[3:]:
            copy.wait()
        total = btile[...]
        for k in steps_z:
            total = total + bz[k - 1]
        btile[...] = total

    high, middle, rest_part = three_parts(mods[0:4, MODEL_WIDTH : 2 * MODEL_WIDTH])
    mod3[0:4, :] = high
    mod3[4:8, :] = middle
    mod3[8:12, :] = rest_part
    mod3[12:16, :] = jnp.zeros((4, MODEL_WIDTH), F32)
    acc_shift[...] = jnp.zeros_like(acc_shift)
    acc_scale[...] = jnp.zeros_like(acc_scale)
    def two_parts(values):
        top = values.astype(BF16)
        return top, (values - top.astype(F32)).astype(BF16)

    def norm_rows(step, carry):
        rows = pl.ds(pl.multiple_of(step * block, block), block)
        grad = gnp[g, rows, :].astype(F32) + gnr[1, rows, :].astype(F32) + gnx[rows, :].astype(F32)
        values = frames[rows, :].astype(F32)
        center = jnp.mean(values, axis=1, keepdims=True)
        centered = values - center
        scaled = lax.rsqrt(jnp.mean(centered * centered, axis=1, keepdims=True) + EPSILON)
        hat = centered * scaled
        base = g * span + step * block
        segment, _ = frame_segments(lens, base, block, 16)
        slot = lanes_of((block, 16))
        chosen = jnp.where((slot < 12) & (slot % 4 == segment), 1.0, 0.0).astype(BF16)
        inner = grad * (1.0 + product(chosen, mod3[...].astype(BF16)))
        mean_one = jnp.mean(inner, axis=1, keepdims=True)
        mean_two = jnp.mean(inner * hat, axis=1, keepdims=True)
        fgrad[rows, :] = (gmid[rows, :] + scaled * (inner - mean_one - hat * mean_two)).astype(BF16)
        position = base + lanes_of((16, block))
        begin = [lens[0, 0], lens[0, 0] + lens[0, 1], lens[0, 0] + lens[0, 1] + lens[0, 2]]
        inside = sum((position >= edge).astype(jnp.int32) for edge in begin)
        members = jnp.where(inside == lanes_of((16, block), 0), 1.0, 0.0).astype(BF16)
        for values, target in ((grad, acc_shift), (grad * hat, acc_scale)):
            top, bottom = two_parts(values)
            target[...] += product(members, top) + product(members, bottom)
        return carry

    fourth_part = MODEL_WIDTH // 2
    mod_legs = {}

    def mods_core():
        for side in range(2):
            mg[side] = mg_in[:, side * fourth_part : (side + 1) * fourth_part]
        mod_legs["core"] = move.send(mg.at[1 - c], mgr, here.core())

    def mods_x():
        mod_legs["core"].wait_recv()
        mgs[...] = mg[c] + mgr[...]
        mod_legs["x"] = move.send(mgs, mgx, here.across_x())

    def mods_z():
        mod_legs["x"].wait_recv()
        ev[z, y, c] = (mgs[...] + mgx[...]).astype(BF16)
        mod_legs["z"] = [move.send(ev.at[z, y, c], ev.at[z, y, c], here.along_z(k)) for k in steps_z]

    def mods_y():
        for copy in mod_legs["z"]:
            copy.wait_recv()
        mod_legs["y"] = move.send(ev.at[:, y, c], ev.at[:, y, c], here.across_y())

    def mods_share():
        mod_legs["y"].wait_recv()
        mod_legs["last"] = move.send(ev.at[:, :, c], ev.at[:, :, c], here.core())

    every_row = 32 * depth
    picks = jnp.where(
        lanes_of((16, every_row), 0) == (lanes_of((16, every_row)) % 16) // 4, 1.0, 0.0
    ).astype(BF16)

    def place_columns(every, start, stride):
        size = every.shape[1]
        result = from_rows(low[...], every)
        summed = product(picks, every)
        for strip in range(4):
            columns = slice(start + strip * stride, start + strip * stride + size)
            dmw[:, columns] = result[32 * strip : 32 * (strip + 1), :]
            mbias[0:1, columns] = summed[strip : strip + 1, :]

    def mods_early():
        mod_legs["last"].wait_recv()
        for side in range(2):
            every = ev[:, :, side].reshape(every_row, fourth_part)
            place_columns(every, 2 * MODEL_WIDTH + side * fourth_part, MODEL_WIDTH)

    def norm_part():
        gn["home"].wait_recv()
        gn["x"].wait_recv()
        lax.fori_loop(0, span // block, norm_rows, 0)
        late[0, 0:4, :] = acc_shift[0:4, :]
        late[0, 4:8, :] = acc_scale[0:4, :]
        mod_legs["row"] = [move.send(late.at[0], late.at[k], here.row_peer(k)) for k in (1, 2, 3)]

    def mods_rows():
        for copy in mod_legs["row"]:
            copy.wait_recv()
        total = (late[0] + late[1]) + (late[2] + late[3])
        joined[0:4, :] = total[0:4, :fourth_part]
        joined[4:8, :] = total[0:4, fourth_part:]
        joined[8:12, :] = total[4:8, :fourth_part]
        joined[12:16, :] = total[4:8, fourth_part:]
        ez[z, y] = joined[...].astype(BF16)
        peers = [here.along_z(k) for k in steps_z] + [here.across_y()]
        peers += [here.at(here.ahead(k), 1 - y, x, c) for k in steps_z]
        mod_legs["all"] = [move.send(ez.at[z, y], ez.at[z, y], peer) for peer in peers]

    def mods_late():
        for copy in mod_legs["all"]:
            copy.wait_recv()
        place_columns(ez[...].reshape(every_row, fourth_part), 0, fourth_part)

    stages = {
        SUM_ONE: sum_first, SUM_TWO: sum_second, SUM_THREE: sum_third, SUM_LAST: sum_last,
        WEIGHTS_Y: weights_y, WEIGHTS_Z: weights_z, WEIGHTS_LAST: weights_last,
    }
    others = {
        ROWS_AWAY: rows_away, ROWS_ACROSS: rows_across, ROWS_HOME: rows_home, NORM: norm_part,
        EARLY_CORE: mods_core, EARLY_X: mods_x, EARLY_Z: mods_z, EARLY_Y: mods_y, EARLY_SHARE: mods_share, EARLY_DONE: mods_early,
        LATE_ROWS: mods_rows, LATE_DONE: mods_late, BIAS_START: bias_start, BIAS_NEXT: bias_next, BIAS_DONE: bias_last,
    }
    clear()
    done = 0
    for code, number in BACKWARD_ORDER:
        if code == ATTEND_BACK:
            ahead = number
            while ahead:
                pair, at = done // steps, done % steps
                now = min(ahead, steps - at)
                back_some(pair, at, at + now)
                done, ahead = done + now, ahead - now
                if done % steps == 0:
                    settle_pair(pair)
                    if pair == 0:
                        clear()
        elif code in others:
            others[code]()
        else:
            stages[code](number)
    for copy in final_locals:
        copy.wait()
    for copy in final:
        copy.wait_recv()
    move.finish(but=bias_legs)


def backward_call(depth, span, own_rows, down_rows, hidden, args):
    rows_all, own_width = 4 * span, MODEL_WIDTH // 4
    half = MODEL_WIDTH // 2
    vmem, anywhere, scalar = (
        pl.BlockSpec(memory_space=pltpu.VMEM),
        pl.BlockSpec(memory_space=pl.ANY),
        pl.BlockSpec(memory_space=pltpu.SMEM),
    )

    def out(shape, dtype):
        return jax.ShapeDtypeStruct(shape, dtype)

    outs = [
        (out((span, MODEL_WIDTH), BF16), vmem),
        (out((own_rows, MODEL_WIDTH), F32), anywhere),
        (out((own_rows, MODEL_WIDTH), F32), anywhere),
        (out((own_rows, MODEL_WIDTH), F32), anywhere),
        (out((own_rows, MODEL_WIDTH), F32), vmem),
        (out((own_rows, hidden), F32), vmem),
        (out((down_rows, MODEL_WIDTH), F32), vmem),
        (out((own_rows, 6 * MODEL_WIDTH), F32), vmem),
        (out((8, 6 * MODEL_WIDTH), F32), vmem),
        (out((56, LANES), F32), vmem),
    ]
    pair_rows = pltpu.VMEM((2, rows_all, LANES), BF16)
    wide_rows = pltpu.VMEM((2, rows_all, 2 * LANES), BF16)
    table = pltpu.VMEM((rows_all, LANES), F32)
    scratch = [
        pair_rows, pair_rows, pair_rows, table,
        pltpu.VMEM((rows_all, MODEL_WIDTH), BF16),
        pltpu.VMEM((3, depth, 2, 4, own_rows, own_width), BF16),
        table, table, wide_rows, wide_rows,
        pltpu.VMEM((rows_all, LANES), BF16),
        table, table,
        pltpu.VMEM((3, rows_all, own_width), BF16),
        pltpu.VMEM((3, depth, 2, 4, own_rows, own_width), BF16),
        pltpu.VMEM((3, depth, 4, own_rows, own_width), BF16),
        pltpu.VMEM((3, depth - 1, 4, own_rows, own_width), BF16),
        pltpu.VMEM((3, 4, own_rows, own_width), F32),
        pltpu.VMEM((4, span, MODEL_WIDTH), BF16),
        pltpu.VMEM((2, span, MODEL_WIDTH), BF16),
        pltpu.VMEM((span, MODEL_WIDTH), BF16),
        pltpu.VMEM((16, MODEL_WIDTH), F32),
        pltpu.VMEM((16, MODEL_WIDTH), F32),
        pltpu.VMEM((16, MODEL_WIDTH), F32),
        pltpu.VMEM((2, 16, half), F32),
        pltpu.VMEM((16, half), F32),
        pltpu.VMEM((16, half), F32),
        pltpu.VMEM((16, half), F32),
        pltpu.VMEM((depth, 2, 2, 16, half), BF16),
        pltpu.VMEM((4, 8, MODEL_WIDTH), F32),
        pltpu.VMEM((16, half), F32),
        pltpu.VMEM((depth, 2, 16, half), BF16),
        pltpu.VMEM((3, 56, LANES), F32),
        pltpu.VMEM((depth - 1, 56, LANES), F32),
    ]
    piece = (own_rows // 2, MODEL_WIDTH)
    for lead in ((depth, 2, 2), (depth, 2, 2), (depth, 2), (depth,), (depth - 1,)):
        scratch += [pltpu.VMEM(lead + piece, BF16)] * 10
    scratch += [pltpu.SemaphoreType.DMA((128,)), pltpu.SemaphoreType.DMA((128,)), pltpu.SemaphoreType.DMA((32,))]
    return pl.pallas_call(
        partial(backward_kernel, depth),
        out_shape=[shape for shape, _ in outs],
        in_specs=[scalar] + [anywhere] * 10 + [vmem] * 6 + [anywhere] * 3,
        out_specs=[spec for _, spec in outs],
        scratch_shapes=scratch,
        compiler_params=pltpu.CompilerParams(
            collective_id=1, has_side_effects=True, vmem_limit_bytes=62 * 1024 * 1024
        ),
        cost_estimate=pl.CostEstimate(flops=2 * 10**10, bytes_accessed=40 * 10**6, transcendentals=10**7),
    )(*args)


def modulated_norm(values, shift_part, scale_part):
    center = jnp.mean(values, axis=-1, keepdims=True)
    centered = values - center
    variance = jnp.mean(centered * centered, axis=-1, keepdims=True)
    return centered * lax.rsqrt(variance + EPSILON) * (1.0 + scale_part) + shift_part


def rotate(values, cosines, sines_table):
    shaped = values.reshape(values.shape[:-1] + (values.shape[-1] // HEAD_DIM, HEAD_DIM))
    first_half = shaped[..., : HEAD_DIM // 2]
    second_half = shaped[..., HEAD_DIM // 2 :]
    cosine = cosines[..., None, :]
    sine_part = sines_table[..., None, :]
    turned = jnp.concatenate(
        [
            first_half * cosine - second_half * sine_part,
            second_half * cosine + first_half * sine_part,
        ],
        axis=-1,
    )
    return turned.reshape(values.shape)


def gelu_tanh(values):
    return jax.nn.gelu(values, approximate=True)


def time_features(time_index):
    halfway = MODEL_WIDTH // 2
    frequency = jnp.exp(jnp.arange(halfway, dtype=jnp.float32) * (-math.log(10000.0) / halfway))
    angles = time_index.astype(jnp.float32)[..., None] * frequency
    return jnp.concatenate([jnp.sin(angles), jnp.cos(angles)], axis=-1)


def segment_starts(segment_lengths):
    return jnp.cumsum(segment_lengths, axis=1) - segment_lengths


def segment_numbers(segment_lengths, frame_positions):
    starts = segment_starts(segment_lengths)
    inside = (frame_positions[None, :, None] >= starts[:, None, :]).astype(jnp.int32)
    return jnp.sum(inside, axis=2) - 1


def segment_layout(segment_lengths, frame_positions):
    starts = segment_starts(segment_lengths)
    segment = segment_numbers(segment_lengths, frame_positions)
    onehot = (segment[..., None] == jnp.arange(SEGS, dtype=jnp.int32)).astype(jnp.float32)
    offset = jnp.sum(onehot * starts[:, None, :].astype(jnp.float32), axis=2)
    relative = frame_positions[None, :].astype(jnp.float32) - offset
    return (onehot, relative)


def rope_tables(relative):
    halfway = HEAD_DIM // 2
    frequency = jnp.exp(jnp.arange(halfway, dtype=jnp.float32) * (-math.log(10000.0) / halfway))
    angles = relative[..., None] * frequency
    return (jnp.cos(angles), jnp.sin(angles))


def project(values, matrix, offset):
    return jnp.einsum(
        "rld,de->rle", values, matrix, preferred_element_type=jnp.float32
    ) + offset.astype(jnp.float32)


def project_back(gradient, matrix):
    return jnp.einsum("rle,de->rld", gradient, matrix, preferred_element_type=jnp.float32)


def weight_gradient(values, gradient):
    return jnp.einsum("rld,rle->de", values, gradient, preferred_element_type=jnp.float32)


def bias_gradient(gradient):
    return jnp.sum(gradient.astype(jnp.float32), axis=(0, 1))


def lift_up(member):
    return member.reshape((1, 1) + member.shape)


def settle(member):
    return member.reshape((-1,) + member.shape[3:])


def spread(member, wide_count, narrow_count):
    return member.reshape((wide_count, narrow_count, -1) + member.shape[1:])


def unpack(member):
    return member.reshape(member.shape[2:])


def on_device(
    frames,
    output_gradient,
    segment_lengths,
    time_index,
    query_weight,
    query_bias,
    key_weight,
    key_bias,
    value_weight,
    value_bias,
    output_projection,
    output_bias,
    up_weight,
    up_bias,
    down_weight,
    down_bias,
    modulation_weight,
    modulation_bias,
):
    narrow_count = lax.axis_size("seq")
    wide_count = lax.axis_size("dp")
    seq_index = lax.axis_index("seq")
    row_count, span_frames, width_total = frames.shape
    row_length = span_frames * narrow_count
    block_rows = min(512, row_length)
    block_count = row_length // block_rows
    local_weights = (
        query_weight,
        query_bias,
        key_weight,
        key_bias,
        value_weight,
        value_bias,
        output_projection,
        output_bias,
        up_weight,
        up_bias,
        down_weight,
        down_bias,
        modulation_bias,
    )
    lifted = [lift_up(member) for member in local_weights]
    halfway_set = (
        lax.all_gather(lifted[0], "dp", axis=0, tiled=True),
        lax.all_gather(lifted[1], "dp", axis=0, tiled=True),
        lax.all_gather(lifted[2], "dp", axis=0, tiled=True),
        lax.all_gather(lifted[3], "dp", axis=0, tiled=True),
        lax.all_gather(lifted[4], "dp", axis=0, tiled=True),
        lax.all_gather(lifted[5], "dp", axis=0, tiled=True),
        lax.all_gather(lifted[6], "dp", axis=0, tiled=True),
        lax.all_gather(lifted[7], "dp", axis=0, tiled=True),
        lax.all_gather(lifted[8], "dp", axis=0, tiled=True),
        lax.all_gather(lifted[9], "dp", axis=0, tiled=True),
        lax.all_gather(lifted[10], "dp", axis=0, tiled=True),
        lax.all_gather(lifted[11], "dp", axis=0, tiled=True),
        lax.all_gather(lifted[12], "dp", axis=0, tiled=True),
    )
    complete_set = (
        lax.all_gather(halfway_set[0], "seq", axis=1, tiled=True),
        lax.all_gather(halfway_set[1], "seq", axis=1, tiled=True),
        lax.all_gather(halfway_set[2], "seq", axis=1, tiled=True),
        lax.all_gather(halfway_set[3], "seq", axis=1, tiled=True),
        lax.all_gather(halfway_set[4], "seq", axis=1, tiled=True),
        lax.all_gather(halfway_set[5], "seq", axis=1, tiled=True),
        lax.all_gather(halfway_set[6], "seq", axis=1, tiled=True),
        lax.all_gather(halfway_set[7], "seq", axis=1, tiled=True),
        lax.all_gather(halfway_set[8], "seq", axis=1, tiled=True),
        lax.all_gather(halfway_set[9], "seq", axis=1, tiled=True),
        lax.all_gather(halfway_set[10], "seq", axis=1, tiled=True),
        lax.all_gather(halfway_set[11], "seq", axis=1, tiled=True),
        lax.all_gather(halfway_set[12], "seq", axis=1, tiled=True),
    )
    gathered = [settle(member) for member in complete_set]
    (
        full_query,
        full_query_bias,
        full_key,
        full_key_bias,
        full_value,
        full_value_bias,
        full_output,
        full_output_bias,
        full_up,
        full_up_bias,
        full_down,
        full_down_bias,
        full_modulation_bias,
    ) = gathered
    local_positions = seq_index * span_frames + jnp.arange(span_frames, dtype=jnp.int32)
    local_onehot, local_relative = segment_layout(segment_lengths, local_positions)
    row_segment = segment_numbers(segment_lengths, jnp.arange(row_length, dtype=jnp.int32))
    cosines, sines_table = rope_tables(local_relative)
    turning = partial(rotate, cosines=cosines, sines_table=sines_table)
    owned_rows = modulation_weight.shape[0]
    owned_start = (lax.axis_index("dp") * narrow_count + seq_index) * owned_rows
    every_time = lax.all_gather(time_index, "dp", axis=0, tiled=True)
    every_low = jax.nn.silu(time_features(every_time)).astype(jnp.bfloat16)
    owned_low = lax.dynamic_slice_in_dim(every_low, owned_start, owned_rows, 2)
    partial_modulation = jnp.einsum(
        "rsd,dc->rsc", owned_low, modulation_weight, preferred_element_type=jnp.float32
    )
    row_share = lax.psum_scatter(partial_modulation, "dp", scatter_dimension=0, tiled=True)
    modulation = lax.psum(row_share.astype(jnp.bfloat16), "seq").astype(
        jnp.float32
    ) + full_modulation_bias.astype(jnp.float32)
    per_frame = jnp.einsum("rls,rsc->rlc", local_onehot, modulation, precision=HIGHEST)
    shift_one, scale_one, gate_one, shift_two, scale_two, gate_two = jnp.split(
        per_frame, 6, axis=-1
    )
    inputs = frames.astype(jnp.float32)
    normed, norm_back = jax.vjp(modulated_norm, inputs, shift_one, scale_one)
    normed_low = normed.astype(jnp.bfloat16)
    query_pre = project(normed_low, full_query, full_query_bias)
    key_pre = project(normed_low, full_key, full_key_bias)
    value_low = project(normed_low, full_value, full_value_bias).astype(jnp.bfloat16)
    query_turned, query_back = jax.vjp(turning, query_pre)
    key_turned, key_back = jax.vjp(turning, key_pre)
    query_heads, key_heads, value_heads = (
        lax.all_to_all(
            query_turned.astype(jnp.bfloat16), "seq", split_axis=2, concat_axis=1, tiled=True
        ),
        lax.all_to_all(
            key_turned.astype(jnp.bfloat16), "seq", split_axis=2, concat_axis=1, tiled=True
        ),
        lax.all_to_all(value_low, "seq", split_axis=2, concat_axis=1, tiled=True),
    )
    local_heads = query_heads.shape[2] // HEAD_DIM
    head_shape = (row_count, row_length, local_heads, HEAD_DIM)
    queries = query_heads.reshape(head_shape)
    keys_all = key_heads.reshape(head_shape)
    values_all = value_heads.reshape(head_shape)
    scaling = HEAD_DIM ** (-0.5)
    positions_all = jnp.arange(row_count * block_count, dtype=jnp.int32)

    def fetch_block(position):
        row_index = position // block_count
        start_row = position % block_count * block_rows
        key_row = lax.dynamic_index_in_dim(keys_all, row_index, 0, keepdims=False)
        value_row = lax.dynamic_index_in_dim(values_all, row_index, 0, keepdims=False)
        segment_row = lax.dynamic_index_in_dim(row_segment, row_index, 0, keepdims=False)
        query_block = lax.dynamic_slice_in_dim(
            lax.dynamic_index_in_dim(queries, row_index, 0, keepdims=False),
            start_row,
            block_rows,
            0,
        )
        segment_block = lax.dynamic_slice_in_dim(segment_row, start_row, block_rows, 0)
        scores = (
            jnp.einsum("bhd,khd->hbk", query_block, key_row, preferred_element_type=jnp.float32)
            * scaling
        )
        scores = jnp.where((segment_block[:, None] == segment_row[None, :])[None], scores, NEGATIVE)
        return (row_index, start_row, query_block, key_row, value_row, scores)

    def forward_block(position):
        row_index, start_row, query_block, key_row, value_row, scores = fetch_block(position)
        highest = jnp.max(scores, axis=2, keepdims=True)
        weights = jnp.exp(scores - highest)
        totals = jnp.sum(weights, axis=2, keepdims=True)
        probabilities = (weights / totals).astype(jnp.bfloat16)
        mixed_block = jnp.einsum(
            "hbk,khd->bhd", probabilities, value_row, preferred_element_type=jnp.float32
        )
        return (
            mixed_block.astype(jnp.bfloat16).reshape(block_rows, -1),
            (highest + jnp.log(totals))[..., 0],
        )

    mixed_blocks, logsums = lax.map(forward_block, positions_all)
    attention_heads = mixed_blocks.reshape(row_count, row_length, -1)
    attention_frames = lax.all_to_all(
        attention_heads, "seq", split_axis=1, concat_axis=2, tiled=True
    )
    branch = project(attention_frames, full_output, full_output_bias)
    middle = inputs + gate_one * branch
    normed_two, norm_two_back = jax.vjp(modulated_norm, middle, shift_two, scale_two)
    normed_two_low = normed_two.astype(jnp.bfloat16)
    hidden = project(normed_two_low, full_up, full_up_bias)
    activated, gelu_back = jax.vjp(gelu_tanh, hidden)
    activated_low = activated.astype(jnp.bfloat16)
    branch_two = project(activated_low, full_down, full_down_bias)
    layer_output = (middle + gate_two * branch_two).astype(jnp.bfloat16)
    cotangent = output_gradient.astype(jnp.float32)
    grad_branch_two = (gate_two * cotangent).astype(jnp.bfloat16)
    grad_gate_two = cotangent * branch_two
    grad_activated = project_back(grad_branch_two, full_down)
    grad_hidden = gelu_back(grad_activated)[0].astype(jnp.bfloat16)
    grad_normed_two = project_back(grad_hidden, full_up)
    grad_middle_part, grad_shift_two, grad_scale_two = norm_two_back(grad_normed_two)
    grad_middle = cotangent + grad_middle_part
    grad_gate_one = grad_middle * branch
    grad_branch = (gate_one * grad_middle).astype(jnp.bfloat16)
    grad_attention = project_back(grad_branch, full_output).astype(jnp.bfloat16)
    grad_heads = lax.all_to_all(grad_attention, "seq", split_axis=2, concat_axis=1, tiled=True)
    grad_outputs = grad_heads.reshape(head_shape)

    def backward_block(running, pair_inputs):
        grad_keys, grad_values = running
        position, logsum = pair_inputs
        row_index, start_row, query_block, key_row, value_row, scores = fetch_block(position)
        grad_block = lax.dynamic_slice_in_dim(
            lax.dynamic_index_in_dim(grad_outputs, row_index, 0, keepdims=False),
            start_row,
            block_rows,
            0,
        )
        probabilities = jnp.exp(scores - logsum[..., None])
        grad_probabilities = jnp.einsum(
            "bhd,khd->hbk", grad_block, value_row, preferred_element_type=jnp.float32
        )
        delta_sum = jnp.sum(probabilities * grad_probabilities, axis=2, keepdims=True)
        grad_scores = (probabilities * (grad_probabilities - delta_sum)).astype(jnp.bfloat16)
        grad_query_block = (
            jnp.einsum("hbk,khd->bhd", grad_scores, key_row, preferred_element_type=jnp.float32)
            * scaling
        )
        key_part = (
            jnp.einsum("hbk,bhd->khd", grad_scores, query_block, preferred_element_type=jnp.float32)
            * scaling
        )
        value_part = jnp.einsum(
            "hbk,bhd->khd",
            probabilities.astype(jnp.bfloat16),
            grad_block,
            preferred_element_type=jnp.float32,
        )
        grad_keys = lax.dynamic_update_index_in_dim(
            grad_keys,
            lax.dynamic_index_in_dim(grad_keys, row_index, 0, keepdims=False) + key_part,
            row_index,
            0,
        )
        grad_values = lax.dynamic_update_index_in_dim(
            grad_values,
            lax.dynamic_index_in_dim(grad_values, row_index, 0, keepdims=False) + value_part,
            row_index,
            0,
        )
        return (
            (grad_keys, grad_values),
            grad_query_block.astype(jnp.bfloat16).reshape(block_rows, -1),
        )

    zero_heads = jnp.zeros(head_shape, jnp.float32)
    (grad_keys_all, grad_values_all), grad_query_blocks = lax.scan(
        backward_block, (zero_heads, zero_heads), (positions_all, logsums)
    )
    flat_shape = (row_count, row_length, -1)
    grad_query_frames, grad_key_frames, grad_value_frames = (
        lax.all_to_all(
            grad_query_blocks.reshape(flat_shape), "seq", split_axis=1, concat_axis=2, tiled=True
        ),
        lax.all_to_all(
            grad_keys_all.reshape(flat_shape).astype(jnp.bfloat16),
            "seq",
            split_axis=1,
            concat_axis=2,
            tiled=True,
        ),
        lax.all_to_all(
            grad_values_all.reshape(flat_shape).astype(jnp.bfloat16),
            "seq",
            split_axis=1,
            concat_axis=2,
            tiled=True,
        ),
    )
    grad_query_pre = query_back(grad_query_frames.astype(jnp.float32))[0].astype(jnp.bfloat16)
    grad_key_pre = key_back(grad_key_frames.astype(jnp.float32))[0].astype(jnp.bfloat16)
    grad_normed = (
        project_back(grad_query_pre, full_query)
        + project_back(grad_key_pre, full_key)
        + project_back(grad_value_frames, full_value)
    )
    grad_inputs_part, grad_shift_one, grad_scale_one = norm_back(grad_normed)
    frames_grad = (grad_middle + grad_inputs_part).astype(jnp.bfloat16)
    grad_per_frame = jnp.concatenate(
        [
            grad_shift_one,
            grad_scale_one,
            grad_gate_one,
            grad_shift_two,
            grad_scale_two,
            grad_gate_two,
        ],
        axis=-1,
    )
    grad_modulation = jnp.einsum("rls,rlc->rsc", local_onehot, grad_per_frame, precision=HIGHEST)
    gradients = (
        weight_gradient(normed_low, grad_query_pre),
        bias_gradient(grad_query_pre),
        weight_gradient(normed_low, grad_key_pre),
        bias_gradient(grad_key_pre),
        weight_gradient(normed_low, grad_value_frames),
        bias_gradient(grad_value_frames),
        weight_gradient(attention_frames, grad_branch),
        bias_gradient(grad_branch),
        weight_gradient(normed_two_low, grad_hidden),
        bias_gradient(grad_hidden),
        weight_gradient(activated_low, grad_branch_two),
        bias_gradient(grad_branch_two),
        jnp.sum(grad_modulation, axis=(0, 1)),
    )
    row_total = lax.psum(grad_modulation.astype(jnp.bfloat16), "seq").astype(jnp.float32)
    every_grad = lax.all_gather(row_total.astype(jnp.bfloat16), "dp", axis=0, tiled=True).astype(
        row_total.dtype
    )
    modulation_weight_grad = jnp.einsum(
        "rsd,rsc->dc", owned_low.astype(jnp.float32), every_grad, precision=HIGHEST
    )
    spreaded = [spread(member, wide_count, narrow_count) for member in gradients]
    first_pass = (
        lax.psum_scatter(
            spreaded[0].astype(jnp.bfloat16), "seq", scatter_dimension=1, tiled=True
        ).astype(jnp.float32),
        lax.psum_scatter(
            spreaded[1].astype(jnp.bfloat16), "seq", scatter_dimension=1, tiled=True
        ).astype(jnp.float32),
        lax.psum_scatter(
            spreaded[2].astype(jnp.bfloat16), "seq", scatter_dimension=1, tiled=True
        ).astype(jnp.float32),
        lax.psum_scatter(
            spreaded[3].astype(jnp.bfloat16), "seq", scatter_dimension=1, tiled=True
        ).astype(jnp.float32),
        lax.psum_scatter(
            spreaded[4].astype(jnp.bfloat16), "seq", scatter_dimension=1, tiled=True
        ).astype(jnp.float32),
        lax.psum_scatter(
            spreaded[5].astype(jnp.bfloat16), "seq", scatter_dimension=1, tiled=True
        ).astype(jnp.float32),
        lax.psum_scatter(
            spreaded[6].astype(jnp.bfloat16), "seq", scatter_dimension=1, tiled=True
        ).astype(jnp.float32),
        lax.psum_scatter(
            spreaded[7].astype(jnp.bfloat16), "seq", scatter_dimension=1, tiled=True
        ).astype(jnp.float32),
        lax.psum_scatter(
            spreaded[8].astype(jnp.bfloat16), "seq", scatter_dimension=1, tiled=True
        ).astype(jnp.float32),
        lax.psum_scatter(
            spreaded[9].astype(jnp.bfloat16), "seq", scatter_dimension=1, tiled=True
        ).astype(jnp.float32),
        lax.psum_scatter(
            spreaded[10].astype(jnp.bfloat16), "seq", scatter_dimension=1, tiled=True
        ).astype(jnp.float32),
        lax.psum_scatter(
            spreaded[11].astype(jnp.bfloat16), "seq", scatter_dimension=1, tiled=True
        ).astype(jnp.float32),
        lax.psum_scatter(
            spreaded[12].astype(jnp.bfloat16), "seq", scatter_dimension=1, tiled=True
        ).astype(jnp.float32),
    )
    second_pass = (
        lax.psum_scatter(first_pass[0], "dp", scatter_dimension=0, tiled=True),
        lax.psum_scatter(first_pass[1], "dp", scatter_dimension=0, tiled=True),
        lax.psum_scatter(first_pass[2], "dp", scatter_dimension=0, tiled=True),
        lax.psum_scatter(first_pass[3], "dp", scatter_dimension=0, tiled=True),
        lax.psum_scatter(first_pass[4], "dp", scatter_dimension=0, tiled=True),
        lax.psum_scatter(first_pass[5], "dp", scatter_dimension=0, tiled=True),
        lax.psum_scatter(first_pass[6], "dp", scatter_dimension=0, tiled=True),
        lax.psum_scatter(first_pass[7], "dp", scatter_dimension=0, tiled=True),
        lax.psum_scatter(first_pass[8], "dp", scatter_dimension=0, tiled=True),
        lax.psum_scatter(first_pass[9], "dp", scatter_dimension=0, tiled=True),
        lax.psum_scatter(first_pass[10], "dp", scatter_dimension=0, tiled=True),
        lax.psum_scatter(first_pass[11], "dp", scatter_dimension=0, tiled=True),
        lax.psum_scatter(first_pass[12], "dp", scatter_dimension=0, tiled=True),
    )
    reduced = [unpack(member) for member in second_pass]
    return (
        layer_output,
        frames_grad,
        reduced[0],
        reduced[1],
        reduced[2],
        reduced[3],
        reduced[4],
        reduced[5],
        reduced[6],
        reduced[7],
        reduced[8],
        reduced[9],
        reduced[10],
        reduced[11],
        modulation_weight_grad,
        reduced[12],
    )


def hand_over_kernel(count, *refs):
    copies = [
        pltpu.make_async_copy(source, target, refs[-1].at[n])
        for n, (source, target) in enumerate(zip(refs[:count], refs[count : 2 * count]))
    ]
    for copy in copies:
        copy.start()
    for copy in copies:
        copy.wait()


def hand_over(*arrays):
    anywhere = pl.BlockSpec(memory_space=pl.ANY)
    return pl.pallas_call(
        partial(hand_over_kernel, len(arrays)),
        out_shape=[jax.ShapeDtypeStruct(array.shape, array.dtype) for array in arrays],
        in_specs=[pl.BlockSpec(memory_space=pltpu.VMEM)] * len(arrays),
        out_specs=[anywhere] * len(arrays),
        scratch_shapes=[pltpu.SemaphoreType.DMA((len(arrays),))],
    )(*arrays)


def on_device_fast(
    frames, output_gradient, segment_lengths, time_index, query_weight, query_bias, key_weight, key_bias,
    value_weight, value_bias, output_projection, output_bias, up_weight, up_bias, down_weight, down_bias,
    modulation_weight, modulation_bias,
):
    seq_index, dp_index = lax.axis_index("seq"), lax.axis_index("dp")
    depth = lax.axis_size("dp") // 2
    own_index = dp_index * 4 + seq_index
    _, span, width = frames.shape
    own_rows, hidden = up_weight.shape
    down_rows = down_weight.shape[0]
    vectors = (query_bias, key_bias, value_bias, output_bias, up_bias, down_bias, modulation_bias)
    biases = [vector.reshape(1, -1) for vector in vectors]
    (output, grad_middle, mg_in, bias_in, mods, low, gwo, gup, gdown, given_heads, qs, ks, vs, oh, lse, normed, wg,
     cosr, sinr) = forward_call(
        depth, span, own_rows, down_rows, hidden,
        (segment_lengths, time_index, frames[0], output_gradient[0], *biases, query_weight, key_weight, value_weight,
         output_projection, up_weight, down_weight, modulation_weight),
    )
    (fgrad, dwq, dwk, dwv, dwo, dup, ddown, dmw, mbias, btile) = backward_call(
        depth, span, own_rows, down_rows, hidden,
        (segment_lengths, given_heads, qs, ks, vs, oh, lse, normed, wg, cosr, sinr, low, mods, frames[0],
         grad_middle, mg_in, bias_in,
         gwo, gup, gdown),
    )
    sums = btile.reshape(-1)

    def own_part(vector, start, size):
        return lax.dynamic_slice_in_dim(vector, start + own_index * size, size)

    lengths = [member.shape[0] for member in (query_bias, key_bias, value_bias, output_bias, up_bias, down_bias)]
    starts = [sum(lengths[:n]) * depth * 8 for n in range(6)]
    bq, bk, bv, bo, bu, bd = [own_part(sums, start, size) for start, size in zip(starts, lengths)]
    bm = own_part(mbias[0], 0, modulation_bias.shape[0])
    output, fgrad, dwq, dwk, dwv, dwo, dup, ddown, dmw = hand_over(
        output, fgrad, dwq, dwk, dwv, dwo, dup, ddown, dmw
    )
    return (
        output[None], fgrad[None], dwq, bq, dwk, bk, dwv, bv, dwo, bo, dup, bu, ddown, bd, dmw, bm,
    )


def fits(mesh, frames, *parameters):
    dp, seq = mesh.shape["dp"], mesh.shape["seq"]
    rows = parameters[3].shape[0] // (dp * seq)
    return seq == 4 and dp % 2 == 0 and rows == 32 and frames.shape[0] == dp


def solution(mesh):
    def run(*arrays):
        return mapped(mesh, on_device_fast if fits(mesh, *arrays) else on_device)(*arrays)

    return run


def mapped(mesh, body):
    return jax.shard_map(
        body,
        mesh=mesh,
        in_specs=(
            P("dp", "seq", None),
            P("dp", "seq", None),
            P("dp", None),
            P("dp", None),
            P(("dp", "seq"), None),
            P(("dp", "seq")),
            P(("dp", "seq"), None),
            P(("dp", "seq")),
            P(("dp", "seq"), None),
            P(("dp", "seq")),
            P(("dp", "seq"), None),
            P(("dp", "seq")),
            P(("dp", "seq"), None),
            P(("dp", "seq")),
            P(("dp", "seq"), None),
            P(("dp", "seq")),
            P(("dp", "seq"), None),
            P(("dp", "seq")),
        ),
        out_specs=(
            P("dp", "seq", None),
            P("dp", "seq", None),
            P(("dp", "seq"), None),
            P(("dp", "seq")),
            P(("dp", "seq"), None),
            P(("dp", "seq")),
            P(("dp", "seq"), None),
            P(("dp", "seq")),
            P(("dp", "seq"), None),
            P(("dp", "seq")),
            P(("dp", "seq"), None),
            P(("dp", "seq")),
            P(("dp", "seq"), None),
            P(("dp", "seq")),
            P(("dp", "seq"), None),
            P(("dp", "seq")),
        ),
        check_vma=False,
    )
```

```python
from functools import partial
import math

import jax
import jax.numpy as jnp
from jax import lax
from jax.experimental import pallas as pl
from jax.experimental.pallas import tpu as pltpu
from jax.sharding import PartitionSpec as P

HEAD_DIM = 64
MODEL_WIDTH = 1024
SEGS = 4
EPSILON = 1e-06
NEGATIVE = -1e30
HIGHEST = lax.Precision.HIGHEST
F32 = jnp.float32
BF16 = jnp.bfloat16
LANES = 128


class Mover:
    def __init__(self, send_sems, recv_sems, local_sems):
        self.send_sems, self.recv_sems, self.local_sems = send_sems, recv_sems, local_sems
        self.count = self.local_count = 0
        self.sent = []

    def send(self, source, target, device):
        slot = self.count
        self.count += 1
        copy = pltpu.make_async_remote_copy(
            src_ref=source,
            dst_ref=target,
            send_sem=self.send_sems.at[slot],
            recv_sem=self.recv_sems.at[slot],
            device_id=device,
            device_id_type=pl.DeviceIdType.MESH,
        )
        copy.start()
        self.sent.append(copy)
        return copy

    def local(self, source, target):
        slot = self.local_count
        self.local_count += 1
        copy = pltpu.make_async_copy(source, target, self.local_sems.at[slot])
        copy.start()
        return copy

    def finish(self, but=()):
        for copy in self.sent:
            if not any(copy is other for other in but):
                copy.wait_send()


class Place:
    def __init__(self, depth):
        dp, seq = lax.axis_index("dp"), lax.axis_index("seq")
        self.depth = depth
        self.z, self.y = dp // 2, dp % 2
        self.x, self.c = seq // 2, seq % 2
        self.seq = seq
        self.index = dp * 4 + seq

    def at(self, z, y, x, c):
        return {"dp": z * 2 + y, "seq": x * 2 + c}

    def core(self):
        return self.at(self.z, self.y, self.x, 1 - self.c)

    def across_x(self):
        return self.at(self.z, self.y, 1 - self.x, self.c)

    def across_y(self):
        return self.at(self.z, 1 - self.y, self.x, self.c)

    def ahead(self, step):
        return (self.z + step) % self.depth

    def along_z(self, step):
        return self.at(self.ahead(step), self.y, self.x, self.c)

    def row_peer(self, step):
        return {"dp": self.z * 2 + self.y, "seq": (self.seq + step) % 4}

    def enter(self, diagonal=False):
        barrier = pltpu.get_barrier_semaphore()
        peers = [self.row_peer(step) for step in (1, 2, 3)] + [self.across_y()]
        peers += [self.along_z(step) for step in range(1, self.depth)]
        if diagonal:
            peers += [self.at(self.ahead(k), 1 - self.y, self.x, self.c) for k in range(1, self.depth)]
        for peer in peers:
            pl.semaphore_signal(barrier, 1, device_id=peer, device_id_type=pl.DeviceIdType.MESH)
        pl.semaphore_wait(barrier, len(peers))


def lanes_of(shape, axis=1):
    return lax.broadcasted_iota(jnp.int32, shape, axis)


def frame_segments(lens, first_row, rows, width):
    position = lanes_of((rows, width), 0) + first_row
    first, second, third = lens[0, 0], lens[0, 0] + lens[0, 1], lens[0, 0] + lens[0, 1] + lens[0, 2]
    segment = (
        (position >= first).astype(jnp.int32)
        + (position >= second).astype(jnp.int32)
        + (position >= third).astype(jnp.int32)
    )
    start = jnp.where(
        segment == 0, 0, jnp.where(segment == 1, first, jnp.where(segment == 2, second, third))
    )
    return segment, position - start


def three_parts(values):
    high = values.astype(BF16).astype(F32)
    rest = values - high
    middle = rest.astype(BF16).astype(F32)
    return high, middle, (rest - middle).astype(BF16).astype(F32)


def swap_halves(values, lane):
    return jnp.where(
        lane % HEAD_DIM < HEAD_DIM // 2, pltpu.roll(values, 96, 1), pltpu.roll(values, 32, 1)
    )


def head_only(values, lane, head):
    return jnp.where((lane >= HEAD_DIM) == bool(head), values.astype(F32), 0.0).astype(BF16)


def across(left, right):
    return lax.dot_general(left, right, (((1,), (1,)), ((), ())), preferred_element_type=F32)


def product(left, right):
    return jnp.dot(left, right, preferred_element_type=F32)


def straight(first, last, body):
    for step in range(first, last):
        body(step, 0)


AXES = (
    (1, 2, 0), (0, 2, 1), (2, 0, 1), (0, 2, 1), (0, 1, 2), (0, 1, 2), (0, 2, 1), (0, 2, 1), (2, 1, 0), (0, 1, 2),
)
(
    GATHER_Z, GATHER_TWO, GATHER_THREE, GATHER_CORE, COLUMNS_Z, COLUMNS_Y, PROJECT, ATTEND, GO_UP, FRAMES_X,
    FRAMES_ON, TABLES, TIMES_Y, SHARE, MOD_Y, MOD_Z, MOD_X, MOD_LAST, FRAMES_CORE, BIAS_Y, BIAS_X, BIAS_CORE,
    BIASES, MODS, OUT, GO_DOWN, BACK, GRADS, WAITS,
) = range(29)
FORWARD_ORDER = (
    (FRAMES_X, 0), (GATHER_Z, 9), (GATHER_Z, 1), (TIMES_Y, 0), (BIAS_Y, 0), (FRAMES_CORE, 0), (GATHER_TWO, 9),
    (COLUMNS_Z, 0), (COLUMNS_Z, 1), (SHARE, 0), (GATHER_Z, 4), (GATHER_Z, 8), (BIAS_X, 0), (MOD_Y, 0),
    (COLUMNS_Y, 0), (GATHER_THREE, 9), (COLUMNS_Y, 1), (COLUMNS_Z, 2), (FRAMES_X, 1), (GATHER_Z, 3), (MOD_Z, 0),
    (GATHER_Z, 0), (GATHER_Z, 2), (GATHER_Z, 7), (GATHER_TWO, 8), (GATHER_Z, 6), (TABLES, 1), (BIAS_CORE, 0),
    (GATHER_TWO, 4), (BIASES, 0), (COLUMNS_Y, 2), (TABLES, 0), (GATHER_TWO, 0), (GATHER_TWO, 1), (FRAMES_ON, 1),
    (MOD_X, 0), (GATHER_Z, 5), (GATHER_TWO, 3), (GATHER_THREE, 1), (GATHER_TWO, 2), (MOD_LAST, 0),
    (GATHER_THREE, 4), (MODS, 0), (PROJECT, 0), (GATHER_CORE, 9), (GATHER_THREE, 3), (GATHER_TWO, 7),
    (FRAMES_ON, 0), (PROJECT, 1), (PROJECT, 2), (GATHER_THREE, 0), (GATHER_TWO, 6), (PROJECT, 3),
    (GATHER_CORE, 1), (GATHER_TWO, 5), (GATHER_THREE, 8), (ATTEND, 1), (GATHER_THREE, 2), (ATTEND, 1),
    (GATHER_CORE, 4), (GATHER_CORE, 3), (GATHER_THREE, 5), (GATHER_THREE, 6), (ATTEND, 2), (GATHER_THREE, 7),
    (ATTEND, 3), (GATHER_CORE, 0), (ATTEND, 1), (GATHER_CORE, 6), (GATHER_CORE, 2), (GATHER_CORE, 5), (OUT, 0),
    (GO_UP, 0), (GATHER_CORE, 7), (GATHER_CORE, 8), (GO_UP, 1), (GO_DOWN, 0), (BACK, 0), (GRADS, 0),
)


def forward_kernel(
    depth,
    lens, times, frames, given_in, bq, bk, bv, bo, bu, bd, bm, wq, wk, wv, wo, up, down, mw,
    output, gmid, mg, btile, mods, low, gwo, gup, gdown, do_all, qs_out, ks_out, vs_out, oh_out, lse_out,
    normed_out, wg_out, cos_out, sin_out,
    att, oh, qs, lse, normed, wg, cosr, sinr, rowbias, wo_all, up_all, down_all,
    bb, xall, mwst, tb, part, recva, suma, recvb, sumb, recvc, sumc, recvd, modh, bmat, mod3, qbias,
    ka, va, qaug, given, mod6, branch, middle, normed_two, active, slope, gbt, gh, gn, gb, ga, sums,
    send_sems, recv_sems, local_sems,
):
    here = Place(depth)
    z, y, x, c, g = here.z, here.y, here.x, here.c, here.seq
    span, width = frames.shape
    hidden = up.shape[1]
    rows_all = span * 4
    block, tall, tile = 128, span, 256
    move = Mover(send_sems, recv_sems, local_sems)
    steps_z = range(1, depth)

    row = lanes_of((16, LANES), 0) % 4
    own_times = jnp.where(
        row == 0, times[0, 0], jnp.where(row == 1, times[0, 1], jnp.where(row == 2, times[0, 2], times[0, 3]))
    )
    tb[z, y] = own_times.astype(F32)
    bb[z, y, x, c] = jnp.zeros((8, LANES), F32)
    for n, vector in enumerate((bq, bk, bv, bo, bu, bd)):
        bb[z, y, x, c, n : n + 1, : vector.shape[1]] = vector[...].astype(F32)
    bb[z, y, x, c, 6:7, :] = bm[:, :LANES].astype(F32)
    bb[z, y, x, c, 7:8, : bm.shape[1] - LANES] = bm[:, LANES:].astype(F32)
    weights = (wq, wk, wv)
    own_width = wg.shape[-1]
    locals_first = [
        move.local(weights[j].at[:, pl.ds(pl.multiple_of(g * own_width, LANES), own_width)], wg.at[j, z, y, g])
        for j in range(3)
    ]
    strip = mw.shape[1] // 4
    local_mw = [
        move.local(mw.at[:, pl.ds(j * strip, strip)], mwst.at[pl.ds(j * 32, 32)]) for j in range(4)
    ]
    local_frames = move.local(frames, xall.at[g])
    local_given = move.local(given_in, given)
    here.enter()

    legs = {}
    shard, wide = wo.shape[0], MODEL_WIDTH
    thin = shard // 2
    flows = []

    def add_flow(source, target, first_row, columns=None):
        rows = pl.ds(first_row, thin)
        if columns is None:
            flows.append((source.at[rows], target.at[:, :, :, :, rows]))
        else:
            columns = pl.ds(columns, wide)
            flows.append((source.at[rows, columns], target.at[:, :, :, :, rows, columns]))

    for side in range(2):
        add_flow(wo, wo_all, side * thin)
    for side in range(2):
        add_flow(up, up_all, side * thin, 0)
        add_flow(up, up_all, side * thin, wide)
    for side in range(4):
        add_flow(down, down_all, side * thin)
    count = len(flows)

    legs, outgoing, owned = {}, [], {}
    here_at = (z, y, x)

    def to_axis(axis):
        if axis == 0:
            return [here.along_z(k) for k in steps_z]
        return [here.across_y() if axis == 1 else here.across_x()]

    def held(number, known):
        place = tuple(slice(None) if axis in known else here_at[axis] for axis in range(3))
        return flows[number][1].at[place + (c,)]

    def first_leg(number):
        source = flows[number][0]
        target = held(number, ())
        owned[number] = move.local(source, target)
        legs[number] = [move.send(source, target, peer) for peer in to_axis(AXES[number][0])]

    def next_leg(number, done):
        if done == 1:
            owned[number].wait()
        for copy in legs[number]:
            copy.wait_recv()
        part = held(number, AXES[number][:done])
        peers = [here.core()] if done == 3 else to_axis(AXES[number][done])
        legs[number] = [move.send(part, part, peer) for peer in peers]
        outgoing.extend(legs[number])

    def second_leg(number):
        next_leg(number, 1)

    def third_leg(number):
        next_leg(number, 2)

    def fourth_leg(number):
        next_leg(number, 3)

    def arrived(*numbers):
        for number in numbers:
            for copy in legs[number]:
                copy.wait_recv()

    times_z = [move.send(tb.at[z, y], tb.at[z, y], here.along_z(k)) for k in steps_z]
    qkv_row = [
        [
            move.send(
                weights[j].at[:, pl.ds(pl.multiple_of((g + k) % 4 * own_width, LANES), own_width)],
                wg.at[j, z, y, g],
                here.row_peer(k),
            )
            for k in (1, 2, 3)
        ]
        for j in range(3)
    ]
    bias_z = [move.send(bb.at[z, y, x, c], bb.at[z, y, x, c], here.along_z(k)) for k in steps_z]
    part_rows = span // 2
    frame_parts = [pl.ds(n * part_rows, part_rows) for n in range(2)]
    half = strip // 2
    sent = {}
    stores = []

    def columns_z(j):
        locals_first[j].wait()
        for copy in qkv_row[j]:
            copy.wait_recv()
        sent["q", j] = [move.send(wg.at[j, z, y], wg.at[j, z, y], here.along_z(k)) for k in steps_z]

    def columns_y(j):
        for copy in sent["q", j]:
            copy.wait_recv()
        sent["p", j] = move.send(wg.at[j, :, y], wg.at[j, :, y], here.across_y())

    def times_across():
        for copy in times_z:
            copy.wait_recv()
        sent["ty"] = move.send(tb.at[:, y], tb.at[:, y], here.across_y())

    def mod_share():
        sent["ty"].wait_recv()
        lane = lanes_of((16 * 2 * depth, LANES))
        row = lanes_of((16 * 2 * depth, LANES), 0)
        feature = here.index * 32 + lane % 32
        halfway = MODEL_WIDTH // 2
        frequency = jnp.exp((feature % halfway).astype(F32) * (-math.log(10000.0) / halfway))
        angle = tb[...].reshape(16 * 2 * depth, LANES) * frequency
        wave = jnp.where(feature < halfway, jnp.sin(angle), jnp.cos(angle))
        gated = wave / (1.0 + jnp.exp(-wave))
        low[...] = jnp.where(lane // 32 == (row % 16) // 4, gated, 0.0).astype(BF16)
        for copy in local_mw:
            copy.wait()
        for side in range(2):
            share = product(low[...], mwst[:, side * half : (side + 1) * half])
            part[side] = share.astype(BF16).reshape(depth, 2, 16, half)
        sent["mc"] = move.send(part.at[1 - c], recva, here.core())

    def mod_y():
        sent["mc"].wait_recv()
        suma[...] = (part[c].astype(F32) + recva[...].astype(F32)).astype(BF16)
        sent["my"] = move.send(suma.at[:, 1 - y], recvb, here.across_y())

    def mod_z():
        sent["my"].wait_recv()
        sumb[...] = (suma[:, y].astype(F32) + recvb[...].astype(F32)).astype(BF16)
        sent["mz"] = [move.send(sumb.at[here.ahead(k)], recvc.at[k - 1], here.along_z(k)) for k in steps_z]

    def mod_x():
        total = sumb[z].astype(F32)
        for k in steps_z:
            sent["mz"][k - 1].wait_recv()
            total = total + recvc[k - 1].astype(F32)
        sumc[...] = total
        sent["mx"] = move.send(sumc, recvd, here.across_x())

    def mod_last():
        sent["mx"].wait_recv()
        modh[c] = sumc[...] + recvd[...]
        sent["ml"] = move.send(modh.at[c], modh.at[c], here.core())

    def frames_core():
        sent["fc"] = move.send(frames, xall.at[g], here.core())

    def frames_x(n):
        sent["fx", n] = move.send(frames.at[frame_parts[n]], xall.at[g, frame_parts[n]], here.across_x())

    frames_here = []

    def frames_in(n):
        if n not in frames_here:
            sent["fx", n].wait_recv()
            frames_here.append(n)

    def frames_on(n):
        frames_in(n)
        theirs = xall.at[(g + 2) % 4, frame_parts[n]]
        sent["on", n] = move.send(theirs, theirs, here.core())

    def bias_y():
        for copy in bias_z:
            copy.wait_recv()
        sent["by"] = move.send(bb.at[:, y, x, c], bb.at[:, y, x, c], here.across_y())

    def bias_x():
        sent["by"].wait_recv()
        sent["bx"] = move.send(bb.at[:, :, x, c], bb.at[:, :, x, c], here.across_x())

    def bias_core():
        sent["bx"].wait_recv()
        sent["bc"] = move.send(bb.at[:, :, :, c], bb.at[:, :, :, c], here.core())

    def tables(step, carry):
        rows = pl.ds(pl.multiple_of(step * block, block), block)
        segment, relative = frame_segments(lens, step * block, block, LANES)
        lane = lanes_of((block, LANES))
        quarter = HEAD_DIM // 2
        frequency = jnp.exp((lane % quarter).astype(F32) * (-math.log(10000.0) / quarter))
        angle = relative.astype(F32) * frequency
        cosr[rows, :] = jnp.cos(angle)
        sine = jnp.sin(angle)
        sinr[rows, :] = jnp.where(lane % HEAD_DIM < quarter, -sine, sine)
        same = segment == lane
        qaug[rows, :] = jnp.where((lane < SEGS) & jnp.logical_not(same), NEGATIVE, 0.0).astype(BF16)
        keyside = jnp.where((lane < SEGS) & same, 1.0, jnp.where((lane >= 4) & (lane < 7), 1.0, 0.0))
        for pair in range(2):
            ka[pair, rows, LANES:] = keyside.astype(BF16)
            va[pair, rows, LANES:] = jnp.where(lane < 3, 1.0, 0.0).astype(BF16)
        return carry

    def tables_half(n):
        lax.fori_loop(n * rows_all // (2 * block), (n + 1) * rows_all // (2 * block), tables, 0)

    def bias_vectors():
        sent["bc"].wait_recv()
        bmat[...] = bb[...].reshape(16 * 2 * depth * 2, LANES).astype(BF16)

        place = lanes_of((LANES, own_width), 0)
        column = lanes_of((LANES, own_width))
        brow, bcol = lanes_of((64, own_width), 0), lanes_of((64, own_width))
        spread = jnp.where(column % 32 == place, 1.0, 0.0).astype(BF16)
        for j in range(3):
            mine = (brow % 8 == j) & (brow // 8 == bcol // 32)
            held = product(bmat[pl.ds(pl.multiple_of(g * 64, 64), 64), :], spread)
            qbias[j : j + 1, :] = jnp.sum(jnp.where(mine, held, 0.0), axis=0, keepdims=True)

        trow, tcol = lanes_of((16 * 2 * depth * 2, tile), 0), lanes_of((16 * 2 * depth * 2, tile))
        place, column = lanes_of((LANES, tile), 0), lanes_of((LANES, tile))

        def row_vector(step, size, source):
            spread = jnp.where(column % size == place, 1.0, 0.0).astype(BF16)
            chosen = (trow % 8 == source) & (trow // 8 == (tcol + step * tile) // size)
            return jnp.sum(jnp.where(chosen, product(bmat[...], spread), 0.0), axis=0, keepdims=True)

        def narrow_vectors(step, carry):
            columns = pl.ds(pl.multiple_of(step * tile, tile), tile)
            rowbias[0:1, columns] = row_vector(step, 32, 3)
            rowbias[2:3, columns] = row_vector(step, 32, 5)
            return carry

        def wide_vector(step, carry):
            rowbias[1:2, pl.ds(pl.multiple_of(step * tile, tile), tile)] = row_vector(step, 64, 4)
            return carry

        lax.fori_loop(0, MODEL_WIDTH // tile, narrow_vectors, 0)
        lax.fori_loop(0, up.shape[1] // tile, wide_vector, 0)

        place = lanes_of((LANES, half), 0)
        column = lanes_of((LANES, half))
        spread_a = jnp.where(column % 192 == place, 1.0, 0.0).astype(BF16)
        spread_b = jnp.where(column % 192 == place + LANES, 1.0, 0.0).astype(BF16)
        brow, bcol = lanes_of((32, half), 0), lanes_of((32, half))
        inside = brow // 8 == bcol // 192
        for q in range(8):
            rows = bmat[q * 32 : (q + 1) * 32, :]
            terms = jnp.where(inside & (brow % 8 == 6), product(rows, spread_a), 0.0)
            terms = terms + jnp.where(inside & (brow % 8 == 7), product(rows, spread_b), 0.0)
            mods[4:5, q * half : (q + 1) * half] = jnp.sum(terms, axis=0, keepdims=True)

    def mod_done():
        sent["ml"].wait_recv()
        for q in range(8):
            j, side = q // 2, q % 2
            columns = slice(q * half, (q + 1) * half)
            mods[0:4, columns] = modh[side, 4 * j : 4 * j + 4, :] + mods[4:5, columns]
        for kept, first, last in ((mod3, 0, 2 * width), (mod6, 2 * width, 6 * width)):
            high, mid, rest = three_parts(mods[0:4, first:last])
            kept[0:4, :] = high
            kept[4:8, :] = mid
            kept[8:12, :] = rest
            kept[12:16, :] = jnp.zeros((4, last - first), F32)

    def project_rows(source):
        block, step = span, source
        rows = pl.ds(pl.multiple_of(step * block, block), block)
        values = xall[source].astype(F32)
        center = jnp.mean(values, axis=1, keepdims=True)
        centered = values - center
        variance = jnp.mean(centered * centered, axis=1, keepdims=True)
        segment, _ = frame_segments(lens, step * block, block, 16)
        slot = lanes_of((block, 16))
        chosen = jnp.where((slot < 12) & (slot % 4 == segment), 1.0, 0.0).astype(BF16)
        parts = mod3[...].astype(BF16)
        shift = product(chosen, parts[:, :MODEL_WIDTH])
        scale = product(chosen, parts[:, MODEL_WIDTH:])
        result = (centered * lax.rsqrt(variance + EPSILON) * (1.0 + scale) + shift).astype(BF16)
        normed[rows, :] = result
        cosine, sine = cosr[rows, :], sinr[rows, :]
        lane = lanes_of((block, LANES))
        for j in range(3):
            weight = wg[j].reshape(MODEL_WIDTH, own_width)
            full = product(result, weight) + qbias[j : j + 1, :]
            for pair in range(2):
                piece = full[:, pair * LANES : (pair + 1) * LANES]
                if j < 2:
                    piece = piece * cosine + swap_halves(piece, lane) * sine
                if j == 0:
                    qs[pair, rows, :] = (piece.astype(BF16).astype(F32) * HEAD_DIM**-0.5).astype(BF16)
                elif j == 1:
                    ka[pair, rows, :LANES] = piece.astype(BF16)
                else:
                    va[pair, rows, :LANES] = piece.astype(BF16)

    def project_span(n):
        if n == 0:
            local_frames.wait()
            for j in range(3):
                sent["p", j].wait_recv()
        elif n == 1:
            sent["fc"].wait_recv()
        elif n == 2:
            for m in range(2):
                frames_in(m)
        else:
            for m in range(2):
                sent["on", m].wait_recv()
        number = (g, x * 2 + 1 - c, (1 - x) * 2 + c, (1 - x) * 2 + 1 - c)[n]
        project_rows(number)
        if n == 3:
            for source, target in (
                (qs, qs_out), (ka.at[:, :, pl.ds(0, LANES)], ks_out), (va.at[:, :, pl.ds(0, LANES)], vs_out),
                (normed, normed_out), (wg, wg_out), (cosr, cos_out), (sinr, sin_out),
            ):
                stores.append(move.local(source, target))

    def attend(pair, step):
        rows = pl.ds(pl.multiple_of(step * tall, tall), tall)
        query = qs[pair, rows, :]
        lane = lanes_of((tall, LANES))
        outs, sums = [], []
        for head in range(2):
            left = jnp.concatenate([head_only(query, lane, head), qaug[rows, :]], axis=1)
            scores = across(left, ka[pair])
            highest = jnp.max(scores, axis=1, keepdims=True)
            mixed = product(jnp.exp(scores - highest).astype(BF16), va[pair])
            total = mixed[:, LANES : LANES + 1]
            outs.append(mixed[:, :LANES] / total)
            sums.append(highest + jnp.log(total))
        oh[pair, rows, :] = jnp.where(lane < HEAD_DIM, outs[0], outs[1]).astype(BF16)
        before = jnp.zeros((tall, LANES), F32) if pair == 0 else lse[rows, :]
        lse[rows, :] = jnp.where(
            lane == 2 * pair, sums[0], jnp.where(lane == 2 * pair + 1, sums[1], before)
        )

    delivered = []

    def attend_next():
        pair, at = len(delivered) // 4, len(delivered) % 4
        k = (2, 1, 3, 0)[at]
        target = (g + k) % 4
        attend(pair, target)
        columns = pl.ds(pl.multiple_of(g * own_width + pair * LANES, LANES), LANES)
        source = oh.at[pair, pl.ds(pl.multiple_of(target * span, span), span)]
        if k:
            delivered.append(move.send(source, att.at[:, columns], here.row_peer(k)))
        else:
            delivered.append(move.local(source, att.at[:, columns]))
        if len(delivered) == 8:
            stores.append(move.local(oh, oh_out))
            stores.append(move.local(lse, lse_out))

    base = g * span

    def tile_at(step):
        return pl.ds(pl.multiple_of(step * tile, tile), tile)

    def per_frame(part, first, rows, columns):
        segment, _ = frame_segments(lens, base + first, rows, 16)
        slot = lanes_of((rows, 16))
        chosen = jnp.where((slot < 12) & (slot % 4 == segment), 1.0, 0.0).astype(BF16)
        return product(chosen, mod6[:, columns].astype(BF16))

    def members(first, rows):
        position = base + first + lanes_of((16, rows))
        edges = [lens[0, 0], lens[0, 0] + lens[0, 1], lens[0, 0] + lens[0, 1] + lens[0, 2]]
        inside = sum((position >= edge).astype(jnp.int32) for edge in edges)
        return jnp.where(inside == lanes_of((16, rows), 0), 1.0, 0.0).astype(BF16)

    def by_segment(inside, values):
        top = values.astype(BF16)
        return product(inside, top) + product(inside, (values - top.astype(F32)).astype(BF16))

    def shifted(part, step):
        return pl.ds(pl.multiple_of(part * width + step * tile, tile), tile)

    def wo_columns(columns):
        return wo_all[:, :, :, :, :, columns].reshape(width, tile)

    def up_columns(columns):
        return up_all[:, :, :, :, :, columns].reshape(width, tile)

    def down_columns(columns):
        return down_all[:, :, :, :, :, columns].reshape(hidden, tile)

    def project_out():
        for at, copy in enumerate(delivered):
            copy.wait() if at % 4 == 3 else copy.wait_recv()
        arrived(0, 1)

        def body(step, carry):
            columns = tile_at(step)
            branch[:, columns] = product(att[...], wo_columns(columns)) + rowbias[0:1, columns]
            return carry

        straight(0, width // tile, body)

        def norm_forward(step, carry):
            rows = pl.ds(pl.multiple_of(step * block, block), block)
            gate = per_frame(0, step * block, block, slice(0, width))
            values = xall[g, rows, :].astype(F32) + gate * branch[rows, :]
            middle[rows, :] = values
            centered = values - jnp.mean(values, axis=1, keepdims=True)
            hat = centered * lax.rsqrt(jnp.mean(centered * centered, axis=1, keepdims=True) + EPSILON)
            shift = per_frame(1, step * block, block, slice(width, 2 * width))
            scale = per_frame(2, step * block, block, slice(2 * width, 3 * width))
            normed_two[rows, :] = (hat * (1.0 + scale) + shift).astype(BF16)
            return carry

        straight(0, span // block, norm_forward)

    root = math.sqrt(2.0 / math.pi)

    def go_up(side):
        arrived(2 + side, 4 + side)

        def body(step, carry):
            columns = tile_at(step)
            value = product(normed_two[...], up_columns(columns)) + rowbias[1:2, columns]
            square = value * value
            turn = jnp.tanh(root * value * (1.0 + 0.044715 * square))
            part_one = 0.5 * (1.0 + turn)
            active[:, columns] = (value * part_one).astype(BF16)
            slope[:, columns] = part_one + 0.5 * value * (1.0 - turn * turn) * root * (
                1.0 + 3 * 0.044715 * square
            )
            return carry

        straight(side * width // tile, (side + 1) * width // tile, body)

    def go_down():
        arrived(6, 7, 8, 9)
        local_given.wait()

        def body(step, carry):
            columns = tile_at(step)
            value = product(active[...], down_columns(columns)) + rowbias[2:3, columns]
            gate = per_frame(3, 0, span, shifted(3, step))
            back = given[:, columns].astype(F32)
            output[:, columns] = (middle[:, columns] + gate * value).astype(BF16)
            gbt[:, columns] = (gate * back).astype(BF16)
            sums[:, shifted(3, step)] = by_segment(members(0, span), back * value)
            return carry

        straight(0, width // tile, body)

    def back_values():
        def hidden_tile(step, carry):
            rows = tile_at(step)
            weight = down_all[step // 2, step % 2].reshape(tile, width)
            gh[:, rows] = (across(gbt[...], weight) * slope[:, rows]).astype(BF16)
            return carry

        straight(0, hidden // tile, hidden_tile)

        def normed_tile(step, carry):
            gn[:, tile_at(step)] = across(gh[...], up_all[step].reshape(tile, hidden))
            return carry

        straight(0, width // tile, normed_tile)
        sums[:, : 3 * width] = jnp.zeros((16, 3 * width), F32)

        def norm_back(step, carry):
            rows = pl.ds(pl.multiple_of(step * block, block), block)
            grad, values = gn[rows, :], middle[rows, :]
            centered = values - jnp.mean(values, axis=1, keepdims=True)
            scaled = lax.rsqrt(jnp.mean(centered * centered, axis=1, keepdims=True) + EPSILON)
            hat = centered * scaled
            inner = grad * (1.0 + per_frame(2, step * block, block, slice(2 * width, 3 * width)))
            mean_one = jnp.mean(inner, axis=1, keepdims=True)
            mean_two = jnp.mean(inner * hat, axis=1, keepdims=True)
            total = given[rows, :].astype(F32) + scaled * (inner - mean_one - hat * mean_two)
            gmid[rows, :] = total
            gb[rows, :] = (per_frame(0, step * block, block, slice(0, width)) * total).astype(BF16)
            inside = members(step * block, block)
            sums[:, :width] += by_segment(inside, total * branch[rows, :])
            sums[:, width : 2 * width] += by_segment(inside, grad)
            sums[:, 2 * width : 3 * width] += by_segment(inside, grad * hat)
            return carry

        straight(0, span // block, norm_back)
        sent["o"] = []
        mine = pl.ds(pl.multiple_of(g * span, span), span)
        for k in (1, 2, 3, 0):
            target = (g + k) % 4
            columns = tile_at(target)
            ga[:, columns] = across(gb[...], wo_all[target].reshape(tile, width)).astype(BF16)
            for pair in range(2):
                source = ga.at[:, pl.ds(pl.multiple_of(target * own_width + pair * LANES, LANES), LANES)]
                place = do_all.at[pair, mine]
                if k:
                    sent["o"].append(move.send(source, place, here.row_peer(k)))
                else:
                    stores.append(move.local(source, place))

    def back_weights():
        for copy in outgoing:
            copy.wait_send()

        def down_tile(step, carry):
            grad = from_rows(active[:, tile_at(step)], gbt[...]).astype(BF16)
            down_all[step // 2, step % 2] = grad.reshape(down_all.shape[2:])
            return carry

        straight(0, hidden // tile, down_tile)
        stores.append(move.local(down_all, gdown))

        def up_tile(step, carry):
            grad = from_rows(normed_two[:, tile_at(step)], gh[...]).astype(BF16)
            up_all[step] = grad.reshape(up_all.shape[1:])
            return carry

        straight(0, width // tile, up_tile)
        stores.append(move.local(up_all, gup))

        def out_tile(step, carry):
            grad = from_rows(att[:, tile_at(step)], gb[...]).astype(BF16)
            wo_all[step] = grad.reshape(wo_all.shape[1:])
            return carry

        straight(0, width // tile, out_tile)
        stores.append(move.local(wo_all, gwo))
        ones = jnp.ones((16, span), BF16)
        btile[0:24, :] = jnp.zeros((24, LANES), F32)
        start = 24
        for grads, size in ((gb, width), (gh, hidden), (gbt, width)):
            total = product(ones, grads[...])
            for n in range(size // LANES):
                btile[start + n : start + n + 1, :] = total[0:1, n * LANES : (n + 1) * LANES]
            start += size // LANES
        for n in range(4):
            mg[4 * n : 4 * n + 4, :] = sums[0:4, n * width : (n + 1) * width]

    numbered = {
        GATHER_Z: first_leg, GATHER_TWO: second_leg, GATHER_THREE: third_leg, GATHER_CORE: fourth_leg, COLUMNS_Z: columns_z, COLUMNS_Y: columns_y,
        PROJECT: project_span, GO_UP: go_up, FRAMES_X: frames_x, FRAMES_ON: frames_on, TABLES: tables_half,
    }
    named = {
        TIMES_Y: times_across, SHARE: mod_share, MOD_Y: mod_y, MOD_Z: mod_z, MOD_X: mod_x, MOD_LAST: mod_last,
        FRAMES_CORE: frames_core, BIAS_Y: bias_y, BIAS_X: bias_x, BIAS_CORE: bias_core, BIASES: bias_vectors, MODS: mod_done,
        OUT: project_out, GO_DOWN: go_down, BACK: back_values, GRADS: back_weights,
    }
    for code, number in FORWARD_ORDER:
        if code in named:
            named[code]()
        elif code == ATTEND:
            for _ in range(number):
                attend_next()
        else:
            numbered[code](number)
    for copy in stores:
        copy.wait()
    for copy in sent["o"]:
        copy.wait_recv()
    move.finish(but=outgoing)

def forward_call(depth, span, own_rows, down_rows, hidden, args):
    rows_all, own_width, width = 4 * span, MODEL_WIDTH // 4, MODEL_WIDTH
    half = 6 * MODEL_WIDTH // 8
    vmem, anywhere, scalar = (
        pl.BlockSpec(memory_space=pltpu.VMEM),
        pl.BlockSpec(memory_space=pl.ANY),
        pl.BlockSpec(memory_space=pltpu.SMEM),
    )

    def out(shape, dtype):
        return jax.ShapeDtypeStruct(shape, dtype)

    heads, table = (2, rows_all, LANES), (rows_all, LANES)
    columns = (3, depth, 2, 4, own_rows, own_width)
    wo_shape = (depth, 2, 2, 2, own_rows, width)
    up_shape = (depth, 2, 2, 2, own_rows, hidden)
    down_shape = (depth, 2, 2, 2, down_rows, width)
    outs = [
        (out((span, width), BF16), vmem),
        (out((span, width), F32), vmem),
        (out((16, width), F32), vmem),
        (out((56, LANES), F32), vmem),
        (out((8, 6 * width), F32), vmem),
        (out((32 * depth, LANES), BF16), vmem),
        (out(wo_shape, BF16), anywhere),
        (out(up_shape, BF16), anywhere),
        (out(down_shape, BF16), anywhere),
        (out(heads, BF16), anywhere),
        (out(heads, BF16), anywhere),
        (out(heads, BF16), anywhere),
        (out(heads, BF16), anywhere),
        (out(heads, BF16), anywhere),
        (out(table, F32), anywhere),
        (out((rows_all, width), BF16), anywhere),
        (out(columns, BF16), anywhere),
        (out(table, F32), anywhere),
        (out(table, F32), anywhere),
    ]
    low, wide = pltpu.VMEM((span, width), BF16), pltpu.VMEM((span, width), F32)
    scratch = [
        low,
        pltpu.VMEM(heads, BF16),
        pltpu.VMEM(heads, BF16),
        pltpu.VMEM(table, F32),
        pltpu.VMEM((rows_all, width), BF16),
        pltpu.VMEM(columns, BF16),
        pltpu.VMEM(table, F32),
        pltpu.VMEM(table, F32),
        pltpu.VMEM((8, hidden), F32),
        pltpu.VMEM(wo_shape, BF16),
        pltpu.VMEM(up_shape, BF16),
        pltpu.VMEM(down_shape, BF16),
        pltpu.VMEM((depth, 2, 2, 2, 8, LANES), F32),
        pltpu.VMEM((4, span, width), BF16),
        pltpu.VMEM((LANES, 2 * half), BF16),
        pltpu.VMEM((depth, 2, 16, LANES), F32),
        pltpu.VMEM((2, depth, 2, 16, half), BF16),
        pltpu.VMEM((depth, 2, 16, half), BF16),
        pltpu.VMEM((depth, 2, 16, half), BF16),
        pltpu.VMEM((depth, 16, half), BF16),
        pltpu.VMEM((depth, 16, half), BF16),
        pltpu.VMEM((depth - 1, 16, half), BF16),
        pltpu.VMEM((16, half), F32),
        pltpu.VMEM((16, half), F32),
        pltpu.VMEM((2, 16, half), F32),
        pltpu.VMEM((64 * depth, LANES), BF16),
        pltpu.VMEM((16, 2 * width), F32),
        pltpu.VMEM((8, own_width), F32),
        pltpu.VMEM((2, rows_all, 2 * LANES), BF16),
        pltpu.VMEM((2, rows_all, 2 * LANES), BF16),
        pltpu.VMEM(table, BF16),
        low,
        pltpu.VMEM((16, 4 * width), F32),
        wide,
        wide,
        low,
        pltpu.VMEM((span, hidden), BF16),
        pltpu.VMEM((span, hidden), F32),
        low,
        pltpu.VMEM((span, hidden), BF16),
        wide,
        low,
        low,
        pltpu.VMEM((16, 4 * width), F32),
        pltpu.SemaphoreType.DMA((144,)),
        pltpu.SemaphoreType.DMA((144,)),
        pltpu.SemaphoreType.DMA((48,)),
    ]
    return pl.pallas_call(
        partial(forward_kernel, depth),
        out_shape=[shape for shape, _ in outs],
        in_specs=[scalar, scalar, anywhere, anywhere] + [vmem] * 7 + [anywhere] * 7,
        out_specs=[spec for _, spec in outs],
        scratch_shapes=scratch,
        compiler_params=pltpu.CompilerParams(
            collective_id=0, has_side_effects=True, vmem_limit_bytes=62 * 1024 * 1024
        ),
        cost_estimate=pl.CostEstimate(flops=2 * 10**10, bytes_accessed=60 * 10**6, transcendentals=10**7),
    )(*args)


def turn_back(values, cosine, sine, lane):
    return values * cosine - swap_halves(values, lane) * sine


def from_rows(left, right):
    return lax.dot_general(left, right, (((0,), (0,)), ((), ())), preferred_element_type=F32)


X_FIRST = (0, 1, 0, 0, 1, 0, 0, 1, 0, 1)
(
    SUM_ONE, SUM_TWO, SUM_THREE, SUM_LAST, WEIGHTS_Y, WEIGHTS_Z, WEIGHTS_LAST, ATTEND_BACK, ROWS_AWAY,
    ROWS_ACROSS, ROWS_HOME, NORM, EARLY_CORE, EARLY_X, EARLY_Z, EARLY_Y, EARLY_SHARE, EARLY_DONE, LATE_ROWS,
    LATE_DONE, BIAS_START, BIAS_NEXT, BIAS_DONE,
) = range(23)
BACKWARD_ORDER = (
    (SUM_ONE, 0), (SUM_ONE, 4), (SUM_ONE, 3), (SUM_ONE, 2), (SUM_ONE, 5), (EARLY_CORE, 0), (SUM_ONE, 1),
    (SUM_ONE, 6), (SUM_TWO, 0), (ATTEND_BACK, 3), (SUM_TWO, 3), (ATTEND_BACK, 1), (EARLY_X, 0), (SUM_ONE, 9),
    (ATTEND_BACK, 1), (SUM_TWO, 1), (ATTEND_BACK, 1), (SUM_TWO, 4), (SUM_THREE, 3), (SUM_THREE, 0),
    (ATTEND_BACK, 1), (EARLY_Z, 0), (SUM_TWO, 2), (SUM_TWO, 5), (SUM_ONE, 8), (SUM_TWO, 6), (ATTEND_BACK, 1),
    (SUM_ONE, 7), (SUM_THREE, 1), (ATTEND_BACK, 1), (SUM_TWO, 9), (EARLY_Y, 0), (SUM_THREE, 4), (SUM_THREE, 5),
    (ATTEND_BACK, 2), (SUM_THREE, 2), (SUM_THREE, 6), (ATTEND_BACK, 1), (SUM_THREE, 9), (SUM_TWO, 8),
    (SUM_TWO, 7), (ROWS_AWAY, 0), (WEIGHTS_Y, 0), (ROWS_ACROSS, 0), (SUM_THREE, 8), (SUM_THREE, 7),
    (WEIGHTS_Y, 2), (WEIGHTS_Z, 0), (BIAS_START, 0), (SUM_LAST, 3), (WEIGHTS_Y, 1), (ROWS_HOME, 0),
    (SUM_LAST, 5), (BIAS_NEXT, 0), (WEIGHTS_Z, 2), (WEIGHTS_Z, 1), (WEIGHTS_LAST, 0), (SUM_LAST, 8), (NORM, 0),
    (SUM_LAST, 2), (SUM_LAST, 1), (LATE_ROWS, 0), (SUM_LAST, 4), (BIAS_NEXT, 0), (WEIGHTS_LAST, 1),
    (BIAS_NEXT, 0), (EARLY_SHARE, 0), (WEIGHTS_LAST, 2), (LATE_DONE, 0), (SUM_LAST, 6), (SUM_LAST, 0),
    (EARLY_DONE, 0), (SUM_LAST, 7), (SUM_LAST, 9), (BIAS_DONE, 0),
)


def backward_kernel(
    depth,
    lens, do_in, qs_in, ks_in, vs_in, oh_in, lse_in, normed_in, wg_in, cos_in, sin_in, low, mods, frames, gmid,
    mg_in, bias_in, gwo, gup, gdown,
    fgrad, dwq, dwk, dwv, dwo, dup, ddown, dmw, mbias, btile,
    qs, do, oh, lse, normed, wg, cosr, sinr, ka, va, qaug, dk_sum, dv_sum, gr, gw, gwy, gwz, gsum,
    gnp, gnr, gnx, mod3, acc_shift, acc_scale, mg, mgr, mgs, mgx, ev, late, joined, ez, brecv, bz,
    *rest,
):
    send_sems, recv_sems, local_sems = rest[-3:]
    buffers = rest[:-3]
    here = Place(depth)
    z, y, x, c, g = here.z, here.y, here.x, here.c, here.seq
    span = frames.shape[0]
    rows_all = span * 4
    own_width = wg.shape[-1]
    move = Mover(send_sems, recv_sems, local_sems)
    steps_z = range(1, depth)

    shard, width = gwo.shape[4], MODEL_WIDTH
    thin = shard // 2
    pieces = []

    def add_piece(source, target, first_row, columns=None):
        rows = pl.ds(first_row, thin)
        if columns is None:
            pieces.append((source.at[:, :, :, :, rows], target.at[rows]))
        else:
            columns = pl.ds(columns, width)
            pieces.append((source.at[:, :, :, :, rows, columns], target.at[rows, columns]))

    for n in range(4):
        add_piece(gdown, ddown, n * thin)
    for n in range(2):
        add_piece(gup, dup, n * thin, 0)
        add_piece(gup, dup, n * thin, width)
    for n in range(2):
        add_piece(gwo, dwo, n * thin)
    count = len(pieces)
    own, first, second, third, fourth = (
        [buffers[count * n + f] for f in range(count)] for n in range(5)
    )
    legs = {}

    loads = [
        move.local(ks_in, ka.at[:, :, pl.ds(0, LANES)]),
        move.local(vs_in, va.at[:, :, pl.ds(0, LANES)]),
        move.local(qs_in, qs),
        move.local(do_in, do),
        move.local(oh_in, oh),
        move.local(lse_in, lse),
        move.local(cos_in, cosr),
        move.local(sin_in, sinr),
    ]
    here.enter(diagonal=True)
    held = []
    for f in range(count):
        source = pieces[f][0]
        legs[f] = move.send(source.at[:, :, :, 1 - c], first[f], here.core())
        held.append(move.local(source.at[:, :, :, c], own[f]))
    late_loads = [move.local(normed_in, normed), move.local(wg_in, wg)]

    def sum_first(f):
        legs[f].wait_recv()
        held[f].wait()

        def add(step, carry):
            own[f][step] = own[f][step] + first[f][step]
            return carry

        lax.fori_loop(0, depth, add, 0)
        if X_FIRST[f]:
            legs[f] = move.send(own[f].at[:, :, 1 - x], second[f], here.across_x())
        else:
            legs[f] = move.send(own[f].at[:, 1 - y], second[f], here.across_y())

    def sum_second(f):
        legs[f].wait_recv()

        def add(step, carry):
            for other in range(2):
                if X_FIRST[f]:
                    own[f][step, other, x] = own[f][step, other, x] + second[f][step, other]
                else:
                    own[f][step, y, other] = own[f][step, y, other] + second[f][step, other]
            return carry

        lax.fori_loop(0, depth, add, 0)
        if X_FIRST[f]:
            legs[f] = move.send(own[f].at[:, 1 - y, x], third[f], here.across_y())
        else:
            legs[f] = move.send(own[f].at[:, y, 1 - x], third[f], here.across_x())

    def sum_third(f):
        legs[f].wait_recv()

        def add(step, carry):
            own[f][step, y, x] = own[f][step, y, x] + third[f][step]
            return carry

        lax.fori_loop(0, depth, add, 0)
        legs[f] = [
            move.send(own[f].at[here.ahead(k), y, x], fourth[f].at[k - 1], here.along_z(k)) for k in steps_z
        ]

    def sum_last(f):
        total = own[f][z, y, x].astype(F32)
        for k in steps_z:
            legs[f][k - 1].wait_recv()
            total = total + fourth[f][k - 1].astype(F32)
        pieces[f][1][...] = total

    def bias_round(peer, slot):
        return move.send(btile, brecv.at[slot], peer)

    block = 128
    for copy in loads:
        copy.wait()

    def columns_of_segments(step, carry):
        rows = pl.ds(pl.multiple_of(step * block, block), block)
        segment, _ = frame_segments(lens, step * block, block, LANES)
        lane = lanes_of((block, LANES))
        same = segment == lane
        qaug[rows, :] = jnp.where((lane < SEGS) & jnp.logical_not(same), NEGATIVE, 0.0).astype(BF16)
        keyside = jnp.where((lane < SEGS) & same, 1.0, jnp.where((lane >= 4) & (lane < 7), 1.0, 0.0))
        for pair in range(2):
            ka[pair, rows, LANES:] = keyside.astype(BF16)
            va[pair, rows, LANES:] = jnp.where(lane < 3, 1.0, 0.0).astype(BF16)
        return carry

    lax.fori_loop(0, rows_all // block, columns_of_segments, 0)

    tall = 256
    steps = rows_all // tall

    def back_block(pair, step):
        rows = pl.ds(pl.multiple_of(step * tall, tall), tall)
        lane = lanes_of((tall, LANES))
        query, given = qs[pair, rows, :], do[pair, rows, :]
        overlap = given.astype(F32) * oh[pair, rows, :].astype(F32)
        mask_columns = qaug[rows, :].astype(F32)
        sums = lse[rows, :]
        grads_q, add_k, add_v = [], 0.0, 0.0
        for head in range(2):
            delta = jnp.sum(jnp.where((lane >= HEAD_DIM) == bool(head), overlap, 0.0), axis=1, keepdims=True)
            logsum = jnp.sum(jnp.where(lane == 2 * pair + head, sums, 0.0), axis=1, keepdims=True)
            a, b, d = three_parts(logsum)
            side = jnp.where(lane == 4, -a, jnp.where(lane == 5, -b, jnp.where(lane == 6, -d, mask_columns)))
            query_head = head_only(query, lane, head)
            left = jnp.concatenate([query_head, side.astype(BF16)], axis=1)
            a, b, d = three_parts(delta)
            side = jnp.where(lane == 0, -a, jnp.where(lane == 1, -b, jnp.where(lane == 2, -d, 0.0)))
            given_head = head_only(given, lane, head)
            right = jnp.concatenate([given_head, side.astype(BF16)], axis=1)
            weights = jnp.exp(across(ka[pair], left))
            grads = (weights * across(va[pair], right)).astype(BF16)
            add_v = add_v + product(weights.astype(BF16), given_head)
            add_k = add_k + product(grads, query_head)
            grads_q.append(from_rows(grads, ka[pair, :, :LANES]))
        dv_sum[...] += add_v
        dk_sum[...] += add_k
        grad_query = jnp.where(lane < HEAD_DIM, grads_q[0], grads_q[1]) * HEAD_DIM**-0.5
        gr[0, rows, pair * LANES : (pair + 1) * LANES] = turn_back(
            grad_query, cosr[rows, :], sinr[rows, :], lane
        ).astype(BF16)

    def back_some(pair, start, stop):
        lax.fori_loop(start, stop, lambda step, carry: (back_block(pair, step), carry)[1], 0)

    def settle_pair(pair):
        def body(step, carry):
            rows = pl.ds(pl.multiple_of(step * block, block), block)
            lane = lanes_of((block, LANES))
            part = slice(pair * LANES, (pair + 1) * LANES)
            gr[1, rows, part] = turn_back(dk_sum[rows, :], cosr[rows, :], sinr[rows, :], lane).astype(BF16)
            gr[2, rows, part] = dv_sum[rows, :].astype(BF16)
            return carry

        lax.fori_loop(0, rows_all // block, body, 0)

    def clear():
        dk_sum[...] = jnp.zeros_like(dk_sum)
        dv_sum[...] = jnp.zeros_like(dv_sum)

    def back_rows(target):
        def body(step, carry):
            rows = pl.ds(pl.multiple_of(target * span + step * block, block), block)
            total = 0.0
            for j in range(3):
                total = total + across(gr[j, rows, :], wg[j].reshape(MODEL_WIDTH, own_width))
            gnp[target, pl.ds(pl.multiple_of(step * block, block), block), :] = total.astype(BF16)
            return carry

        straight(0, span // block, body)

    away_other, away_same = (1 - x) * 2 + (1 - c), (1 - x) * 2 + c
    home_other = x * 2 + (1 - c)
    gn = {}

    def rows_away():
        for copy in late_loads:
            copy.wait()
        back_rows(away_other)
        gn["core"] = move.send(gnp.at[away_other], gnr.at[0], here.core())

    def rows_across():
        back_rows(away_same)
        gn["core"].wait_recv()

        def add_rows(step, carry):
            rows = pl.ds(pl.multiple_of(step * block, block), block)
            gnp[away_same, rows, :] = gnp[away_same, rows, :] + gnr[0, rows, :]
            return carry

        lax.fori_loop(0, span // block, add_rows, 0)
        gn["x"] = move.send(gnp.at[away_same], gnx, here.across_x())

    def rows_home():
        back_rows(home_other)
        gn["home"] = move.send(gnp.at[home_other], gnr.at[1], here.core())
        back_rows(g)

    tile = 256

    def weight_rows(j):
        def body(step, carry):
            columns = pl.ds(pl.multiple_of(step * tile, tile), tile)
            result = from_rows(normed[:, columns], gr[j]).astype(BF16)
            per = 2 * 4 * shard // tile
            lead = result.reshape(tile // (4 * shard), 4, shard, own_width)
            for n in range(tile // (4 * shard)):
                gw[j, step // per, (step % per) * (tile // (4 * shard)) + n] = lead[n]
            return carry

        straight(0, MODEL_WIDTH // tile, body)

    gw_y, gw_z = {}, {}

    def weights_y(j):
        weight_rows(j)
        gw_y[j] = move.send(gw.at[j, :, 1 - y], gwy.at[j], here.across_y())

    def weights_z(j):
        gw_y[j].wait_recv()

        def add(step, carry):
            gw[j, step, y] = gw[j, step, y] + gwy[j, step]
            return carry

        lax.fori_loop(0, depth, add, 0)
        gw_z[j] = [move.send(gw.at[j, here.ahead(k), y], gwz.at[j, k - 1], here.along_z(k)) for k in steps_z]

    outs = (dwq, dwk, dwv)
    final = []
    final_locals = []

    def weights_last(j):
        total = gw[j, z, y].astype(F32)
        for k in steps_z:
            gw_z[j][k - 1].wait_recv()
            total = total + gwz[j, k - 1].astype(F32)
        gsum[j] = total
        columns = pl.ds(pl.multiple_of(g * own_width, LANES), own_width)
        final_locals.append(move.local(gsum.at[j, g], outs[j].at[:, columns]))
        for k in (1, 2, 3):
            final.append(move.send(gsum.at[j, (g + k) % 4], outs[j].at[:, columns], here.row_peer(k)))

    bias_legs = []

    def bias_start():
        ones = jnp.ones((16, rows_all), BF16)
        btile[...] = bias_in[...]
        for j in range(3):
            sums = product(ones, gr[j])
            for half in range(2):
                btile[pl.ds(8 * j + g * 2 + half, 1), :] = sums[0:1, half * LANES : (half + 1) * LANES]
        bias_legs.append(move.send(btile, brecv.at[0], here.core()))

    def bias_next():
        done = len(bias_legs)
        bias_legs[-1].wait()
        btile[...] = btile[...] + brecv[done - 1]
        if done < 3:
            peer = (here.across_x, here.across_y)[done - 1]()
            bias_legs.append(move.send(btile, brecv.at[done], peer))
        else:
            bias_legs.extend([move.send(btile, bz.at[k - 1], here.along_z(k)) for k in steps_z])

    def bias_last():
        for copy in bias_legs[3:]:
            copy.wait()
        total = btile[...]
        for k in steps_z:
            total = total + bz[k - 1]
        btile[...] = total

    high, middle, rest_part = three_parts(mods[0:4, MODEL_WIDTH : 2 * MODEL_WIDTH])
    mod3[0:4, :] = high
    mod3[4:8, :] = middle
    mod3[8:12, :] = rest_part
    mod3[12:16, :] = jnp.zeros((4, MODEL_WIDTH), F32)
    acc_shift[...] = jnp.zeros_like(acc_shift)
    acc_scale[...] = jnp.zeros_like(acc_scale)
    def two_parts(values):
        top = values.astype(BF16)
        return top, (values - top.astype(F32)).astype(BF16)

    def norm_rows(step, carry):
        rows = pl.ds(pl.multiple_of(step * block, block), block)
        grad = gnp[g, rows, :].astype(F32) + gnr[1, rows, :].astype(F32) + gnx[rows, :].astype(F32)
        values = frames[rows, :].astype(F32)
        center = jnp.mean(values, axis=1, keepdims=True)
        centered = values - center
        scaled = lax.rsqrt(jnp.mean(centered * centered, axis=1, keepdims=True) + EPSILON)
        hat = centered * scaled
        base = g * span + step * block
        segment, _ = frame_segments(lens, base, block, 16)
        slot = lanes_of((block, 16))
        chosen = jnp.where((slot < 12) & (slot % 4 == segment), 1.0, 0.0).astype(BF16)
        inner = grad * (1.0 + product(chosen, mod3[...].astype(BF16)))
        mean_one = jnp.mean(inner, axis=1, keepdims=True)
        mean_two = jnp.mean(inner * hat, axis=1, keepdims=True)
        fgrad[rows, :] = (gmid[rows, :] + scaled * (inner - mean_one - hat * mean_two)).astype(BF16)
        position = base + lanes_of((16, block))
        begin = [lens[0, 0], lens[0, 0] + lens[0, 1], lens[0, 0] + lens[0, 1] + lens[0, 2]]
        inside = sum((position >= edge).astype(jnp.int32) for edge in begin)
        members = jnp.where(inside == lanes_of((16, block), 0), 1.0, 0.0).astype(BF16)
        for values, target in ((grad, acc_shift), (grad * hat, acc_scale)):
            top, bottom = two_parts(values)
            target[...] += product(members, top) + product(members, bottom)
        return carry

    fourth_part = MODEL_WIDTH // 2
    mod_legs = {}

    def mods_core():
        for side in range(2):
            mg[side] = mg_in[:, side * fourth_part : (side + 1) * fourth_part]
        mod_legs["core"] = move.send(mg.at[1 - c], mgr, here.core())

    def mods_x():
        mod_legs["core"].wait_recv()
        mgs[...] = mg[c] + mgr[...]
        mod_legs["x"] = move.send(mgs, mgx, here.across_x())

    def mods_z():
        mod_legs["x"].wait_recv()
        ev[z, y, c] = (mgs[...] + mgx[...]).astype(BF16)
        mod_legs["z"] = [move.send(ev.at[z, y, c], ev.at[z, y, c], here.along_z(k)) for k in steps_z]

    def mods_y():
        for copy in mod_legs["z"]:
            copy.wait_recv()
        mod_legs["y"] = move.send(ev.at[:, y, c], ev.at[:, y, c], here.across_y())

    def mods_share():
        mod_legs["y"].wait_recv()
        mod_legs["last"] = move.send(ev.at[:, :, c], ev.at[:, :, c], here.core())

    every_row = 32 * depth
    picks = jnp.where(
        lanes_of((16, every_row), 0) == (lanes_of((16, every_row)) % 16) // 4, 1.0, 0.0
    ).astype(BF16)

    def place_columns(every, start, stride):
        size = every.shape[1]
        result = from_rows(low[...], every)
        summed = product(picks, every)
        for strip in range(4):
            columns = slice(start + strip * stride, start + strip * stride + size)
            dmw[:, columns] = result[32 * strip : 32 * (strip + 1), :]
            mbias[0:1, columns] = summed[strip : strip + 1, :]

    def mods_early():
        mod_legs["last"].wait_recv()
        for side in range(2):
            every = ev[:, :, side].reshape(every_row, fourth_part)
            place_columns(every, 2 * MODEL_WIDTH + side * fourth_part, MODEL_WIDTH)

    def norm_part():
        gn["home"].wait_recv()
        gn["x"].wait_recv()
        straight(0, span // block, norm_rows)
        late[0, 0:4, :] = acc_shift[0:4, :]
        late[0, 4:8, :] = acc_scale[0:4, :]
        mod_legs["row"] = [move.send(late.at[0], late.at[k], here.row_peer(k)) for k in (1, 2, 3)]

    def mods_rows():
        for copy in mod_legs["row"]:
            copy.wait_recv()
        total = (late[0] + late[1]) + (late[2] + late[3])
        joined[0:4, :] = total[0:4, :fourth_part]
        joined[4:8, :] = total[0:4, fourth_part:]
        joined[8:12, :] = total[4:8, :fourth_part]
        joined[12:16, :] = total[4:8, fourth_part:]
        ez[z, y] = joined[...].astype(BF16)
        peers = [here.along_z(k) for k in steps_z] + [here.across_y()]
        peers += [here.at(here.ahead(k), 1 - y, x, c) for k in steps_z]
        mod_legs["all"] = [move.send(ez.at[z, y], ez.at[z, y], peer) for peer in peers]

    def mods_late():
        for copy in mod_legs["all"]:
            copy.wait_recv()
        place_columns(ez[...].reshape(every_row, fourth_part), 0, fourth_part)

    stages = {
        SUM_ONE: sum_first, SUM_TWO: sum_second, SUM_THREE: sum_third, SUM_LAST: sum_last,
        WEIGHTS_Y: weights_y, WEIGHTS_Z: weights_z, WEIGHTS_LAST: weights_last,
    }
    others = {
        ROWS_AWAY: rows_away, ROWS_ACROSS: rows_across, ROWS_HOME: rows_home, NORM: norm_part,
        EARLY_CORE: mods_core, EARLY_X: mods_x, EARLY_Z: mods_z, EARLY_Y: mods_y, EARLY_SHARE: mods_share, EARLY_DONE: mods_early,
        LATE_ROWS: mods_rows, LATE_DONE: mods_late, BIAS_START: bias_start, BIAS_NEXT: bias_next, BIAS_DONE: bias_last,
    }
    clear()
    done = 0
    for code, number in BACKWARD_ORDER:
        if code == ATTEND_BACK:
            ahead = number
            while ahead:
                pair, at = done // steps, done % steps
                now = min(ahead, steps - at)
                back_some(pair, at, at + now)
                done, ahead = done + now, ahead - now
                if done % steps == 0:
                    settle_pair(pair)
                    if pair == 0:
                        clear()
        elif code in others:
            others[code]()
        else:
            stages[code](number)
    for copy in final_locals:
        copy.wait()
    for copy in final:
        copy.wait_recv()
    move.finish(but=bias_legs)


def backward_call(depth, span, own_rows, down_rows, hidden, args):
    rows_all, own_width = 4 * span, MODEL_WIDTH // 4
    half = MODEL_WIDTH // 2
    vmem, anywhere, scalar = (
        pl.BlockSpec(memory_space=pltpu.VMEM),
        pl.BlockSpec(memory_space=pl.ANY),
        pl.BlockSpec(memory_space=pltpu.SMEM),
    )

    def out(shape, dtype):
        return jax.ShapeDtypeStruct(shape, dtype)

    outs = [
        (out((span, MODEL_WIDTH), BF16), vmem),
        (out((own_rows, MODEL_WIDTH), F32), anywhere),
        (out((own_rows, MODEL_WIDTH), F32), anywhere),
        (out((own_rows, MODEL_WIDTH), F32), anywhere),
        (out((own_rows, MODEL_WIDTH), F32), vmem),
        (out((own_rows, hidden), F32), vmem),
        (out((down_rows, MODEL_WIDTH), F32), vmem),
        (out((own_rows, 6 * MODEL_WIDTH), F32), vmem),
        (out((8, 6 * MODEL_WIDTH), F32), vmem),
        (out((56, LANES), F32), vmem),
    ]
    pair_rows = pltpu.VMEM((2, rows_all, LANES), BF16)
    wide_rows = pltpu.VMEM((2, rows_all, 2 * LANES), BF16)
    table = pltpu.VMEM((rows_all, LANES), F32)
    scratch = [
        pair_rows, pair_rows, pair_rows, table,
        pltpu.VMEM((rows_all, MODEL_WIDTH), BF16),
        pltpu.VMEM((3, depth, 2, 4, own_rows, own_width), BF16),
        table, table, wide_rows, wide_rows,
        pltpu.VMEM((rows_all, LANES), BF16),
        table, table,
        pltpu.VMEM((3, rows_all, own_width), BF16),
        pltpu.VMEM((3, depth, 2, 4, own_rows, own_width), BF16),
        pltpu.VMEM((3, depth, 4, own_rows, own_width), BF16),
        pltpu.VMEM((3, depth - 1, 4, own_rows, own_width), BF16),
        pltpu.VMEM((3, 4, own_rows, own_width), F32),
        pltpu.VMEM((4, span, MODEL_WIDTH), BF16),
        pltpu.VMEM((2, span, MODEL_WIDTH), BF16),
        pltpu.VMEM((span, MODEL_WIDTH), BF16),
        pltpu.VMEM((16, MODEL_WIDTH), F32),
        pltpu.VMEM((16, MODEL_WIDTH), F32),
        pltpu.VMEM((16, MODEL_WIDTH), F32),
        pltpu.VMEM((2, 16, half), F32),
        pltpu.VMEM((16, half), F32),
        pltpu.VMEM((16, half), F32),
        pltpu.VMEM((16, half), F32),
        pltpu.VMEM((depth, 2, 2, 16, half), BF16),
        pltpu.VMEM((4, 8, MODEL_WIDTH), F32),
        pltpu.VMEM((16, half), F32),
        pltpu.VMEM((depth, 2, 16, half), BF16),
        pltpu.VMEM((3, 56, LANES), F32),
        pltpu.VMEM((depth - 1, 56, LANES), F32),
    ]
    piece = (own_rows // 2, MODEL_WIDTH)
    for lead in ((depth, 2, 2), (depth, 2, 2), (depth, 2), (depth,), (depth - 1,)):
        scratch += [pltpu.VMEM(lead + piece, BF16)] * 10
    scratch += [pltpu.SemaphoreType.DMA((128,)), pltpu.SemaphoreType.DMA((128,)), pltpu.SemaphoreType.DMA((32,))]
    return pl.pallas_call(
        partial(backward_kernel, depth),
        out_shape=[shape for shape, _ in outs],
        in_specs=[scalar] + [anywhere] * 10 + [vmem] * 6 + [anywhere] * 3,
        out_specs=[spec for _, spec in outs],
        scratch_shapes=scratch,
        compiler_params=pltpu.CompilerParams(
            collective_id=1, has_side_effects=True, vmem_limit_bytes=62 * 1024 * 1024
        ),
        cost_estimate=pl.CostEstimate(flops=2 * 10**10, bytes_accessed=40 * 10**6, transcendentals=10**7),
    )(*args)


def modulated_norm(values, shift_part, scale_part):
    center = jnp.mean(values, axis=-1, keepdims=True)
    centered = values - center
    variance = jnp.mean(centered * centered, axis=-1, keepdims=True)
    return centered * lax.rsqrt(variance + EPSILON) * (1.0 + scale_part) + shift_part


def rotate(values, cosines, sines_table):
    shaped = values.reshape(values.shape[:-1] + (values.shape[-1] // HEAD_DIM, HEAD_DIM))
    first_half = shaped[..., : HEAD_DIM // 2]
    second_half = shaped[..., HEAD_DIM // 2 :]
    cosine = cosines[..., None, :]
    sine_part = sines_table[..., None, :]
    turned = jnp.concatenate(
        [
            first_half * cosine - second_half * sine_part,
            second_half * cosine + first_half * sine_part,
        ],
        axis=-1,
    )
    return turned.reshape(values.shape)


def gelu_tanh(values):
    return jax.nn.gelu(values, approximate=True)


def time_features(time_index):
    halfway = MODEL_WIDTH // 2
    frequency = jnp.exp(jnp.arange(halfway, dtype=jnp.float32) * (-math.log(10000.0) / halfway))
    angles = time_index.astype(jnp.float32)[..., None] * frequency
    return jnp.concatenate([jnp.sin(angles), jnp.cos(angles)], axis=-1)


def segment_starts(segment_lengths):
    return jnp.cumsum(segment_lengths, axis=1) - segment_lengths


def segment_numbers(segment_lengths, frame_positions):
    starts = segment_starts(segment_lengths)
    inside = (frame_positions[None, :, None] >= starts[:, None, :]).astype(jnp.int32)
    return jnp.sum(inside, axis=2) - 1


def segment_layout(segment_lengths, frame_positions):
    starts = segment_starts(segment_lengths)
    segment = segment_numbers(segment_lengths, frame_positions)
    onehot = (segment[..., None] == jnp.arange(SEGS, dtype=jnp.int32)).astype(jnp.float32)
    offset = jnp.sum(onehot * starts[:, None, :].astype(jnp.float32), axis=2)
    relative = frame_positions[None, :].astype(jnp.float32) - offset
    return (onehot, relative)


def rope_tables(relative):
    halfway = HEAD_DIM // 2
    frequency = jnp.exp(jnp.arange(halfway, dtype=jnp.float32) * (-math.log(10000.0) / halfway))
    angles = relative[..., None] * frequency
    return (jnp.cos(angles), jnp.sin(angles))


def project(values, matrix, offset):
    return jnp.einsum(
        "rld,de->rle", values, matrix, preferred_element_type=jnp.float32
    ) + offset.astype(jnp.float32)


def project_back(gradient, matrix):
    return jnp.einsum("rle,de->rld", gradient, matrix, preferred_element_type=jnp.float32)


def weight_gradient(values, gradient):
    return jnp.einsum("rld,rle->de", values, gradient, preferred_element_type=jnp.float32)


def bias_gradient(gradient):
    return jnp.sum(gradient.astype(jnp.float32), axis=(0, 1))


def lift_up(member):
    return member.reshape((1, 1) + member.shape)


def settle(member):
    return member.reshape((-1,) + member.shape[3:])


def spread(member, wide_count, narrow_count):
    return member.reshape((wide_count, narrow_count, -1) + member.shape[1:])


def unpack(member):
    return member.reshape(member.shape[2:])


def on_device(
    frames,
    output_gradient,
    segment_lengths,
    time_index,
    query_weight,
    query_bias,
    key_weight,
    key_bias,
    value_weight,
    value_bias,
    output_projection,
    output_bias,
    up_weight,
    up_bias,
    down_weight,
    down_bias,
    modulation_weight,
    modulation_bias,
):
    narrow_count = lax.axis_size("seq")
    wide_count = lax.axis_size("dp")
    seq_index = lax.axis_index("seq")
    row_count, span_frames, width_total = frames.shape
    row_length = span_frames * narrow_count
    block_rows = min(512, row_length)
    block_count = row_length // block_rows
    local_weights = (
        query_weight,
        query_bias,
        key_weight,
        key_bias,
        value_weight,
        value_bias,
        output_projection,
        output_bias,
        up_weight,
        up_bias,
        down_weight,
        down_bias,
        modulation_bias,
    )
    lifted = [lift_up(member) for member in local_weights]
    halfway_set = (
        lax.all_gather(lifted[0], "dp", axis=0, tiled=True),
        lax.all_gather(lifted[1], "dp", axis=0, tiled=True),
        lax.all_gather(lifted[2], "dp", axis=0, tiled=True),
        lax.all_gather(lifted[3], "dp", axis=0, tiled=True),
        lax.all_gather(lifted[4], "dp", axis=0, tiled=True),
        lax.all_gather(lifted[5], "dp", axis=0, tiled=True),
        lax.all_gather(lifted[6], "dp", axis=0, tiled=True),
        lax.all_gather(lifted[7], "dp", axis=0, tiled=True),
        lax.all_gather(lifted[8], "dp", axis=0, tiled=True),
        lax.all_gather(lifted[9], "dp", axis=0, tiled=True),
        lax.all_gather(lifted[10], "dp", axis=0, tiled=True),
        lax.all_gather(lifted[11], "dp", axis=0, tiled=True),
        lax.all_gather(lifted[12], "dp", axis=0, tiled=True),
    )
    complete_set = (
        lax.all_gather(halfway_set[0], "seq", axis=1, tiled=True),
        lax.all_gather(halfway_set[1], "seq", axis=1, tiled=True),
        lax.all_gather(halfway_set[2], "seq", axis=1, tiled=True),
        lax.all_gather(halfway_set[3], "seq", axis=1, tiled=True),
        lax.all_gather(halfway_set[4], "seq", axis=1, tiled=True),
        lax.all_gather(halfway_set[5], "seq", axis=1, tiled=True),
        lax.all_gather(halfway_set[6], "seq", axis=1, tiled=True),
        lax.all_gather(halfway_set[7], "seq", axis=1, tiled=True),
        lax.all_gather(halfway_set[8], "seq", axis=1, tiled=True),
        lax.all_gather(halfway_set[9], "seq", axis=1, tiled=True),
        lax.all_gather(halfway_set[10], "seq", axis=1, tiled=True),
        lax.all_gather(halfway_set[11], "seq", axis=1, tiled=True),
        lax.all_gather(halfway_set[12], "seq", axis=1, tiled=True),
    )
    gathered = [settle(member) for member in complete_set]
    (
        full_query,
        full_query_bias,
        full_key,
        full_key_bias,
        full_value,
        full_value_bias,
        full_output,
        full_output_bias,
        full_up,
        full_up_bias,
        full_down,
        full_down_bias,
        full_modulation_bias,
    ) = gathered
    local_positions = seq_index * span_frames + jnp.arange(span_frames, dtype=jnp.int32)
    local_onehot, local_relative = segment_layout(segment_lengths, local_positions)
    row_segment = segment_numbers(segment_lengths, jnp.arange(row_length, dtype=jnp.int32))
    cosines, sines_table = rope_tables(local_relative)
    turning = partial(rotate, cosines=cosines, sines_table=sines_table)
    owned_rows = modulation_weight.shape[0]
    owned_start = (lax.axis_index("dp") * narrow_count + seq_index) * owned_rows
    every_time = lax.all_gather(time_index, "dp", axis=0, tiled=True)
    every_low = jax.nn.silu(time_features(every_time)).astype(jnp.bfloat16)
    owned_low = lax.dynamic_slice_in_dim(every_low, owned_start, owned_rows, 2)
    partial_modulation = jnp.einsum(
        "rsd,dc->rsc", owned_low, modulation_weight, preferred_element_type=jnp.float32
    )
    row_share = lax.psum_scatter(partial_modulation, "dp", scatter_dimension=0, tiled=True)
    modulation = lax.psum(row_share.astype(jnp.bfloat16), "seq").astype(
        jnp.float32
    ) + full_modulation_bias.astype(jnp.float32)
    per_frame = jnp.einsum("rls,rsc->rlc", local_onehot, modulation, precision=HIGHEST)
    shift_one, scale_one, gate_one, shift_two, scale_two, gate_two = jnp.split(
        per_frame, 6, axis=-1
    )
    inputs = frames.astype(jnp.float32)
    normed, norm_back = jax.vjp(modulated_norm, inputs, shift_one, scale_one)
    normed_low = normed.astype(jnp.bfloat16)
    query_pre = project(normed_low, full_query, full_query_bias)
    key_pre = project(normed_low, full_key, full_key_bias)
    value_low = project(normed_low, full_value, full_value_bias).astype(jnp.bfloat16)
    query_turned, query_back = jax.vjp(turning, query_pre)
    key_turned, key_back = jax.vjp(turning, key_pre)
    query_heads, key_heads, value_heads = (
        lax.all_to_all(
            query_turned.astype(jnp.bfloat16), "seq", split_axis=2, concat_axis=1, tiled=True
        ),
        lax.all_to_all(
            key_turned.astype(jnp.bfloat16), "seq", split_axis=2, concat_axis=1, tiled=True
        ),
        lax.all_to_all(value_low, "seq", split_axis=2, concat_axis=1, tiled=True),
    )
    local_heads = query_heads.shape[2] // HEAD_DIM
    head_shape = (row_count, row_length, local_heads, HEAD_DIM)
    queries = query_heads.reshape(head_shape)
    keys_all = key_heads.reshape(head_shape)
    values_all = value_heads.reshape(head_shape)
    scaling = HEAD_DIM ** (-0.5)
    positions_all = jnp.arange(row_count * block_count, dtype=jnp.int32)

    def fetch_block(position):
        row_index = position // block_count
        start_row = position % block_count * block_rows
        key_row = lax.dynamic_index_in_dim(keys_all, row_index, 0, keepdims=False)
        value_row = lax.dynamic_index_in_dim(values_all, row_index, 0, keepdims=False)
        segment_row = lax.dynamic_index_in_dim(row_segment, row_index, 0, keepdims=False)
        query_block = lax.dynamic_slice_in_dim(
            lax.dynamic_index_in_dim(queries, row_index, 0, keepdims=False),
            start_row,
            block_rows,
            0,
        )
        segment_block = lax.dynamic_slice_in_dim(segment_row, start_row, block_rows, 0)
        scores = (
            jnp.einsum("bhd,khd->hbk", query_block, key_row, preferred_element_type=jnp.float32)
            * scaling
        )
        scores = jnp.where((segment_block[:, None] == segment_row[None, :])[None], scores, NEGATIVE)
        return (row_index, start_row, query_block, key_row, value_row, scores)

    def forward_block(position):
        row_index, start_row, query_block, key_row, value_row, scores = fetch_block(position)
        highest = jnp.max(scores, axis=2, keepdims=True)
        weights = jnp.exp(scores - highest)
        totals = jnp.sum(weights, axis=2, keepdims=True)
        probabilities = (weights / totals).astype(jnp.bfloat16)
        mixed_block = jnp.einsum(
            "hbk,khd->bhd", probabilities, value_row, preferred_element_type=jnp.float32
        )
        return (
            mixed_block.astype(jnp.bfloat16).reshape(block_rows, -1),
            (highest + jnp.log(totals))[..., 0],
        )

    mixed_blocks, logsums = lax.map(forward_block, positions_all)
    attention_heads = mixed_blocks.reshape(row_count, row_length, -1)
    attention_frames = lax.all_to_all(
        attention_heads, "seq", split_axis=1, concat_axis=2, tiled=True
    )
    branch = project(attention_frames, full_output, full_output_bias)
    middle = inputs + gate_one * branch
    normed_two, norm_two_back = jax.vjp(modulated_norm, middle, shift_two, scale_two)
    normed_two_low = normed_two.astype(jnp.bfloat16)
    hidden = project(normed_two_low, full_up, full_up_bias)
    activated, gelu_back = jax.vjp(gelu_tanh, hidden)
    activated_low = activated.astype(jnp.bfloat16)
    branch_two = project(activated_low, full_down, full_down_bias)
    layer_output = (middle + gate_two * branch_two).astype(jnp.bfloat16)
    cotangent = output_gradient.astype(jnp.float32)
    grad_branch_two = (gate_two * cotangent).astype(jnp.bfloat16)
    grad_gate_two = cotangent * branch_two
    grad_activated = project_back(grad_branch_two, full_down)
    grad_hidden = gelu_back(grad_activated)[0].astype(jnp.bfloat16)
    grad_normed_two = project_back(grad_hidden, full_up)
    grad_middle_part, grad_shift_two, grad_scale_two = norm_two_back(grad_normed_two)
    grad_middle = cotangent + grad_middle_part
    grad_gate_one = grad_middle * branch
    grad_branch = (gate_one * grad_middle).astype(jnp.bfloat16)
    grad_attention = project_back(grad_branch, full_output).astype(jnp.bfloat16)
    grad_heads = lax.all_to_all(grad_attention, "seq", split_axis=2, concat_axis=1, tiled=True)
    grad_outputs = grad_heads.reshape(head_shape)

    def backward_block(running, pair_inputs):
        grad_keys, grad_values = running
        position, logsum = pair_inputs
        row_index, start_row, query_block, key_row, value_row, scores = fetch_block(position)
        grad_block = lax.dynamic_slice_in_dim(
            lax.dynamic_index_in_dim(grad_outputs, row_index, 0, keepdims=False),
            start_row,
            block_rows,
            0,
        )
        probabilities = jnp.exp(scores - logsum[..., None])
        grad_probabilities = jnp.einsum(
            "bhd,khd->hbk", grad_block, value_row, preferred_element_type=jnp.float32
        )
        delta_sum = jnp.sum(probabilities * grad_probabilities, axis=2, keepdims=True)
        grad_scores = (probabilities * (grad_probabilities - delta_sum)).astype(jnp.bfloat16)
        grad_query_block = (
            jnp.einsum("hbk,khd->bhd", grad_scores, key_row, preferred_element_type=jnp.float32)
            * scaling
        )
        key_part = (
            jnp.einsum("hbk,bhd->khd", grad_scores, query_block, preferred_element_type=jnp.float32)
            * scaling
        )
        value_part = jnp.einsum(
            "hbk,bhd->khd",
            probabilities.astype(jnp.bfloat16),
            grad_block,
            preferred_element_type=jnp.float32,
        )
        grad_keys = lax.dynamic_update_index_in_dim(
            grad_keys,
            lax.dynamic_index_in_dim(grad_keys, row_index, 0, keepdims=False) + key_part,
            row_index,
            0,
        )
        grad_values = lax.dynamic_update_index_in_dim(
            grad_values,
            lax.dynamic_index_in_dim(grad_values, row_index, 0, keepdims=False) + value_part,
            row_index,
            0,
        )
        return (
            (grad_keys, grad_values),
            grad_query_block.astype(jnp.bfloat16).reshape(block_rows, -1),
        )

    zero_heads = jnp.zeros(head_shape, jnp.float32)
    (grad_keys_all, grad_values_all), grad_query_blocks = lax.scan(
        backward_block, (zero_heads, zero_heads), (positions_all, logsums)
    )
    flat_shape = (row_count, row_length, -1)
    grad_query_frames, grad_key_frames, grad_value_frames = (
        lax.all_to_all(
            grad_query_blocks.reshape(flat_shape), "seq", split_axis=1, concat_axis=2, tiled=True
        ),
        lax.all_to_all(
            grad_keys_all.reshape(flat_shape).astype(jnp.bfloat16),
            "seq",
            split_axis=1,
            concat_axis=2,
            tiled=True,
        ),
        lax.all_to_all(
            grad_values_all.reshape(flat_shape).astype(jnp.bfloat16),
            "seq",
            split_axis=1,
            concat_axis=2,
            tiled=True,
        ),
    )
    grad_query_pre = query_back(grad_query_frames.astype(jnp.float32))[0].astype(jnp.bfloat16)
    grad_key_pre = key_back(grad_key_frames.astype(jnp.float32))[0].astype(jnp.bfloat16)
    grad_normed = (
        project_back(grad_query_pre, full_query)
        + project_back(grad_key_pre, full_key)
        + project_back(grad_value_frames, full_value)
    )
    grad_inputs_part, grad_shift_one, grad_scale_one = norm_back(grad_normed)
    frames_grad = (grad_middle + grad_inputs_part).astype(jnp.bfloat16)
    grad_per_frame = jnp.concatenate(
        [
            grad_shift_one,
            grad_scale_one,
            grad_gate_one,
            grad_shift_two,
            grad_scale_two,
            grad_gate_two,
        ],
        axis=-1,
    )
    grad_modulation = jnp.einsum("rls,rlc->rsc", local_onehot, grad_per_frame, precision=HIGHEST)
    gradients = (
        weight_gradient(normed_low, grad_query_pre),
        bias_gradient(grad_query_pre),
        weight_gradient(normed_low, grad_key_pre),
        bias_gradient(grad_key_pre),
        weight_gradient(normed_low, grad_value_frames),
        bias_gradient(grad_value_frames),
        weight_gradient(attention_frames, grad_branch),
        bias_gradient(grad_branch),
        weight_gradient(normed_two_low, grad_hidden),
        bias_gradient(grad_hidden),
        weight_gradient(activated_low, grad_branch_two),
        bias_gradient(grad_branch_two),
        jnp.sum(grad_modulation, axis=(0, 1)),
    )
    row_total = lax.psum(grad_modulation.astype(jnp.bfloat16), "seq").astype(jnp.float32)
    every_grad = lax.all_gather(row_total.astype(jnp.bfloat16), "dp", axis=0, tiled=True).astype(
        row_total.dtype
    )
    modulation_weight_grad = jnp.einsum(
        "rsd,rsc->dc", owned_low.astype(jnp.float32), every_grad, precision=HIGHEST
    )
    spreaded = [spread(member, wide_count, narrow_count) for member in gradients]
    first_pass = (
        lax.psum_scatter(
            spreaded[0].astype(jnp.bfloat16), "seq", scatter_dimension=1, tiled=True
        ).astype(jnp.float32),
        lax.psum_scatter(
            spreaded[1].astype(jnp.bfloat16), "seq", scatter_dimension=1, tiled=True
        ).astype(jnp.float32),
        lax.psum_scatter(
            spreaded[2].astype(jnp.bfloat16), "seq", scatter_dimension=1, tiled=True
        ).astype(jnp.float32),
        lax.psum_scatter(
            spreaded[3].astype(jnp.bfloat16), "seq", scatter_dimension=1, tiled=True
        ).astype(jnp.float32),
        lax.psum_scatter(
            spreaded[4].astype(jnp.bfloat16), "seq", scatter_dimension=1, tiled=True
        ).astype(jnp.float32),
        lax.psum_scatter(
            spreaded[5].astype(jnp.bfloat16), "seq", scatter_dimension=1, tiled=True
        ).astype(jnp.float32),
        lax.psum_scatter(
            spreaded[6].astype(jnp.bfloat16), "seq", scatter_dimension=1, tiled=True
        ).astype(jnp.float32),
        lax.psum_scatter(
            spreaded[7].astype(jnp.bfloat16), "seq", scatter_dimension=1, tiled=True
        ).astype(jnp.float32),
        lax.psum_scatter(
            spreaded[8].astype(jnp.bfloat16), "seq", scatter_dimension=1, tiled=True
        ).astype(jnp.float32),
        lax.psum_scatter(
            spreaded[9].astype(jnp.bfloat16), "seq", scatter_dimension=1, tiled=True
        ).astype(jnp.float32),
        lax.psum_scatter(
            spreaded[10].astype(jnp.bfloat16), "seq", scatter_dimension=1, tiled=True
        ).astype(jnp.float32),
        lax.psum_scatter(
            spreaded[11].astype(jnp.bfloat16), "seq", scatter_dimension=1, tiled=True
        ).astype(jnp.float32),
        lax.psum_scatter(
            spreaded[12].astype(jnp.bfloat16), "seq", scatter_dimension=1, tiled=True
        ).astype(jnp.float32),
    )
    second_pass = (
        lax.psum_scatter(first_pass[0], "dp", scatter_dimension=0, tiled=True),
        lax.psum_scatter(first_pass[1], "dp", scatter_dimension=0, tiled=True),
        lax.psum_scatter(first_pass[2], "dp", scatter_dimension=0, tiled=True),
        lax.psum_scatter(first_pass[3], "dp", scatter_dimension=0, tiled=True),
        lax.psum_scatter(first_pass[4], "dp", scatter_dimension=0, tiled=True),
        lax.psum_scatter(first_pass[5], "dp", scatter_dimension=0, tiled=True),
        lax.psum_scatter(first_pass[6], "dp", scatter_dimension=0, tiled=True),
        lax.psum_scatter(first_pass[7], "dp", scatter_dimension=0, tiled=True),
        lax.psum_scatter(first_pass[8], "dp", scatter_dimension=0, tiled=True),
        lax.psum_scatter(first_pass[9], "dp", scatter_dimension=0, tiled=True),
        lax.psum_scatter(first_pass[10], "dp", scatter_dimension=0, tiled=True),
        lax.psum_scatter(first_pass[11], "dp", scatter_dimension=0, tiled=True),
        lax.psum_scatter(first_pass[12], "dp", scatter_dimension=0, tiled=True),
    )
    reduced = [unpack(member) for member in second_pass]
    return (
        layer_output,
        frames_grad,
        reduced[0],
        reduced[1],
        reduced[2],
        reduced[3],
        reduced[4],
        reduced[5],
        reduced[6],
        reduced[7],
        reduced[8],
        reduced[9],
        reduced[10],
        reduced[11],
        modulation_weight_grad,
        reduced[12],
    )


def hand_over_kernel(count, *refs):
    copies = [
        pltpu.make_async_copy(source, target, refs[-1].at[n])
        for n, (source, target) in enumerate(zip(refs[:count], refs[count : 2 * count]))
    ]
    for copy in copies:
        copy.start()
    for copy in copies:
        copy.wait()


def hand_over(*arrays):
    anywhere = pl.BlockSpec(memory_space=pl.ANY)
    return pl.pallas_call(
        partial(hand_over_kernel, len(arrays)),
        out_shape=[jax.ShapeDtypeStruct(array.shape, array.dtype) for array in arrays],
        in_specs=[pl.BlockSpec(memory_space=pltpu.VMEM)] * len(arrays),
        out_specs=[anywhere] * len(arrays),
        scratch_shapes=[pltpu.SemaphoreType.DMA((len(arrays),))],
    )(*arrays)


def on_device_fast(
    frames, output_gradient, segment_lengths, time_index, query_weight, query_bias, key_weight, key_bias,
    value_weight, value_bias, output_projection, output_bias, up_weight, up_bias, down_weight, down_bias,
    modulation_weight, modulation_bias,
):
    seq_index, dp_index = lax.axis_index("seq"), lax.axis_index("dp")
    depth = lax.axis_size("dp") // 2
    own_index = dp_index * 4 + seq_index
    _, span, width = frames.shape
    own_rows, hidden = up_weight.shape
    down_rows = down_weight.shape[0]
    vectors = (query_bias, key_bias, value_bias, output_bias, up_bias, down_bias, modulation_bias)
    biases = [vector.reshape(1, -1) for vector in vectors]
    (output, grad_middle, mg_in, bias_in, mods, low, gwo, gup, gdown, given_heads, qs, ks, vs, oh, lse, normed, wg,
     cosr, sinr) = forward_call(
        depth, span, own_rows, down_rows, hidden,
        (segment_lengths, time_index, frames[0], output_gradient[0], *biases, query_weight, key_weight, value_weight,
         output_projection, up_weight, down_weight, modulation_weight),
    )
    (fgrad, dwq, dwk, dwv, dwo, dup, ddown, dmw, mbias, btile) = backward_call(
        depth, span, own_rows, down_rows, hidden,
        (segment_lengths, given_heads, qs, ks, vs, oh, lse, normed, wg, cosr, sinr, low, mods, frames[0],
         grad_middle, mg_in, bias_in,
         gwo, gup, gdown),
    )
    sums = btile.reshape(-1)

    def own_part(vector, start, size):
        return lax.dynamic_slice_in_dim(vector, start + own_index * size, size)

    lengths = [member.shape[0] for member in (query_bias, key_bias, value_bias, output_bias, up_bias, down_bias)]
    starts = [sum(lengths[:n]) * depth * 8 for n in range(6)]
    bq, bk, bv, bo, bu, bd = [own_part(sums, start, size) for start, size in zip(starts, lengths)]
    bm = own_part(mbias[0], 0, modulation_bias.shape[0])
    output, fgrad, dwq, dwk, dwv, dwo, dup, ddown, dmw = hand_over(
        output, fgrad, dwq, dwk, dwv, dwo, dup, ddown, dmw
    )
    return (
        output[None], fgrad[None], dwq, bq, dwk, bk, dwv, bv, dwo, bo, dup, bu, ddown, bd, dmw, bm,
    )


def fits(mesh, frames, *parameters):
    dp, seq = mesh.shape["dp"], mesh.shape["seq"]
    rows = parameters[3].shape[0] // (dp * seq)
    return seq == 4 and dp % 2 == 0 and rows == 32 and frames.shape[0] == dp


def solution(mesh):
    def run(*arrays):
        return mapped(mesh, on_device_fast if fits(mesh, *arrays) else on_device)(*arrays)

    return run


def mapped(mesh, body):
    return jax.shard_map(
        body,
        mesh=mesh,
        in_specs=(
            P("dp", "seq", None),
            P("dp", "seq", None),
            P("dp", None),
            P("dp", None),
            P(("dp", "seq"), None),
            P(("dp", "seq")),
            P(("dp", "seq"), None),
            P(("dp", "seq")),
            P(("dp", "seq"), None),
            P(("dp", "seq")),
            P(("dp", "seq"), None),
            P(("dp", "seq")),
            P(("dp", "seq"), None),
            P(("dp", "seq")),
            P(("dp", "seq"), None),
            P(("dp", "seq")),
            P(("dp", "seq"), None),
            P(("dp", "seq")),
        ),
        out_specs=(
            P("dp", "seq", None),
            P("dp", "seq", None),
            P(("dp", "seq"), None),
            P(("dp", "seq")),
            P(("dp", "seq"), None),
            P(("dp", "seq")),
            P(("dp", "seq"), None),
            P(("dp", "seq")),
            P(("dp", "seq"), None),
            P(("dp", "seq")),
            P(("dp", "seq"), None),
            P(("dp", "seq")),
            P(("dp", "seq"), None),
            P(("dp", "seq")),
            P(("dp", "seq"), None),
            P(("dp", "seq")),
        ),
        check_vma=False,
    )
```

```python
from functools import partial
import math

import jax
import jax.numpy as jnp
from jax import lax
from jax.experimental import pallas as pl
from jax.experimental.pallas import tpu as pltpu
from jax.sharding import PartitionSpec as P

HEAD_DIM = 64
MODEL_WIDTH = 1024
SEGS = 4
EPSILON = 1e-06
NEGATIVE = -1e30
HIGHEST = lax.Precision.HIGHEST
F32 = jnp.float32
BF16 = jnp.bfloat16
LANES = 128


class Mover:
    def __init__(self, send_sems, recv_sems, local_sems):
        self.send_sems, self.recv_sems, self.local_sems = send_sems, recv_sems, local_sems
        self.count = self.local_count = 0
        self.sent = []

    def send(self, source, target, device):
        slot = self.count
        self.count += 1
        copy = pltpu.make_async_remote_copy(
            src_ref=source,
            dst_ref=target,
            send_sem=self.send_sems.at[slot],
            recv_sem=self.recv_sems.at[slot],
            device_id=device,
            device_id_type=pl.DeviceIdType.MESH,
        )
        copy.start()
        self.sent.append(copy)
        return copy

    def local(self, source, target):
        slot = self.local_count
        self.local_count += 1
        copy = pltpu.make_async_copy(source, target, self.local_sems.at[slot])
        copy.start()
        return copy

    def finish(self, but=()):
        for copy in self.sent:
            if not any(copy is other for other in but):
                copy.wait_send()


class Place:
    def __init__(self, depth):
        dp, seq = lax.axis_index("dp"), lax.axis_index("seq")
        self.depth = depth
        self.z, self.y = dp // 2, dp % 2
        self.x, self.c = seq // 2, seq % 2
        self.seq = seq
        self.index = dp * 4 + seq

    def at(self, z, y, x, c):
        return {"dp": z * 2 + y, "seq": x * 2 + c}

    def core(self):
        return self.at(self.z, self.y, self.x, 1 - self.c)

    def across_x(self):
        return self.at(self.z, self.y, 1 - self.x, self.c)

    def across_y(self):
        return self.at(self.z, 1 - self.y, self.x, self.c)

    def ahead(self, step):
        return (self.z + step) % self.depth

    def along_z(self, step):
        return self.at(self.ahead(step), self.y, self.x, self.c)

    def row_peer(self, step):
        return {"dp": self.z * 2 + self.y, "seq": (self.seq + step) % 4}

    def enter(self, diagonal=False):
        barrier = pltpu.get_barrier_semaphore()
        peers = [self.row_peer(step) for step in (1, 2, 3)] + [self.across_y()]
        peers += [self.along_z(step) for step in range(1, self.depth)]
        if diagonal:
            peers += [self.at(self.ahead(k), 1 - self.y, self.x, self.c) for k in range(1, self.depth)]
        for peer in peers:
            pl.semaphore_signal(barrier, 1, device_id=peer, device_id_type=pl.DeviceIdType.MESH)
        pl.semaphore_wait(barrier, len(peers))


def lanes_of(shape, axis=1):
    return lax.broadcasted_iota(jnp.int32, shape, axis)


def frame_segments(lens, first_row, rows, width):
    position = lanes_of((rows, width), 0) + first_row
    first, second, third = lens[0, 0], lens[0, 0] + lens[0, 1], lens[0, 0] + lens[0, 1] + lens[0, 2]
    segment = (
        (position >= first).astype(jnp.int32)
        + (position >= second).astype(jnp.int32)
        + (position >= third).astype(jnp.int32)
    )
    start = jnp.where(
        segment == 0, 0, jnp.where(segment == 1, first, jnp.where(segment == 2, second, third))
    )
    return segment, position - start


def three_parts(values):
    high = values.astype(BF16).astype(F32)
    rest = values - high
    middle = rest.astype(BF16).astype(F32)
    return high, middle, (rest - middle).astype(BF16).astype(F32)


def swap_halves(values, lane):
    return jnp.where(
        lane % HEAD_DIM < HEAD_DIM // 2, pltpu.roll(values, 96, 1), pltpu.roll(values, 32, 1)
    )


def head_only(values, lane, head):
    return jnp.where((lane >= HEAD_DIM) == bool(head), values.astype(F32), 0.0).astype(BF16)


def across(left, right):
    return lax.dot_general(left, right, (((1,), (1,)), ((), ())), preferred_element_type=F32)


def product(left, right):
    return jnp.dot(left, right, preferred_element_type=F32)


def straight(first, last, body):
    for step in range(first, last):
        body(step, 0)


AXES = (
    (1, 2, 0), (0, 2, 1), (2, 0, 1), (0, 2, 1), (0, 1, 2), (0, 1, 2), (0, 2, 1), (0, 2, 1), (2, 1, 0), (0, 1, 2),
)
(
    GATHER_Z, GATHER_TWO, GATHER_THREE, GATHER_CORE, COLUMNS_Z, COLUMNS_Y, PROJECT, ATTEND, GO_UP, FRAMES_X,
    FRAMES_ON, TABLES, TIMES_Y, SHARE, MOD_Y, MOD_Z, MOD_X, MOD_LAST, FRAMES_CORE, BIAS_Y, BIAS_X, BIAS_CORE,
    BIASES, MODS, OUT, GO_DOWN, BACK, GRADS, WAITS,
) = range(29)
FORWARD_ORDER = (
    (FRAMES_X, 0), (GATHER_Z, 9), (GATHER_Z, 1), (TIMES_Y, 0), (BIAS_Y, 0), (FRAMES_CORE, 0), (GATHER_TWO, 9),
    (COLUMNS_Z, 0), (COLUMNS_Z, 1), (SHARE, 0), (GATHER_Z, 4), (GATHER_Z, 8), (BIAS_X, 0), (MOD_Y, 0),
    (COLUMNS_Y, 0), (GATHER_THREE, 9), (COLUMNS_Y, 1), (COLUMNS_Z, 2), (FRAMES_X, 1), (GATHER_Z, 3), (MOD_Z, 0),
    (GATHER_Z, 0), (GATHER_Z, 2), (GATHER_Z, 7), (GATHER_TWO, 8), (GATHER_Z, 6), (TABLES, 1), (BIAS_CORE, 0),
    (GATHER_TWO, 4), (BIASES, 0), (COLUMNS_Y, 2), (TABLES, 0), (GATHER_TWO, 0), (GATHER_TWO, 1), (FRAMES_ON, 1),
    (MOD_X, 0), (GATHER_Z, 5), (GATHER_TWO, 3), (GATHER_THREE, 1), (GATHER_TWO, 2), (MOD_LAST, 0),
    (GATHER_THREE, 4), (MODS, 0), (PROJECT, 0), (GATHER_CORE, 9), (GATHER_THREE, 3), (GATHER_TWO, 7),
    (FRAMES_ON, 0), (PROJECT, 1), (PROJECT, 2), (GATHER_THREE, 0), (GATHER_TWO, 6), (PROJECT, 3),
    (GATHER_CORE, 1), (GATHER_TWO, 5), (GATHER_THREE, 8), (ATTEND, 1), (GATHER_THREE, 2), (ATTEND, 1),
    (GATHER_CORE, 4), (GATHER_CORE, 3), (GATHER_THREE, 5), (GATHER_THREE, 6), (ATTEND, 2), (GATHER_THREE, 7),
    (ATTEND, 3), (GATHER_CORE, 0), (ATTEND, 1), (GATHER_CORE, 6), (GATHER_CORE, 2), (GATHER_CORE, 5), (OUT, 0),
    (GO_UP, 0), (GATHER_CORE, 7), (GATHER_CORE, 8), (GO_UP, 1), (GO_DOWN, 0), (BACK, 0), (GRADS, 0),
)


def forward_kernel(
    depth,
    lens, times, frames, given_in, bq, bk, bv, bo, bu, bd, bm, wq, wk, wv, wo, up, down, mw,
    output, gmid, mg, btile, mods, low, gwo, gup, gdown, do_all, qs_out, ks_out, vs_out, oh_out, lse_out,
    normed_out, wg_out, cos_out, sin_out,
    att, oh, qs, lse, normed, wg, cosr, sinr, rowbias, wo_all, up_all, down_all,
    bb, xall, mwst, tb, part, recva, suma, recvb, sumb, recvc, sumc, recvd, modh, bmat, mod3, qbias,
    ka, va, qaug, given, mod6, branch, middle, normed_two, active, slope, gbt, gh, gn, gb, ga, sums,
    send_sems, recv_sems, local_sems,
):
    here = Place(depth)
    z, y, x, c, g = here.z, here.y, here.x, here.c, here.seq
    span, width = frames.shape
    hidden = up.shape[1]
    rows_all = span * 4
    block, tall, tile = 128, span, 256
    move = Mover(send_sems, recv_sems, local_sems)
    steps_z = range(1, depth)

    row = lanes_of((16, LANES), 0) % 4
    own_times = jnp.where(
        row == 0, times[0, 0], jnp.where(row == 1, times[0, 1], jnp.where(row == 2, times[0, 2], times[0, 3]))
    )
    tb[z, y] = own_times.astype(F32)
    bb[z, y, x, c] = jnp.zeros((8, LANES), F32)
    for n, vector in enumerate((bq, bk, bv, bo, bu, bd)):
        bb[z, y, x, c, n : n + 1, : vector.shape[1]] = vector[...].astype(F32)
    bb[z, y, x, c, 6:7, :] = bm[:, :LANES].astype(F32)
    bb[z, y, x, c, 7:8, : bm.shape[1] - LANES] = bm[:, LANES:].astype(F32)
    weights = (wq, wk, wv)
    own_width = wg.shape[-1]
    locals_first = [
        move.local(weights[j].at[:, pl.ds(pl.multiple_of(g * own_width, LANES), own_width)], wg.at[j, z, y, g])
        for j in range(3)
    ]
    strip = mw.shape[1] // 4
    local_mw = [
        move.local(mw.at[:, pl.ds(j * strip, strip)], mwst.at[pl.ds(j * 32, 32)]) for j in range(4)
    ]
    local_frames = move.local(frames, xall.at[g])
    local_given = move.local(given_in, given)
    here.enter()

    legs = {}
    shard, wide = wo.shape[0], MODEL_WIDTH
    thin = shard // 2
    flows = []

    def add_flow(source, target, first_row, columns=None):
        rows = pl.ds(first_row, thin)
        if columns is None:
            flows.append((source.at[rows], target.at[:, :, :, :, rows]))
        else:
            columns = pl.ds(columns, wide)
            flows.append((source.at[rows, columns], target.at[:, :, :, :, rows, columns]))

    for side in range(2):
        add_flow(wo, wo_all, side * thin)
    for side in range(2):
        add_flow(up, up_all, side * thin, 0)
        add_flow(up, up_all, side * thin, wide)
    for side in range(4):
        add_flow(down, down_all, side * thin)
    count = len(flows)

    legs, outgoing, owned = {}, [], {}
    here_at = (z, y, x)

    def to_axis(axis):
        if axis == 0:
            return [here.along_z(k) for k in steps_z]
        return [here.across_y() if axis == 1 else here.across_x()]

    def held(number, known):
        place = tuple(slice(None) if axis in known else here_at[axis] for axis in range(3))
        return flows[number][1].at[place + (c,)]

    def first_leg(number):
        source = flows[number][0]
        target = held(number, ())
        owned[number] = move.local(source, target)
        legs[number] = [move.send(source, target, peer) for peer in to_axis(AXES[number][0])]

    def next_leg(number, done):
        if done == 1:
            owned[number].wait()
        for copy in legs[number]:
            copy.wait_recv()
        part = held(number, AXES[number][:done])
        peers = [here.core()] if done == 3 else to_axis(AXES[number][done])
        legs[number] = [move.send(part, part, peer) for peer in peers]
        outgoing.extend(legs[number])

    def second_leg(number):
        next_leg(number, 1)

    def third_leg(number):
        next_leg(number, 2)

    def fourth_leg(number):
        next_leg(number, 3)

    def arrived(*numbers):
        for number in numbers:
            for copy in legs[number]:
                copy.wait_recv()

    times_z = [move.send(tb.at[z, y], tb.at[z, y], here.along_z(k)) for k in steps_z]
    qkv_row = [
        [
            move.send(
                weights[j].at[:, pl.ds(pl.multiple_of((g + k) % 4 * own_width, LANES), own_width)],
                wg.at[j, z, y, g],
                here.row_peer(k),
            )
            for k in (1, 2, 3)
        ]
        for j in range(3)
    ]
    bias_z = [move.send(bb.at[z, y, x, c], bb.at[z, y, x, c], here.along_z(k)) for k in steps_z]
    part_rows = span // 2
    frame_parts = [pl.ds(n * part_rows, part_rows) for n in range(2)]
    half = strip // 2
    sent = {}
    stores = []

    def columns_z(j):
        locals_first[j].wait()
        for copy in qkv_row[j]:
            copy.wait_recv()
        sent["q", j] = [move.send(wg.at[j, z, y], wg.at[j, z, y], here.along_z(k)) for k in steps_z]

    def columns_y(j):
        for copy in sent["q", j]:
            copy.wait_recv()
        sent["p", j] = move.send(wg.at[j, :, y], wg.at[j, :, y], here.across_y())

    def times_across():
        for copy in times_z:
            copy.wait_recv()
        sent["ty"] = move.send(tb.at[:, y], tb.at[:, y], here.across_y())

    def mod_share():
        sent["ty"].wait_recv()
        lane = lanes_of((16 * 2 * depth, LANES))
        row = lanes_of((16 * 2 * depth, LANES), 0)
        feature = here.index * 32 + lane % 32
        halfway = MODEL_WIDTH // 2
        frequency = jnp.exp((feature % halfway).astype(F32) * (-math.log(10000.0) / halfway))
        angle = tb[...].reshape(16 * 2 * depth, LANES) * frequency
        wave = jnp.where(feature < halfway, jnp.sin(angle), jnp.cos(angle))
        gated = wave / (1.0 + jnp.exp(-wave))
        low[...] = jnp.where(lane // 32 == (row % 16) // 4, gated, 0.0).astype(BF16)
        for copy in local_mw:
            copy.wait()
        for side in range(2):
            share = product(low[...], mwst[:, side * half : (side + 1) * half])
            part[side] = share.astype(BF16).reshape(depth, 2, 16, half)
        sent["mc"] = move.send(part.at[1 - c], recva, here.core())

    def mod_y():
        sent["mc"].wait_recv()
        suma[...] = (part[c].astype(F32) + recva[...].astype(F32)).astype(BF16)
        sent["my"] = move.send(suma.at[:, 1 - y], recvb, here.across_y())

    def mod_z():
        sent["my"].wait_recv()
        sumb[...] = (suma[:, y].astype(F32) + recvb[...].astype(F32)).astype(BF16)
        sent["mz"] = [move.send(sumb.at[here.ahead(k)], recvc.at[k - 1], here.along_z(k)) for k in steps_z]

    def mod_x():
        total = sumb[z].astype(F32)
        for k in steps_z:
            sent["mz"][k - 1].wait_recv()
            total = total + recvc[k - 1].astype(F32)
        sumc[...] = total
        sent["mx"] = move.send(sumc, recvd, here.across_x())

    def mod_last():
        sent["mx"].wait_recv()
        modh[c] = sumc[...] + recvd[...]
        sent["ml"] = move.send(modh.at[c], modh.at[c], here.core())

    def frames_core():
        sent["fc"] = move.send(frames, xall.at[g], here.core())

    def frames_x(n):
        sent["fx", n] = move.send(frames.at[frame_parts[n]], xall.at[g, frame_parts[n]], here.across_x())

    frames_here = []

    def frames_in(n):
        if n not in frames_here:
            sent["fx", n].wait_recv()
            frames_here.append(n)

    def frames_on(n):
        frames_in(n)
        theirs = xall.at[(g + 2) % 4, frame_parts[n]]
        sent["on", n] = move.send(theirs, theirs, here.core())

    def bias_y():
        for copy in bias_z:
            copy.wait_recv()
        sent["by"] = move.send(bb.at[:, y, x, c], bb.at[:, y, x, c], here.across_y())

    def bias_x():
        sent["by"].wait_recv()
        sent["bx"] = move.send(bb.at[:, :, x, c], bb.at[:, :, x, c], here.across_x())

    def bias_core():
        sent["bx"].wait_recv()
        sent["bc"] = move.send(bb.at[:, :, :, c], bb.at[:, :, :, c], here.core())

    def tables(step, carry):
        rows = pl.ds(pl.multiple_of(step * block, block), block)
        segment, relative = frame_segments(lens, step * block, block, LANES)
        lane = lanes_of((block, LANES))
        quarter = HEAD_DIM // 2
        frequency = jnp.exp((lane % quarter).astype(F32) * (-math.log(10000.0) / quarter))
        angle = relative.astype(F32) * frequency
        cosr[rows, :] = jnp.cos(angle)
        sine = jnp.sin(angle)
        sinr[rows, :] = jnp.where(lane % HEAD_DIM < quarter, -sine, sine)
        same = segment == lane
        qaug[rows, :] = jnp.where((lane < SEGS) & jnp.logical_not(same), NEGATIVE, 0.0).astype(BF16)
        keyside = jnp.where((lane < SEGS) & same, 1.0, jnp.where((lane >= 4) & (lane < 7), 1.0, 0.0))
        for pair in range(2):
            ka[pair, rows, LANES:] = keyside.astype(BF16)
            va[pair, rows, LANES:] = jnp.where(lane < 3, 1.0, 0.0).astype(BF16)
        return carry

    def tables_half(n):
        lax.fori_loop(n * rows_all // (2 * block), (n + 1) * rows_all // (2 * block), tables, 0)

    def bias_vectors():
        sent["bc"].wait_recv()
        bmat[...] = bb[...].reshape(16 * 2 * depth * 2, LANES).astype(BF16)

        place = lanes_of((LANES, own_width), 0)
        column = lanes_of((LANES, own_width))
        brow, bcol = lanes_of((64, own_width), 0), lanes_of((64, own_width))
        spread = jnp.where(column % 32 == place, 1.0, 0.0).astype(BF16)
        for j in range(3):
            mine = (brow % 8 == j) & (brow // 8 == bcol // 32)
            held = product(bmat[pl.ds(pl.multiple_of(g * 64, 64), 64), :], spread)
            qbias[j : j + 1, :] = jnp.sum(jnp.where(mine, held, 0.0), axis=0, keepdims=True)

        trow, tcol = lanes_of((16 * 2 * depth * 2, tile), 0), lanes_of((16 * 2 * depth * 2, tile))
        place, column = lanes_of((LANES, tile), 0), lanes_of((LANES, tile))

        def row_vector(step, size, source):
            spread = jnp.where(column % size == place, 1.0, 0.0).astype(BF16)
            chosen = (trow % 8 == source) & (trow // 8 == (tcol + step * tile) // size)
            return jnp.sum(jnp.where(chosen, product(bmat[...], spread), 0.0), axis=0, keepdims=True)

        def narrow_vectors(step, carry):
            columns = pl.ds(pl.multiple_of(step * tile, tile), tile)
            rowbias[0:1, columns] = row_vector(step, 32, 3)
            rowbias[2:3, columns] = row_vector(step, 32, 5)
            return carry

        def wide_vector(step, carry):
            rowbias[1:2, pl.ds(pl.multiple_of(step * tile, tile), tile)] = row_vector(step, 64, 4)
            return carry

        lax.fori_loop(0, MODEL_WIDTH // tile, narrow_vectors, 0)
        lax.fori_loop(0, up.shape[1] // tile, wide_vector, 0)

        place = lanes_of((LANES, half), 0)
        column = lanes_of((LANES, half))
        spread_a = jnp.where(column % 192 == place, 1.0, 0.0).astype(BF16)
        spread_b = jnp.where(column % 192 == place + LANES, 1.0, 0.0).astype(BF16)
        brow, bcol = lanes_of((32, half), 0), lanes_of((32, half))
        inside = brow // 8 == bcol // 192
        for q in range(8):
            rows = bmat[q * 32 : (q + 1) * 32, :]
            terms = jnp.where(inside & (brow % 8 == 6), product(rows, spread_a), 0.0)
            terms = terms + jnp.where(inside & (brow % 8 == 7), product(rows, spread_b), 0.0)
            mods[4:5, q * half : (q + 1) * half] = jnp.sum(terms, axis=0, keepdims=True)

    def mod_done():
        sent["ml"].wait_recv()
        for q in range(8):
            j, side = q // 2, q % 2
            columns = slice(q * half, (q + 1) * half)
            mods[0:4, columns] = modh[side, 4 * j : 4 * j + 4, :] + mods[4:5, columns]
        for kept, first, last in ((mod3, 0, 2 * width), (mod6, 2 * width, 6 * width)):
            high, mid, rest = three_parts(mods[0:4, first:last])
            kept[0:4, :] = high
            kept[4:8, :] = mid
            kept[8:12, :] = rest
            kept[12:16, :] = jnp.zeros((4, last - first), F32)

    def project_rows(source):
        block, step = span, source
        rows = pl.ds(pl.multiple_of(step * block, block), block)
        values = xall[source].astype(F32)
        center = jnp.mean(values, axis=1, keepdims=True)
        centered = values - center
        variance = jnp.mean(centered * centered, axis=1, keepdims=True)
        segment, _ = frame_segments(lens, step * block, block, 16)
        slot = lanes_of((block, 16))
        chosen = jnp.where((slot < 12) & (slot % 4 == segment), 1.0, 0.0).astype(BF16)
        parts = mod3[...].astype(BF16)
        shift = product(chosen, parts[:, :MODEL_WIDTH])
        scale = product(chosen, parts[:, MODEL_WIDTH:])
        result = (centered * lax.rsqrt(variance + EPSILON) * (1.0 + scale) + shift).astype(BF16)
        normed[rows, :] = result
        cosine, sine = cosr[rows, :], sinr[rows, :]
        lane = lanes_of((block, LANES))
        for j in range(3):
            weight = wg[j].reshape(MODEL_WIDTH, own_width)
            full = product(result, weight) + qbias[j : j + 1, :]
            for pair in range(2):
                piece = full[:, pair * LANES : (pair + 1) * LANES]
                if j < 2:
                    piece = piece * cosine + swap_halves(piece, lane) * sine
                if j == 0:
                    qs[pair, rows, :] = (piece.astype(BF16).astype(F32) * HEAD_DIM**-0.5).astype(BF16)
                elif j == 1:
                    ka[pair, rows, :LANES] = piece.astype(BF16)
                else:
                    va[pair, rows, :LANES] = piece.astype(BF16)

    def project_span(n):
        if n == 0:
            local_frames.wait()
            for j in range(3):
                sent["p", j].wait_recv()
        elif n == 1:
            sent["fc"].wait_recv()
        elif n == 2:
            for m in range(2):
                frames_in(m)
        else:
            for m in range(2):
                sent["on", m].wait_recv()
        number = (g, x * 2 + 1 - c, (1 - x) * 2 + c, (1 - x) * 2 + 1 - c)[n]
        project_rows(number)
        if n == 3:
            for source, target in (
                (qs, qs_out), (ka.at[:, :, pl.ds(0, LANES)], ks_out), (va.at[:, :, pl.ds(0, LANES)], vs_out),
                (normed, normed_out), (wg, wg_out), (cosr, cos_out), (sinr, sin_out),
            ):
                stores.append(move.local(source, target))

    def attend(pair, step):
        rows = pl.ds(pl.multiple_of(step * tall, tall), tall)
        query = qs[pair, rows, :]
        lane = lanes_of((tall, LANES))
        outs, sums = [], []
        for head in range(2):
            left = jnp.concatenate([head_only(query, lane, head), qaug[rows, :]], axis=1)
            scores = across(left, ka[pair])
            highest = jnp.max(scores, axis=1, keepdims=True)
            mixed = product(jnp.exp(scores - highest).astype(BF16), va[pair])
            total = mixed[:, LANES : LANES + 1]
            outs.append(mixed[:, :LANES] / total)
            sums.append(highest + jnp.log(total))
        oh[pair, rows, :] = jnp.where(lane < HEAD_DIM, outs[0], outs[1]).astype(BF16)
        before = jnp.zeros((tall, LANES), F32) if pair == 0 else lse[rows, :]
        lse[rows, :] = jnp.where(
            lane == 2 * pair, sums[0], jnp.where(lane == 2 * pair + 1, sums[1], before)
        )

    delivered = []

    def attend_next():
        pair, at = len(delivered) // 4, len(delivered) % 4
        k = (2, 1, 3, 0)[at]
        target = (g + k) % 4
        attend(pair, target)
        columns = pl.ds(pl.multiple_of(g * own_width + pair * LANES, LANES), LANES)
        source = oh.at[pair, pl.ds(pl.multiple_of(target * span, span), span)]
        if k:
            delivered.append(move.send(source, att.at[:, columns], here.row_peer(k)))
        else:
            delivered.append(move.local(source, att.at[:, columns]))
        if len(delivered) == 8:
            stores.append(move.local(oh, oh_out))
            stores.append(move.local(lse, lse_out))

    base = g * span

    def tile_at(step):
        return pl.ds(pl.multiple_of(step * tile, tile), tile)

    def per_frame(part, first, rows, columns):
        segment, _ = frame_segments(lens, base + first, rows, 16)
        slot = lanes_of((rows, 16))
        chosen = jnp.where((slot < 12) & (slot % 4 == segment), 1.0, 0.0).astype(BF16)
        return product(chosen, mod6[:, columns].astype(BF16))

    def members(first, rows):
        position = base + first + lanes_of((16, rows))
        edges = [lens[0, 0], lens[0, 0] + lens[0, 1], lens[0, 0] + lens[0, 1] + lens[0, 2]]
        inside = sum((position >= edge).astype(jnp.int32) for edge in edges)
        return jnp.where(inside == lanes_of((16, rows), 0), 1.0, 0.0).astype(BF16)

    def by_segment(inside, values):
        top = values.astype(BF16)
        return product(inside, top) + product(inside, (values - top.astype(F32)).astype(BF16))

    def shifted(part, step):
        return pl.ds(pl.multiple_of(part * width + step * tile, tile), tile)

    def wo_columns(columns):
        return wo_all[:, :, :, :, :, columns].reshape(width, tile)

    def up_columns(columns):
        return up_all[:, :, :, :, :, columns].reshape(width, tile)

    def down_columns(columns):
        return down_all[:, :, :, :, :, columns].reshape(hidden, tile)

    def project_out():
        for at, copy in enumerate(delivered):
            copy.wait() if at % 4 == 3 else copy.wait_recv()
        arrived(0, 1)

        def body(step, carry):
            columns = tile_at(step)
            branch[:, columns] = product(att[...], wo_columns(columns)) + rowbias[0:1, columns]
            return carry

        straight(0, width // tile, body)

        def norm_forward(step, carry):
            rows = pl.ds(pl.multiple_of(step * block, block), block)
            gate = per_frame(0, step * block, block, slice(0, width))
            values = xall[g, rows, :].astype(F32) + gate * branch[rows, :]
            middle[rows, :] = values
            centered = values - jnp.mean(values, axis=1, keepdims=True)
            hat = centered * lax.rsqrt(jnp.mean(centered * centered, axis=1, keepdims=True) + EPSILON)
            shift = per_frame(1, step * block, block, slice(width, 2 * width))
            scale = per_frame(2, step * block, block, slice(2 * width, 3 * width))
            normed_two[rows, :] = (hat * (1.0 + scale) + shift).astype(BF16)
            return carry

        straight(0, span // block, norm_forward)

    root = math.sqrt(2.0 / math.pi)

    def go_up(side):
        arrived(2 + side, 4 + side)

        def body(step, carry):
            columns = tile_at(step)
            value = product(normed_two[...], up_columns(columns)) + rowbias[1:2, columns]
            square = value * value
            turn = jnp.tanh(root * value * (1.0 + 0.044715 * square))
            part_one = 0.5 * (1.0 + turn)
            active[:, columns] = (value * part_one).astype(BF16)
            slope[:, columns] = part_one + 0.5 * value * (1.0 - turn * turn) * root * (
                1.0 + 3 * 0.044715 * square
            )
            return carry

        straight(side * width // tile, (side + 1) * width // tile, body)

    def go_down():
        arrived(6, 7, 8, 9)
        local_given.wait()

        def body(step, carry):
            columns = tile_at(step)
            value = product(active[...], down_columns(columns)) + rowbias[2:3, columns]
            gate = per_frame(3, 0, span, shifted(3, step))
            back = given[:, columns].astype(F32)
            output[:, columns] = (middle[:, columns] + gate * value).astype(BF16)
            gbt[:, columns] = (gate * back).astype(BF16)
            sums[:, shifted(3, step)] = by_segment(members(0, span), back * value)
            return carry

        straight(0, width // tile, body)

    def back_values():
        def hidden_tile(step, carry):
            rows = tile_at(step)
            weight = down_all[step // 2, step % 2].reshape(tile, width)
            gh[:, rows] = (across(gbt[...], weight) * slope[:, rows]).astype(BF16)
            return carry

        straight(0, hidden // tile, hidden_tile)

        def normed_tile(step, carry):
            gn[:, tile_at(step)] = across(gh[...], up_all[step].reshape(tile, hidden))
            return carry

        straight(0, width // tile, normed_tile)
        sums[:, : 3 * width] = jnp.zeros((16, 3 * width), F32)

        def norm_back(step, carry):
            rows = pl.ds(pl.multiple_of(step * block, block), block)
            grad, values = gn[rows, :], middle[rows, :]
            centered = values - jnp.mean(values, axis=1, keepdims=True)
            scaled = lax.rsqrt(jnp.mean(centered * centered, axis=1, keepdims=True) + EPSILON)
            hat = centered * scaled
            inner = grad * (1.0 + per_frame(2, step * block, block, slice(2 * width, 3 * width)))
            mean_one = jnp.mean(inner, axis=1, keepdims=True)
            mean_two = jnp.mean(inner * hat, axis=1, keepdims=True)
            total = given[rows, :].astype(F32) + scaled * (inner - mean_one - hat * mean_two)
            gmid[rows, :] = total
            gb[rows, :] = (per_frame(0, step * block, block, slice(0, width)) * total).astype(BF16)
            inside = members(step * block, block)
            sums[:, :width] += by_segment(inside, total * branch[rows, :])
            sums[:, width : 2 * width] += by_segment(inside, grad)
            sums[:, 2 * width : 3 * width] += by_segment(inside, grad * hat)
            return carry

        straight(0, span // block, norm_back)
        sent["o"] = []
        mine = pl.ds(pl.multiple_of(g * span, span), span)
        for k in (1, 2, 3, 0):
            target = (g + k) % 4
            columns = tile_at(target)
            ga[:, columns] = across(gb[...], wo_all[target].reshape(tile, width)).astype(BF16)
            for pair in range(2):
                source = ga.at[:, pl.ds(pl.multiple_of(target * own_width + pair * LANES, LANES), LANES)]
                place = do_all.at[pair, mine]
                if k:
                    sent["o"].append(move.send(source, place, here.row_peer(k)))
                else:
                    stores.append(move.local(source, place))

    def back_weights():
        for copy in outgoing:
            copy.wait_send()

        def down_tile(step, carry):
            grad = from_rows(active[:, tile_at(step)], gbt[...]).astype(BF16)
            down_all[step // 2, step % 2] = grad.reshape(down_all.shape[2:])
            return carry

        straight(0, hidden // tile, down_tile)
        stores.append(move.local(down_all, gdown))

        def up_tile(step, carry):
            grad = from_rows(normed_two[:, tile_at(step)], gh[...]).astype(BF16)
            up_all[step] = grad.reshape(up_all.shape[1:])
            return carry

        straight(0, width // tile, up_tile)
        stores.append(move.local(up_all, gup))

        def out_tile(step, carry):
            grad = from_rows(att[:, tile_at(step)], gb[...]).astype(BF16)
            wo_all[step] = grad.reshape(wo_all.shape[1:])
            return carry

        straight(0, width // tile, out_tile)
        stores.append(move.local(wo_all, gwo))
        ones = jnp.ones((16, span), BF16)
        btile[0:24, :] = jnp.zeros((24, LANES), F32)
        start = 24
        for grads, size in ((gb, width), (gh, hidden), (gbt, width)):
            total = product(ones, grads[...])
            for n in range(size // LANES):
                btile[start + n : start + n + 1, :] = total[0:1, n * LANES : (n + 1) * LANES]
            start += size // LANES
        for n in range(4):
            mg[4 * n : 4 * n + 4, :] = sums[0:4, n * width : (n + 1) * width]

    numbered = {
        GATHER_Z: first_leg, GATHER_TWO: second_leg, GATHER_THREE: third_leg, GATHER_CORE: fourth_leg, COLUMNS_Z: columns_z, COLUMNS_Y: columns_y,
        PROJECT: project_span, GO_UP: go_up, FRAMES_X: frames_x, FRAMES_ON: frames_on, TABLES: tables_half,
    }
    named = {
        TIMES_Y: times_across, SHARE: mod_share, MOD_Y: mod_y, MOD_Z: mod_z, MOD_X: mod_x, MOD_LAST: mod_last,
        FRAMES_CORE: frames_core, BIAS_Y: bias_y, BIAS_X: bias_x, BIAS_CORE: bias_core, BIASES: bias_vectors, MODS: mod_done,
        OUT: project_out, GO_DOWN: go_down, BACK: back_values, GRADS: back_weights,
    }
    for code, number in FORWARD_ORDER:
        if code in named:
            named[code]()
        elif code == ATTEND:
            for _ in range(number):
                attend_next()
        else:
            numbered[code](number)
    for copy in stores:
        copy.wait()
    for copy in sent["o"]:
        copy.wait_recv()
    move.finish(but=outgoing)

def forward_call(depth, span, own_rows, down_rows, hidden, args):
    rows_all, own_width, width = 4 * span, MODEL_WIDTH // 4, MODEL_WIDTH
    half = 6 * MODEL_WIDTH // 8
    vmem, anywhere, scalar = (
        pl.BlockSpec(memory_space=pltpu.VMEM),
        pl.BlockSpec(memory_space=pl.ANY),
        pl.BlockSpec(memory_space=pltpu.SMEM),
    )

    def out(shape, dtype):
        return jax.ShapeDtypeStruct(shape, dtype)

    heads, table = (2, rows_all, LANES), (rows_all, LANES)
    columns = (3, depth, 2, 4, own_rows, own_width)
    wo_shape = (depth, 2, 2, 2, own_rows, width)
    up_shape = (depth, 2, 2, 2, own_rows, hidden)
    down_shape = (depth, 2, 2, 2, down_rows, width)
    outs = [
        (out((span, width), BF16), vmem),
        (out((span, width), F32), vmem),
        (out((16, width), F32), vmem),
        (out((56, LANES), F32), vmem),
        (out((8, 6 * width), F32), vmem),
        (out((32 * depth, LANES), BF16), vmem),
        (out(wo_shape, BF16), anywhere),
        (out(up_shape, BF16), anywhere),
        (out(down_shape, BF16), anywhere),
        (out(heads, BF16), anywhere),
        (out(heads, BF16), anywhere),
        (out(heads, BF16), anywhere),
        (out(heads, BF16), anywhere),
        (out(heads, BF16), anywhere),
        (out(table, F32), anywhere),
        (out((rows_all, width), BF16), anywhere),
        (out(columns, BF16), anywhere),
        (out(table, F32), anywhere),
        (out(table, F32), anywhere),
    ]
    low, wide = pltpu.VMEM((span, width), BF16), pltpu.VMEM((span, width), F32)
    scratch = [
        low,
        pltpu.VMEM(heads, BF16),
        pltpu.VMEM(heads, BF16),
        pltpu.VMEM(table, F32),
        pltpu.VMEM((rows_all, width), BF16),
        pltpu.VMEM(columns, BF16),
        pltpu.VMEM(table, F32),
        pltpu.VMEM(table, F32),
        pltpu.VMEM((8, hidden), F32),
        pltpu.VMEM(wo_shape, BF16),
        pltpu.VMEM(up_shape, BF16),
        pltpu.VMEM(down_shape, BF16),
        pltpu.VMEM((depth, 2, 2, 2, 8, LANES), F32),
        pltpu.VMEM((4, span, width), BF16),
        pltpu.VMEM((LANES, 2 * half), BF16),
        pltpu.VMEM((depth, 2, 16, LANES), F32),
        pltpu.VMEM((2, depth, 2, 16, half), BF16),
        pltpu.VMEM((depth, 2, 16, half), BF16),
        pltpu.VMEM((depth, 2, 16, half), BF16),
        pltpu.VMEM((depth, 16, half), BF16),
        pltpu.VMEM((depth, 16, half), BF16),
        pltpu.VMEM((depth - 1, 16, half), BF16),
        pltpu.VMEM((16, half), F32),
        pltpu.VMEM((16, half), F32),
        pltpu.VMEM((2, 16, half), F32),
        pltpu.VMEM((64 * depth, LANES), BF16),
        pltpu.VMEM((16, 2 * width), F32),
        pltpu.VMEM((8, own_width), F32),
        pltpu.VMEM((2, rows_all, 2 * LANES), BF16),
        pltpu.VMEM((2, rows_all, 2 * LANES), BF16),
        pltpu.VMEM(table, BF16),
        low,
        pltpu.VMEM((16, 4 * width), F32),
        wide,
        wide,
        low,
        pltpu.VMEM((span, hidden), BF16),
        pltpu.VMEM((span, hidden), F32),
        low,
        pltpu.VMEM((span, hidden), BF16),
        wide,
        low,
        low,
        pltpu.VMEM((16, 4 * width), F32),
        pltpu.SemaphoreType.DMA((144,)),
        pltpu.SemaphoreType.DMA((144,)),
        pltpu.SemaphoreType.DMA((48,)),
    ]
    return pl.pallas_call(
        partial(forward_kernel, depth),
        out_shape=[shape for shape, _ in outs],
        in_specs=[scalar, scalar, anywhere, anywhere] + [vmem] * 7 + [anywhere] * 7,
        out_specs=[spec for _, spec in outs],
        scratch_shapes=scratch,
        compiler_params=pltpu.CompilerParams(
            collective_id=0, has_side_effects=True, vmem_limit_bytes=62 * 1024 * 1024
        ),
        cost_estimate=pl.CostEstimate(flops=2 * 10**10, bytes_accessed=60 * 10**6, transcendentals=10**7),
    )(*args)


def turn_back(values, cosine, sine, lane):
    return values * cosine - swap_halves(values, lane) * sine


def from_rows(left, right):
    return lax.dot_general(left, right, (((0,), (0,)), ((), ())), preferred_element_type=F32)


X_FIRST = (0, 1, 0, 1, 1, 1, 0, 0, 0, 1)
(
    SUM_ONE, SUM_TWO, SUM_THREE, SUM_LAST, WEIGHTS_Y, WEIGHTS_Z, WEIGHTS_LAST, ATTEND_BACK, ROWS_AWAY,
    ROWS_ACROSS, ROWS_HOME, NORM, EARLY_CORE, EARLY_X, EARLY_Z, EARLY_Y, EARLY_SHARE, EARLY_DONE, LATE_ROWS,
    LATE_DONE, BIAS_START, BIAS_NEXT, BIAS_DONE,
) = range(23)
BACKWARD_ORDER = (
    (SUM_ONE, 0), (ATTEND_BACK, 1), (SUM_ONE, 1), (SUM_ONE, 2), (ATTEND_BACK, 1), (SUM_ONE, 4),
    (ATTEND_BACK, 1), (SUM_TWO, 0), (SUM_ONE, 6), (EARLY_CORE, 0), (ATTEND_BACK, 1), (SUM_ONE, 5),
    (ATTEND_BACK, 1), (SUM_TWO, 1), (ATTEND_BACK, 1), (SUM_TWO, 6), (SUM_ONE, 7), (SUM_TWO, 4), (SUM_TWO, 2),
    (ATTEND_BACK, 1), (SUM_THREE, 0), (SUM_THREE, 1), (ATTEND_BACK, 1), (SUM_TWO, 5), (EARLY_X, 0),
    (SUM_ONE, 9), (SUM_ONE, 8), (SUM_THREE, 6), (SUM_TWO, 7), (ATTEND_BACK, 1), (EARLY_Z, 0), (ATTEND_BACK, 1),
    (SUM_THREE, 5), (SUM_THREE, 2), (ATTEND_BACK, 1), (SUM_TWO, 9), (SUM_THREE, 4), (SUM_ONE, 3), (EARLY_Y, 0),
    (ATTEND_BACK, 1), (SUM_THREE, 9), (WEIGHTS_Y, 1), (SUM_TWO, 8), (ROWS_AWAY, 0), (SUM_THREE, 7),
    (SUM_LAST, 1), (SUM_LAST, 4), (SUM_LAST, 5), (SUM_TWO, 3), (ROWS_ACROSS, 0), (SUM_THREE, 8), (WEIGHTS_Y, 2),
    (WEIGHTS_Z, 1), (SUM_LAST, 7), (WEIGHTS_Y, 0), (BIAS_START, 0), (SUM_LAST, 8), (SUM_LAST, 6),
    (EARLY_SHARE, 0), (SUM_THREE, 3), (WEIGHTS_Z, 2), (ROWS_HOME, 0), (WEIGHTS_Z, 0), (BIAS_NEXT, 0),
    (SUM_LAST, 9), (SUM_LAST, 0), (SUM_LAST, 3), (NORM, 0), (SUM_LAST, 2), (LATE_ROWS, 0), (WEIGHTS_LAST, 2),
    (BIAS_NEXT, 0), (WEIGHTS_LAST, 0), (WEIGHTS_LAST, 1), (BIAS_NEXT, 0), (EARLY_DONE, 0), (LATE_DONE, 0),
    (BIAS_DONE, 0),
)


def backward_kernel(
    depth,
    lens, do_in, qs_in, ks_in, vs_in, oh_in, lse_in, normed_in, wg_in, cos_in, sin_in, low, mods, frames, gmid,
    mg_in, bias_in, gwo, gup, gdown,
    fgrad, dwq, dwk, dwv, dwo, dup, ddown, dmw, mbias, btile,
    qs, do, oh, lse, normed, wg, cosr, sinr, ka, va, qaug, dk_sum, dv_sum, gr, gw, gwy, gwz, gsum,
    gnp, gnr, gnx, mod3, acc_shift, acc_scale, mg, mgr, mgs, mgx, ev, late, joined, ez, brecv, bz,
    *rest,
):
    send_sems, recv_sems, local_sems = rest[-3:]
    buffers = rest[:-3]
    here = Place(depth)
    z, y, x, c, g = here.z, here.y, here.x, here.c, here.seq
    span = frames.shape[0]
    rows_all = span * 4
    own_width = wg.shape[-1]
    move = Mover(send_sems, recv_sems, local_sems)
    steps_z = range(1, depth)

    shard, width = gwo.shape[4], MODEL_WIDTH
    thin = shard // 2
    pieces = []

    def add_piece(source, target, first_row, columns=None):
        rows = pl.ds(first_row, thin)
        if columns is None:
            pieces.append((source.at[:, :, :, :, rows], target.at[rows]))
        else:
            columns = pl.ds(columns, width)
            pieces.append((source.at[:, :, :, :, rows, columns], target.at[rows, columns]))

    for n in range(4):
        add_piece(gdown, ddown, n * thin)
    for n in range(2):
        add_piece(gup, dup, n * thin, 0)
        add_piece(gup, dup, n * thin, width)
    for n in range(2):
        add_piece(gwo, dwo, n * thin)
    count = len(pieces)
    own, first, second, third, fourth = (
        [buffers[count * n + f] for f in range(count)] for n in range(5)
    )
    legs = {}

    loads = [
        move.local(ks_in, ka.at[:, :, pl.ds(0, LANES)]),
        move.local(vs_in, va.at[:, :, pl.ds(0, LANES)]),
        move.local(qs_in, qs),
        move.local(do_in, do),
        move.local(oh_in, oh),
        move.local(lse_in, lse),
        move.local(cos_in, cosr),
        move.local(sin_in, sinr),
    ]
    here.enter(diagonal=True)
    held = []
    for f in range(count):
        source = pieces[f][0]
        legs[f] = move.send(source.at[:, :, :, 1 - c], first[f], here.core())
        held.append(move.local(source.at[:, :, :, c], own[f]))
    late_loads = [move.local(normed_in, normed), move.local(wg_in, wg)]

    def sum_first(f):
        legs[f].wait_recv()
        held[f].wait()

        def add(step, carry):
            own[f][step] = own[f][step] + first[f][step]
            return carry

        lax.fori_loop(0, depth, add, 0)
        if X_FIRST[f]:
            legs[f] = move.send(own[f].at[:, :, 1 - x], second[f], here.across_x())
        else:
            legs[f] = move.send(own[f].at[:, 1 - y], second[f], here.across_y())

    def sum_second(f):
        legs[f].wait_recv()

        def add(step, carry):
            for other in range(2):
                if X_FIRST[f]:
                    own[f][step, other, x] = own[f][step, other, x] + second[f][step, other]
                else:
                    own[f][step, y, other] = own[f][step, y, other] + second[f][step, other]
            return carry

        lax.fori_loop(0, depth, add, 0)
        if X_FIRST[f]:
            legs[f] = move.send(own[f].at[:, 1 - y, x], third[f], here.across_y())
        else:
            legs[f] = move.send(own[f].at[:, y, 1 - x], third[f], here.across_x())

    def sum_third(f):
        legs[f].wait_recv()

        def add(step, carry):
            own[f][step, y, x] = own[f][step, y, x] + third[f][step]
            return carry

        lax.fori_loop(0, depth, add, 0)
        legs[f] = [
            move.send(own[f].at[here.ahead(k), y, x], fourth[f].at[k - 1], here.along_z(k)) for k in steps_z
        ]

    def sum_last(f):
        total = own[f][z, y, x].astype(F32)
        for k in steps_z:
            legs[f][k - 1].wait_recv()
            total = total + fourth[f][k - 1].astype(F32)
        pieces[f][1][...] = total

    def bias_round(peer, slot):
        return move.send(btile, brecv.at[slot], peer)

    block = 128

    def columns_of_segments(step, carry):
        rows = pl.ds(pl.multiple_of(step * block, block), block)
        segment, _ = frame_segments(lens, step * block, block, LANES)
        lane = lanes_of((block, LANES))
        same = segment == lane
        qaug[rows, :] = jnp.where((lane < SEGS) & jnp.logical_not(same), NEGATIVE, 0.0).astype(BF16)
        keyside = jnp.where((lane < SEGS) & same, 1.0, jnp.where((lane >= 4) & (lane < 7), 1.0, 0.0))
        for pair in range(2):
            ka[pair, rows, LANES:] = keyside.astype(BF16)
            va[pair, rows, LANES:] = jnp.where(lane < 3, 1.0, 0.0).astype(BF16)
        return carry

    for copy in loads[:2]:
        copy.wait()
    lax.fori_loop(0, rows_all // block, columns_of_segments, 0)
    for copy in loads[2:]:
        copy.wait()

    tall = 256
    steps = rows_all // tall

    def back_block(pair, step):
        rows = pl.ds(pl.multiple_of(step * tall, tall), tall)
        lane = lanes_of((tall, LANES))
        query, given = qs[pair, rows, :], do[pair, rows, :]
        overlap = given.astype(F32) * oh[pair, rows, :].astype(F32)
        mask_columns = qaug[rows, :].astype(F32)
        sums = lse[rows, :]
        grads_q, add_k, add_v = [], 0.0, 0.0
        for head in range(2):
            delta = jnp.sum(jnp.where((lane >= HEAD_DIM) == bool(head), overlap, 0.0), axis=1, keepdims=True)
            logsum = jnp.sum(jnp.where(lane == 2 * pair + head, sums, 0.0), axis=1, keepdims=True)
            a, b, d = three_parts(logsum)
            side = jnp.where(lane == 4, -a, jnp.where(lane == 5, -b, jnp.where(lane == 6, -d, mask_columns)))
            query_head = head_only(query, lane, head)
            left = jnp.concatenate([query_head, side.astype(BF16)], axis=1)
            a, b, d = three_parts(delta)
            side = jnp.where(lane == 0, -a, jnp.where(lane == 1, -b, jnp.where(lane == 2, -d, 0.0)))
            given_head = head_only(given, lane, head)
            right = jnp.concatenate([given_head, side.astype(BF16)], axis=1)
            weights = jnp.exp(across(ka[pair], left))
            grads = (weights * across(va[pair], right)).astype(BF16)
            add_v = add_v + product(weights.astype(BF16), given_head)
            add_k = add_k + product(grads, query_head)
            grads_q.append(from_rows(grads, ka[pair, :, :LANES]))
        dv_sum[...] += add_v
        dk_sum[...] += add_k
        grad_query = jnp.where(lane < HEAD_DIM, grads_q[0], grads_q[1]) * HEAD_DIM**-0.5
        gr[0, rows, pair * LANES : (pair + 1) * LANES] = turn_back(
            grad_query, cosr[rows, :], sinr[rows, :], lane
        ).astype(BF16)

    def back_some(pair, start, stop):
        lax.fori_loop(start, stop, lambda step, carry: (back_block(pair, step), carry)[1], 0)

    def settle_pair(pair):
        def body(step, carry):
            rows = pl.ds(pl.multiple_of(step * block, block), block)
            lane = lanes_of((block, LANES))
            part = slice(pair * LANES, (pair + 1) * LANES)
            gr[1, rows, part] = turn_back(dk_sum[rows, :], cosr[rows, :], sinr[rows, :], lane).astype(BF16)
            gr[2, rows, part] = dv_sum[rows, :].astype(BF16)
            return carry

        lax.fori_loop(0, rows_all // block, body, 0)

    def clear():
        dk_sum[...] = jnp.zeros_like(dk_sum)
        dv_sum[...] = jnp.zeros_like(dv_sum)

    def back_rows(target):
        def body(step, carry):
            rows = pl.ds(pl.multiple_of(target * span + step * block, block), block)
            total = 0.0
            for j in range(3):
                total = total + across(gr[j, rows, :], wg[j].reshape(MODEL_WIDTH, own_width))
            gnp[target, pl.ds(pl.multiple_of(step * block, block), block), :] = total.astype(BF16)
            return carry

        straight(0, span // block, body)

    away_other, away_same = (1 - x) * 2 + (1 - c), (1 - x) * 2 + c
    home_other = x * 2 + (1 - c)
    gn = {}

    def need_late():
        while late_loads:
            late_loads.pop().wait()

    def rows_away():
        need_late()
        back_rows(away_other)
        gn["core"] = move.send(gnp.at[away_other], gnr.at[0], here.core())

    def rows_across():
        back_rows(away_same)
        gn["core"].wait_recv()

        def add_rows(step, carry):
            rows = pl.ds(pl.multiple_of(step * block, block), block)
            gnp[away_same, rows, :] = gnp[away_same, rows, :] + gnr[0, rows, :]
            return carry

        lax.fori_loop(0, span // block, add_rows, 0)
        gn["x"] = move.send(gnp.at[away_same], gnx, here.across_x())

    def rows_home():
        back_rows(home_other)
        gn["home"] = move.send(gnp.at[home_other], gnr.at[1], here.core())
        back_rows(g)

    tile = 256

    def weight_rows(j):
        def body(step, carry):
            columns = pl.ds(pl.multiple_of(step * tile, tile), tile)
            result = from_rows(normed[:, columns], gr[j]).astype(BF16)
            per = 2 * 4 * shard // tile
            lead = result.reshape(tile // (4 * shard), 4, shard, own_width)
            for n in range(tile // (4 * shard)):
                gw[j, step // per, (step % per) * (tile // (4 * shard)) + n] = lead[n]
            return carry

        straight(0, MODEL_WIDTH // tile, body)

    gw_y, gw_z = {}, {}

    def weights_y(j):
        need_late()
        weight_rows(j)
        gw_y[j] = move.send(gw.at[j, :, 1 - y], gwy.at[j], here.across_y())

    def weights_z(j):
        gw_y[j].wait_recv()

        def add(step, carry):
            gw[j, step, y] = gw[j, step, y] + gwy[j, step]
            return carry

        lax.fori_loop(0, depth, add, 0)
        gw_z[j] = [move.send(gw.at[j, here.ahead(k), y], gwz.at[j, k - 1], here.along_z(k)) for k in steps_z]

    outs = (dwq, dwk, dwv)
    final = []
    final_locals = []

    def weights_last(j):
        total = gw[j, z, y].astype(F32)
        for k in steps_z:
            gw_z[j][k - 1].wait_recv()
            total = total + gwz[j, k - 1].astype(F32)
        gsum[j] = total
        columns = pl.ds(pl.multiple_of(g * own_width, LANES), own_width)
        final_locals.append(move.local(gsum.at[j, g], outs[j].at[:, columns]))
        for k in (1, 2, 3):
            final.append(move.send(gsum.at[j, (g + k) % 4], outs[j].at[:, columns], here.row_peer(k)))

    bias_legs = []

    def bias_start():
        ones = jnp.ones((16, rows_all), BF16)
        btile[...] = bias_in[...]
        for j in range(3):
            sums = product(ones, gr[j])
            for half in range(2):
                btile[pl.ds(8 * j + g * 2 + half, 1), :] = sums[0:1, half * LANES : (half + 1) * LANES]
        bias_legs.append(move.send(btile, brecv.at[0], here.core()))

    def bias_next():
        done = len(bias_legs)
        bias_legs[-1].wait()
        btile[...] = btile[...] + brecv[done - 1]
        if done < 3:
            peer = (here.across_x, here.across_y)[done - 1]()
            bias_legs.append(move.send(btile, brecv.at[done], peer))
        else:
            bias_legs.extend([move.send(btile, bz.at[k - 1], here.along_z(k)) for k in steps_z])

    def bias_last():
        for copy in bias_legs[3:]:
            copy.wait()
        total = btile[...]
        for k in steps_z:
            total = total + bz[k - 1]
        btile[...] = total

    high, middle, rest_part = three_parts(mods[0:4, MODEL_WIDTH : 2 * MODEL_WIDTH])
    mod3[0:4, :] = high
    mod3[4:8, :] = middle
    mod3[8:12, :] = rest_part
    mod3[12:16, :] = jnp.zeros((4, MODEL_WIDTH), F32)
    acc_shift[...] = jnp.zeros_like(acc_shift)
    acc_scale[...] = jnp.zeros_like(acc_scale)
    def two_parts(values):
        top = values.astype(BF16)
        return top, (values - top.astype(F32)).astype(BF16)

    def norm_rows(step, carry):
        rows = pl.ds(pl.multiple_of(step * block, block), block)
        grad = gnp[g, rows, :].astype(F32) + gnr[1, rows, :].astype(F32) + gnx[rows, :].astype(F32)
        values = frames[rows, :].astype(F32)
        center = jnp.mean(values, axis=1, keepdims=True)
        centered = values - center
        scaled = lax.rsqrt(jnp.mean(centered * centered, axis=1, keepdims=True) + EPSILON)
        hat = centered * scaled
        base = g * span + step * block
        segment, _ = frame_segments(lens, base, block, 16)
        slot = lanes_of((block, 16))
        chosen = jnp.where((slot < 12) & (slot % 4 == segment), 1.0, 0.0).astype(BF16)
        inner = grad * (1.0 + product(chosen, mod3[...].astype(BF16)))
        mean_one = jnp.mean(inner, axis=1, keepdims=True)
        mean_two = jnp.mean(inner * hat, axis=1, keepdims=True)
        fgrad[rows, :] = (gmid[rows, :] + scaled * (inner - mean_one - hat * mean_two)).astype(BF16)
        position = base + lanes_of((16, block))
        begin = [lens[0, 0], lens[0, 0] + lens[0, 1], lens[0, 0] + lens[0, 1] + lens[0, 2]]
        inside = sum((position >= edge).astype(jnp.int32) for edge in begin)
        members = jnp.where(inside == lanes_of((16, block), 0), 1.0, 0.0).astype(BF16)
        for values, target in ((grad, acc_shift), (grad * hat, acc_scale)):
            top, bottom = two_parts(values)
            target[...] += product(members, top) + product(members, bottom)
        return carry

    fourth_part = MODEL_WIDTH // 2
    mod_legs = {}

    def mods_core():
        for side in range(2):
            mg[side] = mg_in[:, side * fourth_part : (side + 1) * fourth_part]
        mod_legs["core"] = move.send(mg.at[1 - c], mgr, here.core())

    def mods_x():
        mod_legs["core"].wait_recv()
        mgs[...] = mg[c] + mgr[...]
        mod_legs["x"] = move.send(mgs, mgx, here.across_x())

    def mods_z():
        mod_legs["x"].wait_recv()
        ev[z, y, c] = (mgs[...] + mgx[...]).astype(BF16)
        mod_legs["z"] = [move.send(ev.at[z, y, c], ev.at[z, y, c], here.along_z(k)) for k in steps_z]

    def mods_y():
        for copy in mod_legs["z"]:
            copy.wait_recv()
        mod_legs["y"] = move.send(ev.at[:, y, c], ev.at[:, y, c], here.across_y())

    def mods_share():
        mod_legs["y"].wait_recv()
        mod_legs["last"] = move.send(ev.at[:, :, c], ev.at[:, :, c], here.core())

    every_row = 32 * depth
    picks = jnp.where(
        lanes_of((16, every_row), 0) == (lanes_of((16, every_row)) % 16) // 4, 1.0, 0.0
    ).astype(BF16)

    def place_columns(every, start, stride):
        size = every.shape[1]
        result = from_rows(low[...], every)
        summed = product(picks, every)
        for strip in range(4):
            columns = slice(start + strip * stride, start + strip * stride + size)
            dmw[:, columns] = result[32 * strip : 32 * (strip + 1), :]
            mbias[0:1, columns] = summed[strip : strip + 1, :]

    def mods_early():
        mod_legs["last"].wait_recv()
        for side in range(2):
            every = ev[:, :, side].reshape(every_row, fourth_part)
            place_columns(every, 2 * MODEL_WIDTH + side * fourth_part, MODEL_WIDTH)

    def norm_part():
        gn["home"].wait_recv()
        gn["x"].wait_recv()
        straight(0, span // block, norm_rows)
        late[0, 0:4, :] = acc_shift[0:4, :]
        late[0, 4:8, :] = acc_scale[0:4, :]
        mod_legs["row"] = [move.send(late.at[0], late.at[k], here.row_peer(k)) for k in (1, 2, 3)]

    def mods_rows():
        for copy in mod_legs["row"]:
            copy.wait_recv()
        total = (late[0] + late[1]) + (late[2] + late[3])
        joined[0:4, :] = total[0:4, :fourth_part]
        joined[4:8, :] = total[0:4, fourth_part:]
        joined[8:12, :] = total[4:8, :fourth_part]
        joined[12:16, :] = total[4:8, fourth_part:]
        ez[z, y] = joined[...].astype(BF16)
        peers = [here.along_z(k) for k in steps_z] + [here.across_y()]
        peers += [here.at(here.ahead(k), 1 - y, x, c) for k in steps_z]
        mod_legs["all"] = [move.send(ez.at[z, y], ez.at[z, y], peer) for peer in peers]

    def mods_late():
        for copy in mod_legs["all"]:
            copy.wait_recv()
        place_columns(ez[...].reshape(every_row, fourth_part), 0, fourth_part)

    stages = {
        SUM_ONE: sum_first, SUM_TWO: sum_second, SUM_THREE: sum_third, SUM_LAST: sum_last,
        WEIGHTS_Y: weights_y, WEIGHTS_Z: weights_z, WEIGHTS_LAST: weights_last,
    }
    others = {
        ROWS_AWAY: rows_away, ROWS_ACROSS: rows_across, ROWS_HOME: rows_home, NORM: norm_part,
        EARLY_CORE: mods_core, EARLY_X: mods_x, EARLY_Z: mods_z, EARLY_Y: mods_y, EARLY_SHARE: mods_share, EARLY_DONE: mods_early,
        LATE_ROWS: mods_rows, LATE_DONE: mods_late, BIAS_START: bias_start, BIAS_NEXT: bias_next, BIAS_DONE: bias_last,
    }
    clear()
    done = 0
    for code, number in BACKWARD_ORDER:
        if code == ATTEND_BACK:
            ahead = number
            while ahead:
                pair, at = done // steps, done % steps
                now = min(ahead, steps - at)
                back_some(pair, at, at + now)
                done, ahead = done + now, ahead - now
                if done % steps == 0:
                    settle_pair(pair)
                    if pair == 0:
                        clear()
        elif code in others:
            others[code]()
        else:
            stages[code](number)
    for copy in final_locals:
        copy.wait()
    for copy in final:
        copy.wait_recv()
    move.finish(but=bias_legs)


def backward_call(depth, span, own_rows, down_rows, hidden, args):
    rows_all, own_width = 4 * span, MODEL_WIDTH // 4
    half = MODEL_WIDTH // 2
    vmem, anywhere, scalar = (
        pl.BlockSpec(memory_space=pltpu.VMEM),
        pl.BlockSpec(memory_space=pl.ANY),
        pl.BlockSpec(memory_space=pltpu.SMEM),
    )

    def out(shape, dtype):
        return jax.ShapeDtypeStruct(shape, dtype)

    outs = [
        (out((span, MODEL_WIDTH), BF16), vmem),
        (out((own_rows, MODEL_WIDTH), F32), anywhere),
        (out((own_rows, MODEL_WIDTH), F32), anywhere),
        (out((own_rows, MODEL_WIDTH), F32), anywhere),
        (out((own_rows, MODEL_WIDTH), F32), vmem),
        (out((own_rows, hidden), F32), vmem),
        (out((down_rows, MODEL_WIDTH), F32), vmem),
        (out((own_rows, 6 * MODEL_WIDTH), F32), vmem),
        (out((8, 6 * MODEL_WIDTH), F32), vmem),
        (out((56, LANES), F32), vmem),
    ]
    pair_rows = pltpu.VMEM((2, rows_all, LANES), BF16)
    wide_rows = pltpu.VMEM((2, rows_all, 2 * LANES), BF16)
    table = pltpu.VMEM((rows_all, LANES), F32)
    scratch = [
        pair_rows, pair_rows, pair_rows, table,
        pltpu.VMEM((rows_all, MODEL_WIDTH), BF16),
        pltpu.VMEM((3, depth, 2, 4, own_rows, own_width), BF16),
        table, table, wide_rows, wide_rows,
        pltpu.VMEM((rows_all, LANES), BF16),
        table, table,
        pltpu.VMEM((3, rows_all, own_width), BF16),
        pltpu.VMEM((3, depth, 2, 4, own_rows, own_width), BF16),
        pltpu.VMEM((3, depth, 4, own_rows, own_width), BF16),
        pltpu.VMEM((3, depth - 1, 4, own_rows, own_width), BF16),
        pltpu.VMEM((3, 4, own_rows, own_width), F32),
        pltpu.VMEM((4, span, MODEL_WIDTH), BF16),
        pltpu.VMEM((2, span, MODEL_WIDTH), BF16),
        pltpu.VMEM((span, MODEL_WIDTH), BF16),
        pltpu.VMEM((16, MODEL_WIDTH), F32),
        pltpu.VMEM((16, MODEL_WIDTH), F32),
        pltpu.VMEM((16, MODEL_WIDTH), F32),
        pltpu.VMEM((2, 16, half), F32),
        pltpu.VMEM((16, half), F32),
        pltpu.VMEM((16, half), F32),
        pltpu.VMEM((16, half), F32),
        pltpu.VMEM((depth, 2, 2, 16, half), BF16),
        pltpu.VMEM((4, 8, MODEL_WIDTH), F32),
        pltpu.VMEM((16, half), F32),
        pltpu.VMEM((depth, 2, 16, half), BF16),
        pltpu.VMEM((3, 56, LANES), F32),
        pltpu.VMEM((depth - 1, 56, LANES), F32),
    ]
    piece = (own_rows // 2, MODEL_WIDTH)
    for lead in ((depth, 2, 2), (depth, 2, 2), (depth, 2), (depth,), (depth - 1,)):
        scratch += [pltpu.VMEM(lead + piece, BF16)] * 10
    scratch += [pltpu.SemaphoreType.DMA((128,)), pltpu.SemaphoreType.DMA((128,)), pltpu.SemaphoreType.DMA((32,))]
    return pl.pallas_call(
        partial(backward_kernel, depth),
        out_shape=[shape for shape, _ in outs],
        in_specs=[scalar] + [anywhere] * 10 + [vmem] * 6 + [anywhere] * 3,
        out_specs=[spec for _, spec in outs],
        scratch_shapes=scratch,
        compiler_params=pltpu.CompilerParams(
            collective_id=1, has_side_effects=True, vmem_limit_bytes=62 * 1024 * 1024
        ),
        cost_estimate=pl.CostEstimate(flops=2 * 10**10, bytes_accessed=40 * 10**6, transcendentals=10**7),
    )(*args)


def modulated_norm(values, shift_part, scale_part):
    center = jnp.mean(values, axis=-1, keepdims=True)
    centered = values - center
    variance = jnp.mean(centered * centered, axis=-1, keepdims=True)
    return centered * lax.rsqrt(variance + EPSILON) * (1.0 + scale_part) + shift_part


def rotate(values, cosines, sines_table):
    shaped = values.reshape(values.shape[:-1] + (values.shape[-1] // HEAD_DIM, HEAD_DIM))
    first_half = shaped[..., : HEAD_DIM // 2]
    second_half = shaped[..., HEAD_DIM // 2 :]
    cosine = cosines[..., None, :]
    sine_part = sines_table[..., None, :]
    turned = jnp.concatenate(
        [
            first_half * cosine - second_half * sine_part,
            second_half * cosine + first_half * sine_part,
        ],
        axis=-1,
    )
    return turned.reshape(values.shape)


def gelu_tanh(values):
    return jax.nn.gelu(values, approximate=True)


def time_features(time_index):
    halfway = MODEL_WIDTH // 2
    frequency = jnp.exp(jnp.arange(halfway, dtype=jnp.float32) * (-math.log(10000.0) / halfway))
    angles = time_index.astype(jnp.float32)[..., None] * frequency
    return jnp.concatenate([jnp.sin(angles), jnp.cos(angles)], axis=-1)


def segment_starts(segment_lengths):
    return jnp.cumsum(segment_lengths, axis=1) - segment_lengths


def segment_numbers(segment_lengths, frame_positions):
    starts = segment_starts(segment_lengths)
    inside = (frame_positions[None, :, None] >= starts[:, None, :]).astype(jnp.int32)
    return jnp.sum(inside, axis=2) - 1


def segment_layout(segment_lengths, frame_positions):
    starts = segment_starts(segment_lengths)
    segment = segment_numbers(segment_lengths, frame_positions)
    onehot = (segment[..., None] == jnp.arange(SEGS, dtype=jnp.int32)).astype(jnp.float32)
    offset = jnp.sum(onehot * starts[:, None, :].astype(jnp.float32), axis=2)
    relative = frame_positions[None, :].astype(jnp.float32) - offset
    return (onehot, relative)


def rope_tables(relative):
    halfway = HEAD_DIM // 2
    frequency = jnp.exp(jnp.arange(halfway, dtype=jnp.float32) * (-math.log(10000.0) / halfway))
    angles = relative[..., None] * frequency
    return (jnp.cos(angles), jnp.sin(angles))


def project(values, matrix, offset):
    return jnp.einsum(
        "rld,de->rle", values, matrix, preferred_element_type=jnp.float32
    ) + offset.astype(jnp.float32)


def project_back(gradient, matrix):
    return jnp.einsum("rle,de->rld", gradient, matrix, preferred_element_type=jnp.float32)


def weight_gradient(values, gradient):
    return jnp.einsum("rld,rle->de", values, gradient, preferred_element_type=jnp.float32)


def bias_gradient(gradient):
    return jnp.sum(gradient.astype(jnp.float32), axis=(0, 1))


def lift_up(member):
    return member.reshape((1, 1) + member.shape)


def settle(member):
    return member.reshape((-1,) + member.shape[3:])


def spread(member, wide_count, narrow_count):
    return member.reshape((wide_count, narrow_count, -1) + member.shape[1:])


def unpack(member):
    return member.reshape(member.shape[2:])


def on_device(
    frames,
    output_gradient,
    segment_lengths,
    time_index,
    query_weight,
    query_bias,
    key_weight,
    key_bias,
    value_weight,
    value_bias,
    output_projection,
    output_bias,
    up_weight,
    up_bias,
    down_weight,
    down_bias,
    modulation_weight,
    modulation_bias,
):
    narrow_count = lax.axis_size("seq")
    wide_count = lax.axis_size("dp")
    seq_index = lax.axis_index("seq")
    row_count, span_frames, width_total = frames.shape
    row_length = span_frames * narrow_count
    block_rows = min(512, row_length)
    block_count = row_length // block_rows
    local_weights = (
        query_weight,
        query_bias,
        key_weight,
        key_bias,
        value_weight,
        value_bias,
        output_projection,
        output_bias,
        up_weight,
        up_bias,
        down_weight,
        down_bias,
        modulation_bias,
    )
    lifted = [lift_up(member) for member in local_weights]
    halfway_set = (
        lax.all_gather(lifted[0], "dp", axis=0, tiled=True),
        lax.all_gather(lifted[1], "dp", axis=0, tiled=True),
        lax.all_gather(lifted[2], "dp", axis=0, tiled=True),
        lax.all_gather(lifted[3], "dp", axis=0, tiled=True),
        lax.all_gather(lifted[4], "dp", axis=0, tiled=True),
        lax.all_gather(lifted[5], "dp", axis=0, tiled=True),
        lax.all_gather(lifted[6], "dp", axis=0, tiled=True),
        lax.all_gather(lifted[7], "dp", axis=0, tiled=True),
        lax.all_gather(lifted[8], "dp", axis=0, tiled=True),
        lax.all_gather(lifted[9], "dp", axis=0, tiled=True),
        lax.all_gather(lifted[10], "dp", axis=0, tiled=True),
        lax.all_gather(lifted[11], "dp", axis=0, tiled=True),
        lax.all_gather(lifted[12], "dp", axis=0, tiled=True),
    )
    complete_set = (
        lax.all_gather(halfway_set[0], "seq", axis=1, tiled=True),
        lax.all_gather(halfway_set[1], "seq", axis=1, tiled=True),
        lax.all_gather(halfway_set[2], "seq", axis=1, tiled=True),
        lax.all_gather(halfway_set[3], "seq", axis=1, tiled=True),
        lax.all_gather(halfway_set[4], "seq", axis=1, tiled=True),
        lax.all_gather(halfway_set[5], "seq", axis=1, tiled=True),
        lax.all_gather(halfway_set[6], "seq", axis=1, tiled=True),
        lax.all_gather(halfway_set[7], "seq", axis=1, tiled=True),
        lax.all_gather(halfway_set[8], "seq", axis=1, tiled=True),
        lax.all_gather(halfway_set[9], "seq", axis=1, tiled=True),
        lax.all_gather(halfway_set[10], "seq", axis=1, tiled=True),
        lax.all_gather(halfway_set[11], "seq", axis=1, tiled=True),
        lax.all_gather(halfway_set[12], "seq", axis=1, tiled=True),
    )
    gathered = [settle(member) for member in complete_set]
    (
        full_query,
        full_query_bias,
        full_key,
        full_key_bias,
        full_value,
        full_value_bias,
        full_output,
        full_output_bias,
        full_up,
        full_up_bias,
        full_down,
        full_down_bias,
        full_modulation_bias,
    ) = gathered
    local_positions = seq_index * span_frames + jnp.arange(span_frames, dtype=jnp.int32)
    local_onehot, local_relative = segment_layout(segment_lengths, local_positions)
    row_segment = segment_numbers(segment_lengths, jnp.arange(row_length, dtype=jnp.int32))
    cosines, sines_table = rope_tables(local_relative)
    turning = partial(rotate, cosines=cosines, sines_table=sines_table)
    owned_rows = modulation_weight.shape[0]
    owned_start = (lax.axis_index("dp") * narrow_count + seq_index) * owned_rows
    every_time = lax.all_gather(time_index, "dp", axis=0, tiled=True)
    every_low = jax.nn.silu(time_features(every_time)).astype(jnp.bfloat16)
    owned_low = lax.dynamic_slice_in_dim(every_low, owned_start, owned_rows, 2)
    partial_modulation = jnp.einsum(
        "rsd,dc->rsc", owned_low, modulation_weight, preferred_element_type=jnp.float32
    )
    row_share = lax.psum_scatter(partial_modulation, "dp", scatter_dimension=0, tiled=True)
    modulation = lax.psum(row_share.astype(jnp.bfloat16), "seq").astype(
        jnp.float32
    ) + full_modulation_bias.astype(jnp.float32)
    per_frame = jnp.einsum("rls,rsc->rlc", local_onehot, modulation, precision=HIGHEST)
    shift_one, scale_one, gate_one, shift_two, scale_two, gate_two = jnp.split(
        per_frame, 6, axis=-1
    )
    inputs = frames.astype(jnp.float32)
    normed, norm_back = jax.vjp(modulated_norm, inputs, shift_one, scale_one)
    normed_low = normed.astype(jnp.bfloat16)
    query_pre = project(normed_low, full_query, full_query_bias)
    key_pre = project(normed_low, full_key, full_key_bias)
    value_low = project(normed_low, full_value, full_value_bias).astype(jnp.bfloat16)
    query_turned, query_back = jax.vjp(turning, query_pre)
    key_turned, key_back = jax.vjp(turning, key_pre)
    query_heads, key_heads, value_heads = (
        lax.all_to_all(
            query_turned.astype(jnp.bfloat16), "seq", split_axis=2, concat_axis=1, tiled=True
        ),
        lax.all_to_all(
            key_turned.astype(jnp.bfloat16), "seq", split_axis=2, concat_axis=1, tiled=True
        ),
        lax.all_to_all(value_low, "seq", split_axis=2, concat_axis=1, tiled=True),
    )
    local_heads = query_heads.shape[2] // HEAD_DIM
    head_shape = (row_count, row_length, local_heads, HEAD_DIM)
    queries = query_heads.reshape(head_shape)
    keys_all = key_heads.reshape(head_shape)
    values_all = value_heads.reshape(head_shape)
    scaling = HEAD_DIM ** (-0.5)
    positions_all = jnp.arange(row_count * block_count, dtype=jnp.int32)

    def fetch_block(position):
        row_index = position // block_count
        start_row = position % block_count * block_rows
        key_row = lax.dynamic_index_in_dim(keys_all, row_index, 0, keepdims=False)
        value_row = lax.dynamic_index_in_dim(values_all, row_index, 0, keepdims=False)
        segment_row = lax.dynamic_index_in_dim(row_segment, row_index, 0, keepdims=False)
        query_block = lax.dynamic_slice_in_dim(
            lax.dynamic_index_in_dim(queries, row_index, 0, keepdims=False),
            start_row,
            block_rows,
            0,
        )
        segment_block = lax.dynamic_slice_in_dim(segment_row, start_row, block_rows, 0)
        scores = (
            jnp.einsum("bhd,khd->hbk", query_block, key_row, preferred_element_type=jnp.float32)
            * scaling
        )
        scores = jnp.where((segment_block[:, None] == segment_row[None, :])[None], scores, NEGATIVE)
        return (row_index, start_row, query_block, key_row, value_row, scores)

    def forward_block(position):
        row_index, start_row, query_block, key_row, value_row, scores = fetch_block(position)
        highest = jnp.max(scores, axis=2, keepdims=True)
        weights = jnp.exp(scores - highest)
        totals = jnp.sum(weights, axis=2, keepdims=True)
        probabilities = (weights / totals).astype(jnp.bfloat16)
        mixed_block = jnp.einsum(
            "hbk,khd->bhd", probabilities, value_row, preferred_element_type=jnp.float32
        )
        return (
            mixed_block.astype(jnp.bfloat16).reshape(block_rows, -1),
            (highest + jnp.log(totals))[..., 0],
        )

    mixed_blocks, logsums = lax.map(forward_block, positions_all)
    attention_heads = mixed_blocks.reshape(row_count, row_length, -1)
    attention_frames = lax.all_to_all(
        attention_heads, "seq", split_axis=1, concat_axis=2, tiled=True
    )
    branch = project(attention_frames, full_output, full_output_bias)
    middle = inputs + gate_one * branch
    normed_two, norm_two_back = jax.vjp(modulated_norm, middle, shift_two, scale_two)
    normed_two_low = normed_two.astype(jnp.bfloat16)
    hidden = project(normed_two_low, full_up, full_up_bias)
    activated, gelu_back = jax.vjp(gelu_tanh, hidden)
    activated_low = activated.astype(jnp.bfloat16)
    branch_two = project(activated_low, full_down, full_down_bias)
    layer_output = (middle + gate_two * branch_two).astype(jnp.bfloat16)
    cotangent = output_gradient.astype(jnp.float32)
    grad_branch_two = (gate_two * cotangent).astype(jnp.bfloat16)
    grad_gate_two = cotangent * branch_two
    grad_activated = project_back(grad_branch_two, full_down)
    grad_hidden = gelu_back(grad_activated)[0].astype(jnp.bfloat16)
    grad_normed_two = project_back(grad_hidden, full_up)
    grad_middle_part, grad_shift_two, grad_scale_two = norm_two_back(grad_normed_two)
    grad_middle = cotangent + grad_middle_part
    grad_gate_one = grad_middle * branch
    grad_branch = (gate_one * grad_middle).astype(jnp.bfloat16)
    grad_attention = project_back(grad_branch, full_output).astype(jnp.bfloat16)
    grad_heads = lax.all_to_all(grad_attention, "seq", split_axis=2, concat_axis=1, tiled=True)
    grad_outputs = grad_heads.reshape(head_shape)

    def backward_block(running, pair_inputs):
        grad_keys, grad_values = running
        position, logsum = pair_inputs
        row_index, start_row, query_block, key_row, value_row, scores = fetch_block(position)
        grad_block = lax.dynamic_slice_in_dim(
            lax.dynamic_index_in_dim(grad_outputs, row_index, 0, keepdims=False),
            start_row,
            block_rows,
            0,
        )
        probabilities = jnp.exp(scores - logsum[..., None])
        grad_probabilities = jnp.einsum(
            "bhd,khd->hbk", grad_block, value_row, preferred_element_type=jnp.float32
        )
        delta_sum = jnp.sum(probabilities * grad_probabilities, axis=2, keepdims=True)
        grad_scores = (probabilities * (grad_probabilities - delta_sum)).astype(jnp.bfloat16)
        grad_query_block = (
            jnp.einsum("hbk,khd->bhd", grad_scores, key_row, preferred_element_type=jnp.float32)
            * scaling
        )
        key_part = (
            jnp.einsum("hbk,bhd->khd", grad_scores, query_block, preferred_element_type=jnp.float32)
            * scaling
        )
        value_part = jnp.einsum(
            "hbk,bhd->khd",
            probabilities.astype(jnp.bfloat16),
            grad_block,
            preferred_element_type=jnp.float32,
        )
        grad_keys = lax.dynamic_update_index_in_dim(
            grad_keys,
            lax.dynamic_index_in_dim(grad_keys, row_index, 0, keepdims=False) + key_part,
            row_index,
            0,
        )
        grad_values = lax.dynamic_update_index_in_dim(
            grad_values,
            lax.dynamic_index_in_dim(grad_values, row_index, 0, keepdims=False) + value_part,
            row_index,
            0,
        )
        return (
            (grad_keys, grad_values),
            grad_query_block.astype(jnp.bfloat16).reshape(block_rows, -1),
        )

    zero_heads = jnp.zeros(head_shape, jnp.float32)
    (grad_keys_all, grad_values_all), grad_query_blocks = lax.scan(
        backward_block, (zero_heads, zero_heads), (positions_all, logsums)
    )
    flat_shape = (row_count, row_length, -1)
    grad_query_frames, grad_key_frames, grad_value_frames = (
        lax.all_to_all(
            grad_query_blocks.reshape(flat_shape), "seq", split_axis=1, concat_axis=2, tiled=True
        ),
        lax.all_to_all(
            grad_keys_all.reshape(flat_shape).astype(jnp.bfloat16),
            "seq",
            split_axis=1,
            concat_axis=2,
            tiled=True,
        ),
        lax.all_to_all(
            grad_values_all.reshape(flat_shape).astype(jnp.bfloat16),
            "seq",
            split_axis=1,
            concat_axis=2,
            tiled=True,
        ),
    )
    grad_query_pre = query_back(grad_query_frames.astype(jnp.float32))[0].astype(jnp.bfloat16)
    grad_key_pre = key_back(grad_key_frames.astype(jnp.float32))[0].astype(jnp.bfloat16)
    grad_normed = (
        project_back(grad_query_pre, full_query)
        + project_back(grad_key_pre, full_key)
        + project_back(grad_value_frames, full_value)
    )
    grad_inputs_part, grad_shift_one, grad_scale_one = norm_back(grad_normed)
    frames_grad = (grad_middle + grad_inputs_part).astype(jnp.bfloat16)
    grad_per_frame = jnp.concatenate(
        [
            grad_shift_one,
            grad_scale_one,
            grad_gate_one,
            grad_shift_two,
            grad_scale_two,
            grad_gate_two,
        ],
        axis=-1,
    )
    grad_modulation = jnp.einsum("rls,rlc->rsc", local_onehot, grad_per_frame, precision=HIGHEST)
    gradients = (
        weight_gradient(normed_low, grad_query_pre),
        bias_gradient(grad_query_pre),
        weight_gradient(normed_low, grad_key_pre),
        bias_gradient(grad_key_pre),
        weight_gradient(normed_low, grad_value_frames),
        bias_gradient(grad_value_frames),
        weight_gradient(attention_frames, grad_branch),
        bias_gradient(grad_branch),
        weight_gradient(normed_two_low, grad_hidden),
        bias_gradient(grad_hidden),
        weight_gradient(activated_low, grad_branch_two),
        bias_gradient(grad_branch_two),
        jnp.sum(grad_modulation, axis=(0, 1)),
    )
    row_total = lax.psum(grad_modulation.astype(jnp.bfloat16), "seq").astype(jnp.float32)
    every_grad = lax.all_gather(row_total.astype(jnp.bfloat16), "dp", axis=0, tiled=True).astype(
        row_total.dtype
    )
    modulation_weight_grad = jnp.einsum(
        "rsd,rsc->dc", owned_low.astype(jnp.float32), every_grad, precision=HIGHEST
    )
    spreaded = [spread(member, wide_count, narrow_count) for member in gradients]
    first_pass = (
        lax.psum_scatter(
            spreaded[0].astype(jnp.bfloat16), "seq", scatter_dimension=1, tiled=True
        ).astype(jnp.float32),
        lax.psum_scatter(
            spreaded[1].astype(jnp.bfloat16), "seq", scatter_dimension=1, tiled=True
        ).astype(jnp.float32),
        lax.psum_scatter(
            spreaded[2].astype(jnp.bfloat16), "seq", scatter_dimension=1, tiled=True
        ).astype(jnp.float32),
        lax.psum_scatter(
            spreaded[3].astype(jnp.bfloat16), "seq", scatter_dimension=1, tiled=True
        ).astype(jnp.float32),
        lax.psum_scatter(
            spreaded[4].astype(jnp.bfloat16), "seq", scatter_dimension=1, tiled=True
        ).astype(jnp.float32),
        lax.psum_scatter(
            spreaded[5].astype(jnp.bfloat16), "seq", scatter_dimension=1, tiled=True
        ).astype(jnp.float32),
        lax.psum_scatter(
            spreaded[6].astype(jnp.bfloat16), "seq", scatter_dimension=1, tiled=True
        ).astype(jnp.float32),
        lax.psum_scatter(
            spreaded[7].astype(jnp.bfloat16), "seq", scatter_dimension=1, tiled=True
        ).astype(jnp.float32),
        lax.psum_scatter(
            spreaded[8].astype(jnp.bfloat16), "seq", scatter_dimension=1, tiled=True
        ).astype(jnp.float32),
        lax.psum_scatter(
            spreaded[9].astype(jnp.bfloat16), "seq", scatter_dimension=1, tiled=True
        ).astype(jnp.float32),
        lax.psum_scatter(
            spreaded[10].astype(jnp.bfloat16), "seq", scatter_dimension=1, tiled=True
        ).astype(jnp.float32),
        lax.psum_scatter(
            spreaded[11].astype(jnp.bfloat16), "seq", scatter_dimension=1, tiled=True
        ).astype(jnp.float32),
        lax.psum_scatter(
            spreaded[12].astype(jnp.bfloat16), "seq", scatter_dimension=1, tiled=True
        ).astype(jnp.float32),
    )
    second_pass = (
        lax.psum_scatter(first_pass[0], "dp", scatter_dimension=0, tiled=True),
        lax.psum_scatter(first_pass[1], "dp", scatter_dimension=0, tiled=True),
        lax.psum_scatter(first_pass[2], "dp", scatter_dimension=0, tiled=True),
        lax.psum_scatter(first_pass[3], "dp", scatter_dimension=0, tiled=True),
        lax.psum_scatter(first_pass[4], "dp", scatter_dimension=0, tiled=True),
        lax.psum_scatter(first_pass[5], "dp", scatter_dimension=0, tiled=True),
        lax.psum_scatter(first_pass[6], "dp", scatter_dimension=0, tiled=True),
        lax.psum_scatter(first_pass[7], "dp", scatter_dimension=0, tiled=True),
        lax.psum_scatter(first_pass[8], "dp", scatter_dimension=0, tiled=True),
        lax.psum_scatter(first_pass[9], "dp", scatter_dimension=0, tiled=True),
        lax.psum_scatter(first_pass[10], "dp", scatter_dimension=0, tiled=True),
        lax.psum_scatter(first_pass[11], "dp", scatter_dimension=0, tiled=True),
        lax.psum_scatter(first_pass[12], "dp", scatter_dimension=0, tiled=True),
    )
    reduced = [unpack(member) for member in second_pass]
    return (
        layer_output,
        frames_grad,
        reduced[0],
        reduced[1],
        reduced[2],
        reduced[3],
        reduced[4],
        reduced[5],
        reduced[6],
        reduced[7],
        reduced[8],
        reduced[9],
        reduced[10],
        reduced[11],
        modulation_weight_grad,
        reduced[12],
    )


def hand_over_kernel(count, lengths, *refs):
    sources, refs = refs[: count + 2], refs[count + 2 :]
    targets, vectors, sems = refs[:count], refs[count:-1], refs[-1]
    copies = [
        pltpu.make_async_copy(sources[n], targets[n], sems.at[n]) for n in range(count)
    ]
    for copy in copies:
        copy.start()
    index = lax.axis_index("dp") * 4 + lax.axis_index("seq")
    sums, strip = sources[count], sources[count + 1]
    first = 0
    for vector, size in zip(vectors, lengths):
        start = index * size
        row = sums[pl.ds(first + start // LANES, 1), :]
        vector[...] = pltpu.roll(row, (LANES - start % LANES) % LANES, 1)[:, :size]
        first += size * lax.axis_size("dp") * 4 // LANES
    size = vectors[-1].shape[1]
    start = index * size
    wide = strip[0:1, pl.ds(pl.multiple_of(start // LANES * LANES, LANES), 2 * LANES)]
    vectors[-1][...] = pltpu.roll(wide, (2 * LANES - start % LANES) % (2 * LANES), 1)[:, :size]
    for copy in copies:
        copy.wait()


def hand_over(lengths, arrays, sums, strip):
    anywhere, vmem = pl.BlockSpec(memory_space=pl.ANY), pl.BlockSpec(memory_space=pltpu.VMEM)
    count = len(arrays)
    return pl.pallas_call(
        partial(hand_over_kernel, count, lengths[:-1]),
        out_shape=[jax.ShapeDtypeStruct(array.shape, array.dtype) for array in arrays]
        + [jax.ShapeDtypeStruct((1, size), F32) for size in lengths],
        in_specs=[vmem] * (count + 2),
        out_specs=[anywhere] * count + [vmem] * len(lengths),
        scratch_shapes=[pltpu.SemaphoreType.DMA((count,))],
    )(*arrays, sums, strip)


def on_device_fast(
    frames, output_gradient, segment_lengths, time_index, query_weight, query_bias, key_weight, key_bias,
    value_weight, value_bias, output_projection, output_bias, up_weight, up_bias, down_weight, down_bias,
    modulation_weight, modulation_bias,
):
    depth = lax.axis_size("dp") // 2
    _, span, width = frames.shape
    own_rows, hidden = up_weight.shape
    down_rows = down_weight.shape[0]
    vectors = (query_bias, key_bias, value_bias, output_bias, up_bias, down_bias, modulation_bias)
    biases = [vector.reshape(1, -1) for vector in vectors]
    (output, grad_middle, mg_in, bias_in, mods, low, gwo, gup, gdown, given_heads, qs, ks, vs, oh, lse, normed, wg,
     cosr, sinr) = forward_call(
        depth, span, own_rows, down_rows, hidden,
        (segment_lengths, time_index, frames[0], output_gradient[0], *biases, query_weight, key_weight, value_weight,
         output_projection, up_weight, down_weight, modulation_weight),
    )
    (fgrad, dwq, dwk, dwv, dwo, dup, ddown, dmw, mbias, btile) = backward_call(
        depth, span, own_rows, down_rows, hidden,
        (segment_lengths, given_heads, qs, ks, vs, oh, lse, normed, wg, cosr, sinr, low, mods, frames[0],
         grad_middle, mg_in, bias_in,
         gwo, gup, gdown),
    )
    lengths = tuple(vector.shape[0] for vector in vectors)
    output, fgrad, dwq, dwk, dwv, dwo, dup, ddown, dmw, *parts = hand_over(
        lengths, (output, fgrad, dwq, dwk, dwv, dwo, dup, ddown, dmw), btile, mbias
    )
    bq, bk, bv, bo, bu, bd, bm = [part.reshape(-1) for part in parts]
    return (
        output[None], fgrad[None], dwq, bq, dwk, bk, dwv, bv, dwo, bo, dup, bu, ddown, bd, dmw, bm,
    )


def fits(mesh, frames, *parameters):
    dp, seq = mesh.shape["dp"], mesh.shape["seq"]
    rows = parameters[3].shape[0] // (dp * seq)
    return seq == 4 and dp % 2 == 0 and rows == 32 and frames.shape[0] == dp


def solution(mesh):
    def run(*arrays):
        return mapped(mesh, on_device_fast if fits(mesh, *arrays) else on_device)(*arrays)

    return run


def mapped(mesh, body):
    return jax.shard_map(
        body,
        mesh=mesh,
        in_specs=(
            P("dp", "seq", None),
            P("dp", "seq", None),
            P("dp", None),
            P("dp", None),
            P(("dp", "seq"), None),
            P(("dp", "seq")),
            P(("dp", "seq"), None),
            P(("dp", "seq")),
            P(("dp", "seq"), None),
            P(("dp", "seq")),
            P(("dp", "seq"), None),
            P(("dp", "seq")),
            P(("dp", "seq"), None),
            P(("dp", "seq")),
            P(("dp", "seq"), None),
            P(("dp", "seq")),
            P(("dp", "seq"), None),
            P(("dp", "seq")),
        ),
        out_specs=(
            P("dp", "seq", None),
            P("dp", "seq", None),
            P(("dp", "seq"), None),
            P(("dp", "seq")),
            P(("dp", "seq"), None),
            P(("dp", "seq")),
            P(("dp", "seq"), None),
            P(("dp", "seq")),
            P(("dp", "seq"), None),
            P(("dp", "seq")),
            P(("dp", "seq"), None),
            P(("dp", "seq")),
            P(("dp", "seq"), None),
            P(("dp", "seq")),
            P(("dp", "seq"), None),
            P(("dp", "seq")),
        ),
        check_vma=False,
    )
```

```python
from functools import partial
import math

import jax
import jax.numpy as jnp
from jax import lax
from jax.experimental import pallas as pl
from jax.experimental.pallas import tpu as pltpu
from jax.sharding import PartitionSpec as P

HEAD_DIM = 64
MODEL_WIDTH = 1024
SEGS = 4
EPSILON = 1e-06
NEGATIVE = -1e30
HIGHEST = lax.Precision.HIGHEST
F32 = jnp.float32
BF16 = jnp.bfloat16
LANES = 128


class Mover:
    def __init__(self, send_sems, recv_sems, local_sems):
        self.send_sems, self.recv_sems, self.local_sems = send_sems, recv_sems, local_sems
        self.count = self.local_count = 0
        self.sent = []

    def send(self, source, target, device):
        slot = self.count
        self.count += 1
        copy = pltpu.make_async_remote_copy(
            src_ref=source,
            dst_ref=target,
            send_sem=self.send_sems.at[slot],
            recv_sem=self.recv_sems.at[slot],
            device_id=device,
            device_id_type=pl.DeviceIdType.MESH,
        )
        copy.start()
        self.sent.append(copy)
        return copy

    def local(self, source, target):
        slot = self.local_count
        self.local_count += 1
        copy = pltpu.make_async_copy(source, target, self.local_sems.at[slot])
        copy.start()
        return copy

    def finish(self, but=()):
        for copy in self.sent:
            if not any(copy is other for other in but):
                copy.wait_send()


class Place:
    def __init__(self, depth):
        dp, seq = lax.axis_index("dp"), lax.axis_index("seq")
        self.depth = depth
        self.z, self.y = dp // 2, dp % 2
        self.x, self.c = seq // 2, seq % 2
        self.seq = seq
        self.index = dp * 4 + seq

    def at(self, z, y, x, c):
        return {"dp": z * 2 + y, "seq": x * 2 + c}

    def core(self):
        return self.at(self.z, self.y, self.x, 1 - self.c)

    def across_x(self):
        return self.at(self.z, self.y, 1 - self.x, self.c)

    def across_y(self):
        return self.at(self.z, 1 - self.y, self.x, self.c)

    def ahead(self, step):
        return (self.z + step) % self.depth

    def along_z(self, step):
        return self.at(self.ahead(step), self.y, self.x, self.c)

    def row_peer(self, step):
        return {"dp": self.z * 2 + self.y, "seq": (self.seq + step) % 4}

    def enter(self, diagonal=False):
        barrier = pltpu.get_barrier_semaphore()
        peers = [self.row_peer(step) for step in (1, 2, 3)] + [self.across_y()]
        peers += [self.along_z(step) for step in range(1, self.depth)]
        if diagonal:
            peers += [self.at(self.ahead(k), 1 - self.y, self.x, self.c) for k in range(1, self.depth)]
        for peer in peers:
            pl.semaphore_signal(barrier, 1, device_id=peer, device_id_type=pl.DeviceIdType.MESH)
        pl.semaphore_wait(barrier, len(peers))


def lanes_of(shape, axis=1):
    return lax.broadcasted_iota(jnp.int32, shape, axis)


def frame_segments(lens, first_row, rows, width):
    position = lanes_of((rows, width), 0) + first_row
    first, second, third = lens[0, 0], lens[0, 0] + lens[0, 1], lens[0, 0] + lens[0, 1] + lens[0, 2]
    segment = (
        (position >= first).astype(jnp.int32)
        + (position >= second).astype(jnp.int32)
        + (position >= third).astype(jnp.int32)
    )
    start = jnp.where(
        segment == 0, 0, jnp.where(segment == 1, first, jnp.where(segment == 2, second, third))
    )
    return segment, position - start


def three_parts(values):
    high = values.astype(BF16).astype(F32)
    rest = values - high
    middle = rest.astype(BF16).astype(F32)
    return high, middle, (rest - middle).astype(BF16).astype(F32)


def swap_halves(values, lane):
    return jnp.where(
        lane % HEAD_DIM < HEAD_DIM // 2, pltpu.roll(values, 96, 1), pltpu.roll(values, 32, 1)
    )


def head_only(values, lane, head):
    return jnp.where((lane >= HEAD_DIM) == bool(head), values.astype(F32), 0.0).astype(BF16)


def across(left, right):
    return lax.dot_general(left, right, (((1,), (1,)), ((), ())), preferred_element_type=F32)


def product(left, right):
    return jnp.dot(left, right, preferred_element_type=F32)


def straight(first, last, body):
    for step in range(first, last):
        body(step, 0)


AXES = (
    (1, 2, 0), (0, 2, 1), (2, 0, 1), (0, 2, 1), (0, 1, 2), (0, 1, 2), (0, 2, 1), (0, 2, 1), (2, 1, 0), (0, 1, 2),
)
(
    GATHER_Z, GATHER_TWO, GATHER_THREE, GATHER_CORE, COLUMNS_Z, COLUMNS_Y, PROJECT, ATTEND, GO_UP, FRAMES_X,
    FRAMES_ON, TABLES, TIMES_Y, SHARE, MOD_Y, MOD_Z, MOD_X, MOD_LAST, FRAMES_CORE, BIAS_Y, BIAS_X, BIAS_CORE,
    BIASES, MODS, OUT, GO_DOWN, BACK, GRADS, WAITS,
) = range(29)
FORWARD_ORDER = (
    (FRAMES_X, 0), (GATHER_Z, 9), (GATHER_Z, 1), (TIMES_Y, 0), (BIAS_Y, 0), (FRAMES_CORE, 0), (GATHER_TWO, 9),
    (COLUMNS_Z, 0), (COLUMNS_Z, 1), (SHARE, 0), (GATHER_Z, 4), (GATHER_Z, 8), (BIAS_X, 0), (MOD_Y, 0),
    (COLUMNS_Y, 0), (GATHER_THREE, 9), (COLUMNS_Y, 1), (COLUMNS_Z, 2), (FRAMES_X, 1), (GATHER_Z, 3), (MOD_Z, 0),
    (GATHER_Z, 0), (GATHER_Z, 2), (GATHER_Z, 7), (GATHER_TWO, 8), (GATHER_Z, 6), (TABLES, 1), (BIAS_CORE, 0),
    (GATHER_TWO, 4), (BIASES, 0), (COLUMNS_Y, 2), (TABLES, 0), (GATHER_TWO, 0), (GATHER_TWO, 1), (FRAMES_ON, 1),
    (MOD_X, 0), (GATHER_Z, 5), (GATHER_TWO, 3), (GATHER_THREE, 1), (GATHER_TWO, 2), (MOD_LAST, 0),
    (GATHER_THREE, 4), (MODS, 0), (PROJECT, 0), (GATHER_CORE, 9), (GATHER_THREE, 3), (GATHER_TWO, 7),
    (FRAMES_ON, 0), (PROJECT, 1), (PROJECT, 2), (GATHER_THREE, 0), (GATHER_TWO, 6), (PROJECT, 3),
    (GATHER_CORE, 1), (GATHER_TWO, 5), (GATHER_THREE, 8), (ATTEND, 1), (GATHER_THREE, 2), (ATTEND, 1),
    (GATHER_CORE, 4), (GATHER_CORE, 3), (GATHER_THREE, 5), (GATHER_THREE, 6), (ATTEND, 2), (GATHER_THREE, 7),
    (ATTEND, 3), (GATHER_CORE, 0), (ATTEND, 1), (GATHER_CORE, 6), (GATHER_CORE, 2), (GATHER_CORE, 5), (OUT, 0),
    (GO_UP, 0), (GATHER_CORE, 7), (GATHER_CORE, 8), (GO_UP, 1), (GO_DOWN, 0), (BACK, 0), (GRADS, 0),
)


def forward_kernel(
    depth,
    lens, times, frames, given_in, bq, bk, bv, bo, bu, bd, bm, wq, wk, wv, wo, up, down, mw,
    output_out, gmid_out, mg, btile, mods, low, gwo, gup, gdown, do_all, qs_out, ks_out, vs_out, oh_out, lse_out,
    normed_out, wg_out, cos_out, sin_out,
    att, oh, qs, lse, normed, wg, cosr, sinr, rowbias, wo_all, up_all, down_all,
    bb, xall, mwst, tb, part, recva, suma, recvb, sumb, recvc, sumc, recvd, modh, bmat, mod3, qbias,
    output, gmid, ka, va, qaug, given, mod6, branch, middle, normed_two, active, slope, gbt, gh, gn, gb, ga, sums,
    send_sems, recv_sems, local_sems,
):
    here = Place(depth)
    z, y, x, c, g = here.z, here.y, here.x, here.c, here.seq
    span, width = frames.shape
    hidden = up.shape[1]
    rows_all = span * 4
    block, tall, tile = 128, span, 256
    move = Mover(send_sems, recv_sems, local_sems)
    steps_z = range(1, depth)

    row = lanes_of((16, LANES), 0) % 4
    own_times = jnp.where(
        row == 0, times[0, 0], jnp.where(row == 1, times[0, 1], jnp.where(row == 2, times[0, 2], times[0, 3]))
    )
    tb[z, y] = own_times.astype(F32)
    bb[z, y, x, c] = jnp.zeros((8, LANES), F32)
    for n, vector in enumerate((bq, bk, bv, bo, bu, bd)):
        bb[z, y, x, c, n : n + 1, : vector.shape[1]] = vector[...].astype(F32)
    bb[z, y, x, c, 6:7, :] = bm[:, :LANES].astype(F32)
    bb[z, y, x, c, 7:8, : bm.shape[1] - LANES] = bm[:, LANES:].astype(F32)
    weights = (wq, wk, wv)
    own_width = wg.shape[-1]
    locals_first = [
        move.local(weights[j].at[:, pl.ds(pl.multiple_of(g * own_width, LANES), own_width)], wg.at[j, z, y, g])
        for j in range(3)
    ]
    strip = mw.shape[1] // 4
    local_mw = [
        move.local(mw.at[:, pl.ds(j * strip, strip)], mwst.at[pl.ds(j * 32, 32)]) for j in range(4)
    ]
    local_frames = move.local(frames, xall.at[g])
    local_given = move.local(given_in, given)
    here.enter()

    legs = {}
    shard, wide = wo.shape[0], MODEL_WIDTH
    thin = shard // 2
    flows = []

    def add_flow(source, target, first_row, columns=None):
        rows = pl.ds(first_row, thin)
        if columns is None:
            flows.append((source.at[rows], target.at[:, :, :, :, rows]))
        else:
            columns = pl.ds(columns, wide)
            flows.append((source.at[rows, columns], target.at[:, :, :, :, rows, columns]))

    for side in range(2):
        add_flow(wo, wo_all, side * thin)
    for side in range(2):
        add_flow(up, up_all, side * thin, 0)
        add_flow(up, up_all, side * thin, wide)
    for side in range(4):
        add_flow(down, down_all, side * thin)
    count = len(flows)

    legs, outgoing, owned = {}, [], {}
    here_at = (z, y, x)

    def to_axis(axis):
        if axis == 0:
            return [here.along_z(k) for k in steps_z]
        return [here.across_y() if axis == 1 else here.across_x()]

    def held(number, known):
        place = tuple(slice(None) if axis in known else here_at[axis] for axis in range(3))
        return flows[number][1].at[place + (c,)]

    def first_leg(number):
        source = flows[number][0]
        target = held(number, ())
        owned[number] = move.local(source, target)
        legs[number] = [move.send(source, target, peer) for peer in to_axis(AXES[number][0])]

    def next_leg(number, done):
        if done == 1:
            owned[number].wait()
        for copy in legs[number]:
            copy.wait_recv()
        part = held(number, AXES[number][:done])
        peers = [here.core()] if done == 3 else to_axis(AXES[number][done])
        legs[number] = [move.send(part, part, peer) for peer in peers]
        outgoing.extend(legs[number])

    def second_leg(number):
        next_leg(number, 1)

    def third_leg(number):
        next_leg(number, 2)

    def fourth_leg(number):
        next_leg(number, 3)

    def arrived(*numbers):
        for number in numbers:
            for copy in legs[number]:
                copy.wait_recv()

    times_z = [move.send(tb.at[z, y], tb.at[z, y], here.along_z(k)) for k in steps_z]
    qkv_row = [
        [
            move.send(
                weights[j].at[:, pl.ds(pl.multiple_of((g + k) % 4 * own_width, LANES), own_width)],
                wg.at[j, z, y, g],
                here.row_peer(k),
            )
            for k in (1, 2, 3)
        ]
        for j in range(3)
    ]
    bias_z = [move.send(bb.at[z, y, x, c], bb.at[z, y, x, c], here.along_z(k)) for k in steps_z]
    part_rows = span // 2
    frame_parts = [pl.ds(n * part_rows, part_rows) for n in range(2)]
    half = strip // 2
    sent = {}
    stores = []

    def columns_z(j):
        locals_first[j].wait()
        for copy in qkv_row[j]:
            copy.wait_recv()
        sent["q", j] = [move.send(wg.at[j, z, y], wg.at[j, z, y], here.along_z(k)) for k in steps_z]

    def columns_y(j):
        for copy in sent["q", j]:
            copy.wait_recv()
        sent["p", j] = move.send(wg.at[j, :, y], wg.at[j, :, y], here.across_y())

    def times_across():
        for copy in times_z:
            copy.wait_recv()
        sent["ty"] = move.send(tb.at[:, y], tb.at[:, y], here.across_y())

    def mod_share():
        sent["ty"].wait_recv()
        lane = lanes_of((16 * 2 * depth, LANES))
        row = lanes_of((16 * 2 * depth, LANES), 0)
        feature = here.index * 32 + lane % 32
        halfway = MODEL_WIDTH // 2
        frequency = jnp.exp((feature % halfway).astype(F32) * (-math.log(10000.0) / halfway))
        angle = tb[...].reshape(16 * 2 * depth, LANES) * frequency
        wave = jnp.where(feature < halfway, jnp.sin(angle), jnp.cos(angle))
        gated = wave / (1.0 + jnp.exp(-wave))
        low[...] = jnp.where(lane // 32 == (row % 16) // 4, gated, 0.0).astype(BF16)
        for copy in local_mw:
            copy.wait()
        for side in range(2):
            share = product(low[...], mwst[:, side * half : (side + 1) * half])
            part[side] = share.astype(BF16).reshape(depth, 2, 16, half)
        sent["mc"] = move.send(part.at[1 - c], recva, here.core())

    def mod_y():
        sent["mc"].wait_recv()
        suma[...] = (part[c].astype(F32) + recva[...].astype(F32)).astype(BF16)
        sent["my"] = move.send(suma.at[:, 1 - y], recvb, here.across_y())

    def mod_z():
        sent["my"].wait_recv()
        sumb[...] = (suma[:, y].astype(F32) + recvb[...].astype(F32)).astype(BF16)
        sent["mz"] = [move.send(sumb.at[here.ahead(k)], recvc.at[k - 1], here.along_z(k)) for k in steps_z]

    def mod_x():
        total = sumb[z].astype(F32)
        for k in steps_z:
            sent["mz"][k - 1].wait_recv()
            total = total + recvc[k - 1].astype(F32)
        sumc[...] = total
        sent["mx"] = move.send(sumc, recvd, here.across_x())

    def mod_last():
        sent["mx"].wait_recv()
        modh[c] = sumc[...] + recvd[...]
        sent["ml"] = move.send(modh.at[c], modh.at[c], here.core())

    def frames_core():
        sent["fc"] = move.send(frames, xall.at[g], here.core())

    def frames_x(n):
        sent["fx", n] = move.send(frames.at[frame_parts[n]], xall.at[g, frame_parts[n]], here.across_x())

    frames_here = []

    def frames_in(n):
        if n not in frames_here:
            sent["fx", n].wait_recv()
            frames_here.append(n)

    def frames_on(n):
        frames_in(n)
        theirs = xall.at[(g + 2) % 4, frame_parts[n]]
        sent["on", n] = move.send(theirs, theirs, here.core())

    def bias_y():
        for copy in bias_z:
            copy.wait_recv()
        sent["by"] = move.send(bb.at[:, y, x, c], bb.at[:, y, x, c], here.across_y())

    def bias_x():
        sent["by"].wait_recv()
        sent["bx"] = move.send(bb.at[:, :, x, c], bb.at[:, :, x, c], here.across_x())

    def bias_core():
        sent["bx"].wait_recv()
        sent["bc"] = move.send(bb.at[:, :, :, c], bb.at[:, :, :, c], here.core())

    def tables(step, carry):
        rows = pl.ds(pl.multiple_of(step * block, block), block)
        segment, relative = frame_segments(lens, step * block, block, LANES)
        lane = lanes_of((block, LANES))
        quarter = HEAD_DIM // 2
        frequency = jnp.exp((lane % quarter).astype(F32) * (-math.log(10000.0) / quarter))
        angle = relative.astype(F32) * frequency
        cosr[rows, :] = jnp.cos(angle)
        sine = jnp.sin(angle)
        sinr[rows, :] = jnp.where(lane % HEAD_DIM < quarter, -sine, sine)
        same = segment == lane
        qaug[rows, :] = jnp.where((lane < SEGS) & jnp.logical_not(same), NEGATIVE, 0.0).astype(BF16)
        keyside = jnp.where((lane < SEGS) & same, 1.0, jnp.where((lane >= 4) & (lane < 7), 1.0, 0.0))
        for pair in range(2):
            ka[pair, rows, LANES:] = keyside.astype(BF16)
            va[pair, rows, LANES:] = jnp.where(lane < 3, 1.0, 0.0).astype(BF16)
        return carry

    def tables_half(n):
        lax.fori_loop(n * rows_all // (2 * block), (n + 1) * rows_all // (2 * block), tables, 0)

    def bias_vectors():
        sent["bc"].wait_recv()
        bmat[...] = bb[...].reshape(16 * 2 * depth * 2, LANES).astype(BF16)

        place = lanes_of((LANES, own_width), 0)
        column = lanes_of((LANES, own_width))
        brow, bcol = lanes_of((64, own_width), 0), lanes_of((64, own_width))
        spread = jnp.where(column % 32 == place, 1.0, 0.0).astype(BF16)
        for j in range(3):
            mine = (brow % 8 == j) & (brow // 8 == bcol // 32)
            held = product(bmat[pl.ds(pl.multiple_of(g * 64, 64), 64), :], spread)
            qbias[j : j + 1, :] = jnp.sum(jnp.where(mine, held, 0.0), axis=0, keepdims=True)

        trow, tcol = lanes_of((16 * 2 * depth * 2, tile), 0), lanes_of((16 * 2 * depth * 2, tile))
        place, column = lanes_of((LANES, tile), 0), lanes_of((LANES, tile))

        def row_vector(step, size, source):
            spread = jnp.where(column % size == place, 1.0, 0.0).astype(BF16)
            chosen = (trow % 8 == source) & (trow // 8 == (tcol + step * tile) // size)
            return jnp.sum(jnp.where(chosen, product(bmat[...], spread), 0.0), axis=0, keepdims=True)

        def narrow_vectors(step, carry):
            columns = pl.ds(pl.multiple_of(step * tile, tile), tile)
            rowbias[0:1, columns] = row_vector(step, 32, 3)
            rowbias[2:3, columns] = row_vector(step, 32, 5)
            return carry

        def wide_vector(step, carry):
            rowbias[1:2, pl.ds(pl.multiple_of(step * tile, tile), tile)] = row_vector(step, 64, 4)
            return carry

        lax.fori_loop(0, MODEL_WIDTH // tile, narrow_vectors, 0)
        lax.fori_loop(0, up.shape[1] // tile, wide_vector, 0)

        place = lanes_of((LANES, half), 0)
        column = lanes_of((LANES, half))
        spread_a = jnp.where(column % 192 == place, 1.0, 0.0).astype(BF16)
        spread_b = jnp.where(column % 192 == place + LANES, 1.0, 0.0).astype(BF16)
        brow, bcol = lanes_of((32, half), 0), lanes_of((32, half))
        inside = brow // 8 == bcol // 192
        for q in range(8):
            rows = bmat[q * 32 : (q + 1) * 32, :]
            terms = jnp.where(inside & (brow % 8 == 6), product(rows, spread_a), 0.0)
            terms = terms + jnp.where(inside & (brow % 8 == 7), product(rows, spread_b), 0.0)
            mods[4:5, q * half : (q + 1) * half] = jnp.sum(terms, axis=0, keepdims=True)

    def mod_done():
        sent["ml"].wait_recv()
        for q in range(8):
            j, side = q // 2, q % 2
            columns = slice(q * half, (q + 1) * half)
            mods[0:4, columns] = modh[side, 4 * j : 4 * j + 4, :] + mods[4:5, columns]
        for kept, first, last in ((mod3, 0, 2 * width), (mod6, 2 * width, 6 * width)):
            high, mid, rest = three_parts(mods[0:4, first:last])
            kept[0:4, :] = high
            kept[4:8, :] = mid
            kept[8:12, :] = rest
            kept[12:16, :] = jnp.zeros((4, last - first), F32)

    def project_rows(source):
        block, step = span, source
        rows = pl.ds(pl.multiple_of(step * block, block), block)
        values = xall[source].astype(F32)
        center = jnp.mean(values, axis=1, keepdims=True)
        centered = values - center
        variance = jnp.mean(centered * centered, axis=1, keepdims=True)
        segment, _ = frame_segments(lens, step * block, block, 16)
        slot = lanes_of((block, 16))
        chosen = jnp.where((slot < 12) & (slot % 4 == segment), 1.0, 0.0).astype(BF16)
        parts = mod3[...].astype(BF16)
        shift = product(chosen, parts[:, :MODEL_WIDTH])
        scale = product(chosen, parts[:, MODEL_WIDTH:])
        result = (centered * lax.rsqrt(variance + EPSILON) * (1.0 + scale) + shift).astype(BF16)
        normed[rows, :] = result
        cosine, sine = cosr[rows, :], sinr[rows, :]
        lane = lanes_of((block, LANES))
        for j in range(3):
            weight = wg[j].reshape(MODEL_WIDTH, own_width)
            full = product(result, weight) + qbias[j : j + 1, :]
            for pair in range(2):
                piece = full[:, pair * LANES : (pair + 1) * LANES]
                if j < 2:
                    piece = piece * cosine + swap_halves(piece, lane) * sine
                if j == 0:
                    qs[pair, rows, :] = (piece.astype(BF16).astype(F32) * HEAD_DIM**-0.5).astype(BF16)
                elif j == 1:
                    ka[pair, rows, :LANES] = piece.astype(BF16)
                else:
                    va[pair, rows, :LANES] = piece.astype(BF16)

    def project_span(n):
        if n == 0:
            local_frames.wait()
            for j in range(3):
                sent["p", j].wait_recv()
        elif n == 1:
            sent["fc"].wait_recv()
        elif n == 2:
            for m in range(2):
                frames_in(m)
        else:
            for m in range(2):
                sent["on", m].wait_recv()
        number = (g, x * 2 + 1 - c, (1 - x) * 2 + c, (1 - x) * 2 + 1 - c)[n]
        project_rows(number)
        if n == 3:
            for source, target in (
                (qs, qs_out), (ka.at[:, :, pl.ds(0, LANES)], ks_out), (va.at[:, :, pl.ds(0, LANES)], vs_out),
                (normed, normed_out), (wg, wg_out), (cosr, cos_out), (sinr, sin_out),
            ):
                stores.append(move.local(source, target))

    def attend(pair, step):
        rows = pl.ds(pl.multiple_of(step * tall, tall), tall)
        query = qs[pair, rows, :]
        lane = lanes_of((tall, LANES))
        outs, sums = [], []
        for head in range(2):
            left = jnp.concatenate([head_only(query, lane, head), qaug[rows, :]], axis=1)
            scores = across(left, ka[pair])
            highest = jnp.max(scores, axis=1, keepdims=True)
            mixed = product(jnp.exp(scores - highest).astype(BF16), va[pair])
            total = mixed[:, LANES : LANES + 1]
            outs.append(mixed[:, :LANES] / total)
            sums.append(highest + jnp.log(total))
        oh[pair, rows, :] = jnp.where(lane < HEAD_DIM, outs[0], outs[1]).astype(BF16)
        before = jnp.zeros((tall, LANES), F32) if pair == 0 else lse[rows, :]
        lse[rows, :] = jnp.where(
            lane == 2 * pair, sums[0], jnp.where(lane == 2 * pair + 1, sums[1], before)
        )

    delivered = []

    def attend_next():
        pair, at = len(delivered) // 4, len(delivered) % 4
        k = (2, 1, 3, 0)[at]
        target = (g + k) % 4
        attend(pair, target)
        columns = pl.ds(pl.multiple_of(g * own_width + pair * LANES, LANES), LANES)
        source = oh.at[pair, pl.ds(pl.multiple_of(target * span, span), span)]
        if k:
            delivered.append(move.send(source, att.at[:, columns], here.row_peer(k)))
        else:
            delivered.append(move.local(source, att.at[:, columns]))
        if len(delivered) == 8:
            stores.append(move.local(oh, oh_out))
            stores.append(move.local(lse, lse_out))

    base = g * span

    def tile_at(step):
        return pl.ds(pl.multiple_of(step * tile, tile), tile)

    def per_frame(part, first, rows, columns):
        segment, _ = frame_segments(lens, base + first, rows, 16)
        slot = lanes_of((rows, 16))
        chosen = jnp.where((slot < 12) & (slot % 4 == segment), 1.0, 0.0).astype(BF16)
        return product(chosen, mod6[:, columns].astype(BF16))

    def members(first, rows):
        position = base + first + lanes_of((16, rows))
        edges = [lens[0, 0], lens[0, 0] + lens[0, 1], lens[0, 0] + lens[0, 1] + lens[0, 2]]
        inside = sum((position >= edge).astype(jnp.int32) for edge in edges)
        return jnp.where(inside == lanes_of((16, rows), 0), 1.0, 0.0).astype(BF16)

    def by_segment(inside, values):
        top = values.astype(BF16)
        return product(inside, top) + product(inside, (values - top.astype(F32)).astype(BF16))

    def shifted(part, step):
        return pl.ds(pl.multiple_of(part * width + step * tile, tile), tile)

    def wo_columns(columns):
        return wo_all[:, :, :, :, :, columns].reshape(width, tile)

    def up_columns(columns):
        return up_all[:, :, :, :, :, columns].reshape(width, tile)

    def down_columns(columns):
        return down_all[:, :, :, :, :, columns].reshape(hidden, tile)

    def project_out():
        for at, copy in enumerate(delivered):
            copy.wait() if at % 4 == 3 else copy.wait_recv()
        arrived(0, 1)

        def body(step, carry):
            columns = tile_at(step)
            branch[:, columns] = product(att[...], wo_columns(columns)) + rowbias[0:1, columns]
            return carry

        straight(0, width // tile, body)

        def norm_forward(step, carry):
            rows = pl.ds(pl.multiple_of(step * block, block), block)
            gate = per_frame(0, step * block, block, slice(0, width))
            values = xall[g, rows, :].astype(F32) + gate * branch[rows, :]
            middle[rows, :] = values
            centered = values - jnp.mean(values, axis=1, keepdims=True)
            hat = centered * lax.rsqrt(jnp.mean(centered * centered, axis=1, keepdims=True) + EPSILON)
            shift = per_frame(1, step * block, block, slice(width, 2 * width))
            scale = per_frame(2, step * block, block, slice(2 * width, 3 * width))
            normed_two[rows, :] = (hat * (1.0 + scale) + shift).astype(BF16)
            return carry

        straight(0, span // block, norm_forward)

    root = math.sqrt(2.0 / math.pi)

    def go_up(side):
        arrived(2 + side, 4 + side)

        def body(step, carry):
            columns = tile_at(step)
            value = product(normed_two[...], up_columns(columns)) + rowbias[1:2, columns]
            square = value * value
            turn = jnp.tanh(root * value * (1.0 + 0.044715 * square))
            part_one = 0.5 * (1.0 + turn)
            active[:, columns] = (value * part_one).astype(BF16)
            slope[:, columns] = part_one + 0.5 * value * (1.0 - turn * turn) * root * (
                1.0 + 3 * 0.044715 * square
            )
            return carry

        straight(side * width // tile, (side + 1) * width // tile, body)

    def go_down():
        arrived(6, 7, 8, 9)
        local_given.wait()

        def body(step, carry):
            columns = tile_at(step)
            value = product(active[...], down_columns(columns)) + rowbias[2:3, columns]
            gate = per_frame(3, 0, span, shifted(3, step))
            back = given[:, columns].astype(F32)
            output[:, columns] = (middle[:, columns] + gate * value).astype(BF16)
            gbt[:, columns] = (gate * back).astype(BF16)
            sums[:, shifted(3, step)] = by_segment(members(0, span), back * value)
            return carry

        straight(0, width // tile, body)
        stores.append(move.local(output, output_out))

    def back_values():
        def hidden_tile(step, carry):
            rows = tile_at(step)
            weight = down_all[step // 2, step % 2].reshape(tile, width)
            gh[:, rows] = (across(gbt[...], weight) * slope[:, rows]).astype(BF16)
            return carry

        straight(0, hidden // tile, hidden_tile)

        def normed_tile(step, carry):
            gn[:, tile_at(step)] = across(gh[...], up_all[step].reshape(tile, hidden))
            return carry

        straight(0, width // tile, normed_tile)
        sums[:, : 3 * width] = jnp.zeros((16, 3 * width), F32)

        def norm_back(step, carry):
            rows = pl.ds(pl.multiple_of(step * block, block), block)
            grad, values = gn[rows, :], middle[rows, :]
            centered = values - jnp.mean(values, axis=1, keepdims=True)
            scaled = lax.rsqrt(jnp.mean(centered * centered, axis=1, keepdims=True) + EPSILON)
            hat = centered * scaled
            inner = grad * (1.0 + per_frame(2, step * block, block, slice(2 * width, 3 * width)))
            mean_one = jnp.mean(inner, axis=1, keepdims=True)
            mean_two = jnp.mean(inner * hat, axis=1, keepdims=True)
            total = given[rows, :].astype(F32) + scaled * (inner - mean_one - hat * mean_two)
            gmid[rows, :] = total
            gb[rows, :] = (per_frame(0, step * block, block, slice(0, width)) * total).astype(BF16)
            inside = members(step * block, block)
            sums[:, :width] += by_segment(inside, total * branch[rows, :])
            sums[:, width : 2 * width] += by_segment(inside, grad)
            sums[:, 2 * width : 3 * width] += by_segment(inside, grad * hat)
            return carry

        straight(0, span // block, norm_back)
        stores.append(move.local(gmid, gmid_out))
        sent["o"] = []
        mine = pl.ds(pl.multiple_of(g * span, span), span)
        for k in (1, 2, 3, 0):
            target = (g + k) % 4
            columns = tile_at(target)
            ga[:, columns] = across(gb[...], wo_all[target].reshape(tile, width)).astype(BF16)
            for pair in range(2):
                source = ga.at[:, pl.ds(pl.multiple_of(target * own_width + pair * LANES, LANES), LANES)]
                place = do_all.at[pair, mine]
                if k:
                    sent["o"].append(move.send(source, place, here.row_peer(k)))
                else:
                    stores.append(move.local(source, place))

    def back_weights():
        for copy in outgoing:
            copy.wait_send()

        def down_tile(step, carry):
            grad = from_rows(active[:, tile_at(step)], gbt[...]).astype(BF16)
            down_all[step // 2, step % 2] = grad.reshape(down_all.shape[2:])
            return carry

        straight(0, hidden // tile, down_tile)
        stores.append(move.local(down_all, gdown))

        def up_tile(step, carry):
            grad = from_rows(normed_two[:, tile_at(step)], gh[...]).astype(BF16)
            up_all[step] = grad.reshape(up_all.shape[1:])
            return carry

        straight(0, width // tile, up_tile)
        stores.append(move.local(up_all, gup))

        def out_tile(step, carry):
            grad = from_rows(att[:, tile_at(step)], gb[...]).astype(BF16)
            wo_all[step] = grad.reshape(wo_all.shape[1:])
            return carry

        straight(0, width // tile, out_tile)
        stores.append(move.local(wo_all, gwo))
        ones = jnp.ones((16, span), BF16)
        btile[0:24, :] = jnp.zeros((24, LANES), F32)
        start = 24
        for grads, size in ((gb, width), (gh, hidden), (gbt, width)):
            total = product(ones, grads[...])
            for n in range(size // LANES):
                btile[start + n : start + n + 1, :] = total[0:1, n * LANES : (n + 1) * LANES]
            start += size // LANES
        for n in range(4):
            mg[4 * n : 4 * n + 4, :] = sums[0:4, n * width : (n + 1) * width]

    numbered = {
        GATHER_Z: first_leg, GATHER_TWO: second_leg, GATHER_THREE: third_leg, GATHER_CORE: fourth_leg, COLUMNS_Z: columns_z, COLUMNS_Y: columns_y,
        PROJECT: project_span, GO_UP: go_up, FRAMES_X: frames_x, FRAMES_ON: frames_on, TABLES: tables_half,
    }
    named = {
        TIMES_Y: times_across, SHARE: mod_share, MOD_Y: mod_y, MOD_Z: mod_z, MOD_X: mod_x, MOD_LAST: mod_last,
        FRAMES_CORE: frames_core, BIAS_Y: bias_y, BIAS_X: bias_x, BIAS_CORE: bias_core, BIASES: bias_vectors, MODS: mod_done,
        OUT: project_out, GO_DOWN: go_down, BACK: back_values, GRADS: back_weights,
    }
    for code, number in FORWARD_ORDER:
        if code in named:
            named[code]()
        elif code == ATTEND:
            for _ in range(number):
                attend_next()
        else:
            numbered[code](number)
    for copy in stores:
        copy.wait()
    for copy in sent["o"]:
        copy.wait_recv()
    move.finish(but=outgoing)

def forward_call(depth, span, own_rows, down_rows, hidden, args):
    rows_all, own_width, width = 4 * span, MODEL_WIDTH // 4, MODEL_WIDTH
    half = 6 * MODEL_WIDTH // 8
    vmem, anywhere, scalar = (
        pl.BlockSpec(memory_space=pltpu.VMEM),
        pl.BlockSpec(memory_space=pl.ANY),
        pl.BlockSpec(memory_space=pltpu.SMEM),
    )

    def out(shape, dtype):
        return jax.ShapeDtypeStruct(shape, dtype)

    heads, table = (2, rows_all, LANES), (rows_all, LANES)
    columns = (3, depth, 2, 4, own_rows, own_width)
    wo_shape = (depth, 2, 2, 2, own_rows, width)
    up_shape = (depth, 2, 2, 2, own_rows, hidden)
    down_shape = (depth, 2, 2, 2, down_rows, width)
    outs = [
        (out((span, width), BF16), anywhere),
        (out((span, width), F32), anywhere),
        (out((16, width), F32), vmem),
        (out((56, LANES), F32), vmem),
        (out((8, 6 * width), F32), vmem),
        (out((32 * depth, LANES), BF16), vmem),
        (out(wo_shape, BF16), anywhere),
        (out(up_shape, BF16), anywhere),
        (out(down_shape, BF16), anywhere),
        (out(heads, BF16), anywhere),
        (out(heads, BF16), anywhere),
        (out(heads, BF16), anywhere),
        (out(heads, BF16), anywhere),
        (out(heads, BF16), anywhere),
        (out(table, F32), anywhere),
        (out((rows_all, width), BF16), anywhere),
        (out(columns, BF16), anywhere),
        (out(table, F32), anywhere),
        (out(table, F32), anywhere),
    ]
    low, wide = pltpu.VMEM((span, width), BF16), pltpu.VMEM((span, width), F32)
    scratch = [
        low,
        pltpu.VMEM(heads, BF16),
        pltpu.VMEM(heads, BF16),
        pltpu.VMEM(table, F32),
        pltpu.VMEM((rows_all, width), BF16),
        pltpu.VMEM(columns, BF16),
        pltpu.VMEM(table, F32),
        pltpu.VMEM(table, F32),
        pltpu.VMEM((8, hidden), F32),
        pltpu.VMEM(wo_shape, BF16),
        pltpu.VMEM(up_shape, BF16),
        pltpu.VMEM(down_shape, BF16),
        pltpu.VMEM((depth, 2, 2, 2, 8, LANES), F32),
        pltpu.VMEM((4, span, width), BF16),
        pltpu.VMEM((LANES, 2 * half), BF16),
        pltpu.VMEM((depth, 2, 16, LANES), F32),
        pltpu.VMEM((2, depth, 2, 16, half), BF16),
        pltpu.VMEM((depth, 2, 16, half), BF16),
        pltpu.VMEM((depth, 2, 16, half), BF16),
        pltpu.VMEM((depth, 16, half), BF16),
        pltpu.VMEM((depth, 16, half), BF16),
        pltpu.VMEM((depth - 1, 16, half), BF16),
        pltpu.VMEM((16, half), F32),
        pltpu.VMEM((16, half), F32),
        pltpu.VMEM((2, 16, half), F32),
        pltpu.VMEM((64 * depth, LANES), BF16),
        pltpu.VMEM((16, 2 * width), F32),
        pltpu.VMEM((8, own_width), F32),
        low,
        wide,
        pltpu.VMEM((2, rows_all, 2 * LANES), BF16),
        pltpu.VMEM((2, rows_all, 2 * LANES), BF16),
        pltpu.VMEM(table, BF16),
        low,
        pltpu.VMEM((16, 4 * width), F32),
        wide,
        wide,
        low,
        pltpu.VMEM((span, hidden), BF16),
        pltpu.VMEM((span, hidden), F32),
        low,
        pltpu.VMEM((span, hidden), BF16),
        wide,
        low,
        low,
        pltpu.VMEM((16, 4 * width), F32),
        pltpu.SemaphoreType.DMA((144,)),
        pltpu.SemaphoreType.DMA((144,)),
        pltpu.SemaphoreType.DMA((48,)),
    ]
    return pl.pallas_call(
        partial(forward_kernel, depth),
        out_shape=[shape for shape, _ in outs],
        in_specs=[scalar, scalar, anywhere, anywhere] + [vmem] * 7 + [anywhere] * 7,
        out_specs=[spec for _, spec in outs],
        scratch_shapes=scratch,
        compiler_params=pltpu.CompilerParams(
            collective_id=0, has_side_effects=True, vmem_limit_bytes=62 * 1024 * 1024
        ),
        cost_estimate=pl.CostEstimate(flops=2 * 10**10, bytes_accessed=60 * 10**6, transcendentals=10**7),
    )(*args)


def turn_back(values, cosine, sine, lane):
    return values * cosine - swap_halves(values, lane) * sine


def from_rows(left, right):
    return lax.dot_general(left, right, (((0,), (0,)), ((), ())), preferred_element_type=F32)


X_FIRST = (0, 1, 0, 1, 1, 1, 0, 0, 0, 1)
(
    SUM_ONE, SUM_TWO, SUM_THREE, SUM_LAST, WEIGHTS_Y, WEIGHTS_Z, WEIGHTS_LAST, ATTEND_BACK, ROWS_AWAY,
    ROWS_ACROSS, ROWS_HOME, NORM, EARLY_CORE, EARLY_X, EARLY_Z, EARLY_Y, EARLY_SHARE, EARLY_DONE, LATE_ROWS,
    LATE_DONE, BIAS_START, BIAS_NEXT, BIAS_DONE,
) = range(23)
BACKWARD_ORDER = (
    (SUM_ONE, 0), (ATTEND_BACK, 1), (SUM_ONE, 1), (SUM_ONE, 2), (ATTEND_BACK, 1), (SUM_ONE, 4),
    (ATTEND_BACK, 1), (SUM_TWO, 0), (SUM_ONE, 6), (EARLY_CORE, 0), (ATTEND_BACK, 1), (SUM_ONE, 5),
    (ATTEND_BACK, 1), (SUM_TWO, 1), (ATTEND_BACK, 1), (SUM_TWO, 6), (SUM_ONE, 7), (SUM_TWO, 4), (SUM_TWO, 2),
    (ATTEND_BACK, 1), (SUM_THREE, 0), (SUM_THREE, 1), (ATTEND_BACK, 1), (SUM_TWO, 5), (EARLY_X, 0),
    (SUM_ONE, 9), (SUM_ONE, 8), (SUM_THREE, 6), (SUM_TWO, 7), (ATTEND_BACK, 1), (EARLY_Z, 0), (ATTEND_BACK, 1),
    (SUM_THREE, 5), (SUM_THREE, 2), (ATTEND_BACK, 1), (SUM_TWO, 9), (SUM_THREE, 4), (SUM_ONE, 3), (EARLY_Y, 0),
    (ATTEND_BACK, 1), (SUM_THREE, 9), (WEIGHTS_Y, 1), (SUM_TWO, 8), (ROWS_AWAY, 0), (SUM_THREE, 7),
    (SUM_LAST, 1), (SUM_LAST, 4), (SUM_LAST, 5), (SUM_TWO, 3), (ROWS_ACROSS, 0), (SUM_THREE, 8), (WEIGHTS_Y, 2),
    (WEIGHTS_Z, 1), (SUM_LAST, 7), (WEIGHTS_Y, 0), (BIAS_START, 0), (SUM_LAST, 8), (SUM_LAST, 6),
    (EARLY_SHARE, 0), (SUM_THREE, 3), (WEIGHTS_Z, 2), (ROWS_HOME, 0), (WEIGHTS_Z, 0), (BIAS_NEXT, 0),
    (SUM_LAST, 9), (SUM_LAST, 0), (SUM_LAST, 3), (NORM, 0), (SUM_LAST, 2), (LATE_ROWS, 0), (WEIGHTS_LAST, 2),
    (BIAS_NEXT, 0), (WEIGHTS_LAST, 0), (WEIGHTS_LAST, 1), (BIAS_NEXT, 0), (EARLY_DONE, 0), (LATE_DONE, 0),
    (BIAS_DONE, 0),
)


def backward_kernel(
    depth,
    lens, do_in, qs_in, ks_in, vs_in, oh_in, lse_in, normed_in, wg_in, cos_in, sin_in, low, mods, frames_in, gmid_in,
    mg_in, bias_in, gwo, gup, gdown,
    fgrad, dwq, dwk, dwv, dwo, dup, ddown, dmw, mbias, btile,
    qs, do, oh, lse, normed, wg, cosr, sinr, ka, va, qaug, dk_sum, dv_sum, gr, gw, gwy, gwz, gsum,
    gnp, gnr, gnx, mod3, acc_shift, acc_scale, mg, mgr, mgs, mgx, ev, late, joined, ez, brecv, bz,
    frames, gmid,
    *rest,
):
    send_sems, recv_sems, local_sems = rest[-3:]
    buffers = rest[:-3]
    here = Place(depth)
    z, y, x, c, g = here.z, here.y, here.x, here.c, here.seq
    span = frames.shape[0]
    rows_all = span * 4
    own_width = wg.shape[-1]
    move = Mover(send_sems, recv_sems, local_sems)
    steps_z = range(1, depth)

    shard, width = gwo.shape[4], MODEL_WIDTH
    thin = shard // 2
    pieces = []

    def add_piece(source, target, first_row, columns=None):
        rows = pl.ds(first_row, thin)
        if columns is None:
            pieces.append((source.at[:, :, :, :, rows], target.at[rows]))
        else:
            columns = pl.ds(columns, width)
            pieces.append((source.at[:, :, :, :, rows, columns], target.at[rows, columns]))

    for n in range(4):
        add_piece(gdown, ddown, n * thin)
    for n in range(2):
        add_piece(gup, dup, n * thin, 0)
        add_piece(gup, dup, n * thin, width)
    for n in range(2):
        add_piece(gwo, dwo, n * thin)
    count = len(pieces)
    own, first, second, third, fourth = (
        [buffers[count * n + f] for f in range(count)] for n in range(5)
    )
    legs = {}

    loads = [
        move.local(ks_in, ka.at[:, :, pl.ds(0, LANES)]),
        move.local(vs_in, va.at[:, :, pl.ds(0, LANES)]),
        move.local(qs_in, qs),
        move.local(do_in, do),
        move.local(oh_in, oh),
        move.local(lse_in, lse),
        move.local(cos_in, cosr),
        move.local(sin_in, sinr),
    ]
    here.enter(diagonal=True)
    held = []
    for f in range(count):
        source = pieces[f][0]
        legs[f] = move.send(source.at[:, :, :, 1 - c], first[f], here.core())
        held.append(move.local(source.at[:, :, :, c], own[f]))
    late_loads = [move.local(normed_in, normed), move.local(wg_in, wg)]
    late_loads += [move.local(frames_in, frames), move.local(gmid_in, gmid)]

    def sum_first(f):
        legs[f].wait_recv()
        held[f].wait()

        def add(step, carry):
            own[f][step] = own[f][step] + first[f][step]
            return carry

        lax.fori_loop(0, depth, add, 0)
        if X_FIRST[f]:
            legs[f] = move.send(own[f].at[:, :, 1 - x], second[f], here.across_x())
        else:
            legs[f] = move.send(own[f].at[:, 1 - y], second[f], here.across_y())

    def sum_second(f):
        legs[f].wait_recv()

        def add(step, carry):
            for other in range(2):
                if X_FIRST[f]:
                    own[f][step, other, x] = own[f][step, other, x] + second[f][step, other]
                else:
                    own[f][step, y, other] = own[f][step, y, other] + second[f][step, other]
            return carry

        lax.fori_loop(0, depth, add, 0)
        if X_FIRST[f]:
            legs[f] = move.send(own[f].at[:, 1 - y, x], third[f], here.across_y())
        else:
            legs[f] = move.send(own[f].at[:, y, 1 - x], third[f], here.across_x())

    def sum_third(f):
        legs[f].wait_recv()

        def add(step, carry):
            own[f][step, y, x] = own[f][step, y, x] + third[f][step]
            return carry

        lax.fori_loop(0, depth, add, 0)
        legs[f] = [
            move.send(own[f].at[here.ahead(k), y, x], fourth[f].at[k - 1], here.along_z(k)) for k in steps_z
        ]

    def sum_last(f):
        total = own[f][z, y, x].astype(F32)
        for k in steps_z:
            legs[f][k - 1].wait_recv()
            total = total + fourth[f][k - 1].astype(F32)
        pieces[f][1][...] = total

    def bias_round(peer, slot):
        return move.send(btile, brecv.at[slot], peer)

    block = 128

    def columns_of_segments(step, carry):
        rows = pl.ds(pl.multiple_of(step * block, block), block)
        segment, _ = frame_segments(lens, step * block, block, LANES)
        lane = lanes_of((block, LANES))
        same = segment == lane
        qaug[rows, :] = jnp.where((lane < SEGS) & jnp.logical_not(same), NEGATIVE, 0.0).astype(BF16)
        keyside = jnp.where((lane < SEGS) & same, 1.0, jnp.where((lane >= 4) & (lane < 7), 1.0, 0.0))
        for pair in range(2):
            ka[pair, rows, LANES:] = keyside.astype(BF16)
            va[pair, rows, LANES:] = jnp.where(lane < 3, 1.0, 0.0).astype(BF16)
        return carry

    for copy in loads[:2]:
        copy.wait()
    lax.fori_loop(0, rows_all // block, columns_of_segments, 0)
    for copy in loads[2:]:
        copy.wait()

    tall = 256
    steps = rows_all // tall

    def back_block(pair, step):
        rows = pl.ds(pl.multiple_of(step * tall, tall), tall)
        lane = lanes_of((tall, LANES))
        query, given = qs[pair, rows, :], do[pair, rows, :]
        overlap = given.astype(F32) * oh[pair, rows, :].astype(F32)
        mask_columns = qaug[rows, :].astype(F32)
        sums = lse[rows, :]
        grads_q, add_k, add_v = [], 0.0, 0.0
        for head in range(2):
            delta = jnp.sum(jnp.where((lane >= HEAD_DIM) == bool(head), overlap, 0.0), axis=1, keepdims=True)
            logsum = jnp.sum(jnp.where(lane == 2 * pair + head, sums, 0.0), axis=1, keepdims=True)
            a, b, d = three_parts(logsum)
            side = jnp.where(lane == 4, -a, jnp.where(lane == 5, -b, jnp.where(lane == 6, -d, mask_columns)))
            query_head = head_only(query, lane, head)
            left = jnp.concatenate([query_head, side.astype(BF16)], axis=1)
            a, b, d = three_parts(delta)
            side = jnp.where(lane == 0, -a, jnp.where(lane == 1, -b, jnp.where(lane == 2, -d, 0.0)))
            given_head = head_only(given, lane, head)
            right = jnp.concatenate([given_head, side.astype(BF16)], axis=1)
            weights = jnp.exp(across(ka[pair], left))
            grads = (weights * across(va[pair], right)).astype(BF16)
            add_v = add_v + product(weights.astype(BF16), given_head)
            add_k = add_k + product(grads, query_head)
            grads_q.append(from_rows(grads, ka[pair, :, :LANES]))
        dv_sum[...] += add_v
        dk_sum[...] += add_k
        grad_query = jnp.where(lane < HEAD_DIM, grads_q[0], grads_q[1]) * HEAD_DIM**-0.5
        gr[0, rows, pair * LANES : (pair + 1) * LANES] = turn_back(
            grad_query, cosr[rows, :], sinr[rows, :], lane
        ).astype(BF16)

    def back_some(pair, start, stop):
        lax.fori_loop(start, stop, lambda step, carry: (back_block(pair, step), carry)[1], 0)

    def settle_pair(pair):
        def body(step, carry):
            rows = pl.ds(pl.multiple_of(step * block, block), block)
            lane = lanes_of((block, LANES))
            part = slice(pair * LANES, (pair + 1) * LANES)
            gr[1, rows, part] = turn_back(dk_sum[rows, :], cosr[rows, :], sinr[rows, :], lane).astype(BF16)
            gr[2, rows, part] = dv_sum[rows, :].astype(BF16)
            return carry

        lax.fori_loop(0, rows_all // block, body, 0)

    def clear():
        dk_sum[...] = jnp.zeros_like(dk_sum)
        dv_sum[...] = jnp.zeros_like(dv_sum)

    def back_rows(target):
        def body(step, carry):
            rows = pl.ds(pl.multiple_of(target * span + step * block, block), block)
            total = 0.0
            for j in range(3):
                total = total + across(gr[j, rows, :], wg[j].reshape(MODEL_WIDTH, own_width))
            gnp[target, pl.ds(pl.multiple_of(step * block, block), block), :] = total.astype(BF16)
            return carry

        straight(0, span // block, body)

    away_other, away_same = (1 - x) * 2 + (1 - c), (1 - x) * 2 + c
    home_other = x * 2 + (1 - c)
    gn = {}

    def need_late():
        while late_loads:
            late_loads.pop().wait()

    def rows_away():
        need_late()
        back_rows(away_other)
        gn["core"] = move.send(gnp.at[away_other], gnr.at[0], here.core())

    def rows_across():
        back_rows(away_same)
        gn["core"].wait_recv()

        def add_rows(step, carry):
            rows = pl.ds(pl.multiple_of(step * block, block), block)
            gnp[away_same, rows, :] = gnp[away_same, rows, :] + gnr[0, rows, :]
            return carry

        lax.fori_loop(0, span // block, add_rows, 0)
        gn["x"] = move.send(gnp.at[away_same], gnx, here.across_x())

    def rows_home():
        back_rows(home_other)
        gn["home"] = move.send(gnp.at[home_other], gnr.at[1], here.core())
        back_rows(g)

    tile = 256

    def weight_rows(j):
        def body(step, carry):
            columns = pl.ds(pl.multiple_of(step * tile, tile), tile)
            result = from_rows(normed[:, columns], gr[j]).astype(BF16)
            per = 2 * 4 * shard // tile
            lead = result.reshape(tile // (4 * shard), 4, shard, own_width)
            for n in range(tile // (4 * shard)):
                gw[j, step // per, (step % per) * (tile // (4 * shard)) + n] = lead[n]
            return carry

        straight(0, MODEL_WIDTH // tile, body)

    gw_y, gw_z = {}, {}

    def weights_y(j):
        need_late()
        weight_rows(j)
        gw_y[j] = move.send(gw.at[j, :, 1 - y], gwy.at[j], here.across_y())

    def weights_z(j):
        gw_y[j].wait_recv()

        def add(step, carry):
            gw[j, step, y] = gw[j, step, y] + gwy[j, step]
            return carry

        lax.fori_loop(0, depth, add, 0)
        gw_z[j] = [move.send(gw.at[j, here.ahead(k), y], gwz.at[j, k - 1], here.along_z(k)) for k in steps_z]

    outs = (dwq, dwk, dwv)
    final = []
    final_locals = []

    def weights_last(j):
        total = gw[j, z, y].astype(F32)
        for k in steps_z:
            gw_z[j][k - 1].wait_recv()
            total = total + gwz[j, k - 1].astype(F32)
        gsum[j] = total
        columns = pl.ds(pl.multiple_of(g * own_width, LANES), own_width)
        final_locals.append(move.local(gsum.at[j, g], outs[j].at[:, columns]))
        for k in (1, 2, 3):
            final.append(move.send(gsum.at[j, (g + k) % 4], outs[j].at[:, columns], here.row_peer(k)))

    bias_legs = []

    def bias_start():
        ones = jnp.ones((16, rows_all), BF16)
        btile[...] = bias_in[...]
        for j in range(3):
            sums = product(ones, gr[j])
            for half in range(2):
                btile[pl.ds(8 * j + g * 2 + half, 1), :] = sums[0:1, half * LANES : (half + 1) * LANES]
        bias_legs.append(move.send(btile, brecv.at[0], here.core()))

    def bias_next():
        done = len(bias_legs)
        bias_legs[-1].wait()
        btile[...] = btile[...] + brecv[done - 1]
        if done < 3:
            peer = (here.across_x, here.across_y)[done - 1]()
            bias_legs.append(move.send(btile, brecv.at[done], peer))
        else:
            bias_legs.extend([move.send(btile, bz.at[k - 1], here.along_z(k)) for k in steps_z])

    def bias_last():
        for copy in bias_legs[3:]:
            copy.wait()
        total = btile[...]
        for k in steps_z:
            total = total + bz[k - 1]
        btile[...] = total

    high, middle, rest_part = three_parts(mods[0:4, MODEL_WIDTH : 2 * MODEL_WIDTH])
    mod3[0:4, :] = high
    mod3[4:8, :] = middle
    mod3[8:12, :] = rest_part
    mod3[12:16, :] = jnp.zeros((4, MODEL_WIDTH), F32)
    acc_shift[...] = jnp.zeros_like(acc_shift)
    acc_scale[...] = jnp.zeros_like(acc_scale)
    def two_parts(values):
        top = values.astype(BF16)
        return top, (values - top.astype(F32)).astype(BF16)

    def norm_rows(step, carry):
        rows = pl.ds(pl.multiple_of(step * block, block), block)
        grad = gnp[g, rows, :].astype(F32) + gnr[1, rows, :].astype(F32) + gnx[rows, :].astype(F32)
        values = frames[rows, :].astype(F32)
        center = jnp.mean(values, axis=1, keepdims=True)
        centered = values - center
        scaled = lax.rsqrt(jnp.mean(centered * centered, axis=1, keepdims=True) + EPSILON)
        hat = centered * scaled
        base = g * span + step * block
        segment, _ = frame_segments(lens, base, block, 16)
        slot = lanes_of((block, 16))
        chosen = jnp.where((slot < 12) & (slot % 4 == segment), 1.0, 0.0).astype(BF16)
        inner = grad * (1.0 + product(chosen, mod3[...].astype(BF16)))
        mean_one = jnp.mean(inner, axis=1, keepdims=True)
        mean_two = jnp.mean(inner * hat, axis=1, keepdims=True)
        fgrad[rows, :] = (gmid[rows, :] + scaled * (inner - mean_one - hat * mean_two)).astype(BF16)
        position = base + lanes_of((16, block))
        begin = [lens[0, 0], lens[0, 0] + lens[0, 1], lens[0, 0] + lens[0, 1] + lens[0, 2]]
        inside = sum((position >= edge).astype(jnp.int32) for edge in begin)
        members = jnp.where(inside == lanes_of((16, block), 0), 1.0, 0.0).astype(BF16)
        for values, target in ((grad, acc_shift), (grad * hat, acc_scale)):
            top, bottom = two_parts(values)
            target[...] += product(members, top) + product(members, bottom)
        return carry

    fourth_part = MODEL_WIDTH // 2
    mod_legs = {}

    def mods_core():
        for side in range(2):
            mg[side] = mg_in[:, side * fourth_part : (side + 1) * fourth_part]
        mod_legs["core"] = move.send(mg.at[1 - c], mgr, here.core())

    def mods_x():
        mod_legs["core"].wait_recv()
        mgs[...] = mg[c] + mgr[...]
        mod_legs["x"] = move.send(mgs, mgx, here.across_x())

    def mods_z():
        mod_legs["x"].wait_recv()
        ev[z, y, c] = (mgs[...] + mgx[...]).astype(BF16)
        mod_legs["z"] = [move.send(ev.at[z, y, c], ev.at[z, y, c], here.along_z(k)) for k in steps_z]

    def mods_y():
        for copy in mod_legs["z"]:
            copy.wait_recv()
        mod_legs["y"] = move.send(ev.at[:, y, c], ev.at[:, y, c], here.across_y())

    def mods_share():
        mod_legs["y"].wait_recv()
        mod_legs["last"] = move.send(ev.at[:, :, c], ev.at[:, :, c], here.core())

    every_row = 32 * depth
    picks = jnp.where(
        lanes_of((16, every_row), 0) == (lanes_of((16, every_row)) % 16) // 4, 1.0, 0.0
    ).astype(BF16)

    def place_columns(every, start, stride):
        size = every.shape[1]
        result = from_rows(low[...], every)
        summed = product(picks, every)
        for strip in range(4):
            columns = slice(start + strip * stride, start + strip * stride + size)
            dmw[:, columns] = result[32 * strip : 32 * (strip + 1), :]
            mbias[0:1, columns] = summed[strip : strip + 1, :]

    def mods_early():
        mod_legs["last"].wait_recv()
        for side in range(2):
            every = ev[:, :, side].reshape(every_row, fourth_part)
            place_columns(every, 2 * MODEL_WIDTH + side * fourth_part, MODEL_WIDTH)

    def norm_part():
        gn["home"].wait_recv()
        gn["x"].wait_recv()
        straight(0, span // block, norm_rows)
        late[0, 0:4, :] = acc_shift[0:4, :]
        late[0, 4:8, :] = acc_scale[0:4, :]
        mod_legs["row"] = [move.send(late.at[0], late.at[k], here.row_peer(k)) for k in (1, 2, 3)]

    def mods_rows():
        for copy in mod_legs["row"]:
            copy.wait_recv()
        total = (late[0] + late[1]) + (late[2] + late[3])
        joined[0:4, :] = total[0:4, :fourth_part]
        joined[4:8, :] = total[0:4, fourth_part:]
        joined[8:12, :] = total[4:8, :fourth_part]
        joined[12:16, :] = total[4:8, fourth_part:]
        ez[z, y] = joined[...].astype(BF16)
        peers = [here.along_z(k) for k in steps_z] + [here.across_y()]
        peers += [here.at(here.ahead(k), 1 - y, x, c) for k in steps_z]
        mod_legs["all"] = [move.send(ez.at[z, y], ez.at[z, y], peer) for peer in peers]

    def mods_late():
        for copy in mod_legs["all"]:
            copy.wait_recv()
        place_columns(ez[...].reshape(every_row, fourth_part), 0, fourth_part)

    stages = {
        SUM_ONE: sum_first, SUM_TWO: sum_second, SUM_THREE: sum_third, SUM_LAST: sum_last,
        WEIGHTS_Y: weights_y, WEIGHTS_Z: weights_z, WEIGHTS_LAST: weights_last,
    }
    others = {
        ROWS_AWAY: rows_away, ROWS_ACROSS: rows_across, ROWS_HOME: rows_home, NORM: norm_part,
        EARLY_CORE: mods_core, EARLY_X: mods_x, EARLY_Z: mods_z, EARLY_Y: mods_y, EARLY_SHARE: mods_share, EARLY_DONE: mods_early,
        LATE_ROWS: mods_rows, LATE_DONE: mods_late, BIAS_START: bias_start, BIAS_NEXT: bias_next, BIAS_DONE: bias_last,
    }
    clear()
    done = 0
    for code, number in BACKWARD_ORDER:
        if code == ATTEND_BACK:
            ahead = number
            while ahead:
                pair, at = done // steps, done % steps
                now = min(ahead, steps - at)
                back_some(pair, at, at + now)
                done, ahead = done + now, ahead - now
                if done % steps == 0:
                    settle_pair(pair)
                    if pair == 0:
                        clear()
        elif code in others:
            others[code]()
        else:
            stages[code](number)
    for copy in final_locals:
        copy.wait()
    for copy in final:
        copy.wait_recv()
    move.finish(but=bias_legs)


def backward_call(depth, span, own_rows, down_rows, hidden, args):
    rows_all, own_width = 4 * span, MODEL_WIDTH // 4
    half = MODEL_WIDTH // 2
    vmem, anywhere, scalar = (
        pl.BlockSpec(memory_space=pltpu.VMEM),
        pl.BlockSpec(memory_space=pl.ANY),
        pl.BlockSpec(memory_space=pltpu.SMEM),
    )

    def out(shape, dtype):
        return jax.ShapeDtypeStruct(shape, dtype)

    outs = [
        (out((span, MODEL_WIDTH), BF16), vmem),
        (out((own_rows, MODEL_WIDTH), F32), anywhere),
        (out((own_rows, MODEL_WIDTH), F32), anywhere),
        (out((own_rows, MODEL_WIDTH), F32), anywhere),
        (out((own_rows, MODEL_WIDTH), F32), vmem),
        (out((own_rows, hidden), F32), vmem),
        (out((down_rows, MODEL_WIDTH), F32), vmem),
        (out((own_rows, 6 * MODEL_WIDTH), F32), vmem),
        (out((8, 6 * MODEL_WIDTH), F32), vmem),
        (out((56, LANES), F32), vmem),
    ]
    pair_rows = pltpu.VMEM((2, rows_all, LANES), BF16)
    wide_rows = pltpu.VMEM((2, rows_all, 2 * LANES), BF16)
    table = pltpu.VMEM((rows_all, LANES), F32)
    scratch = [
        pair_rows, pair_rows, pair_rows, table,
        pltpu.VMEM((rows_all, MODEL_WIDTH), BF16),
        pltpu.VMEM((3, depth, 2, 4, own_rows, own_width), BF16),
        table, table, wide_rows, wide_rows,
        pltpu.VMEM((rows_all, LANES), BF16),
        table, table,
        pltpu.VMEM((3, rows_all, own_width), BF16),
        pltpu.VMEM((3, depth, 2, 4, own_rows, own_width), BF16),
        pltpu.VMEM((3, depth, 4, own_rows, own_width), BF16),
        pltpu.VMEM((3, depth - 1, 4, own_rows, own_width), BF16),
        pltpu.VMEM((3, 4, own_rows, own_width), F32),
        pltpu.VMEM((4, span, MODEL_WIDTH), BF16),
        pltpu.VMEM((2, span, MODEL_WIDTH), BF16),
        pltpu.VMEM((span, MODEL_WIDTH), BF16),
        pltpu.VMEM((16, MODEL_WIDTH), F32),
        pltpu.VMEM((16, MODEL_WIDTH), F32),
        pltpu.VMEM((16, MODEL_WIDTH), F32),
        pltpu.VMEM((2, 16, half), F32),
        pltpu.VMEM((16, half), F32),
        pltpu.VMEM((16, half), F32),
        pltpu.VMEM((16, half), F32),
        pltpu.VMEM((depth, 2, 2, 16, half), BF16),
        pltpu.VMEM((4, 8, MODEL_WIDTH), F32),
        pltpu.VMEM((16, half), F32),
        pltpu.VMEM((depth, 2, 16, half), BF16),
        pltpu.VMEM((3, 56, LANES), F32),
        pltpu.VMEM((depth - 1, 56, LANES), F32),
        pltpu.VMEM((span, MODEL_WIDTH), BF16),
        pltpu.VMEM((span, MODEL_WIDTH), F32),
    ]
    piece = (own_rows // 2, MODEL_WIDTH)
    for lead in ((depth, 2, 2), (depth, 2, 2), (depth, 2), (depth,), (depth - 1,)):
        scratch += [pltpu.VMEM(lead + piece, BF16)] * 10
    scratch += [pltpu.SemaphoreType.DMA((128,)), pltpu.SemaphoreType.DMA((128,)), pltpu.SemaphoreType.DMA((32,))]
    return pl.pallas_call(
        partial(backward_kernel, depth),
        out_shape=[shape for shape, _ in outs],
        in_specs=[scalar] + [anywhere] * 10 + [vmem] * 2 + [anywhere] * 2 + [vmem] * 2 + [anywhere] * 3,
        out_specs=[spec for _, spec in outs],
        scratch_shapes=scratch,
        compiler_params=pltpu.CompilerParams(
            collective_id=1, has_side_effects=True, vmem_limit_bytes=62 * 1024 * 1024
        ),
        cost_estimate=pl.CostEstimate(flops=2 * 10**10, bytes_accessed=40 * 10**6, transcendentals=10**7),
    )(*args)


def modulated_norm(values, shift_part, scale_part):
    center = jnp.mean(values, axis=-1, keepdims=True)
    centered = values - center
    variance = jnp.mean(centered * centered, axis=-1, keepdims=True)
    return centered * lax.rsqrt(variance + EPSILON) * (1.0 + scale_part) + shift_part


def rotate(values, cosines, sines_table):
    shaped = values.reshape(values.shape[:-1] + (values.shape[-1] // HEAD_DIM, HEAD_DIM))
    first_half = shaped[..., : HEAD_DIM // 2]
    second_half = shaped[..., HEAD_DIM // 2 :]
    cosine = cosines[..., None, :]
    sine_part = sines_table[..., None, :]
    turned = jnp.concatenate(
        [
            first_half * cosine - second_half * sine_part,
            second_half * cosine + first_half * sine_part,
        ],
        axis=-1,
    )
    return turned.reshape(values.shape)


def gelu_tanh(values):
    return jax.nn.gelu(values, approximate=True)


def time_features(time_index):
    halfway = MODEL_WIDTH // 2
    frequency = jnp.exp(jnp.arange(halfway, dtype=jnp.float32) * (-math.log(10000.0) / halfway))
    angles = time_index.astype(jnp.float32)[..., None] * frequency
    return jnp.concatenate([jnp.sin(angles), jnp.cos(angles)], axis=-1)


def segment_starts(segment_lengths):
    return jnp.cumsum(segment_lengths, axis=1) - segment_lengths


def segment_numbers(segment_lengths, frame_positions):
    starts = segment_starts(segment_lengths)
    inside = (frame_positions[None, :, None] >= starts[:, None, :]).astype(jnp.int32)
    return jnp.sum(inside, axis=2) - 1


def segment_layout(segment_lengths, frame_positions):
    starts = segment_starts(segment_lengths)
    segment = segment_numbers(segment_lengths, frame_positions)
    onehot = (segment[..., None] == jnp.arange(SEGS, dtype=jnp.int32)).astype(jnp.float32)
    offset = jnp.sum(onehot * starts[:, None, :].astype(jnp.float32), axis=2)
    relative = frame_positions[None, :].astype(jnp.float32) - offset
    return (onehot, relative)


def rope_tables(relative):
    halfway = HEAD_DIM // 2
    frequency = jnp.exp(jnp.arange(halfway, dtype=jnp.float32) * (-math.log(10000.0) / halfway))
    angles = relative[..., None] * frequency
    return (jnp.cos(angles), jnp.sin(angles))


def project(values, matrix, offset):
    return jnp.einsum(
        "rld,de->rle", values, matrix, preferred_element_type=jnp.float32
    ) + offset.astype(jnp.float32)


def project_back(gradient, matrix):
    return jnp.einsum("rle,de->rld", gradient, matrix, preferred_element_type=jnp.float32)


def weight_gradient(values, gradient):
    return jnp.einsum("rld,rle->de", values, gradient, preferred_element_type=jnp.float32)


def bias_gradient(gradient):
    return jnp.sum(gradient.astype(jnp.float32), axis=(0, 1))


def lift_up(member):
    return member.reshape((1, 1) + member.shape)


def settle(member):
    return member.reshape((-1,) + member.shape[3:])


def spread(member, wide_count, narrow_count):
    return member.reshape((wide_count, narrow_count, -1) + member.shape[1:])


def unpack(member):
    return member.reshape(member.shape[2:])


def on_device(
    frames,
    output_gradient,
    segment_lengths,
    time_index,
    query_weight,
    query_bias,
    key_weight,
    key_bias,
    value_weight,
    value_bias,
    output_projection,
    output_bias,
    up_weight,
    up_bias,
    down_weight,
    down_bias,
    modulation_weight,
    modulation_bias,
):
    narrow_count = lax.axis_size("seq")
    wide_count = lax.axis_size("dp")
    seq_index = lax.axis_index("seq")
    row_count, span_frames, width_total = frames.shape
    row_length = span_frames * narrow_count
    block_rows = min(512, row_length)
    block_count = row_length // block_rows
    local_weights = (
        query_weight,
        query_bias,
        key_weight,
        key_bias,
        value_weight,
        value_bias,
        output_projection,
        output_bias,
        up_weight,
        up_bias,
        down_weight,
        down_bias,
        modulation_bias,
    )
    lifted = [lift_up(member) for member in local_weights]
    halfway_set = (
        lax.all_gather(lifted[0], "dp", axis=0, tiled=True),
        lax.all_gather(lifted[1], "dp", axis=0, tiled=True),
        lax.all_gather(lifted[2], "dp", axis=0, tiled=True),
        lax.all_gather(lifted[3], "dp", axis=0, tiled=True),
        lax.all_gather(lifted[4], "dp", axis=0, tiled=True),
        lax.all_gather(lifted[5], "dp", axis=0, tiled=True),
        lax.all_gather(lifted[6], "dp", axis=0, tiled=True),
        lax.all_gather(lifted[7], "dp", axis=0, tiled=True),
        lax.all_gather(lifted[8], "dp", axis=0, tiled=True),
        lax.all_gather(lifted[9], "dp", axis=0, tiled=True),
        lax.all_gather(lifted[10], "dp", axis=0, tiled=True),
        lax.all_gather(lifted[11], "dp", axis=0, tiled=True),
        lax.all_gather(lifted[12], "dp", axis=0, tiled=True),
    )
    complete_set = (
        lax.all_gather(halfway_set[0], "seq", axis=1, tiled=True),
        lax.all_gather(halfway_set[1], "seq", axis=1, tiled=True),
        lax.all_gather(halfway_set[2], "seq", axis=1, tiled=True),
        lax.all_gather(halfway_set[3], "seq", axis=1, tiled=True),
        lax.all_gather(halfway_set[4], "seq", axis=1, tiled=True),
        lax.all_gather(halfway_set[5], "seq", axis=1, tiled=True),
        lax.all_gather(halfway_set[6], "seq", axis=1, tiled=True),
        lax.all_gather(halfway_set[7], "seq", axis=1, tiled=True),
        lax.all_gather(halfway_set[8], "seq", axis=1, tiled=True),
        lax.all_gather(halfway_set[9], "seq", axis=1, tiled=True),
        lax.all_gather(halfway_set[10], "seq", axis=1, tiled=True),
        lax.all_gather(halfway_set[11], "seq", axis=1, tiled=True),
        lax.all_gather(halfway_set[12], "seq", axis=1, tiled=True),
    )
    gathered = [settle(member) for member in complete_set]
    (
        full_query,
        full_query_bias,
        full_key,
        full_key_bias,
        full_value,
        full_value_bias,
        full_output,
        full_output_bias,
        full_up,
        full_up_bias,
        full_down,
        full_down_bias,
        full_modulation_bias,
    ) = gathered
    local_positions = seq_index * span_frames + jnp.arange(span_frames, dtype=jnp.int32)
    local_onehot, local_relative = segment_layout(segment_lengths, local_positions)
    row_segment = segment_numbers(segment_lengths, jnp.arange(row_length, dtype=jnp.int32))
    cosines, sines_table = rope_tables(local_relative)
    turning = partial(rotate, cosines=cosines, sines_table=sines_table)
    owned_rows = modulation_weight.shape[0]
    owned_start = (lax.axis_index("dp") * narrow_count + seq_index) * owned_rows
    every_time = lax.all_gather(time_index, "dp", axis=0, tiled=True)
    every_low = jax.nn.silu(time_features(every_time)).astype(jnp.bfloat16)
    owned_low = lax.dynamic_slice_in_dim(every_low, owned_start, owned_rows, 2)
    partial_modulation = jnp.einsum(
        "rsd,dc->rsc", owned_low, modulation_weight, preferred_element_type=jnp.float32
    )
    row_share = lax.psum_scatter(partial_modulation, "dp", scatter_dimension=0, tiled=True)
    modulation = lax.psum(row_share.astype(jnp.bfloat16), "seq").astype(
        jnp.float32
    ) + full_modulation_bias.astype(jnp.float32)
    per_frame = jnp.einsum("rls,rsc->rlc", local_onehot, modulation, precision=HIGHEST)
    shift_one, scale_one, gate_one, shift_two, scale_two, gate_two = jnp.split(
        per_frame, 6, axis=-1
    )
    inputs = frames.astype(jnp.float32)
    normed, norm_back = jax.vjp(modulated_norm, inputs, shift_one, scale_one)
    normed_low = normed.astype(jnp.bfloat16)
    query_pre = project(normed_low, full_query, full_query_bias)
    key_pre = project(normed_low, full_key, full_key_bias)
    value_low = project(normed_low, full_value, full_value_bias).astype(jnp.bfloat16)
    query_turned, query_back = jax.vjp(turning, query_pre)
    key_turned, key_back = jax.vjp(turning, key_pre)
    query_heads, key_heads, value_heads = (
        lax.all_to_all(
            query_turned.astype(jnp.bfloat16), "seq", split_axis=2, concat_axis=1, tiled=True
        ),
        lax.all_to_all(
            key_turned.astype(jnp.bfloat16), "seq", split_axis=2, concat_axis=1, tiled=True
        ),
        lax.all_to_all(value_low, "seq", split_axis=2, concat_axis=1, tiled=True),
    )
    local_heads = query_heads.shape[2] // HEAD_DIM
    head_shape = (row_count, row_length, local_heads, HEAD_DIM)
    queries = query_heads.reshape(head_shape)
    keys_all = key_heads.reshape(head_shape)
    values_all = value_heads.reshape(head_shape)
    scaling = HEAD_DIM ** (-0.5)
    positions_all = jnp.arange(row_count * block_count, dtype=jnp.int32)

    def fetch_block(position):
        row_index = position // block_count
        start_row = position % block_count * block_rows
        key_row = lax.dynamic_index_in_dim(keys_all, row_index, 0, keepdims=False)
        value_row = lax.dynamic_index_in_dim(values_all, row_index, 0, keepdims=False)
        segment_row = lax.dynamic_index_in_dim(row_segment, row_index, 0, keepdims=False)
        query_block = lax.dynamic_slice_in_dim(
            lax.dynamic_index_in_dim(queries, row_index, 0, keepdims=False),
            start_row,
            block_rows,
            0,
        )
        segment_block = lax.dynamic_slice_in_dim(segment_row, start_row, block_rows, 0)
        scores = (
            jnp.einsum("bhd,khd->hbk", query_block, key_row, preferred_element_type=jnp.float32)
            * scaling
        )
        scores = jnp.where((segment_block[:, None] == segment_row[None, :])[None], scores, NEGATIVE)
        return (row_index, start_row, query_block, key_row, value_row, scores)

    def forward_block(position):
        row_index, start_row, query_block, key_row, value_row, scores = fetch_block(position)
        highest = jnp.max(scores, axis=2, keepdims=True)
        weights = jnp.exp(scores - highest)
        totals = jnp.sum(weights, axis=2, keepdims=True)
        probabilities = (weights / totals).astype(jnp.bfloat16)
        mixed_block = jnp.einsum(
            "hbk,khd->bhd", probabilities, value_row, preferred_element_type=jnp.float32
        )
        return (
            mixed_block.astype(jnp.bfloat16).reshape(block_rows, -1),
            (highest + jnp.log(totals))[..., 0],
        )

    mixed_blocks, logsums = lax.map(forward_block, positions_all)
    attention_heads = mixed_blocks.reshape(row_count, row_length, -1)
    attention_frames = lax.all_to_all(
        attention_heads, "seq", split_axis=1, concat_axis=2, tiled=True
    )
    branch = project(attention_frames, full_output, full_output_bias)
    middle = inputs + gate_one * branch
    normed_two, norm_two_back = jax.vjp(modulated_norm, middle, shift_two, scale_two)
    normed_two_low = normed_two.astype(jnp.bfloat16)
    hidden = project(normed_two_low, full_up, full_up_bias)
    activated, gelu_back = jax.vjp(gelu_tanh, hidden)
    activated_low = activated.astype(jnp.bfloat16)
    branch_two = project(activated_low, full_down, full_down_bias)
    layer_output = (middle + gate_two * branch_two).astype(jnp.bfloat16)
    cotangent = output_gradient.astype(jnp.float32)
    grad_branch_two = (gate_two * cotangent).astype(jnp.bfloat16)
    grad_gate_two = cotangent * branch_two
    grad_activated = project_back(grad_branch_two, full_down)
    grad_hidden = gelu_back(grad_activated)[0].astype(jnp.bfloat16)
    grad_normed_two = project_back(grad_hidden, full_up)
    grad_middle_part, grad_shift_two, grad_scale_two = norm_two_back(grad_normed_two)
    grad_middle = cotangent + grad_middle_part
    grad_gate_one = grad_middle * branch
    grad_branch = (gate_one * grad_middle).astype(jnp.bfloat16)
    grad_attention = project_back(grad_branch, full_output).astype(jnp.bfloat16)
    grad_heads = lax.all_to_all(grad_attention, "seq", split_axis=2, concat_axis=1, tiled=True)
    grad_outputs = grad_heads.reshape(head_shape)

    def backward_block(running, pair_inputs):
        grad_keys, grad_values = running
        position, logsum = pair_inputs
        row_index, start_row, query_block, key_row, value_row, scores = fetch_block(position)
        grad_block = lax.dynamic_slice_in_dim(
            lax.dynamic_index_in_dim(grad_outputs, row_index, 0, keepdims=False),
            start_row,
            block_rows,
            0,
        )
        probabilities = jnp.exp(scores - logsum[..., None])
        grad_probabilities = jnp.einsum(
            "bhd,khd->hbk", grad_block, value_row, preferred_element_type=jnp.float32
        )
        delta_sum = jnp.sum(probabilities * grad_probabilities, axis=2, keepdims=True)
        grad_scores = (probabilities * (grad_probabilities - delta_sum)).astype(jnp.bfloat16)
        grad_query_block = (
            jnp.einsum("hbk,khd->bhd", grad_scores, key_row, preferred_element_type=jnp.float32)
            * scaling
        )
        key_part = (
            jnp.einsum("hbk,bhd->khd", grad_scores, query_block, preferred_element_type=jnp.float32)
            * scaling
        )
        value_part = jnp.einsum(
            "hbk,bhd->khd",
            probabilities.astype(jnp.bfloat16),
            grad_block,
            preferred_element_type=jnp.float32,
        )
        grad_keys = lax.dynamic_update_index_in_dim(
            grad_keys,
            lax.dynamic_index_in_dim(grad_keys, row_index, 0, keepdims=False) + key_part,
            row_index,
            0,
        )
        grad_values = lax.dynamic_update_index_in_dim(
            grad_values,
            lax.dynamic_index_in_dim(grad_values, row_index, 0, keepdims=False) + value_part,
            row_index,
            0,
        )
        return (
            (grad_keys, grad_values),
            grad_query_block.astype(jnp.bfloat16).reshape(block_rows, -1),
        )

    zero_heads = jnp.zeros(head_shape, jnp.float32)
    (grad_keys_all, grad_values_all), grad_query_blocks = lax.scan(
        backward_block, (zero_heads, zero_heads), (positions_all, logsums)
    )
    flat_shape = (row_count, row_length, -1)
    grad_query_frames, grad_key_frames, grad_value_frames = (
        lax.all_to_all(
            grad_query_blocks.reshape(flat_shape), "seq", split_axis=1, concat_axis=2, tiled=True
        ),
        lax.all_to_all(
            grad_keys_all.reshape(flat_shape).astype(jnp.bfloat16),
            "seq",
            split_axis=1,
            concat_axis=2,
            tiled=True,
        ),
        lax.all_to_all(
            grad_values_all.reshape(flat_shape).astype(jnp.bfloat16),
            "seq",
            split_axis=1,
            concat_axis=2,
            tiled=True,
        ),
    )
    grad_query_pre = query_back(grad_query_frames.astype(jnp.float32))[0].astype(jnp.bfloat16)
    grad_key_pre = key_back(grad_key_frames.astype(jnp.float32))[0].astype(jnp.bfloat16)
    grad_normed = (
        project_back(grad_query_pre, full_query)
        + project_back(grad_key_pre, full_key)
        + project_back(grad_value_frames, full_value)
    )
    grad_inputs_part, grad_shift_one, grad_scale_one = norm_back(grad_normed)
    frames_grad = (grad_middle + grad_inputs_part).astype(jnp.bfloat16)
    grad_per_frame = jnp.concatenate(
        [
            grad_shift_one,
            grad_scale_one,
            grad_gate_one,
            grad_shift_two,
            grad_scale_two,
            grad_gate_two,
        ],
        axis=-1,
    )
    grad_modulation = jnp.einsum("rls,rlc->rsc", local_onehot, grad_per_frame, precision=HIGHEST)
    gradients = (
        weight_gradient(normed_low, grad_query_pre),
        bias_gradient(grad_query_pre),
        weight_gradient(normed_low, grad_key_pre),
        bias_gradient(grad_key_pre),
        weight_gradient(normed_low, grad_value_frames),
        bias_gradient(grad_value_frames),
        weight_gradient(attention_frames, grad_branch),
        bias_gradient(grad_branch),
        weight_gradient(normed_two_low, grad_hidden),
        bias_gradient(grad_hidden),
        weight_gradient(activated_low, grad_branch_two),
        bias_gradient(grad_branch_two),
        jnp.sum(grad_modulation, axis=(0, 1)),
    )
    row_total = lax.psum(grad_modulation.astype(jnp.bfloat16), "seq").astype(jnp.float32)
    every_grad = lax.all_gather(row_total.astype(jnp.bfloat16), "dp", axis=0, tiled=True).astype(
        row_total.dtype
    )
    modulation_weight_grad = jnp.einsum(
        "rsd,rsc->dc", owned_low.astype(jnp.float32), every_grad, precision=HIGHEST
    )
    spreaded = [spread(member, wide_count, narrow_count) for member in gradients]
    first_pass = (
        lax.psum_scatter(
            spreaded[0].astype(jnp.bfloat16), "seq", scatter_dimension=1, tiled=True
        ).astype(jnp.float32),
        lax.psum_scatter(
            spreaded[1].astype(jnp.bfloat16), "seq", scatter_dimension=1, tiled=True
        ).astype(jnp.float32),
        lax.psum_scatter(
            spreaded[2].astype(jnp.bfloat16), "seq", scatter_dimension=1, tiled=True
        ).astype(jnp.float32),
        lax.psum_scatter(
            spreaded[3].astype(jnp.bfloat16), "seq", scatter_dimension=1, tiled=True
        ).astype(jnp.float32),
        lax.psum_scatter(
            spreaded[4].astype(jnp.bfloat16), "seq", scatter_dimension=1, tiled=True
        ).astype(jnp.float32),
        lax.psum_scatter(
            spreaded[5].astype(jnp.bfloat16), "seq", scatter_dimension=1, tiled=True
        ).astype(jnp.float32),
        lax.psum_scatter(
            spreaded[6].astype(jnp.bfloat16), "seq", scatter_dimension=1, tiled=True
        ).astype(jnp.float32),
        lax.psum_scatter(
            spreaded[7].astype(jnp.bfloat16), "seq", scatter_dimension=1, tiled=True
        ).astype(jnp.float32),
        lax.psum_scatter(
            spreaded[8].astype(jnp.bfloat16), "seq", scatter_dimension=1, tiled=True
        ).astype(jnp.float32),
        lax.psum_scatter(
            spreaded[9].astype(jnp.bfloat16), "seq", scatter_dimension=1, tiled=True
        ).astype(jnp.float32),
        lax.psum_scatter(
            spreaded[10].astype(jnp.bfloat16), "seq", scatter_dimension=1, tiled=True
        ).astype(jnp.float32),
        lax.psum_scatter(
            spreaded[11].astype(jnp.bfloat16), "seq", scatter_dimension=1, tiled=True
        ).astype(jnp.float32),
        lax.psum_scatter(
            spreaded[12].astype(jnp.bfloat16), "seq", scatter_dimension=1, tiled=True
        ).astype(jnp.float32),
    )
    second_pass = (
        lax.psum_scatter(first_pass[0], "dp", scatter_dimension=0, tiled=True),
        lax.psum_scatter(first_pass[1], "dp", scatter_dimension=0, tiled=True),
        lax.psum_scatter(first_pass[2], "dp", scatter_dimension=0, tiled=True),
        lax.psum_scatter(first_pass[3], "dp", scatter_dimension=0, tiled=True),
        lax.psum_scatter(first_pass[4], "dp", scatter_dimension=0, tiled=True),
        lax.psum_scatter(first_pass[5], "dp", scatter_dimension=0, tiled=True),
        lax.psum_scatter(first_pass[6], "dp", scatter_dimension=0, tiled=True),
        lax.psum_scatter(first_pass[7], "dp", scatter_dimension=0, tiled=True),
        lax.psum_scatter(first_pass[8], "dp", scatter_dimension=0, tiled=True),
        lax.psum_scatter(first_pass[9], "dp", scatter_dimension=0, tiled=True),
        lax.psum_scatter(first_pass[10], "dp", scatter_dimension=0, tiled=True),
        lax.psum_scatter(first_pass[11], "dp", scatter_dimension=0, tiled=True),
        lax.psum_scatter(first_pass[12], "dp", scatter_dimension=0, tiled=True),
    )
    reduced = [unpack(member) for member in second_pass]
    return (
        layer_output,
        frames_grad,
        reduced[0],
        reduced[1],
        reduced[2],
        reduced[3],
        reduced[4],
        reduced[5],
        reduced[6],
        reduced[7],
        reduced[8],
        reduced[9],
        reduced[10],
        reduced[11],
        modulation_weight_grad,
        reduced[12],
    )


def hand_over_kernel(count, lengths, *refs):
    sources, refs = refs[: count + 2], refs[count + 2 :]
    targets, vectors, sems = refs[:count], refs[count:-1], refs[-1]
    copies = [
        pltpu.make_async_copy(sources[n], targets[n], sems.at[n]) for n in range(count)
    ]
    for copy in copies:
        copy.start()
    index = lax.axis_index("dp") * 4 + lax.axis_index("seq")
    sums, strip = sources[count], sources[count + 1]
    first = 0
    for vector, size in zip(vectors, lengths):
        start = index * size
        row = sums[pl.ds(first + start // LANES, 1), :]
        vector[...] = pltpu.roll(row, (LANES - start % LANES) % LANES, 1)[:, :size]
        first += size * lax.axis_size("dp") * 4 // LANES
    size = vectors[-1].shape[1]
    start = index * size
    wide = strip[0:1, pl.ds(pl.multiple_of(start // LANES * LANES, LANES), 2 * LANES)]
    vectors[-1][...] = pltpu.roll(wide, (2 * LANES - start % LANES) % (2 * LANES), 1)[:, :size]
    for copy in copies:
        copy.wait()


def hand_over(lengths, arrays, sums, strip):
    anywhere, vmem = pl.BlockSpec(memory_space=pl.ANY), pl.BlockSpec(memory_space=pltpu.VMEM)
    count = len(arrays)
    return pl.pallas_call(
        partial(hand_over_kernel, count, lengths[:-1]),
        out_shape=[jax.ShapeDtypeStruct(array.shape, array.dtype) for array in arrays]
        + [jax.ShapeDtypeStruct((1, size), F32) for size in lengths],
        in_specs=[vmem] * (count + 2),
        out_specs=[anywhere] * count + [vmem] * len(lengths),
        scratch_shapes=[pltpu.SemaphoreType.DMA((count,))],
    )(*arrays, sums, strip)


def on_device_fast(
    frames, output_gradient, segment_lengths, time_index, query_weight, query_bias, key_weight, key_bias,
    value_weight, value_bias, output_projection, output_bias, up_weight, up_bias, down_weight, down_bias,
    modulation_weight, modulation_bias,
):
    depth = lax.axis_size("dp") // 2
    _, span, width = frames.shape
    own_rows, hidden = up_weight.shape
    down_rows = down_weight.shape[0]
    vectors = (query_bias, key_bias, value_bias, output_bias, up_bias, down_bias, modulation_bias)
    biases = [vector.reshape(1, -1) for vector in vectors]
    (output, grad_middle, mg_in, bias_in, mods, low, gwo, gup, gdown, given_heads, qs, ks, vs, oh, lse, normed, wg,
     cosr, sinr) = forward_call(
        depth, span, own_rows, down_rows, hidden,
        (segment_lengths, time_index, frames[0], output_gradient[0], *biases, query_weight, key_weight, value_weight,
         output_projection, up_weight, down_weight, modulation_weight),
    )
    (fgrad, dwq, dwk, dwv, dwo, dup, ddown, dmw, mbias, btile) = backward_call(
        depth, span, own_rows, down_rows, hidden,
        (segment_lengths, given_heads, qs, ks, vs, oh, lse, normed, wg, cosr, sinr, low, mods, frames[0],
         grad_middle, mg_in, bias_in,
         gwo, gup, gdown),
    )
    lengths = tuple(vector.shape[0] for vector in vectors)
    output, fgrad, dwq, dwk, dwv, dwo, dup, ddown, dmw, *parts = hand_over(
        lengths, (output, fgrad, dwq, dwk, dwv, dwo, dup, ddown, dmw), btile, mbias
    )
    bq, bk, bv, bo, bu, bd, bm = [part.reshape(-1) for part in parts]
    return (
        output[None], fgrad[None], dwq, bq, dwk, bk, dwv, bv, dwo, bo, dup, bu, ddown, bd, dmw, bm,
    )


def fits(mesh, frames, *parameters):
    dp, seq = mesh.shape["dp"], mesh.shape["seq"]
    rows = parameters[3].shape[0] // (dp * seq)
    return seq == 4 and dp % 2 == 0 and rows == 32 and frames.shape[0] == dp


def solution(mesh):
    def run(*arrays):
        return mapped(mesh, on_device_fast if fits(mesh, *arrays) else on_device)(*arrays)

    return run


def mapped(mesh, body):
    return jax.shard_map(
        body,
        mesh=mesh,
        in_specs=(
            P("dp", "seq", None),
            P("dp", "seq", None),
            P("dp", None),
            P("dp", None),
            P(("dp", "seq"), None),
            P(("dp", "seq")),
            P(("dp", "seq"), None),
            P(("dp", "seq")),
            P(("dp", "seq"), None),
            P(("dp", "seq")),
            P(("dp", "seq"), None),
            P(("dp", "seq")),
            P(("dp", "seq"), None),
            P(("dp", "seq")),
            P(("dp", "seq"), None),
            P(("dp", "seq")),
            P(("dp", "seq"), None),
            P(("dp", "seq")),
        ),
        out_specs=(
            P("dp", "seq", None),
            P("dp", "seq", None),
            P(("dp", "seq"), None),
            P(("dp", "seq")),
            P(("dp", "seq"), None),
            P(("dp", "seq")),
            P(("dp", "seq"), None),
            P(("dp", "seq")),
            P(("dp", "seq"), None),
            P(("dp", "seq")),
            P(("dp", "seq"), None),
            P(("dp", "seq")),
            P(("dp", "seq"), None),
            P(("dp", "seq")),
            P(("dp", "seq"), None),
            P(("dp", "seq")),
        ),
        check_vma=False,
    )
```
